32 devices in a mesh: img: 4 (over y, x), sp: 8 (over z, core).
Axes of the slice: x: 2, y: 2, z: 4, core: 2. Of those that a mesh axis runs over, the one named last changes fastest.
Arguments:
- image_in: bfloat16 [4, 64, 64, 512], P('img', 'sp'), may hold values from -16 to 16
- time_embed: bfloat16 [4, 2048], P('img'), may hold values from -6 to 6
- caption: bfloat16 [4, 128, 2048], P('img'), may hold values from -6 to 6
- caption_mask: int32 [4, 128], P('img'), may hold values 0 or 1
- conv_in: bfloat16 [512, 3, 3, 512], P('img', None, None, 'sp'), may hold values from -0.09375 to 0.09375
- conv_out: bfloat16 [512, 3, 3, 512], P('img', None, None, 'sp'), may hold values from -0.09375 to 0.09375
- embed_proj: bfloat16 [2048, 1024], P('img', 'sp'), may hold values from -0.125 to 0.125
- qkv_proj: bfloat16 [512, 1536], P('img', 'sp'), may hold values from -0.25 to 0.25
- caption_proj: bfloat16 [2048, 1024], P('img', 'sp'), may hold values from -0.125 to 0.125
- out_proj: bfloat16 [512, 512], P('img', 'sp'), may hold values from -2 to 2
- norm_gains: bfloat16 [3, 512], P(None, 'img'), may hold values from 0.099609375 to 1.8984375
- norm_biases: bfloat16 [3, 512], P(None, 'img'), may hold values from -3 to 3
- cotangent: bfloat16 [4, 64, 64, 512], P('img', 'sp'), may hold values from -16 to 16
Outputs:
- output: bfloat16 [4, 64, 64, 512], P('img', 'sp')
- grad_image: float32 [4, 64, 64, 512], P('img', 'sp')
- grad_embed: float32 [4, 2048], P('img')
- grad_caption: float32 [4, 128, 2048], P('img', 'sp')
- grad_conv_in: float32 [512, 3, 3, 512], P('img', None, None, 'sp')
- grad_conv_out: float32 [512, 3, 3, 512], P('img', None, None, 'sp')
- grad_embed_proj: float32 [2048, 1024], P('img', 'sp')
- grad_qkv_proj: float32 [512, 1536], P('img', 'sp')
- grad_caption_proj: float32 [2048, 1024], P('img', 'sp')
- grad_out_proj: float32 [512, 512], P('img', 'sp')
- grad_norm_gains: float32 [3, 512], P(None, 'img')
- grad_norm_biases: float32 [3, 512], P(None, 'img')
The draws below stay inside these ranges and needn't reach their ends.
All inputs are finite; a program needn't handle non-finite values. No bound on the sum of `caption_mask` on one device may be relied on, other than what follows from the above.
Results may differ from the reference program's by a relative error of at most 0.011.
Values may be sent and summed in bfloat16 or wider, within the bound.
A program may use at most 256 MiB of HBM per device.

```python
import jax
import jax.numpy as jnp
from jax import lax

C = 512
HEADS = 8
HEAD_DIM = 64
GROUPS = 32
EMB = 2048
TEXT_WIDTH = 2048
TEXT_LEN = 128
H = 64
W = 64
IMAGES = 4


def shaped_field(base, channel_key, offset_key, rise, offset_size, channel_low, channel_high, ramp_size):
    row_place = jnp.arange(H, dtype=jnp.float32) / (H - 1)
    row_scale = jnp.exp(jnp.log(rise) * (row_place - 0.5))
    row_mean = ramp_size * (2.0 * row_place - 1.0)
    channel_scale = jnp.exp(jax.random.uniform(channel_key, (IMAGES, 1, 1, C), jnp.float32, jnp.log(channel_low), jnp.log(channel_high)))
    offsets = offset_size * jax.random.normal(offset_key, (IMAGES, 1, 1, C), jnp.float32)
    field_out = base * row_scale[None, :, None, None] * channel_scale + offsets + row_mean[None, :, None, None]
    return jnp.clip(field_out, -16.0, 16.0)


def draw_image_in(key, part):
    key = jax.random.fold_in(key, 5)
    base_key, channel_key, offset_key = jax.random.split(key, 3)
    base = jax.random.normal(base_key, (IMAGES, H, W, C), jnp.float32)
    field_out = shaped_field(base, channel_key, offset_key, 3.0, 0.5, 0.3, 3.0, 3.0)
    return field_out.astype(jnp.bfloat16)


def draw_cotangent(key, part):
    key = jax.random.fold_in(key, 9)
    base_key, channel_key, offset_key = jax.random.split(key, 3)
    base = jax.random.normal(base_key, (IMAGES, H, W, C), jnp.float32)
    field_out = shaped_field(base, channel_key, offset_key, 3.0, 0.2, 0.5, 2.0, 0.0)
    return field_out.astype(jnp.bfloat16)


def with_ends(drawn, own_key, least, high):
    index_at = [jax.random.randint(jax.random.fold_in(own_key, axis), (), 0, length) for axis, length in enumerate(drawn.shape)]
    widest = drawn.shape.index(max(drawn.shape))
    neighbour = index_at[:widest] + [(index_at[widest] + 1) % drawn.shape[widest]] + index_at[widest + 1:]
    return drawn.at[tuple(index_at)].set(least).at[tuple(neighbour)].set(high)


def block_scale(rng, dims, pieces, low, top_value):
    def one(dim, blocks):
        steps = jax.random.uniform(jax.random.fold_in(jax.random.fold_in(rng, 6), dim), (blocks,), jnp.float32, low / len(pieces), top_value / len(pieces))
        return jnp.repeat(jnp.exp(steps), dims[dim] // blocks).reshape((-1,) + (1,) * (len(dims) - dim - 1))

    factor_of = one(*pieces[0])
    for cut in pieces[1:]:
        factor_of = factor_of * one(*cut)
    return factor_of


def noise(own_key, extent, scale, most, pieces=(), kind=jnp.bfloat16):
    values = jax.random.normal(own_key, extent, jnp.float32) * scale
    if len(pieces) > 0:
        values = block_scale(own_key, extent, pieces, -0.22, 0.18) * values
    return jnp.clip(values, min=-most, max=most).astype(kind)


def setup_inputs(seed: int = 0) -> dict:
    streams_of = jax.random.split(jax.random.key(seed), 14)
    image_in = draw_image_in(jax.random.fold_in(streams_of[13], 71), 0)
    time_embed = noise(streams_of[1], (IMAGES, EMB), 1.0, 6.0, ((0, 4),))
    caption = noise(streams_of[2], (IMAGES, TEXT_LEN, TEXT_WIDTH), 1.0, 6.0, ((0, 4),))
    caption_mask = with_ends((jax.random.randint(streams_of[3], (IMAGES, TEXT_LEN), 0, 4) < 3).astype(jnp.int32), jax.random.fold_in(streams_of[3], 1), 0, 1)
    conv_in = noise(streams_of[4], (C, 3, 3, C), (9 * C) ** -0.5, 0.09375, ((0, 4), (3, 8)))
    conv_out = noise(streams_of[5], (C, 3, 3, C), (9 * C) ** -0.5, 0.09375, ((0, 4), (3, 8)))
    embed_proj = noise(streams_of[6], (EMB, 2 * C), EMB ** -0.5, 0.125, ((0, 4), (1, 8)))
    qkv_proj = noise(streams_of[7], (C, 3 * C), C ** -0.5, 0.25, ((0, 4), (1, 8)))
    caption_proj = noise(streams_of[8], (TEXT_WIDTH, 2 * C), TEXT_WIDTH ** -0.5, 0.125, ((0, 4), (1, 8)))
    out_proj = noise(streams_of[9], (C, C), (max(H * W // C, 1) ** 0.5 * C ** -0.5), 2.0, ((0, 4), (1, 8)))
    norm_gains = jnp.clip(1.0 + 0.18 * jax.random.normal(streams_of[10], (3, C), jnp.float32), 0.099609375, 1.8984375).astype(jnp.bfloat16)
    norm_biases = noise(streams_of[11], (3, C), 0.5, 3.0, ((1, 4),))
    cotangent = draw_cotangent(jax.random.fold_in(streams_of[13], 71), 0)
    return {"image_in": image_in, "time_embed": time_embed, "caption": caption, "caption_mask": caption_mask, "conv_in": conv_in, "conv_out": conv_out, "embed_proj": embed_proj, "qkv_proj": qkv_proj, "caption_proj": caption_proj, "out_proj": out_proj, "norm_gains": norm_gains, "norm_biases": norm_biases, "cotangent": cotangent}


EPSILON = 1e-05
PRECISE = lax.Precision.HIGHEST
MASKED = -1e+30

@jax.custom_vjp
def low(v):
    return lax.optimization_barrier(v.astype(jnp.bfloat16)).astype(jnp.float32)

@jax.custom_vjp
def low_back(v):
    return v

def low_keep(v):
    return (low(v), None)

def low_pass(kept, grad):
    return (grad,)

def back_keep(v):
    return (v, None)

def back_low(kept, grad):
    return (low(grad),)
low.defvjp(low_keep, low_pass)
low_back.defvjp(back_keep, back_low)

def sigmoid_linear(values):
    return values * jax.nn.sigmoid(values)

def group_norm(tensor, norm_gain, norm_bias):
    shape = tensor.shape
    grouped = tensor.reshape(shape[:-1] + (GROUPS, shape[-1] // GROUPS))
    center = lax.optimization_barrier(jnp.mean(grouped, axis=(1, 2, 4), keepdims=True))
    spread = lax.optimization_barrier(jnp.mean(jnp.square(grouped - center), axis=(1, 2, 4), keepdims=True))
    normed = (grouped - center) * lax.rsqrt(spread + EPSILON)
    return normed.reshape(shape) * norm_gain + norm_bias

def convolve(tensor, weight):
    return lax.conv_general_dilated(tensor, weight.transpose(1, 2, 0, 3), (1, 1), 'SAME', dimension_numbers=('NHWC', 'HWIO', 'NHWC'), precision=PRECISE)

def attend_image(queries, key_heads, value_heads, keep_mask):
    length_all = queries.shape[0]
    block_len = 512 if length_all % 512 == 0 else length_all

    @jax.checkpoint
    def one_block(carried, query_block):
        scores = jnp.einsum('qhd,khd->hqk', query_block, key_heads, precision=PRECISE) * HEAD_DIM ** (-0.5)
        scores = low_back(scores)
        scores = jnp.where(keep_mask[None, None, :], scores, MASKED)
        row_peak = lax.optimization_barrier(jnp.max(scores, axis=-1, keepdims=True))
        weights = jnp.exp(scores - row_peak)
        weights = low(weights / lax.optimization_barrier(jnp.sum(weights, axis=-1, keepdims=True)))
        return (carried, jnp.einsum('hqk,khd->qhd', weights, value_heads, precision=PRECISE))
    _, outputs = lax.scan(one_block, jnp.zeros((), jnp.float32), queries.reshape(length_all // block_len, block_len, HEADS, HEAD_DIM))
    return outputs.reshape(length_all, HEADS * HEAD_DIM)

def forward(image_in, time_embed, caption, caption_mask, conv_in, conv_out, embed_proj, qkv_proj, caption_proj, out_proj, norm_gains, norm_biases):
    images = image_in.shape[0]
    first_act = low(sigmoid_linear(group_norm(image_in, norm_gains[0], norm_biases[0])))
    hidden_one = low_back(convolve(first_act, conv_in))
    embedded = low(sigmoid_linear(time_embed))
    modulation = jnp.dot(embedded, embed_proj, precision=PRECISE)
    scale_term = modulation[:, None, None, :C]
    shift_term = modulation[:, None, None, C:]
    second_pre = group_norm(hidden_one, norm_gains[1], norm_biases[1]) * (1.0 + scale_term) + shift_term
    second_act = low(sigmoid_linear(second_pre))
    hidden_two = low_back(convolve(second_act, conv_out))
    residual = image_in + hidden_two
    normed = low(group_norm(residual, norm_gains[2], norm_biases[2])).reshape(images, H * W, C)
    projected = low_back(low(jnp.einsum('ntc,cd->ntd', normed, qkv_proj, precision=PRECISE)))
    caption_kv = low_back(low(jnp.einsum('nlc,cd->nld', caption, caption_proj, precision=PRECISE)))
    queries = projected[..., :C].reshape(images, H * W, HEADS, HEAD_DIM)
    key_heads = jnp.concatenate([caption_kv[..., :C], projected[..., C:2 * C]], axis=1).reshape(images, TEXT_LEN + H * W, HEADS, HEAD_DIM)
    value_heads = jnp.concatenate([caption_kv[..., C:], projected[..., 2 * C:]], axis=1).reshape(images, TEXT_LEN + H * W, HEADS, HEAD_DIM)
    keep_all = jnp.concatenate([caption_mask > 0, jnp.full((images, H * W), True)], axis=1)

    def per_image(members):
        return attend_image(members[0], members[1], members[2], members[3])
    attended = lax.map(per_image, (queries, key_heads, value_heads, keep_all))
    attended = low_back(low(attended))
    return residual + jnp.einsum('ntc,cd->ntd', attended, out_proj, precision=PRECISE).reshape(images, H, W, C)

def reference(image_in, time_embed, caption, caption_mask, conv_in, conv_out, embed_proj, qkv_proj, caption_proj, out_proj, norm_gains, norm_biases, cotangent):
    floats = [member.astype(jnp.float32) for member in (image_in, time_embed, caption, conv_in, conv_out, embed_proj, qkv_proj, caption_proj, out_proj, norm_gains, norm_biases)]

    def forward_all(*arrays):
        return forward(arrays[0], arrays[1], arrays[2], caption_mask, arrays[3], arrays[4], arrays[5], arrays[6], arrays[7], arrays[8], arrays[9], arrays[10])
    output, pullback = jax.vjp(forward_all, *floats)
    gradients = pullback(cotangent.astype(jnp.float32))
    return (output.astype(jnp.bfloat16), gradients[0], gradients[1], gradients[2], gradients[3], gradients[4], gradients[5], gradients[6], gradients[7], gradients[8], gradients[9], gradients[10])
```

```python
import jax
import jax.numpy as jnp
from jax import lax
from jax.sharding import PartitionSpec as P

HEADS = 8
GROUPS = 32
EPSILON = 1e-05
PRECISE = lax.Precision.HIGHEST
MASKED = -1e30
BF16 = jnp.bfloat16
F32 = jnp.float32


def dot(a, b, ca, cb):
    return lax.dot_general(a, b, (((ca,), (cb,)), ((), ())), preferred_element_type=F32)


def silu(v):
    return v * jax.nn.sigmoid(v)


def silu_slope(v):
    s = jax.nn.sigmoid(v)
    return s * (1.0 + v * (1.0 - s))


def gather(x, axis, dim):
    return lax.all_gather(x, axis, axis=dim, tiled=True)


def scatter_sum(x, axis, dim):
    return lax.psum_scatter(x, axis, scatter_dimension=dim, tiled=True)


def swap(x, axis, split, concat):
    return lax.all_to_all(x, axis, split, concat, tiled=True)


def halo(x):
    count = lax.axis_size("sp")
    above = lax.ppermute(x[:, -1:], "sp", [(i, i + 1) for i in range(count - 1)])
    below = lax.ppermute(x[:, :1], "sp", [(i + 1, i) for i in range(count - 1)])
    return above, below


def group_sum(v):
    c = v.shape[-1]
    g = v.reshape(v.shape[:-1] + (GROUPS, c // GROUPS))
    s = jnp.sum(g, axis=-1, keepdims=True)
    return jnp.broadcast_to(s, g.shape).reshape(v.shape)


def norm_stats(x):
    n, r, w, c = x.shape
    cells = r * w * (c // GROUPS)
    parts = lax.axis_size("sp")
    mean = group_sum(jnp.sum(x, axis=(1, 2))) / cells
    dev = group_sum(jnp.sum(jnp.square(x - mean[:, None, None, :]), axis=(1, 2)))
    both = lax.all_gather(jnp.stack([mean, dev]), "sp")
    means, devs = both[:, 0], both[:, 1]
    center = jnp.mean(means, axis=0)
    var = (jnp.sum(devs, axis=0) + cells * jnp.sum(jnp.square(means - center), axis=0)) / (
        cells * parts
    )
    return center, lax.rsqrt(var + EPSILON)


def hat_of(x, center, inverse):
    return (x - center[:, None, None, :]) * inverse[:, None, None, :]


def norm_back(u, hat, inverse, gain, sum_u, sum_uh, members):
    s1 = group_sum(sum_u * gain) / members
    s2 = group_sum(sum_uh * gain) / members
    return inverse[:, None, None, :] * (
        u * gain - s1[:, None, None, :] - hat * s2[:, None, None, :]
    )


def pad_cols(x):
    return jnp.pad(x, ((0, 0), (0, 0), (1, 1), (0, 0)))


def conv(padded, weight_t, transposed):
    n, rp, wp, c = padded.shape
    r, w = rp - 2, wp - 2
    total = None
    for i in range(3):
        for j in range(3):
            a = padded[:, i : i + r, j : j + w].reshape(n * r * w, c)
            part = dot(a, weight_t[2 - i, 2 - j], 1, 0) if transposed else dot(a, weight_t[i, j], 1, 1)
            total = part if total is None else total + part
    return total.reshape(n, r, w, -1)


def conv_grad(padded, g):
    n, r, w, c = g.shape
    gf = g.reshape(n * r * w, c)
    rows = []
    for i in range(3):
        for j in range(3):
            a = padded[:, i : i + r, j : j + w].reshape(n * r * w, -1)
            rows.append(dot(gf, a, 0, 0))
    return jnp.stack(rows).reshape(3, 3, c, -1)


def to_pairs(x, images):
    n, px, h, d = x.shape
    y = x.transpose(0, 2, 1, 3).reshape(n * h, px, d)
    return swap(y, "sp", 0, 1)


def from_pairs(x, images):
    y = swap(x, "sp", 1, 0)
    return y.reshape(images, HEADS, y.shape[1], y.shape[2]).transpose(0, 2, 1, 3)


def attention(q, k, v, g, tk, tv, keep, scale):
    p, length, d = q.shape
    block = min(512, length)
    keys = jnp.concatenate([tk, k], axis=1)
    values = jnp.concatenate([tv, v], axis=1)
    text = tk.shape[1]
    keep_all = jnp.concatenate([keep, jnp.ones((p, length), bool)], axis=1)

    def step(carry, blk):
        dk, dv = carry
        qb, gb = blk
        s = jnp.einsum("pqd,pkd->pqk", qb, keys, preferred_element_type=F32) * scale
        s = jnp.where(keep_all[:, None, :], s, MASKED)
        peak = jnp.max(s, axis=-1, keepdims=True)
        e = jnp.exp(s - peak)
        prob = e / jnp.sum(e, axis=-1, keepdims=True)
        pb = prob.astype(BF16)
        o = jnp.einsum("pqk,pkd->pqd", pb, values, preferred_element_type=F32)
        row = jnp.sum(o * gb.astype(F32), axis=-1, keepdims=True)
        dp = jnp.einsum("pqd,pkd->pqk", gb, values, preferred_element_type=F32)
        ds = (prob * (dp - row)).astype(BF16)
        dq = jnp.einsum("pqk,pkd->pqd", ds, keys, preferred_element_type=F32) * scale
        dk = dk + jnp.einsum("pqk,pqd->pkd", ds, qb, preferred_element_type=F32)
        dv = dv + jnp.einsum("pqk,pqd->pkd", pb, gb, preferred_element_type=F32)
        return (dk, dv), (o.astype(BF16), dq.astype(BF16))

    zeros = jnp.zeros((p, text + length, d), F32)
    cut = lambda t: t.reshape(p, length // block, block, d).swapaxes(0, 1)
    (dk, dv), (o, dq) = lax.scan(step, (zeros, zeros), (cut(q), cut(g)))
    join = lambda t: t.swapaxes(0, 1).reshape(p, length, d)
    dk = (dk * scale).astype(BF16)
    dv = dv.astype(BF16)
    return join(o), join(dq), dk[:, text:], dv[:, text:], dk[:, :text], dv[:, :text]


def body(
    image_in, time_embed, caption, caption_mask, conv_in, conv_out, embed_proj, qkv_proj,
    caption_proj, out_proj, norm_gains, norm_biases, cotangent,
):
    n, rows, width, chans = image_in.shape
    n_img, n_sp = lax.axis_size("img"), lax.axis_size("sp")
    img, sp = lax.axis_index("img"), lax.axis_index("sp")
    px = rows * width
    members = px * n_sp * (chans // GROUPS)
    d = chans // HEADS
    scale = d ** -0.5
    pairs = n * HEADS // n_sp

    def whole(w):
        w = gather(w, "img", w.ndim - 1)
        return gather(w, "sp", w.ndim - 2)

    w_in = whole(conv_in.transpose(1, 2, 3, 0))
    w_out = whole(conv_out.transpose(1, 2, 3, 0))
    w_qkv = whole(qkv_proj.T)
    w_proj = whole(out_proj.T)
    affine = gather(jnp.concatenate([norm_gains, norm_biases]), "img", 1).astype(F32)
    gains, biases = affine[:3], affine[3:]

    embedded = silu(time_embed.astype(F32)).astype(BF16)
    emb_all = swap(embedded, "img", 1, 0)
    mod = scatter_sum(jnp.dot(emb_all, embed_proj, preferred_element_type=F32), "img", 0)
    mod = gather(mod, "sp", 1)
    scale_term, shift_term = mod[:, :chans], mod[:, chans:]
    cap_all = swap(caption, "img", 2, 0)
    cap_flat = cap_all.reshape(-1, cap_all.shape[2])
    kv = jnp.dot(cap_flat, caption_proj, preferred_element_type=F32)
    kv = scatter_sum(kv.reshape(cap_all.shape[0], cap_all.shape[1], -1), "img", 0).astype(BF16)
    kv = gather(kv, "sp", 2)
    text = kv.shape[1]
    kv_heads = kv.reshape(n, text, 2, HEADS, d).transpose(2, 0, 3, 1, 4).reshape(2, n * HEADS, text, d)
    mine = lax.dynamic_slice_in_dim(kv_heads, sp * pairs, pairs, 1)
    keep = jnp.repeat(caption_mask > 0, HEADS, axis=0)
    keep = lax.dynamic_slice_in_dim(keep, sp * pairs, pairs, 0)

    image_f = image_in.astype(F32)
    c0, i0 = norm_stats(image_f)
    hat0 = hat_of(image_f, c0, i0)
    first = hat0 * gains[0] + biases[0]
    act0 = silu(first).astype(BF16)
    above, below = halo(act0)
    pad0 = pad_cols(jnp.concatenate([above, act0, below], axis=1))
    hidden = conv(pad0, w_in, False)
    c1, i1 = norm_stats(hidden)
    hat1 = hat_of(hidden, c1, i1)
    second = hat1 * gains[1] + biases[1]
    pre = second * (1.0 + scale_term[:, None, None, :]) + shift_term[:, None, None, :]
    act1 = silu(pre).astype(BF16)
    above, below = halo(act1)
    pad1 = pad_cols(jnp.concatenate([above, act1, below], axis=1))
    residual = image_f + conv(pad1, w_out, False)
    c2, i2 = norm_stats(residual)
    hat2 = hat_of(residual, c2, i2)
    normed = (hat2 * gains[2] + biases[2]).astype(BF16).reshape(n * px, chans)
    qkv = dot(normed, w_qkv, 1, 1).astype(BF16)
    cot = cotangent.reshape(n * px, chans)
    g_att = dot(cot, w_proj, 1, 0).astype(BF16)
    four = jnp.concatenate([qkv, g_att], axis=1).reshape(n, px, 4, HEADS, d)
    packed = to_pairs(four.transpose(0, 1, 3, 2, 4).reshape(n, px, HEADS, 4 * d), n)
    q, k, v, g = (packed[..., j * d : (j + 1) * d] for j in range(4))
    o, dq, dk, dv, dtk, dtv = attention(q, k, v, g, mine[0], mine[1], keep, scale)
    back = from_pairs(jnp.concatenate([o, dq, dk, dv], axis=-1), n)
    back = back.reshape(n * px, HEADS, 4, d).transpose(0, 2, 1, 3).reshape(n * px, 4 * chans)
    attended, proj_grad = back[:, :chans], back[:, chans:]
    output = residual + dot(attended, w_proj, 1, 1).reshape(image_in.shape)

    grad_out = dot(cot, attended, 0, 0)
    grad_qkv = dot(proj_grad, normed, 0, 0)
    normed_grad = dot(proj_grad, w_qkv, 1, 0).reshape(image_in.shape)

    def sums(u, hat):
        both = jnp.stack([jnp.sum(u, axis=(1, 2)), jnp.sum(u * hat, axis=(1, 2))])
        return lax.psum(both, "sp")

    su2, sh2 = sums(normed_grad, hat2)
    residual_grad = cotangent.astype(F32) + norm_back(
        normed_grad, hat2, i2, gains[2], su2, sh2, members
    )
    g2 = residual_grad.astype(BF16)
    above, below = halo(g2)
    gpad = pad_cols(jnp.concatenate([above, g2, below], axis=1))
    grad_conv_out = conv_grad(pad1, g2)
    pre_grad = conv(gpad, w_out, True) * silu_slope(pre)
    sa, sb = sums(pre_grad, hat1)
    fac = 1.0 + scale_term
    shift_grad = sa
    scale_grad = sb * gains[1] + sa * biases[1]
    u1 = pre_grad * fac[:, None, None, :]
    su1, sh1 = sa * fac, sb * fac
    g1 = norm_back(u1, hat1, i1, gains[1], su1, sh1, members).astype(BF16)
    above, below = halo(g1)
    gpad = pad_cols(jnp.concatenate([above, g1, below], axis=1))
    grad_conv_in = conv_grad(pad0, g1)
    u0 = conv(gpad, w_in, True) * silu_slope(first)
    su0, sh0 = sums(u0, hat0)
    grad_image = residual_grad + norm_back(u0, hat0, i0, gains[0], su0, sh0, members)

    mod_grad = jnp.concatenate([scale_grad, shift_grad], axis=1)
    cols = embed_proj.shape[1]
    mod_all = gather(mod_grad, "img", 0)
    mod_cols = lax.dynamic_slice_in_dim(mod_all, sp * cols, cols, 1)
    grad_embed_proj = jnp.einsum("ne,nd->ed", emb_all.astype(F32), mod_cols, precision=PRECISE)
    part = jnp.einsum("nd,ed->ne", mod_cols, embed_proj.astype(F32), precision=PRECISE)
    part = swap(lax.psum(part, "sp"), "img", 0, 1)
    grad_embed = part * silu_slope(time_embed.astype(F32))

    tg = gather(jnp.stack([dtk, dtv]), "sp", 1).reshape(2, n, HEADS, text, d)
    tg = tg.transpose(1, 3, 0, 2, 4).reshape(n, text, 2 * chans)
    cols = caption_proj.shape[1]
    tg = gather(lax.dynamic_slice_in_dim(tg, sp * cols, cols, 2), "img", 0).reshape(-1, cols)
    grad_caption_proj = dot(cap_flat, tg, 0, 0)
    gc = dot(tg, caption_proj, 1, 1).reshape(cap_all.shape)
    gc = scatter_sum(gc, "sp", 1)
    grad_caption = swap(gc, "img", 0, 2)

    grads = jnp.concatenate(
        [jnp.sum(t, axis=0)[None] for t in (sh0, sh1, sh2, su0, su1, su2)]
    )
    grads = scatter_sum(grads, "img", 1)

    def shared(w):
        w = scatter_sum(w, "sp", w.ndim - 2)
        return scatter_sum(w, "img", w.ndim - 1)

    return (
        output.astype(BF16),
        grad_image,
        grad_embed,
        grad_caption,
        shared(grad_conv_in).transpose(3, 0, 1, 2),
        shared(grad_conv_out).transpose(3, 0, 1, 2),
        grad_embed_proj,
        shared(grad_qkv).T,
        grad_caption_proj,
        shared(grad_out).T,
        grads[:3],
        grads[3:],
    )


def solution(mesh):
    rows = P("img", "sp", None, None)
    kernel = P("img", None, None, "sp")
    flat = P("img", "sp")
    return jax.shard_map(
        body,
        mesh=mesh,
        in_specs=(
            rows, P("img", None), P("img", None, None), P("img", None), kernel, kernel,
            flat, flat, flat, flat, P(None, "img"), P(None, "img"), rows,
        ),
        out_specs=(
            rows, rows, P("img", None), P("img", "sp", None), kernel, kernel,
            flat, flat, flat, flat, P(None, "img"), P(None, "img"),
        ),
        check_vma=False,
    )
```

```python
import functools

import jax
import jax.numpy as jnp
from jax import lax
from jax.experimental import pallas as pl
from jax.experimental.pallas import tpu as pltpu
from jax.sharding import PartitionSpec as P

HEADS = 8
GROUPS = 32
EPSILON = 1e-05
PRECISE = lax.Precision.HIGHEST
MASKED = -1e30
BF16 = jnp.bfloat16
F32 = jnp.float32
MESH = pl.DeviceIdType.MESH
VMEM_BYTES = 60 * 1024 * 1024


def dot(a, b, ca, cb):
    return lax.dot_general(a, b, (((ca,), (cb,)), ((), ())), preferred_element_type=F32)


def silu(v):
    return v * jax.nn.sigmoid(v)


def silu_slope(v):
    s = jax.nn.sigmoid(v)
    return s * (1.0 + v * (1.0 - s))


def gather(x, axis, dim):
    return lax.all_gather(x, axis, axis=dim, tiled=True)


def scatter_sum(x, axis, dim):
    return lax.psum_scatter(x, axis, scatter_dimension=dim, tiled=True)


def swap(x, axis, split, concat):
    return lax.all_to_all(x, axis, split, concat, tiled=True)


def halo(x):
    count = lax.axis_size("sp")
    above = lax.ppermute(x[:, -1:], "sp", [(i, i + 1) for i in range(count - 1)])
    below = lax.ppermute(x[:, :1], "sp", [(i + 1, i) for i in range(count - 1)])
    return above, below


def group_sum(v):
    c = v.shape[-1]
    g = v.reshape(v.shape[:-1] + (GROUPS, c // GROUPS))
    s = jnp.sum(g, axis=-1, keepdims=True)
    return jnp.broadcast_to(s, g.shape).reshape(v.shape)


def norm_stats(x):
    n, r, w, c = x.shape
    cells = r * w * (c // GROUPS)
    parts = lax.axis_size("sp")
    mean = group_sum(jnp.sum(x, axis=(1, 2))) / cells
    dev = group_sum(jnp.sum(jnp.square(x - mean[:, None, None, :]), axis=(1, 2)))
    both = lax.all_gather(jnp.stack([mean, dev]), "sp")
    means, devs = both[:, 0], both[:, 1]
    center = jnp.mean(means, axis=0)
    var = (jnp.sum(devs, axis=0) + cells * jnp.sum(jnp.square(means - center), axis=0)) / (
        cells * parts
    )
    return center, lax.rsqrt(var + EPSILON)


def hat_of(x, center, inverse):
    return (x - center[:, None, None, :]) * inverse[:, None, None, :]


def norm_back(u, hat, inverse, gain, sum_u, sum_uh, members):
    s1 = group_sum(sum_u * gain) / members
    s2 = group_sum(sum_uh * gain) / members
    return inverse[:, None, None, :] * (
        u * gain - s1[:, None, None, :] - hat * s2[:, None, None, :]
    )


def pad_cols(x):
    return jnp.pad(x, ((0, 0), (0, 0), (1, 1), (0, 0)))


def conv(padded, weight_t, transposed):
    n, rp, wp, c = padded.shape
    r, w = rp - 2, wp - 2
    total = None
    for i in range(3):
        for j in range(3):
            a = padded[:, i : i + r, j : j + w].reshape(n * r * w, c)
            part = dot(a, weight_t[2 - i, 2 - j], 1, 0) if transposed else dot(a, weight_t[i, j], 1, 1)
            total = part if total is None else total + part
    return total.reshape(n, r, w, -1)


def conv_grad(padded, g):
    n, r, w, c = g.shape
    gf = g.reshape(n * r * w, c)
    rows = []
    for i in range(3):
        for j in range(3):
            a = padded[:, i : i + r, j : j + w].reshape(n * r * w, -1)
            rows.append(dot(gf, a, 0, 0))
    return jnp.stack(rows).reshape(3, 3, c, -1)


def to_pairs(x, images):
    n, px, h, d = x.shape
    y = x.transpose(0, 2, 1, 3).reshape(n * h, px, d)
    return swap(y, "sp", 0, 1)


def from_pairs(x, images):
    y = swap(x, "sp", 1, 0)
    return y.reshape(images, HEADS, y.shape[1], y.shape[2]).transpose(0, 2, 1, 3)


def attention_plain(q, k, v, g, tk, tv, keep, scale):
    p, length, d = q.shape
    block = min(512, length)
    keys = jnp.concatenate([tk, k], axis=1)
    values = jnp.concatenate([tv, v], axis=1)
    text = tk.shape[1]
    keep_all = jnp.concatenate([keep, jnp.ones((p, length), bool)], axis=1)

    def step(carry, blk):
        dk, dv = carry
        qb, gb = blk
        s = jnp.einsum("pqd,pkd->pqk", qb, keys, preferred_element_type=F32) * scale
        s = jnp.where(keep_all[:, None, :], s, MASKED)
        peak = jnp.max(s, axis=-1, keepdims=True)
        e = jnp.exp(s - peak)
        prob = e / jnp.sum(e, axis=-1, keepdims=True)
        pb = prob.astype(BF16)
        o = jnp.einsum("pqk,pkd->pqd", pb, values, preferred_element_type=F32)
        row = jnp.sum(o * gb.astype(F32), axis=-1, keepdims=True)
        dp = jnp.einsum("pqd,pkd->pqk", gb, values, preferred_element_type=F32)
        ds = (prob * (dp - row)).astype(BF16)
        dq = jnp.einsum("pqk,pkd->pqd", ds, keys, preferred_element_type=F32) * scale
        dk = dk + jnp.einsum("pqk,pqd->pkd", ds, qb, preferred_element_type=F32)
        dv = dv + jnp.einsum("pqk,pqd->pkd", pb, gb, preferred_element_type=F32)
        return (dk, dv), (o.astype(BF16), dq.astype(BF16))

    zeros = jnp.zeros((p, text + length, d), F32)
    cut = lambda t: t.reshape(p, length // block, block, d).swapaxes(0, 1)
    (dk, dv), (o, dq) = lax.scan(step, (zeros, zeros), (cut(q), cut(g)))
    join = lambda t: t.swapaxes(0, 1).reshape(p, length, d)
    dk = (dk * scale).astype(BF16)
    dv = dv.astype(BF16)
    return join(o), join(dq), dk[:, text:], dv[:, text:], dk[:, :text], dv[:, :text]


def plain_body(
    image_in, time_embed, caption, caption_mask, conv_in, conv_out, embed_proj, qkv_proj,
    caption_proj, out_proj, norm_gains, norm_biases, cotangent,
):
    n, rows, width, chans = image_in.shape
    n_img, n_sp = lax.axis_size("img"), lax.axis_size("sp")
    img, sp = lax.axis_index("img"), lax.axis_index("sp")
    px = rows * width
    members = px * n_sp * (chans // GROUPS)
    d = chans // HEADS
    scale = d ** -0.5
    pairs = n * HEADS // n_sp

    def whole(w):
        w = gather(w, "img", w.ndim - 1)
        return gather(w, "sp", w.ndim - 2)

    w_in = whole(conv_in.transpose(1, 2, 3, 0))
    w_out = whole(conv_out.transpose(1, 2, 3, 0))
    w_qkv = whole(qkv_proj.T)
    w_proj = whole(out_proj.T)
    affine = gather(jnp.concatenate([norm_gains, norm_biases]), "img", 1).astype(F32)
    gains, biases = affine[:3], affine[3:]

    embedded = silu(time_embed.astype(F32)).astype(BF16)
    emb_all = swap(embedded, "img", 1, 0)
    mod = scatter_sum(jnp.dot(emb_all, embed_proj, preferred_element_type=F32), "img", 0)
    mod = gather(mod, "sp", 1)
    scale_term, shift_term = mod[:, :chans], mod[:, chans:]
    cap_all = swap(caption, "img", 2, 0)
    cap_flat = cap_all.reshape(-1, cap_all.shape[2])
    kv = jnp.dot(cap_flat, caption_proj, preferred_element_type=F32)
    kv = scatter_sum(kv.reshape(cap_all.shape[0], cap_all.shape[1], -1), "img", 0).astype(BF16)
    kv = gather(kv, "sp", 2)
    text = kv.shape[1]
    kv_heads = kv.reshape(n, text, 2, HEADS, d).transpose(2, 0, 3, 1, 4).reshape(2, n * HEADS, text, d)
    mine = lax.dynamic_slice_in_dim(kv_heads, sp * pairs, pairs, 1)
    keep = jnp.repeat(caption_mask > 0, HEADS, axis=0)
    keep = lax.dynamic_slice_in_dim(keep, sp * pairs, pairs, 0)

    image_f = image_in.astype(F32)
    c0, i0 = norm_stats(image_f)
    hat0 = hat_of(image_f, c0, i0)
    first = hat0 * gains[0] + biases[0]
    act0 = silu(first).astype(BF16)
    above, below = halo(act0)
    pad0 = pad_cols(jnp.concatenate([above, act0, below], axis=1))
    hidden = conv(pad0, w_in, False)
    c1, i1 = norm_stats(hidden)
    hat1 = hat_of(hidden, c1, i1)
    second = hat1 * gains[1] + biases[1]
    pre = second * (1.0 + scale_term[:, None, None, :]) + shift_term[:, None, None, :]
    act1 = silu(pre).astype(BF16)
    above, below = halo(act1)
    pad1 = pad_cols(jnp.concatenate([above, act1, below], axis=1))
    residual = image_f + conv(pad1, w_out, False)
    c2, i2 = norm_stats(residual)
    hat2 = hat_of(residual, c2, i2)
    normed = (hat2 * gains[2] + biases[2]).astype(BF16).reshape(n * px, chans)
    qkv = dot(normed, w_qkv, 1, 1).astype(BF16)
    cot = cotangent.reshape(n * px, chans)
    g_att = dot(cot, w_proj, 1, 0).astype(BF16)
    four = jnp.concatenate([qkv, g_att], axis=1).reshape(n, px, 4, HEADS, d)
    packed = to_pairs(four.transpose(0, 1, 3, 2, 4).reshape(n, px, HEADS, 4 * d), n)
    q, k, v, g = (packed[..., j * d : (j + 1) * d] for j in range(4))
    o, dq, dk, dv, dtk, dtv = attention_plain(q, k, v, g, mine[0], mine[1], keep, scale)
    back = from_pairs(jnp.concatenate([o, dq, dk, dv], axis=-1), n)
    back = back.reshape(n * px, HEADS, 4, d).transpose(0, 2, 1, 3).reshape(n * px, 4 * chans)
    attended, proj_grad = back[:, :chans], back[:, chans:]
    output = residual + dot(attended, w_proj, 1, 1).reshape(image_in.shape)

    grad_out = dot(cot, attended, 0, 0)
    grad_qkv = dot(proj_grad, normed, 0, 0)
    normed_grad = dot(proj_grad, w_qkv, 1, 0).reshape(image_in.shape)

    def sums(u, hat):
        both = jnp.stack([jnp.sum(u, axis=(1, 2)), jnp.sum(u * hat, axis=(1, 2))])
        return lax.psum(both, "sp")

    su2, sh2 = sums(normed_grad, hat2)
    residual_grad = cotangent.astype(F32) + norm_back(
        normed_grad, hat2, i2, gains[2], su2, sh2, members
    )
    g2 = residual_grad.astype(BF16)
    above, below = halo(g2)
    gpad = pad_cols(jnp.concatenate([above, g2, below], axis=1))
    grad_conv_out = conv_grad(pad1, g2)
    pre_grad = conv(gpad, w_out, True) * silu_slope(pre)
    sa, sb = sums(pre_grad, hat1)
    fac = 1.0 + scale_term
    shift_grad = sa
    scale_grad = sb * gains[1] + sa * biases[1]
    u1 = pre_grad * fac[:, None, None, :]
    su1, sh1 = sa * fac, sb * fac
    g1 = norm_back(u1, hat1, i1, gains[1], su1, sh1, members).astype(BF16)
    above, below = halo(g1)
    gpad = pad_cols(jnp.concatenate([above, g1, below], axis=1))
    grad_conv_in = conv_grad(pad0, g1)
    u0 = conv(gpad, w_in, True) * silu_slope(first)
    su0, sh0 = sums(u0, hat0)
    grad_image = residual_grad + norm_back(u0, hat0, i0, gains[0], su0, sh0, members)

    mod_grad = jnp.concatenate([scale_grad, shift_grad], axis=1)
    cols = embed_proj.shape[1]
    mod_all = gather(mod_grad, "img", 0)
    mod_cols = lax.dynamic_slice_in_dim(mod_all, sp * cols, cols, 1)
    grad_embed_proj = jnp.einsum("ne,nd->ed", emb_all.astype(F32), mod_cols, precision=PRECISE)
    part = jnp.einsum("nd,ed->ne", mod_cols, embed_proj.astype(F32), precision=PRECISE)
    part = swap(lax.psum(part, "sp"), "img", 0, 1)
    grad_embed = part * silu_slope(time_embed.astype(F32))

    tg = gather(jnp.stack([dtk, dtv]), "sp", 1).reshape(2, n, HEADS, text, d)
    tg = tg.transpose(1, 3, 0, 2, 4).reshape(n, text, 2 * chans)
    cols = caption_proj.shape[1]
    tg = gather(lax.dynamic_slice_in_dim(tg, sp * cols, cols, 2), "img", 0).reshape(-1, cols)
    grad_caption_proj = dot(cap_flat, tg, 0, 0)
    gc = dot(tg, caption_proj, 1, 1).reshape(cap_all.shape)
    gc = scatter_sum(gc, "sp", 1)
    grad_caption = swap(gc, "img", 0, 2)

    grads = jnp.concatenate(
        [jnp.sum(t, axis=0)[None] for t in (sh0, sh1, sh2, su0, su1, su2)]
    )
    grads = scatter_sum(grads, "img", 1)

    def shared(w):
        w = scatter_sum(w, "sp", w.ndim - 2)
        return scatter_sum(w, "img", w.ndim - 1)

    return (
        output.astype(BF16),
        grad_image,
        grad_embed,
        grad_caption,
        shared(grad_conv_in).transpose(3, 0, 1, 2),
        shared(grad_conv_out).transpose(3, 0, 1, 2),
        grad_embed_proj,
        shared(grad_qkv).T,
        grad_caption_proj,
        shared(grad_out).T,
        grads[:3],
        grads[3:],
    )


class Place:
    def __init__(self):
        self.i = lax.axis_index("img")
        self.s = lax.axis_index("sp")
        self.z = lax.div(self.s, 2)
        self.c = lax.rem(self.s, 2)
        x = lax.rem(self.i, 2)
        y = lax.div(self.i, 2)
        self.ix = self.i + 1 - 2 * x
        self.iy = self.i + 2 - 4 * y
        self.id = 3 - self.i
        self.sib = (self.i, self.s + 1 - 2 * self.c)
        self.xn = (self.ix, self.s)
        self.yn = (self.iy, self.s)

    def zp(self, k, nz):
        return (self.i, 2 * lax.rem(self.z + k, nz) + self.c)

    def rp(self, k, n_sp):
        return (self.i, lax.rem(self.s + k, n_sp))


def greet(peers):
    bar = pltpu.get_barrier_semaphore()
    for p in peers:
        pl.semaphore_signal(bar, inc=1, device_id=p, device_id_type=MESH)


def greeted(count):
    pl.semaphore_wait(pltpu.get_barrier_semaphore(), count)


def remote(src, dst, ssem, rsem, dev):
    cp = pltpu.make_async_remote_copy(
        src_ref=src, dst_ref=dst, send_sem=ssem, recv_sem=rsem, device_id=dev, device_id_type=MESH
    )
    cp.start()
    return cp


def params(cid=None, grid=0):
    extra = {} if cid is None else {"collective_id": cid, "has_side_effects": True}
    if grid:
        extra["dimension_semantics"] = ("arbitrary",) * grid
    return pltpu.CompilerParams(vmem_limit_bytes=VMEM_BYTES, **extra)


ANY = pl.BlockSpec(memory_space=pl.ANY)
VM = pl.BlockSpec(memory_space=pltpu.VMEM)
def trade_kernel(n_sp, na, *refs):
    ins, outs = refs[: na + 1], refs[na + 1 : 2 * na + 2]
    ssem, rsem, lsem = refs[2 * na + 2 :]
    at = Place()
    peers = [at.rp(k, n_sp) for k in range(1, n_sp)]
    greet(peers)
    local = [pltpu.make_async_copy(ins[a].at[at.s], outs[a].at[at.s], lsem.at[a]) for a in range(na)]
    local.append(pltpu.make_async_copy(ins[na], outs[na].at[at.s], lsem.at[na]))
    for cp in local:
        cp.start()
    greeted(len(peers))
    sent = []
    for k in range(1, n_sp):
        dev = at.rp(k, n_sp)
        for a in range(na):
            sent.append(remote(ins[a].at[dev[1]], outs[a].at[at.s], ssem.at[a, k], rsem.at[a, k], dev))
        sent.append(remote(ins[na], outs[na].at[at.s], ssem.at[na, k], rsem.at[na, k], dev))
    for cp in local:
        cp.wait()
    for cp in sent:
        cp.wait()


def trade(parts, common, n_sp, cid):
    na = len(parts)
    shapes = [p.shape for p in parts] + [(n_sp,) + common.shape]
    return pl.pallas_call(
        functools.partial(trade_kernel, n_sp, na),
        out_shape=[jax.ShapeDtypeStruct(s, BF16) for s in shapes],
        in_specs=[ANY] * (na + 1),
        out_specs=[ANY] * (na + 1),
        scratch_shapes=[
            pltpu.SemaphoreType.DMA((na + 1, n_sp)),
            pltpu.SemaphoreType.DMA((na + 1, n_sp)),
            pltpu.SemaphoreType.DMA((na + 1,)),
        ],
        compiler_params=params(cid),
        name="trade",
    )(*parts, common)


def exchange_scratch(n_sp, width, halo_types, chans):
    out = [pltpu.VMEM((8, chans), F32), pltpu.VMEM((n_sp, 8, chans), F32)]
    for ty in halo_types:
        out += [pltpu.VMEM((width, chans), ty), pltpu.VMEM((width, chans), ty)]
    count = n_sp - 1 + 2 * len(halo_types)
    return out + [pltpu.SemaphoreType.DMA((count,)), pltpu.SemaphoreType.DMA((count,))]


def exchange_greet(n_sp):
    at = Place()
    greet([at.rp(k, n_sp) for k in range(1, n_sp)])


def exchange(n_sp, width, scratch, edges):
    at = Place()
    mine, every = scratch[0], scratch[1]
    ssem, rsem = scratch[-2:]
    greeted(n_sp - 1)
    sent = []
    for e, ref in enumerate(edges):
        above, below = scratch[2 + 2 * e], scratch[3 + 2 * e]
        px = ref.shape[0]
        j = n_sp - 1 + 2 * e
        sent.append(remote(ref.at[px - width :], above, ssem.at[j], rsem.at[j], at.rp(1, n_sp)))
        sent.append(remote(ref.at[:width], below, ssem.at[j + 1], rsem.at[j + 1], at.rp(n_sp - 1, n_sp)))
    for k in range(1, n_sp):
        sent.append(remote(mine, every.at[at.s], ssem.at[k - 1], rsem.at[k - 1], at.rp(k, n_sp)))
    every[at.s] = mine[...]
    for cp in sent:
        cp.wait()


def channel_stats(mine, v):
    mean = jnp.sum(v, axis=0, keepdims=True) / v.shape[0]
    dev = v - mean
    mine[0:1, :] = mean
    mine[1:2, :] = jnp.sum(dev * dev, axis=0, keepdims=True)


def group_total(rows):
    c = rows.shape[1]
    size = c // GROUPS
    a = lax.broadcasted_iota(jnp.int32, (c, c), 0)
    b = lax.broadcasted_iota(jnp.int32, (c, c), 1)
    same = jnp.where(lax.div(a, size) == lax.div(b, size), 1.0, 0.0)
    return lax.dot_general(
        rows, same, (((1,), (0,)), ((), ())), preferred_element_type=F32, precision=PRECISE
    )


def combine_stats(every, px):
    n_sp, _, c = every.shape
    size = c // GROUPS
    means = [every[j, 0:1, :] for j in range(n_sp)]
    center_c = sum(means) / n_sp
    dev = sum(every[j, 1:2, :] for j in range(n_sp))
    dev = dev + px * sum((m - center_c) * (m - center_c) for m in means)
    center = group_total(jnp.broadcast_to(center_c, (8, c)))[0:1] / size
    off = center_c - center
    dev = dev + (px * n_sp) * (off * off)
    var = group_total(jnp.broadcast_to(dev, (8, c)))[0:1] / (px * n_sp * size)
    return center, lax.rsqrt(var + EPSILON)


def combine_sums(every):
    n_sp = every.shape[0]
    total = every[0]
    for j in range(1, n_sp):
        total = total + every[j]
    return total


def edge_flags(n_sp, s):
    return jnp.where(s > 0, 1.0, 0.0), jnp.where(s < n_sp - 1, 1.0, 0.0)


def shifted(dst, row, width, block):
    col = lax.broadcasted_iota(jnp.int32, block.shape, 0)
    r = slice(row * width, (row + 1) * width)
    dst[1, r, :] = block.astype(BF16)
    dst[0, r, :] = jnp.where(col == 0, 0.0, pltpu.roll(block, 1, 0)).astype(BF16)
    dst[2, r, :] = jnp.where(col == width - 1, 0.0, pltpu.roll(block, width - 1, 0)).astype(BF16)


def joined(w_ref, *lead):
    return jnp.concatenate([w_ref[(j,) + lead] for j in range(4)], axis=-1)


def conv_kernel(n_sp, width, refs_in, x, up, dn, every, rows, w, *rest):
    base = None
    if refs_in:
        base, rest = rest[0], rest[1:]
    out, act, stats, above, below, a3 = rest[:6]
    scratch = rest[6:]
    step = pl.program_id(0)
    px, c = out.shape
    height = px // width

    @pl.when(step == 0)
    def _():
        exchange_greet(n_sp)
        center, inverse = combine_stats(every, px)
        mul = inverse * rows[0:1, :] * rows[2:3, :]
        add = rows[1:2, :] * rows[2:3, :] + rows[3:4, :]
        has_up, has_dn = edge_flags(n_sp, lax.axis_index("sp"))
        for r in range(height + 2):
            if r == 0:
                v = up[...]
            elif r == height + 1:
                v = dn[...]
            else:
                v = x[(r - 1) * width : r * width, :]
            v = silu((v.astype(F32) - center) * mul + add)
            if r == 0:
                v = v * has_up
            elif r == height + 1:
                v = v * has_dn
            act[r * width : (r + 1) * width, :] = v.astype(BF16)
            shifted(a3, r, width, v)
        if base is None:
            out[...] = jnp.zeros_like(out)
        else:
            out[...] = base[...].astype(F32)

    i, j = lax.div(step, 3), lax.rem(step, 3)
    lhs = a3[j, pl.ds(pl.multiple_of(i * width, width), px), :]
    out[...] += dot(lhs, joined(w, 0), 1, 1)

    @pl.when(step == 8)
    def _():
        channel_stats(scratch[0], out[...])
        exchange(n_sp, width, scratch, [out])
        stats[...] = scratch[1][...]
        above[...] = scratch[2][...]
        below[...] = scratch[3][...]


def whole_spec(shape):
    return pl.BlockSpec(shape, lambda t: (0,) * len(shape))


def conv_call(x, up, dn, every, rows, w, base, n_sp, width, cid):
    px, c = x.shape
    padded = px + 2 * width
    ins = [x, up, dn, every, rows, w] + ([] if base is None else [base])
    in_specs = [whole_spec(v.shape) for v in ins]
    in_specs[5] = pl.BlockSpec((4, 1, c, 128), lambda t: (0, t, 0, 0))
    outs = [((px, c), F32), ((padded, c), BF16), ((n_sp, 8, c), F32), ((width, c), F32), ((width, c), F32)]
    return pl.pallas_call(
        functools.partial(conv_kernel, n_sp, width, base is not None),
        grid=(9,),
        in_specs=in_specs,
        out_specs=[whole_spec(s) for s, _ in outs],
        out_shape=[jax.ShapeDtypeStruct(s, ty) for s, ty in outs],
        scratch_shapes=[pltpu.VMEM((3, padded, c), BF16)] + exchange_scratch(n_sp, width, [F32], c),
        compiler_params=params(cid, 1),
        name="conv_forward",
    )(*ins)


def qkv_kernel(n_sp, res, every, rows, w_qkv, w_proj, cot, normed, qk, vg, qk_s, vg_s, ssem, rsem, lsem):
    at = Place()
    px, c = res.shape
    d = c // HEADS
    peers = [at.rp(k, n_sp) for k in range(1, n_sp)]
    greet(peers)
    center, inverse = combine_stats(every, px)
    n = ((res[...] - center) * (inverse * rows[0:1, :]) + rows[1:2, :]).astype(BF16)
    normed[...] = n
    wq = joined(w_qkv)
    wp = joined(w_proj)
    q = dot(n, wq[:c], 1, 1).astype(BF16)
    k = dot(n, wq[c : 2 * c], 1, 1).astype(BF16)
    v = dot(n, wq[2 * c :], 1, 1).astype(BF16)
    g = dot(cot[...], wp, 1, 0).astype(BF16)
    for h in range(HEADS):
        cut = slice(h * d, (h + 1) * d)
        qk_s[h] = jnp.concatenate([q[:, cut], k[:, cut]], axis=1)
        vg_s[h] = jnp.concatenate([v[:, cut], g[:, cut]], axis=1)
    local = []
    for a, (src, dst) in enumerate(((qk_s, qk), (vg_s, vg))):
        cp = pltpu.make_async_copy(src.at[at.s], dst.at[at.s], lsem.at[a])
        cp.start()
        local.append(cp)
    greeted(len(peers))
    sent = []
    for j in range(1, n_sp):
        dev = at.rp(j, n_sp)
        for a, (src, dst) in enumerate(((qk_s, qk), (vg_s, vg))):
            sent.append(remote(src.at[dev[1]], dst.at[at.s], ssem.at[a, j], rsem.at[a, j], dev))
    for cp in local:
        cp.wait()
    for cp in sent:
        cp.wait()


def qkv_call(res, every, rows, w_qkv, w_proj, cot, n_sp, cid):
    px, c = res.shape
    big = jax.ShapeDtypeStruct((n_sp, px, 128), BF16)
    return pl.pallas_call(
        functools.partial(qkv_kernel, n_sp),
        out_shape=[jax.ShapeDtypeStruct((px, c), BF16), big, big],
        in_specs=[VM] * 6,
        out_specs=[VM, ANY, ANY],
        scratch_shapes=[
            pltpu.VMEM((HEADS, px, 128), BF16),
            pltpu.VMEM((HEADS, px, 128), BF16),
            pltpu.SemaphoreType.DMA((2, n_sp)),
            pltpu.SemaphoreType.DMA((2, n_sp)),
            pltpu.SemaphoreType.DMA((2,)),
        ],
        compiler_params=params(cid),
        name="project_and_send",
    )(res, every, rows, w_qkv, w_proj, cot)


def post_kernel(
    n_sp, width, od, dkv, w_qkv, w_proj, res, cot, normed, every, rows,
    output, g_out, g_qkv, n_grad, stats, above, below, *scratch,
):
    exchange_greet(n_sp)
    px, c = res.shape
    d = c // HEADS
    att = jnp.concatenate([od[h][:, :d] for h in range(HEADS)], axis=1)
    pg = jnp.concatenate(
        [od[h][:, d:] for h in range(HEADS)]
        + [dkv[h][:, :d] for h in range(HEADS)]
        + [dkv[h][:, d:] for h in range(HEADS)],
        axis=1,
    )
    wq = joined(w_qkv)
    wp = joined(w_proj)
    ng = dot(pg, wq, 1, 0)
    n_grad[...] = ng
    center, inverse = combine_stats(every, px)
    hat = (res[...] - center) * inverse
    scratch[0][0:1, :] = jnp.sum(ng, axis=0, keepdims=True)
    scratch[0][1:2, :] = jnp.sum(ng * hat, axis=0, keepdims=True)
    output[...] = (res[...] + dot(att, wp, 1, 1)).astype(BF16)
    go = dot(cot[...], att, 0, 0).astype(BF16)
    gq = dot(pg, normed[...], 0, 0).astype(BF16)
    for j in range(4):
        g_out[j] = go[:, j * 128 : (j + 1) * 128]
        g_qkv[j] = gq[:, j * 128 : (j + 1) * 128]
    exchange(n_sp, width, scratch, [n_grad])
    stats[...] = scratch[1][...]
    above[...] = scratch[2][...]
    below[...] = scratch[3][...]


def post_call(od, dkv, w_qkv, w_proj, res, cot, normed, every, rows, n_sp, width, cid):
    px, c = res.shape
    outs = [
        ((px, c), BF16), ((4, c, 128), BF16), ((4, 3 * c, 128), BF16), ((px, c), F32),
        ((n_sp, 8, c), F32), ((width, c), F32), ((width, c), F32),
    ]
    return pl.pallas_call(
        functools.partial(post_kernel, n_sp, width),
        out_shape=[jax.ShapeDtypeStruct(s, ty) for s, ty in outs],
        in_specs=[VM] * 9,
        out_specs=[VM] * len(outs),
        scratch_shapes=exchange_scratch(n_sp, width, [F32], c),
        compiler_params=params(cid),
        name="project_back",
    )(od, dkv, w_qkv, w_proj, res, cot, normed, every, rows)


def back_kernel(n_sp, width, has_base, x, every, rows, act, u, ua, ub, sums, every2, rows2, y, ya, yb, *rest):
    if has_base:
        cot, cota, cotb = rest[:3]
        rest = rest[3:]
    w = rest[0]
    rest = rest[1:]
    if has_base:
        dw, out, stats, above, below, res_grad = rest[:6]
        rest = rest[6:]
    else:
        dw, out, stats, above, below = rest[:5]
        rest = rest[5:]
    a3, g3, gt = rest[:3]
    scratch = rest[3:]
    step = pl.program_id(0)
    px, c = u.shape
    height = px // width
    members = px * n_sp * (c // GROUPS)

    @pl.when(step == 0)
    def _():
        exchange_greet(n_sp)
        center, inverse = combine_stats(every2, px)
        gain, fac = rows2[0:1, :], rows2[2:3, :]
        total = combine_sums(sums) * (gain * fac)
        total = group_total(total) / members
        s1, s2 = total[0:1, :], total[1:2, :]
        mul = gain * fac
        has_up, has_dn = edge_flags(n_sp, lax.axis_index("sp"))
        for r in range(height + 2):
            if r == 0:
                uu, yy, flag = ua[...], ya[...], has_up
            elif r == height + 1:
                uu, yy, flag = ub[...], yb[...], has_dn
            else:
                cut = slice((r - 1) * width, r * width)
                uu, yy, flag = u[cut, :], y[cut, :], None
            hat = (yy - center) * inverse
            g = inverse * (uu * mul - s1 - hat * s2)
            if has_base:
                cc = cota[...] if r == 0 else cotb[...] if r == height + 1 else cot[cut, :]
                g = g + cc.astype(F32)
            if flag is not None:
                g = g * flag
            elif has_base:
                res_grad[cut, :] = g
            g = g.astype(BF16).astype(F32)
            shifted(g3, r, width, g)
            shifted(a3, r, width, act[r * width : (r + 1) * width, :].astype(F32))
        gt[...] = g3[1, width : width + px, :].T
        out[...] = jnp.zeros_like(out)

    i, j = lax.div(step, 3), lax.rem(step, 3)
    lhs = g3[2 - j, pl.ds(pl.multiple_of((2 - i) * width, width), px), :]
    out[...] += dot(lhs, joined(w, 0), 1, 0)
    part = dot(gt[...], a3[j, pl.ds(pl.multiple_of(i * width, width), px), :], 1, 0).astype(BF16)
    for b in range(4):
        dw[b, 0] = part[:, b * 128 : (b + 1) * 128]

    @pl.when(step == 8)
    def _():
        center, inverse = combine_stats(every, px)
        hat = (x[...].astype(F32) - center) * inverse
        pre = hat * (rows[0:1, :] * rows[2:3, :]) + (rows[1:2, :] * rows[2:3, :] + rows[3:4, :])
        v = out[...] * silu_slope(pre)
        out[...] = v
        scratch[0][0:1, :] = jnp.sum(v, axis=0, keepdims=True)
        scratch[0][1:2, :] = jnp.sum(v * hat, axis=0, keepdims=True)
        exchange(n_sp, width, scratch, [out])
        stats[...] = scratch[1][...]
        above[...] = scratch[2][...]
        below[...] = scratch[3][...]


def back_call(x, every, rows, act, u, ua, ub, sums, every2, rows2, y, ya, yb, base, w, n_sp, width, cid):
    px, c = u.shape
    padded = px + 2 * width
    ins = [x, every, rows, act, u, ua, ub, sums, every2, rows2, y, ya, yb] + list(base or ()) + [w]
    in_specs = [whole_spec(v.shape) for v in ins]
    in_specs[-1] = pl.BlockSpec((4, 1, c, 128), lambda t: (0, t, 0, 0))
    outs = [((4, 9, c, 128), BF16), ((px, c), F32), ((n_sp, 8, c), F32), ((width, c), F32), ((width, c), F32)]
    out_specs = [whole_spec(s) for s, _ in outs]
    out_specs[0] = pl.BlockSpec((4, 1, c, 128), lambda t: (0, t, 0, 0))
    if base:
        outs.append(((px, c), F32))
        out_specs.append(whole_spec((px, c)))
    return pl.pallas_call(
        functools.partial(back_kernel, n_sp, width, bool(base)),
        grid=(9,),
        in_specs=in_specs,
        out_specs=out_specs,
        out_shape=[jax.ShapeDtypeStruct(s, ty) for s, ty in outs],
        scratch_shapes=[
            pltpu.VMEM((3, padded, c), BF16), pltpu.VMEM((3, padded, c), BF16), pltpu.VMEM((c, px), BF16),
        ]
        + exchange_scratch(n_sp, width, [F32], c),
        compiler_params=params(cid, 1),
        name="conv_backward",
    )(*ins)


def attention_kernel(L, T, BQ, BK, qk, vg, text, bias, od, dkv, dt, k_s, v_s, s_s, e_s, dk_s, dv_s):
    d = qk.shape[1] // 2
    step = pl.program_id(0)

    @pl.when(step == 0)
    def _():
        ones = (lax.broadcasted_iota(jnp.int32, (1, d), 1) == 0).astype(BF16)
        head = lax.axis_index("sp")
        pair, odd = lax.div(head, 2), lax.rem(head, 2)
        picked = []
        for j in (pair, HEADS // 2 + pair):
            blk = text[j].astype(F32)
            picked.append(jnp.where(odd > 0, blk[:, d:], blk[:, :d]).astype(BF16))
        k_s[0:T, :] = picked[0]
        v_s[0:T, :] = jnp.concatenate([picked[1], jnp.broadcast_to(ones, (T, d))], axis=1)
        k_s[T:, :] = qk[:, d:]
        v_s[T:, :] = jnp.concatenate([vg[:, :d], jnp.broadcast_to(ones, (L, d))], axis=1)
        dk_s[...] = jnp.zeros_like(dk_s)
        dv_s[...] = jnp.zeros_like(dv_s)

    r = pl.ds(pl.multiple_of(step * BQ, BQ), BQ)
    scale = d ** -0.5
    q = (qk[r, :][:, :d].astype(F32) * scale).astype(BF16)
    g = vg[r, :][:, d:]
    blocks = [(0, T)] + [(T + j * BK, BK) for j in range(L // BK)]
    peak = None
    for at, n in blocks:
        s = dot(q, k_s[at : at + n, :], 1, 1)
        if at == 0:
            s = s + bias[...]
        s_s[:, at : at + n] = s
        for j in range(n // 128):
            part = s[:, 128 * j : 128 * j + 128]
            peak = part if peak is None else jnp.maximum(peak, part)
    peak = jnp.max(peak, axis=1, keepdims=True)
    o = jnp.zeros((BQ, 2 * d), F32)
    for at, n in blocks:
        e = jnp.exp(s_s[:, at : at + n] - peak).astype(BF16)
        e_s[:, at : at + n] = e
        o = o + dot(e, v_s[at : at + n, :], 1, 0)
    inverse = 1.0 / o[:, d : d + 1]
    o = o[:, :d] * inverse
    g = g.astype(F32) * inverse
    row = jnp.sum(o * g, axis=1, keepdims=True)
    g = g.astype(BF16)
    gt, qt = g.T, q.T
    dq = jnp.zeros((BQ, d), F32)
    for at, n in blocks:
        e = e_s[:, at : at + n]
        dp = dot(g, v_s[at : at + n, :d], 1, 1)
        ds = (e.astype(F32) * (dp - row)).astype(BF16)
        dq = dq + dot(ds, k_s[at : at + n, :], 1, 0)
        dv_s[:, at : at + n] += dot(gt, e, 1, 0)
        dk_s[:, at : at + n] += dot(qt, ds, 1, 0)
    od[...] = jnp.concatenate([o, dq * scale], axis=1).astype(BF16)

    @pl.when(step == pl.num_programs(0) - 1)
    def _():
        both = jnp.concatenate([dk_s[...], dv_s[...]], axis=0).astype(BF16).T
        dt[...] = both[:T]
        dkv[...] = both[T:]


def attention_call(qk, vg, text, bias):
    (L, d2), T = qk.shape, text.shape[1]
    BQ, BK = 256, 1024
    full = lambda shape: pl.BlockSpec(shape, lambda t: (0, 0))
    return pl.pallas_call(
        functools.partial(attention_kernel, L, T, BQ, BK),
        grid=(L // BQ,),
        in_specs=[full((L, d2)), full((L, d2)), pl.BlockSpec(text.shape, lambda t: (0, 0, 0)), full((1, T))],
        out_specs=[pl.BlockSpec((BQ, d2), lambda t: (t, 0)), full((L, d2)), full((T, d2))],
        out_shape=[jax.ShapeDtypeStruct(s, BF16) for s in ((L, d2), (L, d2), (T, d2))],
        scratch_shapes=[
            pltpu.VMEM((T + L, d2 // 2), BF16),
            pltpu.VMEM((T + L, d2), BF16),
            pltpu.VMEM((BQ, T + L), F32),
            pltpu.VMEM((BQ, T + L), BF16),
            pltpu.VMEM((d2 // 2, T + L), F32),
            pltpu.VMEM((d2 // 2, T + L), F32),
        ],
        compiler_params=params(None, 1),
        name="attention",
    )(qk, vg, text, bias)


class Mail:
    def __init__(self, ssem, rsem):
        self.ssem, self.rsem, self.sent = ssem, rsem, []

    def send(self, src, dst, dev):
        j = len(self.sent)
        cp = remote(src, dst, self.ssem.at[j], self.rsem.at[j], dev)
        self.sent.append(cp)
        return cp


def img_peers(at):
    return [(lax.rem(at.i + k, 4), at.s) for k in range(1, 4)]


HEAD_MAIL = 3 * 3 + 3 + 2 * 7 + 7 + 4


def head_kernel(nz, width, dims, *refs):
    na = len(dims)
    ins, refs = refs[:na], refs[na:]
    x, cot, emb, cap, w_emb, w_cap, affine = refs[:7]
    outs, refs = refs[7 : 7 + na], refs[7 + na :]
    st0, xa, xb, ca, cb, rows, kv_all, cap_all, emb_all = refs[:9]
    (ssem, rsem, lsem, mine, every, h0, h1, h2, h3, aff_s, emb_s, cap_s, part, part_r, kv_s, kv_r, mod_s, mod_r,
     msend, mrecv) = refs[9:]
    n_sp = 2 * nz
    at = Place()
    line = [at.rp(k, n_sp) for k in range(1, n_sp)]
    grid = img_peers(at)
    greet(line + grid)
    mail = Mail(msend, mrecv)
    local = []
    sent = {}
    kinds = {}

    def view(a, ii, k, core, half=None):
        r = dims[a][1]
        sp = 2 * lax.rem(at.z - k + nz, nz) + core
        if half is None:
            return outs[a].at[ii, :, pl.ds(pl.multiple_of(sp * r, r), r), :]
        h = r // 2
        return outs[a].at[ii, :, pl.ds(pl.multiple_of(sp * r + half * h, h), h), :]

    def send(a, kind, src, dst, dev):
        j = kinds.setdefault(kind, len(kinds))
        sent[a, kind] = remote(src, dst, ssem.at[a, j], rsem.at[a, j], dev)

    def forward(a, kind, ref, dev):
        send(a, kind, ref, ref, dev)

    def first(a):
        own = view(a, at.i, 0, at.c)
        for k in range(1, nz):
            send(a, ("z", k), ins[a], own, at.zp(k, nz))
        send(a, ("x", 0), ins[a], own, at.xn)
        send(a, ("y", 0), ins[a], own, at.yn)
        send(a, ("s", 0), ins[a], own, at.sib)

    def second(a):
        for k in range(1, nz):
            sent[a, ("z", k)].wait_recv()
            got = view(a, at.i, k, at.c)
            forward(a, ("x", k), got, at.xn)
            forward(a, ("y", k), got, at.yn)
            forward(a, ("s", k), got, at.sib)

    def third(a):
        for k in range(nz):
            sent[a, ("x", k)].wait_recv()
            forward(a, ("da", k), view(a, at.ix, k, at.c, 0), at.yn)
            forward(a, ("sx", k), view(a, at.ix, k, at.c), at.sib)
            sent[a, ("y", k)].wait_recv()
            forward(a, ("db", k), view(a, at.iy, k, at.c, 1), at.xn)
            forward(a, ("sy", k), view(a, at.iy, k, at.c), at.sib)

    def fourth(a):
        for k in range(nz):
            sent[a, ("da", k)].wait_recv()
            forward(a, ("sa", k), view(a, at.id, k, at.c, 0), at.sib)
            sent[a, ("db", k)].wait_recv()
            forward(a, ("sb", k), view(a, at.id, k, at.c, 1), at.sib)

    channel_stats(mine, x[...].astype(F32))
    greeted(n_sp + 2)
    first(0)
    e = cap.shape[1] // 4
    round1 = []
    for dev in grid:
        round1.append(mail.send(affine, aff_s.at[at.i], dev))
        round1.append(mail.send(emb.at[dev[0]], emb_s.at[at.i], dev))
        round1.append(mail.send(cap.at[:, pl.ds(pl.multiple_of(dev[0] * e, e), e)], cap_s.at[at.i], dev))
    own_cap = pltpu.make_async_copy(cap.at[:, pl.ds(pl.multiple_of(at.i * e, e), e)], cap_s.at[at.i], lsem.at[na])
    own_cap.start()
    aff_s[at.i] = affine[...]
    emb_s[at.i] = emb[at.i]
    px = x.shape[0]
    stat = []
    for ref, above, below in ((x, h0, h1), (cot, h2, h3)):
        stat.append(mail.send(ref.at[px - width :], above, line[0]))
        stat.append(mail.send(ref.at[:width], below, line[-1]))
    for dev in line:
        stat.append(mail.send(mine, every.at[at.s], dev))
    every[at.s] = mine[...]
    for a in range(na):
        cp = pltpu.make_async_copy(ins[a], view(a, at.i, 0, at.c), lsem.at[a])
        cp.start()
        local.append(cp)
    tokens = cap.shape[0]
    round2, round3 = [], []

    def extras(tick):
        if tick == 1:
            own_cap.wait()
            for cp in round1:
                cp.wait_recv()
            for j in range(4):
                part[j, :tokens] = dot(cap_s[j], w_cap[...], 1, 0)
                part[j, tokens:] = dot(emb_s[j].astype(BF16), w_emb[...], 1, 0)
            for dev in grid:
                round2.append(mail.send(part.at[dev[0]], part_r.at[at.i], dev))
            part_r[at.i] = part[at.i]
        if tick == 2:
            for cp in round2:
                cp.wait_recv()
            total = part_r[0] + part_r[1] + part_r[2] + part_r[3]
            kv_s[...] = total[:tokens].astype(BF16)
            mod_s[...] = total[tokens:]
            for dev in line:
                round3.append(mail.send(kv_s, kv_r.at[at.s], dev))
                round3.append(mail.send(mod_s, mod_r.at[at.s], dev))
            kv_r[at.s] = kv_s[...]
            mod_r[at.s] = mod_s[...]
        if tick == 4:
            for cp in round3 + stat:
                cp.wait_recv()
            kv_all[...] = kv_r[...]
            cap_all[...] = cap_s[...]
            emb_all[...] = jnp.concatenate([emb_s[j][0:1] for j in range(4)] + [jnp.zeros((4, e), F32)])
            st0[...] = every[...]
            for dst, src in ((xa, h0), (xb, h1), (ca, h2), (cb, h3)):
                dst[...] = src[...]
            aff = jnp.concatenate([aff_s[j] for j in range(4)], axis=1)
            mod = jnp.concatenate([mod_r[j][0:1] for j in range(n_sp)], axis=1)
            c = aff.shape[1]
            rows[...] = jnp.zeros_like(rows)
            for j in range(3):
                rows[j, 0:1] = aff[j : j + 1]
                rows[j, 1:2] = aff[3 + j : 4 + j]
                rows[j, 2:3] = 1.0 + mod[:, :c] if j == 1 else jnp.ones((1, c), F32)
            rows[1, 3:4] = mod[:, c:]

    stages = (first, second, third, fourth)
    for tick in range(1, na + 3):
        for a in range(na):
            stage = tick - a
            if 0 <= stage < 4 and (stage, a) != (0, 0):
                stages[stage](a)
        extras(tick)
    for cp in local:
        cp.wait()
    for (a, kind), cp in sent.items():
        if kind[0] in ("s", "sx", "sy", "sa", "sb"):
            cp.wait_recv()
        cp.wait_send()
    for cp in mail.sent:
        cp.wait_send()


def head_call(chunks, x, cot, emb, cap, w_emb, w_cap, affine, nz, width, cid):
    dims = [c.shape[:2] for c in chunks]
    na = len(chunks)
    n_sp = 2 * nz
    copies = 3 * nz - 1 + 7 * nz
    px, c = x.shape
    tokens, wide = cap.shape
    e = wide // 4
    edge = ((width, c), BF16)
    outs = [
        ((n_sp, 8, c), F32), edge, edge, edge, edge, ((3, 8, c), F32), ((n_sp, tokens, 128), BF16),
        ((4, tokens, e), BF16), ((8, e), F32),
    ]
    return pl.pallas_call(
        functools.partial(head_kernel, nz, width, dims),
        out_shape=[jax.ShapeDtypeStruct((4, t, n_sp * r, 128), BF16) for t, r in dims]
        + [jax.ShapeDtypeStruct(s, ty) for s, ty in outs],
        in_specs=[ANY] * na + [VM, VM, VM, ANY, VM, VM, VM],
        out_specs=[ANY] * na + [VM] * len(outs),
        scratch_shapes=[
            pltpu.SemaphoreType.DMA((na, copies)),
            pltpu.SemaphoreType.DMA((na, copies)),
            pltpu.SemaphoreType.DMA((na + 1,)),
            pltpu.VMEM((8, c), F32),
            pltpu.VMEM((n_sp, 8, c), F32),
            pltpu.VMEM((width, c), BF16), pltpu.VMEM((width, c), BF16),
            pltpu.VMEM((width, c), BF16), pltpu.VMEM((width, c), BF16),
            pltpu.VMEM((4, 8, 128), F32),
            pltpu.VMEM((4, 8, e), F32),
            pltpu.VMEM((4, tokens, e), BF16),
            pltpu.VMEM((4, tokens + 8, 128), F32),
            pltpu.VMEM((4, tokens + 8, 128), F32),
            pltpu.VMEM((tokens, 128), BF16),
            pltpu.VMEM((n_sp, tokens, 128), BF16),
            pltpu.VMEM((8, 128), F32),
            pltpu.VMEM((n_sp, 8, 128), F32),
            pltpu.SemaphoreType.DMA((HEAD_MAIL,)),
            pltpu.SemaphoreType.DMA((HEAD_MAIL,)),
        ],
        compiler_params=params(cid),
        name="gather_weights",
    )(*chunks, x, cot, emb, cap, w_emb, w_cap, affine)


class Reducer:
    NAMES = ("q", "sb", "da", "db", "rx", "ry", "r", "zr")

    def __init__(self, at, nz, arrays, ssem, rsem, lsem):
        self.at, self.nz, self.arrays = at, nz, arrays
        self.ssem, self.rsem, self.lsem = ssem, rsem, lsem
        self.sent, self.local, self.groups = {}, {}, []

    @staticmethod
    def buffers(nz, t, r):
        return [
            pltpu.VMEM((4, t, nz, r, 128), BF16),
            pltpu.VMEM((4, t, nz, r, 128), BF16),
            pltpu.VMEM((t, nz, r // 2, 128), BF16),
            pltpu.VMEM((t, nz, r // 2, 128), BF16),
            pltpu.VMEM((t, nz, r, 128), BF16),
            pltpu.VMEM((t, nz, r, 128), BF16),
            pltpu.VMEM((t, nz, r, 128), BF16),
            pltpu.VMEM((nz - 1, t, r, 128), BF16),
        ]

    def send(self, g, j, src, dst, dev):
        self.sent[g, j] = remote(src, dst, self.ssem.at[g, j], self.rsem.at[g, j], dev)

    def load(self, a, t0, t1):
        g = len(self.groups)
        self.groups.append((a, t0, t1))
        src, hbm, _, b = self.arrays[a]
        if hbm:
            cp = pltpu.make_async_copy(src.at[:, t0:t1, :, self.at.c], b["q"].at[:, t0:t1], self.lsem.at[g])
            cp.start()
            self.local[g] = cp
        return g

    def start(self, g):
        a, t0, t1 = self.groups[g]
        src, _, _, b = self.arrays[a]
        self.send(g, 0, src.at[:, t0:t1, :, 1 - self.at.c], b["sb"].at[:, t0:t1], self.at.sib)

    def stage1(self, g):
        a, t0, t1 = self.groups[g]
        src, hbm, _, b = self.arrays[a]
        q, sb, at = b["q"], b["sb"], self.at
        if hbm:
            self.local[g].wait()
        self.sent[g, 0].wait_recv()
        n = t1 - t0

        def add(j, _):
            ii, tt = lax.div(j, n), t0 + lax.rem(j, n)
            own = q[ii, tt] if hbm else src[ii, tt, :, at.c]
            q[ii, tt] = (own.astype(F32) + sb[ii, tt].astype(F32)).astype(BF16)
            return 0

        lax.fori_loop(0, 4 * n, add, 0)
        h = q.shape[3] // 2
        self.send(g, 1, q.at[at.id, t0:t1, :, :h], b["da"].at[t0:t1], at.yn)
        self.send(g, 2, q.at[at.id, t0:t1, :, h:], b["db"].at[t0:t1], at.xn)

    def stage2(self, g):
        a, t0, t1 = self.groups[g]
        b, at = self.arrays[a][3], self.at
        q = b["q"]
        h = q.shape[3] // 2
        self.sent[g, 1].wait_recv()
        self.sent[g, 2].wait_recv()

        def add(tt, _):
            q[at.ix, tt, :, :h] = (q[at.ix, tt, :, :h].astype(F32) + b["da"][tt].astype(F32)).astype(BF16)
            q[at.iy, tt, :, h:] = (q[at.iy, tt, :, h:].astype(F32) + b["db"][tt].astype(F32)).astype(BF16)
            return 0

        lax.fori_loop(t0, t1, add, 0)
        self.send(g, 3, q.at[at.ix, t0:t1], b["rx"].at[t0:t1], at.xn)
        self.send(g, 4, q.at[at.iy, t0:t1], b["ry"].at[t0:t1], at.yn)

    def stage3(self, g):
        a, t0, t1 = self.groups[g]
        b, at = self.arrays[a][3], self.at
        self.sent[g, 3].wait_recv()
        self.sent[g, 4].wait_recv()

        def add(tt, _):
            total = b["q"][at.i, tt].astype(F32) + b["rx"][tt].astype(F32) + b["ry"][tt].astype(F32)
            b["r"][tt] = total.astype(BF16)
            return 0

        lax.fori_loop(t0, t1, add, 0)
        for k in range(1, self.nz):
            dev = at.zp(k, self.nz)
            there = lax.rem(at.z + k, self.nz)
            self.send(g, 4 + k, b["r"].at[t0:t1, there], b["zr"].at[k - 1, t0:t1], dev)

    def stage4(self, g):
        a, t0, t1 = self.groups[g]
        _, _, out, b = self.arrays[a]
        at = self.at
        for k in range(1, self.nz):
            self.sent[g, 4 + k].wait_recv()

        def add(tt, _):
            total = (
                b["q"][at.i, tt, at.z].astype(F32) + b["rx"][tt, at.z].astype(F32) + b["ry"][tt, at.z].astype(F32)
            )
            for k in range(1, self.nz):
                total = total + b["zr"][k - 1, tt].astype(F32)
            out[tt] = total
            return 0

        lax.fori_loop(t0, t1, add, 0)

    def finish(self):
        for cp in self.sent.values():
            cp.wait_send()


class Pipeline:
    def __init__(self, red):
        self.red, self.queue = red, []

    def add(self, g):
        self.red.start(g)
        self.queue.append([g, 1])

    def tick(self):
        for item in list(self.queue):
            g, stage = item
            getattr(self.red, "stage%d" % stage)(g)
            item[1] += 1
            if stage == 4:
                self.queue.remove(item)

    def drain(self):
        while self.queue:
            self.tick()


TAIL_MAIL = 6 + 14 + 6 + 3 + 7
TAIL_GROUPS = 7


def tail_kernel(nz, width, *refs):
    (g_out, g_small, x, st0, rows, act, u, ua, ub, su1, su2, st1, y, ya, yb, w, res_grad,
     dt_all, cap_all, emb_all, w_emb, w_cap, temb) = refs[:23]
    image_grad, s_in, s_out, s_small, g_temb, g_cap, g_wemb, g_wcap, g_aff = refs[23:32]
    refs = refs[32:]
    names = Reducer.NAMES
    bufs = [dict(zip(names, refs[8 * a : 8 * a + 8])) for a in range(3)]
    (ssem, rsem, lsem, msend, mrecv, dw, a3, g3, gt, acc, mine, every, tg_s, tg_r, mod_s, mod_r,
     gc_s, gc_r, pe_s, pe_r, gs_s, gs_r, ps_s, ps_r, aff_s, aff_r) = refs[24:]
    n_sp = 2 * nz
    at = Place()
    line = [at.rp(k, n_sp) for k in range(1, n_sp)]
    grid = img_peers(at)
    greet(line + grid)
    mail = Mail(msend, mrecv)
    red = Reducer(
        at, nz,
        [(g_out, True, s_out, bufs[0]), (g_small, True, s_small, bufs[1]), (dw, False, s_in, bufs[2])],
        ssem, rsem, lsem,
    )
    pipe = Pipeline(red)
    early = [red.load(0, 0, 3), red.load(0, 3, 6), red.load(0, 6, 9), red.load(1, 0, 1)]
    px, c = u.shape
    height = px // width
    members = px * n_sp * (c // GROUPS)
    d = c // HEADS
    rows0, rows1 = rows[0], rows[1]
    gain1, bias1, fac1 = rows1[0:1], rows1[1:2], rows1[2:3]

    t1 = combine_sums(su1)
    t2 = combine_sums(su2)
    mod = jnp.concatenate([t1[1:2] * gain1 + t1[0:1] * bias1, t1[0:1]], axis=1)
    for j in range(n_sp):
        mod_s[j] = jnp.broadcast_to(mod[:, j * 128 : (j + 1) * 128], (8, 128))
    first = 2 * lax.rem(at.s, nz)
    value = lax.div(at.s, nz)
    halves = []
    for j in range(2):
        blk = dt_all[first + j].astype(F32)
        halves.append(jnp.where(value > 0, blk[:, d:], blk[:, :d]))
    tg_s[...] = jnp.concatenate(halves, axis=1).astype(BF16)
    greeted(n_sp + 2)
    for g in early:
        pipe.add(g)
    round_a = []
    for dev in grid:
        round_a.append(mail.send(tg_s, tg_r.at[at.i], dev))
        round_a.append(mail.send(mod_s.at[at.s], mod_r.at[at.i], dev))
    tg_r[at.i] = tg_s[...]
    mod_r[at.i] = mod_s[at.s]

    center, inverse = combine_stats(st1, px)
    total = group_total(t1 * (gain1 * fac1)) / members
    s1, s2 = total[0:1, :], total[1:2, :]
    mul = gain1 * fac1
    has_up, has_dn = edge_flags(n_sp, at.s)
    for r in range(height + 2):
        cut = slice((r - 1) * width, r * width)
        if r == 0:
            uu, yy = ua[...], ya[...]
        elif r == height + 1:
            uu, yy = ub[...], yb[...]
        else:
            uu, yy = u[cut, :], y[cut, :]
        g = inverse * (uu * mul - s1 - (yy - center) * inverse * s2)
        if r == 0:
            g = g * has_up
        elif r == height + 1:
            g = g * has_dn
        shifted(g3, r, width, g.astype(BF16).astype(F32))
        shifted(a3, r, width, act[r * width : (r + 1) * width, :].astype(F32))
    gt[...] = g3[1, width : width + px, :].T
    pipe.tick()

    def weight_taps(t0, t1):
        def one(tap, _):
            i, j = lax.div(tap, 3), lax.rem(tap, 3)
            part = dot(gt[...], a3[j, pl.ds(pl.multiple_of(i * width, width), px), :], 1, 0).astype(BF16)
            for b in range(4):
                dw[b, tap] = part[:, b * 128 : (b + 1) * 128].reshape(nz, 2, c // n_sp, 128)
            return 0

        lax.fori_loop(t0, t1, one, 0)
        pipe.add(red.load(2, t0, t1))

    def input_taps(t0, t1):
        def one(tap, _):
            i, j = lax.div(tap, 3), lax.rem(tap, 3)
            lhs = g3[2 - j, pl.ds(pl.multiple_of((2 - i) * width, width), px), :]
            part = dot(lhs, joined(w, tap), 1, 0)
            acc[...] = part + jnp.where(tap > 0, acc[...], 0.0)
            return 0

        lax.fori_loop(t0, t1, one, 0)

    weight_taps(0, 3)
    pipe.tick()
    weight_taps(3, 6)
    for cp in round_a:
        cp.wait_recv()
    tokens = tg_s.shape[0]
    flat_tg = tg_r[...].reshape(4 * tokens, 128)
    g_wcap[...] = dot(cap_all[...].reshape(4 * tokens, cap_all.shape[2]), flat_tg, 0, 0)
    gc_s[...] = dot(flat_tg, w_cap[...], 1, 1).astype(BF16).reshape(gc_s.shape)
    mods = jnp.concatenate([mod_r[j][0:1] for j in range(4)] + [jnp.zeros((4, 128), F32)])
    exact = lambda a, b, ca, cb: lax.dot_general(
        a, b, (((ca,), (cb,)), ((), ())), preferred_element_type=F32, precision=PRECISE
    )
    emb_t = emb_all[...].T
    g_wemb[...] = sum(emb_t[:, j : j + 1] * mods[j : j + 1] for j in range(4))
    pe_s[...] = exact(mods, w_emb[...].astype(F32), 1, 1)
    share = tokens // n_sp
    round_b = []
    for dev in line:
        cut = pl.ds(pl.multiple_of(dev[1] * share, share), share)
        round_b.append(mail.send(gc_s.at[:, cut, :], gc_r.at[at.s], dev))
        round_b.append(mail.send(pe_s, pe_r.at[at.s], dev))
    gc_r[at.s] = gc_s[:, pl.ds(pl.multiple_of(at.s * share, share), share), :]
    pe_r[at.s] = pe_s[...]
    pipe.tick()
    weight_taps(6, 9)
    pipe.tick()
    input_taps(0, 3)
    pipe.tick()
    for cp in round_b:
        cp.wait_recv()
    gc = gc_r[0].astype(F32)
    pe = pe_r[0]
    for j in range(1, n_sp):
        gc = gc + gc_r[j].astype(F32)
        pe = pe + pe_r[j]
    gs_s[...] = gc
    for j in range(4):
        ps_s[j] = jnp.broadcast_to(pe[j : j + 1], pe.shape)
    round_c = []
    for dev in grid:
        round_c.append(mail.send(gs_s.at[dev[0]], gs_r.at[at.i], dev))
        round_c.append(mail.send(ps_s.at[dev[0]], ps_r.at[at.i], dev))
    gs_r[at.i] = gs_s[at.i]
    ps_r[at.i] = ps_s[at.i]
    input_taps(3, 6)
    pipe.tick()
    input_taps(6, 9)
    pipe.tick()

    center, inverse = combine_stats(st0, px)
    hat = (x[...].astype(F32) - center) * inverse
    gain0 = rows0[0:1]
    v = acc[...] * silu_slope(hat * gain0 + rows0[1:2])
    acc[...] = v
    mine[...] = jnp.zeros_like(mine)
    mine[0:1, :] = jnp.sum(v, axis=0, keepdims=True)
    mine[1:2, :] = jnp.sum(v * hat, axis=0, keepdims=True)
    round_d = [mail.send(mine, every.at[at.s], dev) for dev in line]
    every[at.s] = mine[...]
    pipe.tick()
    for cp in round_d:
        cp.wait_recv()
    t0 = combine_sums(every)
    zero = jnp.zeros((2, c), F32)
    aff = jnp.concatenate([t0[1:2], t1[1:2] * fac1, t2[1:2], t0[0:1], t1[0:1] * fac1, t2[0:1], zero])
    for j in range(4):
        aff_s[j] = aff[:, j * 128 : (j + 1) * 128]
    round_e = [mail.send(aff_s.at[dev[0]], aff_r.at[at.i], dev) for dev in grid]
    aff_r[at.i] = aff_s[at.i]
    total = group_total(t0 * gain0) / members
    image_grad[...] = res_grad[...] + inverse * (acc[...] * gain0 - total[0:1] - hat * total[1:2])
    pipe.drain()
    for cp in round_c + round_e:
        cp.wait_recv()
    g_cap[...] = jnp.concatenate([gs_r[j] for j in range(4)], axis=1)
    g_temb[...] = jnp.concatenate([ps_r[j] for j in range(4)], axis=1) * silu_slope(temb[...])
    g_aff[...] = aff_r[0] + aff_r[1] + aff_r[2] + aff_r[3]
    red.finish()
    for cp in mail.sent:
        cp.wait_send()


def tail_call(g_out, g_small, x, st0, rows, act, u, ua, ub, su1, su2, st1, y, ya, yb, w, res_grad,
              dt_all, cap_all, emb_all, w_emb, w_cap, temb, nz, width, cid):
    px, c = u.shape
    n_sp = 2 * nz
    padded = px + 2 * width
    r = c // n_sp
    rs = g_small.shape[4]
    tokens = dt_all.shape[1]
    e = cap_all.shape[2]
    share = tokens // n_sp
    ins = [g_out, g_small, x, st0, rows, act, u, ua, ub, su1, su2, st1, y, ya, yb, w, res_grad,
           dt_all, cap_all, emb_all, w_emb, w_cap, temb]
    outs = [(px, c), (9, r, 128), (9, r, 128), (1, rs, 128), (8, 4 * e), (share, 4 * e), (e, 128), (e, 128), (8, 128)]
    vm = pltpu.VMEM
    return pl.pallas_call(
        functools.partial(tail_kernel, nz, width),
        out_shape=[jax.ShapeDtypeStruct(s, F32) for s in outs],
        in_specs=[ANY, ANY] + [VM] * (len(ins) - 2),
        out_specs=[VM] * len(outs),
        scratch_shapes=Reducer.buffers(nz, 9, r) + Reducer.buffers(nz, 1, rs) + Reducer.buffers(nz, 9, r)
        + [
            pltpu.SemaphoreType.DMA((TAIL_GROUPS, 4 + nz)),
            pltpu.SemaphoreType.DMA((TAIL_GROUPS, 4 + nz)),
            pltpu.SemaphoreType.DMA((TAIL_GROUPS,)),
            pltpu.SemaphoreType.DMA((TAIL_MAIL,)),
            pltpu.SemaphoreType.DMA((TAIL_MAIL,)),
            vm((4, 9, nz, 2, r, 128), BF16),
            vm((3, padded, c), BF16), vm((3, padded, c), BF16), vm((c, px), BF16), vm((px, c), F32),
            vm((8, c), F32), vm((n_sp, 8, c), F32),
            vm((tokens, 128), BF16), vm((4, tokens, 128), BF16),
            vm((n_sp, 8, 128), F32), vm((4, 8, 128), F32),
            vm((4, tokens, e), BF16), vm((n_sp, 4, share, e), BF16),
            vm((8, e), F32), vm((n_sp, 8, e), F32),
            vm((4, share, e), F32), vm((4, share, e), F32),
            vm((4, 8, e), F32), vm((4, 8, e), F32),
            vm((4, 8, 128), F32), vm((4, 8, 128), F32),
        ],
        compiler_params=params(cid),
        name="first_backward_and_sums",
    )(*ins)


def fast_body(
    image_in, time_embed, caption, caption_mask, conv_in, conv_out, embed_proj, qkv_proj,
    caption_proj, out_proj, norm_gains, norm_biases, cotangent,
):
    n, height, width, c = image_in.shape
    n_img, n_sp = lax.axis_size("img"), lax.axis_size("sp")
    sp = lax.axis_index("sp")
    nz = n_sp // 2
    px = height * width
    d = c // HEADS
    x = image_in.reshape(px, c)
    cot = cotangent.reshape(px, c)

    flat = lambda w: w.transpose(1, 2, 3, 0).reshape(9, w.shape[3], w.shape[0])
    small = jnp.concatenate([qkv_proj.T, out_proj.T], axis=0)[None]
    affine = jnp.concatenate([norm_gains, norm_biases, jnp.zeros_like(norm_gains[:2])]).astype(F32)
    temb = jnp.broadcast_to(time_embed.astype(F32), (8, time_embed.shape[1]))
    emb = silu(temb).astype(BF16).astype(F32).reshape(8, 4, -1).transpose(1, 0, 2)
    (w_in, w_out, w_small, st0, xa, xb, ca, cb, rows, kv_all, cap_all, emb_all) = head_call(
        [flat(conv_in), flat(conv_out), small], x, cot, emb, caption[0], embed_proj, caption_proj, affine, nz, width, 0
    )
    cut = qkv_proj.shape[1]
    w_small = w_small.reshape(4, n_sp, -1, 128)
    w_qkv = w_small[:, :, :cut].reshape(4, 3 * c, 128)
    w_proj = w_small[:, :, cut:].reshape(4, c, 128)
    bias = jnp.where(caption_mask > 0, 0.0, MASKED).astype(F32)

    hidden, act0, st1, ha, hb = conv_call(x, xa, xb, st0, rows[0], w_in, None, n_sp, width, 1)
    res, act1, st2, ra, rb = conv_call(hidden, ha, hb, st1, rows[1], w_out, x, n_sp, width, 2)
    normed, qk, vg = qkv_call(res, st2, rows[2], w_qkv, w_proj, cot, n_sp, 3)
    od, dkv, dt = attention_call(qk.reshape(-1, 2 * d), vg.reshape(-1, 2 * d), kv_all, bias)
    od, dkv, dt_all = trade([od.reshape(n_sp, px, 2 * d), dkv.reshape(n_sp, px, 2 * d)], dt, n_sp, 4)

    output, g_out, g_qkv, ng, su2, na, nb = post_call(
        od, dkv, w_qkv, w_proj, res, cot, normed, st2, rows[2], n_sp, width, 5
    )
    g_conv_out, pre_grad, su1, pa, pb, res_grad = back_call(
        hidden, st1, rows[1], act1, ng, na, nb, su2, st2, rows[2], res, ra, rb,
        (cot, ca, cb), w_out, n_sp, width, 6,
    )
    g_small = jnp.concatenate(
        [g_qkv.reshape(4, n_sp, cut, 128), g_out.reshape(4, n_sp, c // n_sp, 128)], axis=2
    ).reshape(4, 1, nz, 2, -1, 128)
    g_conv_out = g_conv_out.reshape(4, 9, nz, 2, -1, 128)
    grad_image, s_in, s_out, s_small, g_temb, g_cap, g_wemb, g_wcap, g_aff = tail_call(
        g_conv_out, g_small, x, st0, rows, act0, pre_grad, pa, pb, su1, su2, st1, hidden, ha, hb, w_in, res_grad,
        dt_all, cap_all, emb_all, embed_proj, caption_proj, temb, nz, width, 7,
    )
    unflat = lambda g: g.reshape(3, 3, g.shape[1], 128).transpose(3, 0, 1, 2)
    return (
        output.reshape(image_in.shape),
        grad_image.reshape(image_in.shape),
        g_temb[:1],
        g_cap[None],
        unflat(s_in),
        unflat(s_out),
        g_wemb,
        s_small[0, :cut].T,
        g_wcap,
        s_small[0, cut:].T,
        g_aff[:3],
        g_aff[3:6],
    )


def body(*args):
    image_in, qkv_proj = args[0], args[7]
    n, height, width, c = image_in.shape
    n_img, n_sp = lax.axis_size("img"), lax.axis_size("sp")
    fits = n == 1 and n_img == 4 and n_sp == HEADS and c == 512 and width == 64
    return fast_body(*args) if fits else plain_body(*args)


def solution(mesh):
    rows = P("img", "sp", None, None)
    kernel = P("img", None, None, "sp")
    flat = P("img", "sp")
    return jax.shard_map(
        body,
        mesh=mesh,
        in_specs=(
            rows, P("img", None), P("img", None, None), P("img", None), kernel, kernel,
            flat, flat, flat, flat, P(None, "img"), P(None, "img"), rows,
        ),
        out_specs=(
            rows, rows, P("img", None), P("img", "sp", None), kernel, kernel,
            flat, flat, flat, flat, P(None, "img"), P(None, "img"),
        ),
        check_vma=False,
    )
```

```python
import functools

import jax
import jax.numpy as jnp
from jax import lax
from jax.experimental import pallas as pl
from jax.experimental.pallas import tpu as pltpu
from jax.sharding import PartitionSpec as P

HEADS = 8
GROUPS = 32
EPSILON = 1e-05
PRECISE = lax.Precision.HIGHEST
MASKED = -1e30
BF16 = jnp.bfloat16
F32 = jnp.float32
MESH = pl.DeviceIdType.MESH
VMEM_BYTES = 60 * 1024 * 1024


def dot(a, b, ca, cb):
    return lax.dot_general(a, b, (((ca,), (cb,)), ((), ())), preferred_element_type=F32)


def silu(v):
    return v * jax.nn.sigmoid(v)


def silu_slope(v):
    s = jax.nn.sigmoid(v)
    return s * (1.0 + v * (1.0 - s))


def gather(x, axis, dim):
    return lax.all_gather(x, axis, axis=dim, tiled=True)


def scatter_sum(x, axis, dim):
    return lax.psum_scatter(x, axis, scatter_dimension=dim, tiled=True)


def swap(x, axis, split, concat):
    return lax.all_to_all(x, axis, split, concat, tiled=True)


def halo(x):
    count = lax.axis_size("sp")
    above = lax.ppermute(x[:, -1:], "sp", [(i, i + 1) for i in range(count - 1)])
    below = lax.ppermute(x[:, :1], "sp", [(i + 1, i) for i in range(count - 1)])
    return above, below


def group_sum(v):
    c = v.shape[-1]
    g = v.reshape(v.shape[:-1] + (GROUPS, c // GROUPS))
    s = jnp.sum(g, axis=-1, keepdims=True)
    return jnp.broadcast_to(s, g.shape).reshape(v.shape)


def norm_stats(x):
    n, r, w, c = x.shape
    cells = r * w * (c // GROUPS)
    parts = lax.axis_size("sp")
    mean = group_sum(jnp.sum(x, axis=(1, 2))) / cells
    dev = group_sum(jnp.sum(jnp.square(x - mean[:, None, None, :]), axis=(1, 2)))
    both = lax.all_gather(jnp.stack([mean, dev]), "sp")
    means, devs = both[:, 0], both[:, 1]
    center = jnp.mean(means, axis=0)
    var = (jnp.sum(devs, axis=0) + cells * jnp.sum(jnp.square(means - center), axis=0)) / (
        cells * parts
    )
    return center, lax.rsqrt(var + EPSILON)


def hat_of(x, center, inverse):
    return (x - center[:, None, None, :]) * inverse[:, None, None, :]


def norm_back(u, hat, inverse, gain, sum_u, sum_uh, members):
    s1 = group_sum(sum_u * gain) / members
    s2 = group_sum(sum_uh * gain) / members
    return inverse[:, None, None, :] * (
        u * gain - s1[:, None, None, :] - hat * s2[:, None, None, :]
    )


def pad_cols(x):
    return jnp.pad(x, ((0, 0), (0, 0), (1, 1), (0, 0)))


def conv(padded, weight_t, transposed):
    n, rp, wp, c = padded.shape
    r, w = rp - 2, wp - 2
    total = None
    for i in range(3):
        for j in range(3):
            a = padded[:, i : i + r, j : j + w].reshape(n * r * w, c)
            part = dot(a, weight_t[2 - i, 2 - j], 1, 0) if transposed else dot(a, weight_t[i, j], 1, 1)
            total = part if total is None else total + part
    return total.reshape(n, r, w, -1)


def conv_grad(padded, g):
    n, r, w, c = g.shape
    gf = g.reshape(n * r * w, c)
    rows = []
    for i in range(3):
        for j in range(3):
            a = padded[:, i : i + r, j : j + w].reshape(n * r * w, -1)
            rows.append(dot(gf, a, 0, 0))
    return jnp.stack(rows).reshape(3, 3, c, -1)


def to_pairs(x, images):
    n, px, h, d = x.shape
    y = x.transpose(0, 2, 1, 3).reshape(n * h, px, d)
    return swap(y, "sp", 0, 1)


def from_pairs(x, images):
    y = swap(x, "sp", 1, 0)
    return y.reshape(images, HEADS, y.shape[1], y.shape[2]).transpose(0, 2, 1, 3)


def attention_plain(q, k, v, g, tk, tv, keep, scale):
    p, length, d = q.shape
    block = min(512, length)
    keys = jnp.concatenate([tk, k], axis=1)
    values = jnp.concatenate([tv, v], axis=1)
    text = tk.shape[1]
    keep_all = jnp.concatenate([keep, jnp.ones((p, length), bool)], axis=1)

    def step(carry, blk):
        dk, dv = carry
        qb, gb = blk
        s = jnp.einsum("pqd,pkd->pqk", qb, keys, preferred_element_type=F32) * scale
        s = jnp.where(keep_all[:, None, :], s, MASKED)
        peak = jnp.max(s, axis=-1, keepdims=True)
        e = jnp.exp(s - peak)
        prob = e / jnp.sum(e, axis=-1, keepdims=True)
        pb = prob.astype(BF16)
        o = jnp.einsum("pqk,pkd->pqd", pb, values, preferred_element_type=F32)
        row = jnp.sum(o * gb.astype(F32), axis=-1, keepdims=True)
        dp = jnp.einsum("pqd,pkd->pqk", gb, values, preferred_element_type=F32)
        ds = (prob * (dp - row)).astype(BF16)
        dq = jnp.einsum("pqk,pkd->pqd", ds, keys, preferred_element_type=F32) * scale
        dk = dk + jnp.einsum("pqk,pqd->pkd", ds, qb, preferred_element_type=F32)
        dv = dv + jnp.einsum("pqk,pqd->pkd", pb, gb, preferred_element_type=F32)
        return (dk, dv), (o.astype(BF16), dq.astype(BF16))

    zeros = jnp.zeros((p, text + length, d), F32)
    cut = lambda t: t.reshape(p, length // block, block, d).swapaxes(0, 1)
    (dk, dv), (o, dq) = lax.scan(step, (zeros, zeros), (cut(q), cut(g)))
    join = lambda t: t.swapaxes(0, 1).reshape(p, length, d)
    dk = (dk * scale).astype(BF16)
    dv = dv.astype(BF16)
    return join(o), join(dq), dk[:, text:], dv[:, text:], dk[:, :text], dv[:, :text]


def plain_body(
    image_in, time_embed, caption, caption_mask, conv_in, conv_out, embed_proj, qkv_proj,
    caption_proj, out_proj, norm_gains, norm_biases, cotangent,
):
    n, rows, width, chans = image_in.shape
    n_img, n_sp = lax.axis_size("img"), lax.axis_size("sp")
    img, sp = lax.axis_index("img"), lax.axis_index("sp")
    px = rows * width
    members = px * n_sp * (chans // GROUPS)
    d = chans // HEADS
    scale = d ** -0.5
    pairs = n * HEADS // n_sp

    def whole(w):
        w = gather(w, "img", w.ndim - 1)
        return gather(w, "sp", w.ndim - 2)

    w_in = whole(conv_in.transpose(1, 2, 3, 0))
    w_out = whole(conv_out.transpose(1, 2, 3, 0))
    w_qkv = whole(qkv_proj.T)
    w_proj = whole(out_proj.T)
    affine = gather(jnp.concatenate([norm_gains, norm_biases]), "img", 1).astype(F32)
    gains, biases = affine[:3], affine[3:]

    embedded = silu(time_embed.astype(F32)).astype(BF16)
    emb_all = swap(embedded, "img", 1, 0)
    mod = scatter_sum(jnp.dot(emb_all, embed_proj, preferred_element_type=F32), "img", 0)
    mod = gather(mod, "sp", 1)
    scale_term, shift_term = mod[:, :chans], mod[:, chans:]
    cap_all = swap(caption, "img", 2, 0)
    cap_flat = cap_all.reshape(-1, cap_all.shape[2])
    kv = jnp.dot(cap_flat, caption_proj, preferred_element_type=F32)
    kv = scatter_sum(kv.reshape(cap_all.shape[0], cap_all.shape[1], -1), "img", 0).astype(BF16)
    kv = gather(kv, "sp", 2)
    text = kv.shape[1]
    kv_heads = kv.reshape(n, text, 2, HEADS, d).transpose(2, 0, 3, 1, 4).reshape(2, n * HEADS, text, d)
    mine = lax.dynamic_slice_in_dim(kv_heads, sp * pairs, pairs, 1)
    keep = jnp.repeat(caption_mask > 0, HEADS, axis=0)
    keep = lax.dynamic_slice_in_dim(keep, sp * pairs, pairs, 0)

    image_f = image_in.astype(F32)
    c0, i0 = norm_stats(image_f)
    hat0 = hat_of(image_f, c0, i0)
    first = hat0 * gains[0] + biases[0]
    act0 = silu(first).astype(BF16)
    above, below = halo(act0)
    pad0 = pad_cols(jnp.concatenate([above, act0, below], axis=1))
    hidden = conv(pad0, w_in, False)
    c1, i1 = norm_stats(hidden)
    hat1 = hat_of(hidden, c1, i1)
    second = hat1 * gains[1] + biases[1]
    pre = second * (1.0 + scale_term[:, None, None, :]) + shift_term[:, None, None, :]
    act1 = silu(pre).astype(BF16)
    above, below = halo(act1)
    pad1 = pad_cols(jnp.concatenate([above, act1, below], axis=1))
    residual = image_f + conv(pad1, w_out, False)
    c2, i2 = norm_stats(residual)
    hat2 = hat_of(residual, c2, i2)
    normed = (hat2 * gains[2] + biases[2]).astype(BF16).reshape(n * px, chans)
    qkv = dot(normed, w_qkv, 1, 1).astype(BF16)
    cot = cotangent.reshape(n * px, chans)
    g_att = dot(cot, w_proj, 1, 0).astype(BF16)
    four = jnp.concatenate([qkv, g_att], axis=1).reshape(n, px, 4, HEADS, d)
    packed = to_pairs(four.transpose(0, 1, 3, 2, 4).reshape(n, px, HEADS, 4 * d), n)
    q, k, v, g = (packed[..., j * d : (j + 1) * d] for j in range(4))
    o, dq, dk, dv, dtk, dtv = attention_plain(q, k, v, g, mine[0], mine[1], keep, scale)
    back = from_pairs(jnp.concatenate([o, dq, dk, dv], axis=-1), n)
    back = back.reshape(n * px, HEADS, 4, d).transpose(0, 2, 1, 3).reshape(n * px, 4 * chans)
    attended, proj_grad = back[:, :chans], back[:, chans:]
    output = residual + dot(attended, w_proj, 1, 1).reshape(image_in.shape)

    grad_out = dot(cot, attended, 0, 0)
    grad_qkv = dot(proj_grad, normed, 0, 0)
    normed_grad = dot(proj_grad, w_qkv, 1, 0).reshape(image_in.shape)

    def sums(u, hat):
        both = jnp.stack([jnp.sum(u, axis=(1, 2)), jnp.sum(u * hat, axis=(1, 2))])
        return lax.psum(both, "sp")

    su2, sh2 = sums(normed_grad, hat2)
    residual_grad = cotangent.astype(F32) + norm_back(
        normed_grad, hat2, i2, gains[2], su2, sh2, members
    )
    g2 = residual_grad.astype(BF16)
    above, below = halo(g2)
    gpad = pad_cols(jnp.concatenate([above, g2, below], axis=1))
    grad_conv_out = conv_grad(pad1, g2)
    pre_grad = conv(gpad, w_out, True) * silu_slope(pre)
    sa, sb = sums(pre_grad, hat1)
    fac = 1.0 + scale_term
    shift_grad = sa
    scale_grad = sb * gains[1] + sa * biases[1]
    u1 = pre_grad * fac[:, None, None, :]
    su1, sh1 = sa * fac, sb * fac
    g1 = norm_back(u1, hat1, i1, gains[1], su1, sh1, members).astype(BF16)
    above, below = halo(g1)
    gpad = pad_cols(jnp.concatenate([above, g1, below], axis=1))
    grad_conv_in = conv_grad(pad0, g1)
    u0 = conv(gpad, w_in, True) * silu_slope(first)
    su0, sh0 = sums(u0, hat0)
    grad_image = residual_grad + norm_back(u0, hat0, i0, gains[0], su0, sh0, members)

    mod_grad = jnp.concatenate([scale_grad, shift_grad], axis=1)
    cols = embed_proj.shape[1]
    mod_all = gather(mod_grad, "img", 0)
    mod_cols = lax.dynamic_slice_in_dim(mod_all, sp * cols, cols, 1)
    grad_embed_proj = jnp.einsum("ne,nd->ed", emb_all.astype(F32), mod_cols, precision=PRECISE)
    part = jnp.einsum("nd,ed->ne", mod_cols, embed_proj.astype(F32), precision=PRECISE)
    part = swap(lax.psum(part, "sp"), "img", 0, 1)
    grad_embed = part * silu_slope(time_embed.astype(F32))

    tg = gather(jnp.stack([dtk, dtv]), "sp", 1).reshape(2, n, HEADS, text, d)
    tg = tg.transpose(1, 3, 0, 2, 4).reshape(n, text, 2 * chans)
    cols = caption_proj.shape[1]
    tg = gather(lax.dynamic_slice_in_dim(tg, sp * cols, cols, 2), "img", 0).reshape(-1, cols)
    grad_caption_proj = dot(cap_flat, tg, 0, 0)
    gc = dot(tg, caption_proj, 1, 1).reshape(cap_all.shape)
    gc = scatter_sum(gc, "sp", 1)
    grad_caption = swap(gc, "img", 0, 2)

    grads = jnp.concatenate(
        [jnp.sum(t, axis=0)[None] for t in (sh0, sh1, sh2, su0, su1, su2)]
    )
    grads = scatter_sum(grads, "img", 1)

    def shared(w):
        w = scatter_sum(w, "sp", w.ndim - 2)
        return scatter_sum(w, "img", w.ndim - 1)

    return (
        output.astype(BF16),
        grad_image,
        grad_embed,
        grad_caption,
        shared(grad_conv_in).transpose(3, 0, 1, 2),
        shared(grad_conv_out).transpose(3, 0, 1, 2),
        grad_embed_proj,
        shared(grad_qkv).T,
        grad_caption_proj,
        shared(grad_out).T,
        grads[:3],
        grads[3:],
    )


class Place:
    def __init__(self):
        self.i = lax.axis_index("img")
        self.s = lax.axis_index("sp")
        self.z = lax.div(self.s, 2)
        self.c = lax.rem(self.s, 2)
        x = lax.rem(self.i, 2)
        y = lax.div(self.i, 2)
        self.ix = self.i + 1 - 2 * x
        self.iy = self.i + 2 - 4 * y
        self.id = 3 - self.i
        self.sib = (self.i, self.s + 1 - 2 * self.c)
        self.xn = (self.ix, self.s)
        self.yn = (self.iy, self.s)

    def zp(self, k, nz):
        return (self.i, 2 * lax.rem(self.z + k, nz) + self.c)

    def rp(self, k, n_sp):
        return (self.i, lax.rem(self.s + k, n_sp))


def greet(peers):
    bar = pltpu.get_barrier_semaphore()
    for p in peers:
        pl.semaphore_signal(bar, inc=1, device_id=p, device_id_type=MESH)


def greeted(count):
    pl.semaphore_wait(pltpu.get_barrier_semaphore(), count)


def remote(src, dst, ssem, rsem, dev):
    cp = pltpu.make_async_remote_copy(
        src_ref=src, dst_ref=dst, send_sem=ssem, recv_sem=rsem, device_id=dev, device_id_type=MESH
    )
    cp.start()
    return cp


def params(cid=None, grid=0):
    extra = {} if cid is None else {"collective_id": cid, "has_side_effects": True}
    if grid:
        extra["dimension_semantics"] = ("arbitrary",) * grid
    return pltpu.CompilerParams(vmem_limit_bytes=VMEM_BYTES, **extra)


ANY = pl.BlockSpec(memory_space=pl.ANY)
VM = pl.BlockSpec(memory_space=pltpu.VMEM)
def trade_kernel(n_sp, na, *refs):
    ins, outs = refs[: na + 1], refs[na + 1 : 2 * na + 2]
    ssem, rsem, lsem = refs[2 * na + 2 :]
    at = Place()
    peers = [at.rp(k, n_sp) for k in range(1, n_sp)]
    greet(peers)
    local = [pltpu.make_async_copy(ins[a].at[at.s], outs[a].at[at.s], lsem.at[a]) for a in range(na)]
    local.append(pltpu.make_async_copy(ins[na], outs[na].at[at.s], lsem.at[na]))
    for cp in local:
        cp.start()
    greeted(len(peers))
    sent = []
    for k in range(1, n_sp):
        dev = at.rp(k, n_sp)
        for a in range(na):
            sent.append(remote(ins[a].at[dev[1]], outs[a].at[at.s], ssem.at[a, k], rsem.at[a, k], dev))
        sent.append(remote(ins[na], outs[na].at[at.s], ssem.at[na, k], rsem.at[na, k], dev))
    for cp in local:
        cp.wait()
    for cp in sent:
        cp.wait()


def trade(parts, common, n_sp, cid):
    na = len(parts)
    shapes = [p.shape for p in parts] + [(n_sp,) + common.shape]
    return pl.pallas_call(
        functools.partial(trade_kernel, n_sp, na),
        out_shape=[jax.ShapeDtypeStruct(s, BF16) for s in shapes],
        in_specs=[ANY] * (na + 1),
        out_specs=[ANY] * (na + 1),
        scratch_shapes=[
            pltpu.SemaphoreType.DMA((na + 1, n_sp)),
            pltpu.SemaphoreType.DMA((na + 1, n_sp)),
            pltpu.SemaphoreType.DMA((na + 1,)),
        ],
        compiler_params=params(cid),
        name="trade",
    )(*parts, common)


def exchange_scratch(n_sp, width, halo_types, chans):
    out = [pltpu.VMEM((8, chans), F32), pltpu.VMEM((n_sp, 8, chans), F32)]
    for ty in halo_types:
        out += [pltpu.VMEM((width, chans), ty), pltpu.VMEM((width, chans), ty)]
    count = n_sp - 1 + 2 * len(halo_types)
    return out + [pltpu.SemaphoreType.DMA((count,)), pltpu.SemaphoreType.DMA((count,))]


def exchange_greet(n_sp):
    at = Place()
    greet([at.rp(k, n_sp) for k in range(1, n_sp)])


def exchange(n_sp, width, scratch, edges):
    at = Place()
    mine, every = scratch[0], scratch[1]
    ssem, rsem = scratch[-2:]
    greeted(n_sp - 1)
    sent = []
    for e, ref in enumerate(edges):
        above, below = scratch[2 + 2 * e], scratch[3 + 2 * e]
        px = ref.shape[0]
        j = n_sp - 1 + 2 * e
        sent.append(remote(ref.at[px - width :], above, ssem.at[j], rsem.at[j], at.rp(1, n_sp)))
        sent.append(remote(ref.at[:width], below, ssem.at[j + 1], rsem.at[j + 1], at.rp(n_sp - 1, n_sp)))
    for k in range(1, n_sp):
        sent.append(remote(mine, every.at[at.s], ssem.at[k - 1], rsem.at[k - 1], at.rp(k, n_sp)))
    every[at.s] = mine[...]
    for cp in sent:
        cp.wait()


def channel_stats(mine, v):
    mean = jnp.sum(v, axis=0, keepdims=True) / v.shape[0]
    dev = v - mean
    mine[0:1, :] = mean
    mine[1:2, :] = jnp.sum(dev * dev, axis=0, keepdims=True)


def group_total(rows):
    c = rows.shape[1]
    size = c // GROUPS
    a = lax.broadcasted_iota(jnp.int32, (128, 128), 0)
    b = lax.broadcasted_iota(jnp.int32, (128, 128), 1)
    same = jnp.where(lax.bitwise_xor(a, b) < size, 1.0, 0.0).astype(BF16)
    high = rows.astype(BF16)
    rest = rows - high.astype(F32)
    mid = rest.astype(BF16)
    low = (rest - mid.astype(F32)).astype(BF16)
    parts = jnp.concatenate([high.astype(F32), mid.astype(F32), low.astype(F32)]).astype(BF16)
    total = jnp.concatenate(
        [dot(parts[:, j * 128 : (j + 1) * 128], same, 1, 0) for j in range(c // 128)], axis=1
    )
    n = rows.shape[0]
    return total[:n] + total[n : 2 * n] + total[2 * n :]


def combine_stats(every, px):
    n_sp, _, c = every.shape
    size = c // GROUPS
    means = [every[j, 0:1, :] for j in range(n_sp)]
    center_c = sum(means) / n_sp
    dev = sum(every[j, 1:2, :] for j in range(n_sp))
    dev = dev + px * sum((m - center_c) * (m - center_c) for m in means)
    center = group_total(jnp.broadcast_to(center_c, (8, c)))[0:1] / size
    off = center_c - center
    dev = dev + (px * n_sp) * (off * off)
    var = group_total(jnp.broadcast_to(dev, (8, c)))[0:1] / (px * n_sp * size)
    return center, lax.rsqrt(var + EPSILON)


def combine_sums(every):
    n_sp = every.shape[0]
    total = every[0]
    for j in range(1, n_sp):
        total = total + every[j]
    return total


def edge_flags(n_sp, s):
    return jnp.where(s > 0, 1.0, 0.0), jnp.where(s < n_sp - 1, 1.0, 0.0)


def shifted(dst, row, width, block):
    col = lax.broadcasted_iota(jnp.int32, block.shape, 0)
    r = slice(row * width, (row + 1) * width)
    dst[1, r, :] = block.astype(BF16)
    dst[0, r, :] = jnp.where(col == 0, 0.0, pltpu.roll(block, 1, 0)).astype(BF16)
    dst[2, r, :] = jnp.where(col == width - 1, 0.0, pltpu.roll(block, width - 1, 0)).astype(BF16)


def joined(w_ref, *lead):
    return jnp.concatenate([w_ref[(j,) + lead] for j in range(4)], axis=-1)


def split_small(whole, n_sp):
    c = whole.shape[1]
    cols, out = 3 * c // n_sp, c // n_sp
    chunk = cols + out
    return (
        jnp.concatenate([whole[j * chunk : j * chunk + cols] for j in range(n_sp)]),
        jnp.concatenate([whole[j * chunk + cols : (j + 1) * chunk] for j in range(n_sp)]),
    )


def conv_kernel(n_sp, width, refs_in, x, up, dn, every, rows, w, *rest):
    base = None
    if refs_in:
        base, rest = rest[0], rest[1:]
    out, act, stats, above, below, a3 = rest[:6]
    scratch = rest[6:]
    step = pl.program_id(0)
    px, c = out.shape
    height = px // width

    @pl.when(step == 0)
    def _():
        exchange_greet(n_sp)
        center, inverse = combine_stats(every, px)
        mul = inverse * rows[0:1, :] * rows[2:3, :]
        add = rows[1:2, :] * rows[2:3, :] + rows[3:4, :]
        has_up, has_dn = edge_flags(n_sp, lax.axis_index("sp"))
        for r in range(height + 2):
            if r == 0:
                v = up[...]
            elif r == height + 1:
                v = dn[...]
            else:
                v = x[(r - 1) * width : r * width, :]
            v = silu((v.astype(F32) - center) * mul + add)
            if r == 0:
                v = v * has_up
            elif r == height + 1:
                v = v * has_dn
            act[r * width : (r + 1) * width, :] = v.astype(BF16)
            shifted(a3, r, width, v)
        if base is None:
            out[...] = jnp.zeros_like(out)
        else:
            out[...] = base[...].astype(F32)

    i, j = lax.div(step, 3), lax.rem(step, 3)
    lhs = a3[j, pl.ds(pl.multiple_of(i * width, width), px), :]
    out[...] += dot(lhs, joined(w, 0), 1, 1)

    @pl.when(step == 8)
    def _():
        channel_stats(scratch[0], out[...])
        exchange(n_sp, width, scratch, [out])
        stats[...] = scratch[1][...]
        above[...] = scratch[2][...]
        below[...] = scratch[3][...]


def whole_spec(shape):
    return pl.BlockSpec(shape, lambda t: (0,) * len(shape))


def conv_call(x, up, dn, every, rows, w, base, n_sp, width, cid):
    px, c = x.shape
    padded = px + 2 * width
    ins = [x, up, dn, every, rows, w] + ([] if base is None else [base])
    in_specs = [whole_spec(v.shape) for v in ins]
    in_specs[5] = pl.BlockSpec((4, 1, c, 128), lambda t: (0, t, 0, 0))
    outs = [((px, c), F32), ((padded, c), BF16), ((n_sp, 8, c), F32), ((width, c), F32), ((width, c), F32)]
    return pl.pallas_call(
        functools.partial(conv_kernel, n_sp, width, base is not None),
        grid=(9,),
        in_specs=in_specs,
        out_specs=[whole_spec(s) for s, _ in outs],
        out_shape=[jax.ShapeDtypeStruct(s, ty) for s, ty in outs],
        scratch_shapes=[pltpu.VMEM((3, padded, c), BF16)] + exchange_scratch(n_sp, width, [F32], c),
        compiler_params=params(cid, 1),
        name="conv_forward",
    )(*ins)


def qkv_kernel(n_sp, res, every, rows, w_small, cot, normed, qk, vg, qk_s, vg_s, ssem, rsem, lsem):
    at = Place()
    px, c = res.shape
    d = c // HEADS
    peers = [at.rp(k, n_sp) for k in range(1, n_sp)]
    greet(peers)
    center, inverse = combine_stats(every, px)
    n = ((res[...] - center) * (inverse * rows[0:1, :]) + rows[1:2, :]).astype(BF16)
    normed[...] = n
    wq, wp = split_small(joined(w_small), n_sp)
    q = dot(n, wq[:c], 1, 1).astype(BF16)
    k = dot(n, wq[c : 2 * c], 1, 1).astype(BF16)
    v = dot(n, wq[2 * c :], 1, 1).astype(BF16)
    g = dot(cot[...], wp, 1, 0).astype(BF16)
    for h in range(HEADS):
        cut = slice(h * d, (h + 1) * d)
        qk_s[h] = jnp.concatenate([q[:, cut], k[:, cut]], axis=1)
        vg_s[h] = jnp.concatenate([v[:, cut], g[:, cut]], axis=1)
    local = []
    for a, (src, dst) in enumerate(((qk_s, qk), (vg_s, vg))):
        cp = pltpu.make_async_copy(src.at[at.s], dst.at[at.s], lsem.at[a])
        cp.start()
        local.append(cp)
    greeted(len(peers))
    sent = []
    for j in range(1, n_sp):
        dev = at.rp(j, n_sp)
        for a, (src, dst) in enumerate(((qk_s, qk), (vg_s, vg))):
            sent.append(remote(src.at[dev[1]], dst.at[at.s], ssem.at[a, j], rsem.at[a, j], dev))
    for cp in local:
        cp.wait()
    for cp in sent:
        cp.wait()


def qkv_call(res, every, rows, w_small, cot, n_sp, cid):
    px, c = res.shape
    big = jax.ShapeDtypeStruct((n_sp, px, 128), BF16)
    return pl.pallas_call(
        functools.partial(qkv_kernel, n_sp),
        out_shape=[jax.ShapeDtypeStruct((px, c), BF16), big, big],
        in_specs=[VM] * 5,
        out_specs=[VM, ANY, ANY],
        scratch_shapes=[
            pltpu.VMEM((HEADS, px, 128), BF16),
            pltpu.VMEM((HEADS, px, 128), BF16),
            pltpu.SemaphoreType.DMA((2, n_sp)),
            pltpu.SemaphoreType.DMA((2, n_sp)),
            pltpu.SemaphoreType.DMA((2,)),
        ],
        compiler_params=params(cid),
        name="project_and_send",
    )(res, every, rows, w_small, cot)


def attention_kernel(L, T, BQ, BK, qk, vg, text, keep, od, dkv, dt, k_s, v_s, s_s, e_s, dk_s, dv_s):
    d = qk.shape[1] // 2
    step = pl.program_id(0)

    @pl.when(step == 0)
    def _():
        ones = (lax.broadcasted_iota(jnp.int32, (1, d), 1) == 0).astype(BF16)
        head = lax.axis_index("sp")
        pair, odd = lax.div(head, 2), lax.rem(head, 2)
        picked = []
        for j in (pair, HEADS // 2 + pair):
            blk = text[j].astype(F32)
            picked.append(jnp.where(odd > 0, blk[:, d:], blk[:, :d]).astype(BF16))
        k_s[0:T, :] = picked[0]
        v_s[0:T, :] = jnp.concatenate([picked[1], jnp.broadcast_to(ones, (T, d))], axis=1)
        k_s[T:, :] = qk[:, d:]
        v_s[T:, :] = jnp.concatenate([vg[:, :d], jnp.broadcast_to(ones, (L, d))], axis=1)
        dk_s[...] = jnp.zeros_like(dk_s)
        dv_s[...] = jnp.zeros_like(dv_s)

    r = pl.ds(pl.multiple_of(step * BQ, BQ), BQ)
    scale = d ** -0.5
    q = (qk[r, :][:, :d].astype(F32) * scale).astype(BF16)
    g = vg[r, :][:, d:]
    blocks = [(0, T)] + [(T + j * BK, BK) for j in range(L // BK)]
    peak = None
    for at, n in blocks:
        s = dot(q, k_s[at : at + n, :], 1, 1)
        if at == 0:
            s = jnp.where(keep[...] > 0, s, MASKED)
        s_s[:, at : at + n] = s
        for j in range(n // 128):
            part = s[:, 128 * j : 128 * j + 128]
            peak = part if peak is None else jnp.maximum(peak, part)
    peak = jnp.max(peak, axis=1, keepdims=True)
    o = jnp.zeros((BQ, 2 * d), F32)
    for at, n in blocks:
        e = jnp.exp(s_s[:, at : at + n] - peak).astype(BF16)
        e_s[:, at : at + n] = e
        o = o + dot(e, v_s[at : at + n, :], 1, 0)
    inverse = 1.0 / o[:, d : d + 1]
    o = o[:, :d] * inverse
    g = g.astype(F32) * inverse
    row = jnp.sum(o * g, axis=1, keepdims=True)
    g = g.astype(BF16)
    gt, qt = g.T, q.T
    dq = jnp.zeros((BQ, d), F32)
    for at, n in blocks:
        e = e_s[:, at : at + n]
        dp = dot(g, v_s[at : at + n, :d], 1, 1)
        ds = (e.astype(F32) * (dp - row)).astype(BF16)
        dq = dq + dot(ds, k_s[at : at + n, :], 1, 0)
        dv_s[:, at : at + n] += dot(gt, e, 1, 0)
        dk_s[:, at : at + n] += dot(qt, ds, 1, 0)
    od[...] = jnp.concatenate([o, dq * scale], axis=1).astype(BF16)

    @pl.when(step == pl.num_programs(0) - 1)
    def _():
        both = jnp.concatenate([dk_s[...], dv_s[...]], axis=0).astype(BF16).T
        dt[...] = both[:T]
        dkv[...] = both[T:]


def attention_call(qk, vg, text, keep):
    (L, d2), T = qk.shape, text.shape[1]
    BQ, BK = 256, 1024
    full = lambda shape: pl.BlockSpec(shape, lambda t: (0, 0))
    return pl.pallas_call(
        functools.partial(attention_kernel, L, T, BQ, BK),
        grid=(L // BQ,),
        in_specs=[full((L, d2)), full((L, d2)), pl.BlockSpec(text.shape, lambda t: (0, 0, 0)), full((1, T))],
        out_specs=[pl.BlockSpec((BQ, d2), lambda t: (t, 0)), full((L, d2)), full((T, d2))],
        out_shape=[jax.ShapeDtypeStruct(s, BF16) for s in ((L, d2), (L, d2), (T, d2))],
        scratch_shapes=[
            pltpu.VMEM((T + L, d2 // 2), BF16),
            pltpu.VMEM((T + L, d2), BF16),
            pltpu.VMEM((BQ, T + L), F32),
            pltpu.VMEM((BQ, T + L), BF16),
            pltpu.VMEM((d2 // 2, T + L), F32),
            pltpu.VMEM((d2 // 2, T + L), F32),
        ],
        compiler_params=params(None, 1),
        name="attention",
    )(qk, vg, text, keep)


class Mail:
    def __init__(self, ssem, rsem):
        self.ssem, self.rsem, self.sent = ssem, rsem, []

    def send(self, src, dst, dev):
        j = len(self.sent)
        cp = remote(src, dst, self.ssem.at[j], self.rsem.at[j], dev)
        self.sent.append(cp)
        return cp


def img_peers(at):
    return [(lax.rem(at.i + k, 4), at.s) for k in range(1, 4)]


HEAD_MAIL = 3 * 3 + 3 + 2 * 7 + 7 + 4


def head_kernel(nz, width, dims, *refs):
    na = len(dims)
    ins, refs = refs[: na - 1], refs[na - 1 :]
    x, cot, temb, cap, w_emb, w_cap, gains, biases, w_qkv, w_proj = refs[:10]
    outs, refs = refs[10 : 10 + na], refs[10 + na :]
    st0, xa, xb, ca, cb, rows, kv_all, cap_all, emb_all = refs[:9]
    (ssem, rsem, lsem, mine, every, h0, h1, h2, h3, aff_s, emb_s, cap_s, part, part_r, kv_s, kv_r, mod_s, mod_r,
     msend, mrecv, emb, affine, small) = refs[9:]
    ins = list(ins) + [small]
    n_sp = 2 * nz
    at = Place()
    line = [at.rp(k, n_sp) for k in range(1, n_sp)]
    grid = img_peers(at)
    greet(line + grid)
    mail = Mail(msend, mrecv)
    local = []
    sent = {}
    kinds = {}

    def view(a, ii, k, core, half=None):
        r = dims[a][1]
        sp = 2 * lax.rem(at.z - k + nz, nz) + core
        if half is None:
            return outs[a].at[ii, :, pl.ds(pl.multiple_of(sp * r, r), r), :]
        h = r // 2
        return outs[a].at[ii, :, pl.ds(pl.multiple_of(sp * r + half * h, h), h), :]

    def send(a, kind, src, dst, dev):
        j = kinds.setdefault(kind, len(kinds))
        sent[a, kind] = remote(src, dst, ssem.at[a, j], rsem.at[a, j], dev)

    def forward(a, kind, ref, dev):
        send(a, kind, ref, ref, dev)

    def first(a):
        own = view(a, at.i, 0, at.c)
        for k in range(1, nz):
            send(a, ("z", k), ins[a], own, at.zp(k, nz))
        send(a, ("x", 0), ins[a], own, at.xn)
        send(a, ("y", 0), ins[a], own, at.yn)
        send(a, ("s", 0), ins[a], own, at.sib)

    def second(a):
        for k in range(1, nz):
            sent[a, ("z", k)].wait_recv()
            got = view(a, at.i, k, at.c)
            forward(a, ("x", k), got, at.xn)
            forward(a, ("y", k), got, at.yn)
            forward(a, ("s", k), got, at.sib)

    def third(a):
        for k in range(nz):
            sent[a, ("x", k)].wait_recv()
            forward(a, ("da", k), view(a, at.ix, k, at.c, 0), at.yn)
            forward(a, ("sx", k), view(a, at.ix, k, at.c), at.sib)
            sent[a, ("y", k)].wait_recv()
            forward(a, ("db", k), view(a, at.iy, k, at.c, 1), at.xn)
            forward(a, ("sy", k), view(a, at.iy, k, at.c), at.sib)

    def fourth(a):
        for k in range(nz):
            sent[a, ("da", k)].wait_recv()
            forward(a, ("sa", k), view(a, at.id, k, at.c, 0), at.sib)
            sent[a, ("db", k)].wait_recv()
            forward(a, ("sb", k), view(a, at.id, k, at.c, 1), at.sib)

    cut = w_qkv.shape[0]
    small[0, :cut] = w_qkv[...]
    small[0, cut:] = w_proj[...]
    e = cap.shape[1] // 4
    embedded = silu(temb[...].astype(F32)).astype(BF16).astype(F32)
    for j in range(4):
        emb[j] = jnp.broadcast_to(embedded[:, j * e : (j + 1) * e], (8, e))
    affine[0:3] = gains[...].astype(F32)
    affine[3:6] = biases[...].astype(F32)
    channel_stats(mine, x[...].astype(F32))
    greeted(n_sp + 2)
    first(0)
    round1 = []
    for dev in grid:
        round1.append(mail.send(affine, aff_s.at[at.i], dev))
        round1.append(mail.send(emb.at[dev[0]], emb_s.at[at.i], dev))
        round1.append(mail.send(cap.at[:, pl.ds(pl.multiple_of(dev[0] * e, e), e)], cap_s.at[at.i], dev))
    own_cap = pltpu.make_async_copy(cap.at[:, pl.ds(pl.multiple_of(at.i * e, e), e)], cap_s.at[at.i], lsem.at[na])
    own_cap.start()
    aff_s[at.i] = affine[...]
    emb_s[at.i] = emb[at.i]
    px = x.shape[0]
    stat = []
    for ref, above, below in ((x, h0, h1), (cot, h2, h3)):
        stat.append(mail.send(ref.at[px - width :], above, line[0]))
        stat.append(mail.send(ref.at[:width], below, line[-1]))
    for dev in line:
        stat.append(mail.send(mine, every.at[at.s], dev))
    every[at.s] = mine[...]
    for a in range(na):
        cp = pltpu.make_async_copy(ins[a], view(a, at.i, 0, at.c), lsem.at[a])
        cp.start()
        local.append(cp)
    tokens = cap.shape[0]
    round2, round3 = [], []

    def extras(tick):
        if tick == 1:
            own_cap.wait()
            for cp in round1:
                cp.wait_recv()
            for j in range(4):
                part[j, :tokens] = dot(cap_s[j], w_cap[...], 1, 0)
                part[j, tokens:] = dot(emb_s[j].astype(BF16), w_emb[...], 1, 0)
            for dev in grid:
                round2.append(mail.send(part.at[dev[0]], part_r.at[at.i], dev))
            part_r[at.i] = part[at.i]
        if tick == 2:
            for cp in round2:
                cp.wait_recv()
            total = part_r[0] + part_r[1] + part_r[2] + part_r[3]
            kv_s[...] = total[:tokens].astype(BF16)
            mod_s[...] = total[tokens:]
            for dev in line:
                round3.append(mail.send(kv_s, kv_r.at[at.s], dev))
                round3.append(mail.send(mod_s, mod_r.at[at.s], dev))
            kv_r[at.s] = kv_s[...]
            mod_r[at.s] = mod_s[...]
        if tick == 4:
            for cp in round3 + stat:
                cp.wait_recv()
            kv_all[...] = kv_r[...]
            cap_all[...] = cap_s[...]
            emb_all[...] = jnp.concatenate([emb_s[j][0:1] for j in range(4)] + [jnp.zeros((4, e), F32)])
            st0[...] = every[...]
            for dst, src in ((xa, h0), (xb, h1), (ca, h2), (cb, h3)):
                dst[...] = src[...]
            aff = jnp.concatenate([aff_s[j] for j in range(4)], axis=1)
            mod = jnp.concatenate([mod_r[j][0:1] for j in range(n_sp)], axis=1)
            c = aff.shape[1]
            rows[...] = jnp.zeros_like(rows)
            for j in range(3):
                rows[j, 0:1] = aff[j : j + 1]
                rows[j, 1:2] = aff[3 + j : 4 + j]
                rows[j, 2:3] = 1.0 + mod[:, :c] if j == 1 else jnp.ones((1, c), F32)
            rows[1, 3:4] = mod[:, c:]

    stages = (first, second, third, fourth)
    for tick in range(1, na + 3):
        for a in range(na):
            stage = tick - a
            if 0 <= stage < 4 and (stage, a) != (0, 0):
                stages[stage](a)
        extras(tick)
    for cp in local:
        cp.wait()
    for (a, kind), cp in sent.items():
        if kind[0] in ("s", "sx", "sy", "sa", "sb"):
            cp.wait_recv()
        cp.wait_send()
    for cp in mail.sent:
        cp.wait_send()


def head_call(chunks, x, cot, temb, cap, w_emb, w_cap, gains, biases, w_qkv, w_proj, nz, width, cid):
    dims = [c.shape[:2] for c in chunks] + [(1, w_qkv.shape[0] + w_proj.shape[0])]
    na = len(dims)
    n_sp = 2 * nz
    copies = 3 * nz - 1 + 7 * nz
    px, c = x.shape
    tokens, wide = cap.shape
    e = wide // 4
    edge = ((width, c), BF16)
    outs = [
        ((n_sp, 8, c), F32), edge, edge, edge, edge, ((3, 8, c), F32), ((n_sp, tokens, 128), BF16),
        ((4, tokens, e), BF16), ((8, e), F32),
    ]
    return pl.pallas_call(
        functools.partial(head_kernel, nz, width, dims),
        out_shape=[jax.ShapeDtypeStruct((4, t, n_sp * r, 128), BF16) for t, r in dims]
        + [jax.ShapeDtypeStruct(s, ty) for s, ty in outs],
        in_specs=[ANY] * (na - 1) + [VM, VM, VM, ANY] + [VM] * 6,
        out_specs=[ANY] * na + [VM] * len(outs),
        scratch_shapes=[
            pltpu.SemaphoreType.DMA((na, copies)),
            pltpu.SemaphoreType.DMA((na, copies)),
            pltpu.SemaphoreType.DMA((na + 1,)),
            pltpu.VMEM((8, c), F32),
            pltpu.VMEM((n_sp, 8, c), F32),
            pltpu.VMEM((width, c), BF16), pltpu.VMEM((width, c), BF16),
            pltpu.VMEM((width, c), BF16), pltpu.VMEM((width, c), BF16),
            pltpu.VMEM((4, 8, 128), F32),
            pltpu.VMEM((4, 8, e), F32),
            pltpu.VMEM((4, tokens, e), BF16),
            pltpu.VMEM((4, tokens + 8, 128), F32),
            pltpu.VMEM((4, tokens + 8, 128), F32),
            pltpu.VMEM((tokens, 128), BF16),
            pltpu.VMEM((n_sp, tokens, 128), BF16),
            pltpu.VMEM((8, 128), F32),
            pltpu.VMEM((n_sp, 8, 128), F32),
            pltpu.SemaphoreType.DMA((HEAD_MAIL,)),
            pltpu.SemaphoreType.DMA((HEAD_MAIL,)),
            pltpu.VMEM((4, 8, e), F32),
            pltpu.VMEM((8, 128), F32),
            pltpu.VMEM((1,) + dims[-1][1:] + (128,), BF16),
        ],
        compiler_params=params(cid),
        name="gather_weights",
    )(*chunks, x, cot, temb, cap, w_emb, w_cap, gains, biases, w_qkv, w_proj)


class Reducer:
    NAMES = ("d", "sb", "da", "db", "rx", "ry", "r", "zr")

    def __init__(self, at, nz, arrays, ssem, rsem):
        self.at, self.nz, self.arrays = at, nz, arrays
        self.ssem, self.rsem = ssem, rsem
        self.sent, self.groups = {}, []

    @staticmethod
    def buffers(nz, t, r):
        return [
            pltpu.VMEM((2, 4, t, nz, r, 128), BF16),
            pltpu.VMEM((4, t, nz, r, 128), BF16),
            pltpu.VMEM((t, nz, r // 2, 128), BF16),
            pltpu.VMEM((t, nz, r // 2, 128), BF16),
            pltpu.VMEM((t, nz, r, 128), BF16),
            pltpu.VMEM((t, nz, r, 128), BF16),
            pltpu.VMEM((t, nz, r, 128), BF16),
            pltpu.VMEM((nz - 1, t, r, 128), BF16),
        ]

    def send(self, g, j, src, dst, dev):
        self.sent[g, j] = remote(src, dst, self.ssem.at[g, j], self.rsem.at[g, j], dev)

    def add(self, a, t0, t1):
        g = len(self.groups)
        self.groups.append((a, t0, t1))
        b = self.arrays[a][1]
        self.send(g, 0, b["d"].at[1 - self.at.c, :, t0:t1], b["sb"].at[:, t0:t1], self.at.sib)

    def run(self, stage, *groups):
        one = (self.stage1, self.stage2, self.stage3, self.stage4)[stage - 1]
        for g in groups:
            one(g, *self.groups[g])

    def stage1(self, g, a, t0, t1):
        b, at = self.arrays[a][1], self.at
        d, sb = b["d"], b["sb"]
        self.sent[g, 0].wait_recv()
        n = t1 - t0

        def add(j, _):
            ii, tt = lax.div(j, n), t0 + lax.rem(j, n)
            d[at.c, ii, tt] = (d[at.c, ii, tt].astype(F32) + sb[ii, tt].astype(F32)).astype(BF16)
            return 0

        lax.fori_loop(0, 4 * n, add, 0)
        h = d.shape[4] // 2
        self.send(g, 1, d.at[at.c, at.id, t0:t1, :, :h], b["da"].at[t0:t1], at.yn)
        self.send(g, 2, d.at[at.c, at.id, t0:t1, :, h:], b["db"].at[t0:t1], at.xn)

    def stage2(self, g, a, t0, t1):
        b, at = self.arrays[a][1], self.at
        d = b["d"]
        h = d.shape[4] // 2
        self.sent[g, 1].wait_recv()
        self.sent[g, 2].wait_recv()

        def add(tt, _):
            d[at.c, at.ix, tt, :, :h] = (
                d[at.c, at.ix, tt, :, :h].astype(F32) + b["da"][tt].astype(F32)
            ).astype(BF16)
            d[at.c, at.iy, tt, :, h:] = (
                d[at.c, at.iy, tt, :, h:].astype(F32) + b["db"][tt].astype(F32)
            ).astype(BF16)
            return 0

        lax.fori_loop(t0, t1, add, 0)
        self.send(g, 3, d.at[at.c, at.ix, t0:t1], b["rx"].at[t0:t1], at.xn)
        self.send(g, 4, d.at[at.c, at.iy, t0:t1], b["ry"].at[t0:t1], at.yn)

    def stage3(self, g, a, t0, t1):
        b, at = self.arrays[a][1], self.at
        self.sent[g, 3].wait_recv()
        self.sent[g, 4].wait_recv()

        def add(tt, _):
            total = b["d"][at.c, at.i, tt].astype(F32) + b["rx"][tt].astype(F32) + b["ry"][tt].astype(F32)
            b["r"][tt] = total.astype(BF16)
            return 0

        lax.fori_loop(t0, t1, add, 0)
        for k in range(1, self.nz):
            there = lax.rem(at.z + k, self.nz)
            self.send(g, 4 + k, b["r"].at[t0:t1, there], b["zr"].at[k - 1, t0:t1], at.zp(k, self.nz))

    def stage4(self, g, a, t0, t1):
        (out, b), at = self.arrays[a], self.at
        for k in range(1, self.nz):
            self.sent[g, 4 + k].wait_recv()

        def add(tt, _):
            total = (
                b["d"][at.c, at.i, tt, at.z].astype(F32)
                + b["rx"][tt, at.z].astype(F32)
                + b["ry"][tt, at.z].astype(F32)
            )
            for k in range(1, self.nz):
                total = total + b["zr"][k - 1, tt].astype(F32)
            out[tt] = total
            return 0

        lax.fori_loop(t0, t1, add, 0)

    def finish(self):
        for cp in self.sent.values():
            cp.wait_send()


BACK_MAIL = 6 + 14 + 6 + 3 + 7 + 9 + 9
BACK_GROUPS = 7
BIG = 10


def conv_taps(t0, t1, w, ring, rsem, one):
    slots = ring.shape[0]

    def step(tap, _):
        slot = lax.rem(tap, slots)
        pltpu.make_async_copy(w.at[:, tap], ring.at[slot], rsem.at[slot]).wait()
        one(tap, jnp.concatenate([ring[slot, j] for j in range(4)], axis=-1))

        @pl.when(tap + slots < 9)
        def _():
            pltpu.make_async_copy(w.at[:, tap + slots], ring.at[slot], rsem.at[slot]).start()

        return 0

    lax.fori_loop(t0, t1, step, 0)


def ring_start(w, ring, rsem):
    for j in range(ring.shape[0]):
        pltpu.make_async_copy(w.at[:, j], ring.at[j], rsem.at[j]).start()


def backward_kernel(nz, width, *refs):
    hbm, refs = refs[:BIG], refs[BIG:]
    w_in, w_out = refs[:2]
    (st0, st1, st2, rows, ca, cb, ra, rb, ha, hb, dt_all, cap_all, emb_all, w_emb, w_cap, temb) = refs[2:18]
    output, image_grad, s_in, s_out, s_small, g_temb, g_cap, g_wemb, g_wcap, g_aff = refs[18:28]
    refs = refs[28:]
    big, refs = refs[:BIG], refs[BIG:]
    bufs = [dict(zip(Reducer.NAMES, refs[8 * a : 8 * a + 8])) for a in range(3)]
    (bsem, gsend, grecv, msend, mrecv, ring, rsem, a3, g3, gt, acc, ng, pre_grad, res_grad,
     mine, every, na, nb, pa, pb, tg_s, tg_r, mod_s, mod_r,
     gc_s, gc_r, pe_s, pe_r, gs_s, gs_r, ps_s, ps_r, aff_s, aff_r) = refs[24:]
    n_sp = 2 * nz
    at = Place()
    line = [at.rp(k, n_sp) for k in range(1, n_sp)]
    grid = img_peers(at)
    greet(line + grid)
    loads = []
    for j in range(BIG):
        cp = pltpu.make_async_copy(hbm[j], big[j], bsem.at[j])
        cp.start()
        loads.append(cp)
    od, dkv, w_small, res, cot, normed, act1, hidden, act0, x = big
    ring_start(w_out, ring, rsem)
    mail = Mail(msend, mrecv)
    red = Reducer(at, nz, [(s_out, bufs[0]), (s_small, bufs[1]), (s_in, bufs[2])], gsend, grecv)
    px, c = res.shape
    height = px // width
    members = px * n_sp * (c // GROUPS)
    d = c // HEADS
    cols = 3 * c // n_sp

    def publish(j, rows01, edges):
        out = []
        for ref, above, below in edges:
            out.append(mail.send(ref.at[px - width :], above, line[0]))
            out.append(mail.send(ref.at[:width], below, line[-1]))
        mine[j] = jnp.zeros((8, c), F32)
        mine[j, 0:1] = rows01[0]
        mine[j, 1:2] = rows01[1]
        for dev in line:
            out.append(mail.send(mine.at[j], every.at[j, at.s], dev))
        every[j, at.s] = mine[j]
        return out

    for j in range(6):
        loads[j].wait()
    att = jnp.concatenate([od[h][:, :d] for h in range(HEADS)], axis=1)
    pg = jnp.concatenate(
        [od[h][:, d:] for h in range(HEADS)]
        + [dkv[h][:, :d] for h in range(HEADS)]
        + [dkv[h][:, d:] for h in range(HEADS)],
        axis=1,
    )
    wq, wp = split_small(joined(w_small), n_sp)
    ng[...] = dot(pg, wq, 1, 0)
    center2, inverse2 = combine_stats(st2, px)
    hat = (res[...] - center2) * inverse2
    u = ng[...]
    sums = (jnp.sum(u, axis=0, keepdims=True), jnp.sum(u * hat, axis=0, keepdims=True))
    greeted(n_sp + 2)
    round_2 = publish(2, sums, [(ng, na, nb)])
    gq = dot(pg, normed[...], 0, 0).astype(BF16)
    go = dot(cot[...], att, 0, 0).astype(BF16)
    small = bufs[1]["d"]
    for j in range(n_sp):
        for b in range(4):
            lanes = slice(b * 128, (b + 1) * 128)
            small[j % 2, b, 0, j // 2, :cols] = gq[j * cols : (j + 1) * cols, lanes]
            small[j % 2, b, 0, j // 2, cols:] = go[j * (c // n_sp) : (j + 1) * (c // n_sp), lanes]
    red.add(1, 0, 1)
    output[...] = (res[...] + dot(att, wp, 1, 1)).astype(BF16)

    first = 2 * lax.rem(at.s, nz)
    value = lax.div(at.s, nz)
    halves = []
    for j in range(2):
        blk = dt_all[first + j].astype(F32)
        halves.append(jnp.where(value > 0, blk[:, d:], blk[:, :d]))
    tg_s[...] = jnp.concatenate(halves, axis=1).astype(BF16)
    round_a = [mail.send(tg_s, tg_r.at[at.i], dev) for dev in grid]
    tg_r[at.i] = tg_s[...]

    has_up, has_dn = edge_flags(n_sp, at.s)

    def upstream(j, uu, ua, ub, center, inverse, yy, ya, yb, act, base, keep):
        total = combine_sums(every[j])
        mul = rows[j, 0:1] * rows[j, 2:3]
        back = group_total(total * mul) / members
        s1, s2 = back[0:1, :], back[1:2, :]
        for r in range(height + 2):
            cut = slice((r - 1) * width, r * width)
            top, end = r == 0, r == height + 1
            un = ua[...] if top else ub[...] if end else uu[cut, :]
            yn = ya[...] if top else yb[...] if end else yy[cut, :]
            g = inverse * (un * mul - s1 - (yn - center) * inverse * s2)
            if base:
                g = g + (base[1][...] if top else base[2][...] if end else base[0][cut, :]).astype(F32)
            if top:
                g = g * has_up
            elif end:
                g = g * has_dn
            elif keep is not None:
                keep[cut, :] = g
            shifted(g3, r, width, g.astype(BF16).astype(F32))
            shifted(a3, r, width, act[r * width : (r + 1) * width, :].astype(F32))
        gt[...] = g3[1, width : width + px, :].T
        return total

    def weight_taps(a, t0, t1):
        dst = bufs[a]["d"]

        def one(tap, _):
            i, j = lax.div(tap, 3), lax.rem(tap, 3)
            part = dot(gt[...], a3[j, pl.ds(pl.multiple_of(i * width, width), px), :], 1, 0).astype(BF16)
            r = c // n_sp
            for k in range(n_sp):
                for b in range(4):
                    dst[k % 2, b, tap, k // 2] = part[k * r : (k + 1) * r, b * 128 : (b + 1) * 128]
            return 0

        lax.fori_loop(t0, t1, one, 0)
        red.add(a, t0, t1)

    def input_taps(w):
        def one(tap, wt):
            i, j = lax.div(tap, 3), lax.rem(tap, 3)
            lhs = g3[2 - j, pl.ds(pl.multiple_of((2 - i) * width, width), px), :]
            acc[...] = dot(lhs, wt, 1, 0) + jnp.where(tap > 0, acc[...], 0.0)

        conv_taps(0, 9, w, ring, rsem, one)

    for cp in round_2:
        cp.wait_recv()
    loads[6].wait()
    t2 = upstream(2, ng, na, nb, center2, inverse2, res, ra, rb, act1, (cot, ca, cb), res_grad)
    red.run(1, 0)
    for tap in (0, 3, 6):
        weight_taps(0, tap, tap + 3)
    red.run(2, 0)
    input_taps(w_out)
    ring_start(w_in, ring, rsem)
    for j in range(7, BIG):
        loads[j].wait()
    center1, inverse1 = combine_stats(st1, px)
    hat = (hidden[...] - center1) * inverse1
    gain1, bias1, fac1 = rows[1, 0:1], rows[1, 1:2], rows[1, 2:3]
    v = acc[...] * silu_slope(hat * (gain1 * fac1) + (bias1 * fac1 + rows[1, 3:4]))
    pre_grad[...] = v
    sums = (jnp.sum(v, axis=0, keepdims=True), jnp.sum(v * hat, axis=0, keepdims=True))
    round_1 = publish(1, sums, [(pre_grad, pa, pb)])
    red.run(1, 1, 2, 3)
    red.run(3, 0)

    exact = lambda a, b, ca_, cb_: lax.dot_general(
        a, b, (((ca_,), (cb_,)), ((), ())), preferred_element_type=F32, precision=PRECISE
    )
    tokens = tg_s.shape[0]
    share = tokens // n_sp
    for cp in round_a:
        cp.wait_recv()
    flat_tg = tg_r[...].reshape(4 * tokens, 128)
    g_wcap[...] = dot(cap_all[...].reshape(4 * tokens, cap_all.shape[2]), flat_tg, 0, 0)
    gc_s[...] = dot(flat_tg, w_cap[...], 1, 1).astype(BF16).reshape(gc_s.shape)
    round_b = []
    for dev in line:
        cut = pl.ds(pl.multiple_of(dev[1] * share, share), share)
        round_b.append(mail.send(gc_s.at[:, cut, :], gc_r.at[at.s], dev))
    gc_r[at.s] = gc_s[:, pl.ds(pl.multiple_of(at.s * share, share), share), :]

    for cp in round_1:
        cp.wait_recv()
    t1 = upstream(1, pre_grad, pa, pb, center1, inverse1, hidden, ha, hb, act0, None, None)
    mod = jnp.concatenate([t1[1:2] * gain1 + t1[0:1] * bias1, t1[0:1]], axis=1)
    for j in range(n_sp):
        mod_s[j] = jnp.broadcast_to(mod[:, j * 128 : (j + 1) * 128], (8, 128))
    round_m = [mail.send(mod_s.at[at.s], mod_r.at[at.i], dev) for dev in grid]
    mod_r[at.i] = mod_s[at.s]
    red.run(2, 1)
    weight_taps(2, 0, 3)
    red.run(2, 2)
    weight_taps(2, 3, 6)
    red.run(2, 3)
    weight_taps(2, 6, 9)
    input_taps(w_in)

    center0, inverse0 = combine_stats(st0, px)
    hat = (x[...].astype(F32) - center0) * inverse0
    gain0 = rows[0, 0:1]
    v = acc[...] * silu_slope(hat * gain0 + rows[0, 1:2])
    acc[...] = v
    sums = (jnp.sum(v, axis=0, keepdims=True), jnp.sum(v * hat, axis=0, keepdims=True))
    round_0 = publish(0, sums, [])
    red.run(1, 4, 5, 6)
    red.run(4, 0)
    for cp in round_m:
        cp.wait_recv()
    mods = jnp.concatenate([mod_r[j][0:1] for j in range(4)] + [jnp.zeros((4, 128), F32)])
    emb_t = emb_all[...].T
    g_wemb[...] = sum(emb_t[:, j : j + 1] * mods[j : j + 1] for j in range(4))
    pe_s[...] = exact(mods, w_emb[...].astype(F32), 1, 1)
    round_p = [mail.send(pe_s, pe_r.at[at.s], dev) for dev in line]
    pe_r[at.s] = pe_s[...]
    for cp in round_0:
        cp.wait_recv()
    t0 = combine_sums(every[0])
    zero = jnp.zeros((2, c), F32)
    aff = jnp.concatenate([t0[1:2], t1[1:2] * fac1, t2[1:2], t0[0:1], t1[0:1] * fac1, t2[0:1], zero])
    for j in range(4):
        aff_s[j] = aff[:, j * 128 : (j + 1) * 128]
    round_e = [mail.send(aff_s.at[dev[0]], aff_r.at[at.i], dev) for dev in grid]
    aff_r[at.i] = aff_s[at.i]
    total = group_total(t0 * gain0) / members
    image_grad[...] = res_grad[...] + inverse0 * (acc[...] * gain0 - total[0:1] - hat * total[1:2])
    for g in (1, 2, 3):
        red.run(3, g)
        red.run(2, g + 3)
    for cp in round_b + round_p:
        cp.wait_recv()
    gc = gc_r[0].astype(F32)
    pe = pe_r[0]
    for j in range(1, n_sp):
        gc = gc + gc_r[j].astype(F32)
        pe = pe + pe_r[j]
    gs_s[...] = gc
    for j in range(4):
        ps_s[j] = jnp.broadcast_to(pe[j : j + 1], pe.shape)
    round_c = []
    for dev in grid:
        round_c.append(mail.send(gs_s.at[dev[0]], gs_r.at[at.i], dev))
        round_c.append(mail.send(ps_s.at[dev[0]], ps_r.at[at.i], dev))
    gs_r[at.i] = gs_s[at.i]
    ps_r[at.i] = ps_s[at.i]
    red.run(4, 1, 2, 3)
    red.run(3, 4, 5, 6)
    red.run(4, 4, 5, 6)
    red.finish()
    for cp in round_c + round_e:
        cp.wait_recv()
    g_cap[...] = jnp.concatenate([gs_r[j] for j in range(4)], axis=1)
    g_temb[...] = jnp.concatenate([ps_r[j] for j in range(4)], axis=1) * silu_slope(temb[...].astype(F32))
    g_aff[...] = aff_r[0] + aff_r[1] + aff_r[2] + aff_r[3]
    for cp in mail.sent:
        cp.wait_send()


def backward_call(big, w_in, w_out, small, nz, width, cid):
    px, c = big[3].shape
    n_sp = 2 * nz
    padded = px + 2 * width
    r = c // n_sp
    rs = big[2].shape[1] // n_sp
    dt_all, cap_all = small[10], small[11]
    tokens = dt_all.shape[1]
    e = cap_all.shape[2]
    share = tokens // n_sp
    outs = [
        ((px, c), BF16), ((px, c), F32), ((9, r, 128), F32), ((9, r, 128), F32), ((1, rs, 128), F32),
        ((8, 4 * e), F32), ((share, 4 * e), F32), ((e, 128), F32), ((e, 128), F32), ((8, 128), F32),
    ]
    vm = pltpu.VMEM
    return pl.pallas_call(
        functools.partial(backward_kernel, nz, width),
        out_shape=[jax.ShapeDtypeStruct(s, ty) for s, ty in outs],
        in_specs=[ANY] * (len(big) + 2) + [VM] * len(small),
        out_specs=[VM] * len(outs),
        scratch_shapes=[vm(v.shape, v.dtype) for v in big]
        + Reducer.buffers(nz, 9, r) + Reducer.buffers(nz, 1, rs) + Reducer.buffers(nz, 9, r)
        + [
            pltpu.SemaphoreType.DMA((len(big),)),
            pltpu.SemaphoreType.DMA((BACK_GROUPS, 4 + nz)),
            pltpu.SemaphoreType.DMA((BACK_GROUPS, 4 + nz)),
            pltpu.SemaphoreType.DMA((BACK_MAIL,)),
            pltpu.SemaphoreType.DMA((BACK_MAIL,)),
            vm((3, 4, c, 128), BF16),
            pltpu.SemaphoreType.DMA((3,)),
            vm((3, padded, c), BF16), vm((3, padded, c), BF16), vm((c, px), BF16),
            vm((px, c), F32), vm((px, c), F32), vm((px, c), F32), vm((px, c), F32),
            vm((3, 8, c), F32), vm((3, n_sp, 8, c), F32),
            vm((width, c), F32), vm((width, c), F32), vm((width, c), F32), vm((width, c), F32),
            vm((tokens, 128), BF16), vm((4, tokens, 128), BF16),
            vm((n_sp, 8, 128), F32), vm((4, 8, 128), F32),
            vm((4, tokens, e), BF16), vm((n_sp, 4, share, e), BF16),
            vm((8, e), F32), vm((n_sp, 8, e), F32),
            vm((4, share, e), F32), vm((4, share, e), F32),
            vm((4, 8, e), F32), vm((4, 8, e), F32),
            vm((4, 8, 128), F32), vm((4, 8, 128), F32),
        ],
        compiler_params=params(cid),
        name="backward",
    )(*big, w_in, w_out, *small)


def emit_kernel(cut, *refs):
    ins, outs, mids, loads, stores = refs[:10], refs[10:22], refs[22:31], refs[31], refs[32]
    output, image, s_in, s_out, s_small, g_temb, g_cap, g_wemb, g_wcap, g_aff = ins
    pairs = [
        (output, outs[0]), (image, outs[1]), (g_cap, outs[3]), (s_in, outs[4]), (s_out, outs[5]), (g_wemb, outs[6]),
        (s_small.at[0, :cut], outs[7]), (g_wcap, outs[8]), (s_small.at[0, cut:], outs[9]),
    ]
    copies = [pltpu.make_async_copy(src, mid, loads.at[j]) for j, ((src, _), mid) in enumerate(zip(pairs, mids))]
    for cp in copies:
        cp.start()
    backs = []
    for j, cp in enumerate(copies):
        cp.wait()
        backs.append(pltpu.make_async_copy(mids[j], pairs[j][1], stores.at[j]))
        backs[-1].start()
    outs[2][...] = g_temb[0:1, :]
    outs[10][...] = g_aff[0:3, :]
    outs[11][...] = g_aff[3:6, :]
    for cp in backs:
        cp.wait()


def emit_call(parts, cut):
    output, image, s_in, s_out, s_small, g_temb, g_cap, g_wemb, g_wcap, g_aff = parts
    rest = s_small.shape[1] - cut
    like = lambda v: jax.ShapeDtypeStruct(v.shape, v.dtype)
    f32 = lambda *s: jax.ShapeDtypeStruct(s, F32)
    shapes = [
        like(output), like(image), f32(1, g_temb.shape[1]), like(g_cap), like(s_in), like(s_out), like(g_wemb),
        f32(cut, 128), like(g_wcap), f32(rest, 128), f32(3, 128), f32(3, 128),
    ]
    in_specs = [ANY] * 10
    in_specs[5] = in_specs[9] = VM
    out_specs = [ANY] * 12
    out_specs[2] = out_specs[10] = out_specs[11] = VM
    return pl.pallas_call(
        functools.partial(emit_kernel, cut),
        out_shape=shapes,
        in_specs=in_specs,
        out_specs=out_specs,
        scratch_shapes=[pltpu.VMEM(shapes[j].shape, shapes[j].dtype) for j in (0, 1, 3, 4, 5, 6, 7, 8, 9)]
        + [pltpu.SemaphoreType.DMA((9,)), pltpu.SemaphoreType.DMA((9,))],
        compiler_params=params(),
        name="emit",
    )(*parts)


def fast_body(
    image_in, time_embed, caption, caption_mask, conv_in, conv_out, embed_proj, qkv_proj,
    caption_proj, out_proj, norm_gains, norm_biases, cotangent,
):
    n, height, width, c = image_in.shape
    n_img, n_sp = lax.axis_size("img"), lax.axis_size("sp")
    sp = lax.axis_index("sp")
    nz = n_sp // 2
    px = height * width
    d = c // HEADS
    x = image_in.reshape(px, c)
    cot = cotangent.reshape(px, c)

    flat = lambda w: w.transpose(1, 2, 3, 0).reshape(9, w.shape[3], w.shape[0])
    (w_in, w_out, w_small, st0, xa, xb, ca, cb, rows, kv_all, cap_all, emb_all) = head_call(
        [flat(conv_in), flat(conv_out)], x, cot, time_embed, caption[0], embed_proj, caption_proj,
        norm_gains, norm_biases, qkv_proj.T, out_proj.T, nz, width, 0,
    )
    w_small = w_small.reshape(4, -1, 128)

    hidden, act0, st1, ha, hb = conv_call(x, xa, xb, st0, rows[0], w_in, None, n_sp, width, 1)
    res, act1, st2, ra, rb = conv_call(hidden, ha, hb, st1, rows[1], w_out, x, n_sp, width, 2)
    normed, qk, vg = qkv_call(res, st2, rows[2], w_small, cot, n_sp, 3)
    od, dkv, dt = attention_call(qk.reshape(-1, 2 * d), vg.reshape(-1, 2 * d), kv_all, caption_mask)
    od, dkv, dt_all = trade([od.reshape(n_sp, px, 2 * d), dkv.reshape(n_sp, px, 2 * d)], dt, n_sp, 4)

    parts = backward_call(
        [od, dkv, w_small, res, cot, normed, act1, hidden, act0, x], w_in, w_out,
        [st0, st1, st2, rows, ca, cb, ra, rb, ha, hb, dt_all, cap_all, emb_all, embed_proj, caption_proj, time_embed],
        nz, width, 5,
    )
    output, image, g_temb, g_cap, s_in, s_out, g_wemb, g_qkv, g_wcap, g_out, g_gains, g_biases = emit_call(
        parts, qkv_proj.shape[1]
    )
    unflat = lambda g: g.reshape(3, 3, g.shape[1], 128).transpose(3, 0, 1, 2)
    return (
        output.reshape(image_in.shape), image.reshape(image_in.shape), g_temb, g_cap[None], unflat(s_in), unflat(s_out),
        g_wemb, g_qkv.T, g_wcap, g_out.T, g_gains, g_biases,
    )


def body(*args):
    image_in, qkv_proj = args[0], args[7]
    n, height, width, c = image_in.shape
    n_img, n_sp = lax.axis_size("img"), lax.axis_size("sp")
    fits = n == 1 and n_img == 4 and n_sp == HEADS and c == 512 and width == 64
    return fast_body(*args) if fits else plain_body(*args)


def solution(mesh):
    rows = P("img", "sp", None, None)
    kernel = P("img", None, None, "sp")
    flat = P("img", "sp")
    return jax.shard_map(
        body,
        mesh=mesh,
        in_specs=(
            rows, P("img", None), P("img", None, None), P("img", None), kernel, kernel,
            flat, flat, flat, flat, P(None, "img"), P(None, "img"), rows,
        ),
        out_specs=(
            rows, rows, P("img", None), P("img", "sp", None), kernel, kernel,
            flat, flat, flat, flat, P(None, "img"), P(None, "img"),
        ),
        check_vma=False,
    )
```

```python
import functools

import jax
import jax.numpy as jnp
from jax import lax
from jax.experimental import pallas as pl
from jax.experimental.pallas import tpu as pltpu
from jax.sharding import PartitionSpec as P

HEADS = 8
GROUPS = 32
EPSILON = 1e-05
PRECISE = lax.Precision.HIGHEST
MASKED = -1e30
BF16 = jnp.bfloat16
F32 = jnp.float32
MESH = pl.DeviceIdType.MESH
VMEM_BYTES = 60 * 1024 * 1024


def dot(a, b, ca, cb):
    return lax.dot_general(a, b, (((ca,), (cb,)), ((), ())), preferred_element_type=F32)


def silu(v):
    return v * jax.nn.sigmoid(v)


def silu_slope(v):
    s = jax.nn.sigmoid(v)
    return s * (1.0 + v * (1.0 - s))


def gather(x, axis, dim):
    return lax.all_gather(x, axis, axis=dim, tiled=True)


def scatter_sum(x, axis, dim):
    return lax.psum_scatter(x, axis, scatter_dimension=dim, tiled=True)


def swap(x, axis, split, concat):
    return lax.all_to_all(x, axis, split, concat, tiled=True)


def halo(x):
    count = lax.axis_size("sp")
    above = lax.ppermute(x[:, -1:], "sp", [(i, i + 1) for i in range(count - 1)])
    below = lax.ppermute(x[:, :1], "sp", [(i + 1, i) for i in range(count - 1)])
    return above, below


def group_sum(v):
    c = v.shape[-1]
    g = v.reshape(v.shape[:-1] + (GROUPS, c // GROUPS))
    s = jnp.sum(g, axis=-1, keepdims=True)
    return jnp.broadcast_to(s, g.shape).reshape(v.shape)


def norm_stats(x):
    n, r, w, c = x.shape
    cells = r * w * (c // GROUPS)
    parts = lax.axis_size("sp")
    mean = group_sum(jnp.sum(x, axis=(1, 2))) / cells
    dev = group_sum(jnp.sum(jnp.square(x - mean[:, None, None, :]), axis=(1, 2)))
    both = lax.all_gather(jnp.stack([mean, dev]), "sp")
    means, devs = both[:, 0], both[:, 1]
    center = jnp.mean(means, axis=0)
    var = (jnp.sum(devs, axis=0) + cells * jnp.sum(jnp.square(means - center), axis=0)) / (
        cells * parts
    )
    return center, lax.rsqrt(var + EPSILON)


def hat_of(x, center, inverse):
    return (x - center[:, None, None, :]) * inverse[:, None, None, :]


def norm_back(u, hat, inverse, gain, sum_u, sum_uh, members):
    s1 = group_sum(sum_u * gain) / members
    s2 = group_sum(sum_uh * gain) / members
    return inverse[:, None, None, :] * (
        u * gain - s1[:, None, None, :] - hat * s2[:, None, None, :]
    )


def pad_cols(x):
    return jnp.pad(x, ((0, 0), (0, 0), (1, 1), (0, 0)))


def conv(padded, weight_t, transposed):
    n, rp, wp, c = padded.shape
    r, w = rp - 2, wp - 2
    total = None
    for i in range(3):
        for j in range(3):
            a = padded[:, i : i + r, j : j + w].reshape(n * r * w, c)
            part = dot(a, weight_t[2 - i, 2 - j], 1, 0) if transposed else dot(a, weight_t[i, j], 1, 1)
            total = part if total is None else total + part
    return total.reshape(n, r, w, -1)


def conv_grad(padded, g):
    n, r, w, c = g.shape
    gf = g.reshape(n * r * w, c)
    rows = []
    for i in range(3):
        for j in range(3):
            a = padded[:, i : i + r, j : j + w].reshape(n * r * w, -1)
            rows.append(dot(gf, a, 0, 0))
    return jnp.stack(rows).reshape(3, 3, c, -1)


def to_pairs(x, images):
    n, px, h, d = x.shape
    y = x.transpose(0, 2, 1, 3).reshape(n * h, px, d)
    return swap(y, "sp", 0, 1)


def from_pairs(x, images):
    y = swap(x, "sp", 1, 0)
    return y.reshape(images, HEADS, y.shape[1], y.shape[2]).transpose(0, 2, 1, 3)


def attention_plain(q, k, v, g, tk, tv, keep, scale):
    p, length, d = q.shape
    block = min(512, length)
    keys = jnp.concatenate([tk, k], axis=1)
    values = jnp.concatenate([tv, v], axis=1)
    text = tk.shape[1]
    keep_all = jnp.concatenate([keep, jnp.ones((p, length), bool)], axis=1)

    def step(carry, blk):
        dk, dv = carry
        qb, gb = blk
        s = jnp.einsum("pqd,pkd->pqk", qb, keys, preferred_element_type=F32) * scale
        s = jnp.where(keep_all[:, None, :], s, MASKED)
        peak = jnp.max(s, axis=-1, keepdims=True)
        e = jnp.exp(s - peak)
        prob = e / jnp.sum(e, axis=-1, keepdims=True)
        pb = prob.astype(BF16)
        o = jnp.einsum("pqk,pkd->pqd", pb, values, preferred_element_type=F32)
        row = jnp.sum(o * gb.astype(F32), axis=-1, keepdims=True)
        dp = jnp.einsum("pqd,pkd->pqk", gb, values, preferred_element_type=F32)
        ds = (prob * (dp - row)).astype(BF16)
        dq = jnp.einsum("pqk,pkd->pqd", ds, keys, preferred_element_type=F32) * scale
        dk = dk + jnp.einsum("pqk,pqd->pkd", ds, qb, preferred_element_type=F32)
        dv = dv + jnp.einsum("pqk,pqd->pkd", pb, gb, preferred_element_type=F32)
        return (dk, dv), (o.astype(BF16), dq.astype(BF16))

    zeros = jnp.zeros((p, text + length, d), F32)
    cut = lambda t: t.reshape(p, length // block, block, d).swapaxes(0, 1)
    (dk, dv), (o, dq) = lax.scan(step, (zeros, zeros), (cut(q), cut(g)))
    join = lambda t: t.swapaxes(0, 1).reshape(p, length, d)
    dk = (dk * scale).astype(BF16)
    dv = dv.astype(BF16)
    return join(o), join(dq), dk[:, text:], dv[:, text:], dk[:, :text], dv[:, :text]


def plain_body(
    image_in, time_embed, caption, caption_mask, conv_in, conv_out, embed_proj, qkv_proj,
    caption_proj, out_proj, norm_gains, norm_biases, cotangent,
):
    n, rows, width, chans = image_in.shape
    n_img, n_sp = lax.axis_size("img"), lax.axis_size("sp")
    img, sp = lax.axis_index("img"), lax.axis_index("sp")
    px = rows * width
    members = px * n_sp * (chans // GROUPS)
    d = chans // HEADS
    scale = d ** -0.5
    pairs = n * HEADS // n_sp

    def whole(w):
        w = gather(w, "img", w.ndim - 1)
        return gather(w, "sp", w.ndim - 2)

    w_in = whole(conv_in.transpose(1, 2, 3, 0))
    w_out = whole(conv_out.transpose(1, 2, 3, 0))
    w_qkv = whole(qkv_proj.T)
    w_proj = whole(out_proj.T)
    affine = gather(jnp.concatenate([norm_gains, norm_biases]), "img", 1).astype(F32)
    gains, biases = affine[:3], affine[3:]

    embedded = silu(time_embed.astype(F32)).astype(BF16)
    emb_all = swap(embedded, "img", 1, 0)
    mod = scatter_sum(jnp.dot(emb_all, embed_proj, preferred_element_type=F32), "img", 0)
    mod = gather(mod, "sp", 1)
    scale_term, shift_term = mod[:, :chans], mod[:, chans:]
    cap_all = swap(caption, "img", 2, 0)
    cap_flat = cap_all.reshape(-1, cap_all.shape[2])
    kv = jnp.dot(cap_flat, caption_proj, preferred_element_type=F32)
    kv = scatter_sum(kv.reshape(cap_all.shape[0], cap_all.shape[1], -1), "img", 0).astype(BF16)
    kv = gather(kv, "sp", 2)
    text = kv.shape[1]
    kv_heads = kv.reshape(n, text, 2, HEADS, d).transpose(2, 0, 3, 1, 4).reshape(2, n * HEADS, text, d)
    mine = lax.dynamic_slice_in_dim(kv_heads, sp * pairs, pairs, 1)
    keep = jnp.repeat(caption_mask > 0, HEADS, axis=0)
    keep = lax.dynamic_slice_in_dim(keep, sp * pairs, pairs, 0)

    image_f = image_in.astype(F32)
    c0, i0 = norm_stats(image_f)
    hat0 = hat_of(image_f, c0, i0)
    first = hat0 * gains[0] + biases[0]
    act0 = silu(first).astype(BF16)
    above, below = halo(act0)
    pad0 = pad_cols(jnp.concatenate([above, act0, below], axis=1))
    hidden = conv(pad0, w_in, False)
    c1, i1 = norm_stats(hidden)
    hat1 = hat_of(hidden, c1, i1)
    second = hat1 * gains[1] + biases[1]
    pre = second * (1.0 + scale_term[:, None, None, :]) + shift_term[:, None, None, :]
    act1 = silu(pre).astype(BF16)
    above, below = halo(act1)
    pad1 = pad_cols(jnp.concatenate([above, act1, below], axis=1))
    residual = image_f + conv(pad1, w_out, False)
    c2, i2 = norm_stats(residual)
    hat2 = hat_of(residual, c2, i2)
    normed = (hat2 * gains[2] + biases[2]).astype(BF16).reshape(n * px, chans)
    qkv = dot(normed, w_qkv, 1, 1).astype(BF16)
    cot = cotangent.reshape(n * px, chans)
    g_att = dot(cot, w_proj, 1, 0).astype(BF16)
    four = jnp.concatenate([qkv, g_att], axis=1).reshape(n, px, 4, HEADS, d)
    packed = to_pairs(four.transpose(0, 1, 3, 2, 4).reshape(n, px, HEADS, 4 * d), n)
    q, k, v, g = (packed[..., j * d : (j + 1) * d] for j in range(4))
    o, dq, dk, dv, dtk, dtv = attention_plain(q, k, v, g, mine[0], mine[1], keep, scale)
    back = from_pairs(jnp.concatenate([o, dq, dk, dv], axis=-1), n)
    back = back.reshape(n * px, HEADS, 4, d).transpose(0, 2, 1, 3).reshape(n * px, 4 * chans)
    attended, proj_grad = back[:, :chans], back[:, chans:]
    output = residual + dot(attended, w_proj, 1, 1).reshape(image_in.shape)

    grad_out = dot(cot, attended, 0, 0)
    grad_qkv = dot(proj_grad, normed, 0, 0)
    normed_grad = dot(proj_grad, w_qkv, 1, 0).reshape(image_in.shape)

    def sums(u, hat):
        both = jnp.stack([jnp.sum(u, axis=(1, 2)), jnp.sum(u * hat, axis=(1, 2))])
        return lax.psum(both, "sp")

    su2, sh2 = sums(normed_grad, hat2)
    residual_grad = cotangent.astype(F32) + norm_back(
        normed_grad, hat2, i2, gains[2], su2, sh2, members
    )
    g2 = residual_grad.astype(BF16)
    above, below = halo(g2)
    gpad = pad_cols(jnp.concatenate([above, g2, below], axis=1))
    grad_conv_out = conv_grad(pad1, g2)
    pre_grad = conv(gpad, w_out, True) * silu_slope(pre)
    sa, sb = sums(pre_grad, hat1)
    fac = 1.0 + scale_term
    shift_grad = sa
    scale_grad = sb * gains[1] + sa * biases[1]
    u1 = pre_grad * fac[:, None, None, :]
    su1, sh1 = sa * fac, sb * fac
    g1 = norm_back(u1, hat1, i1, gains[1], su1, sh1, members).astype(BF16)
    above, below = halo(g1)
    gpad = pad_cols(jnp.concatenate([above, g1, below], axis=1))
    grad_conv_in = conv_grad(pad0, g1)
    u0 = conv(gpad, w_in, True) * silu_slope(first)
    su0, sh0 = sums(u0, hat0)
    grad_image = residual_grad + norm_back(u0, hat0, i0, gains[0], su0, sh0, members)

    mod_grad = jnp.concatenate([scale_grad, shift_grad], axis=1)
    cols = embed_proj.shape[1]
    mod_all = gather(mod_grad, "img", 0)
    mod_cols = lax.dynamic_slice_in_dim(mod_all, sp * cols, cols, 1)
    grad_embed_proj = jnp.einsum("ne,nd->ed", emb_all.astype(F32), mod_cols, precision=PRECISE)
    part = jnp.einsum("nd,ed->ne", mod_cols, embed_proj.astype(F32), precision=PRECISE)
    part = swap(lax.psum(part, "sp"), "img", 0, 1)
    grad_embed = part * silu_slope(time_embed.astype(F32))

    tg = gather(jnp.stack([dtk, dtv]), "sp", 1).reshape(2, n, HEADS, text, d)
    tg = tg.transpose(1, 3, 0, 2, 4).reshape(n, text, 2 * chans)
    cols = caption_proj.shape[1]
    tg = gather(lax.dynamic_slice_in_dim(tg, sp * cols, cols, 2), "img", 0).reshape(-1, cols)
    grad_caption_proj = dot(cap_flat, tg, 0, 0)
    gc = dot(tg, caption_proj, 1, 1).reshape(cap_all.shape)
    gc = scatter_sum(gc, "sp", 1)
    grad_caption = swap(gc, "img", 0, 2)

    grads = jnp.concatenate(
        [jnp.sum(t, axis=0)[None] for t in (sh0, sh1, sh2, su0, su1, su2)]
    )
    grads = scatter_sum(grads, "img", 1)

    def shared(w):
        w = scatter_sum(w, "sp", w.ndim - 2)
        return scatter_sum(w, "img", w.ndim - 1)

    return (
        output.astype(BF16),
        grad_image,
        grad_embed,
        grad_caption,
        shared(grad_conv_in).transpose(3, 0, 1, 2),
        shared(grad_conv_out).transpose(3, 0, 1, 2),
        grad_embed_proj,
        shared(grad_qkv).T,
        grad_caption_proj,
        shared(grad_out).T,
        grads[:3],
        grads[3:],
    )


class Place:
    def __init__(self):
        self.i = lax.axis_index("img")
        self.s = lax.axis_index("sp")
        self.z = lax.div(self.s, 2)
        self.c = lax.rem(self.s, 2)
        x = lax.rem(self.i, 2)
        y = lax.div(self.i, 2)
        self.ix = self.i + 1 - 2 * x
        self.iy = self.i + 2 - 4 * y
        self.id = 3 - self.i
        self.sib = (self.i, self.s + 1 - 2 * self.c)
        self.xn = (self.ix, self.s)
        self.yn = (self.iy, self.s)

    def zp(self, k, nz):
        return (self.i, 2 * lax.rem(self.z + k, nz) + self.c)

    def rp(self, k, n_sp):
        return (self.i, lax.rem(self.s + k, n_sp))


def greet(peers):
    bar = pltpu.get_barrier_semaphore()
    for p in peers:
        pl.semaphore_signal(bar, inc=1, device_id=p, device_id_type=MESH)


def greeted(count):
    pl.semaphore_wait(pltpu.get_barrier_semaphore(), count)


def remote(src, dst, ssem, rsem, dev):
    cp = pltpu.make_async_remote_copy(
        src_ref=src, dst_ref=dst, send_sem=ssem, recv_sem=rsem, device_id=dev, device_id_type=MESH
    )
    cp.start()
    return cp


def params(cid=None, grid=0):
    extra = {} if cid is None else {"collective_id": cid, "has_side_effects": True}
    if grid:
        extra["dimension_semantics"] = ("arbitrary",) * grid
    return pltpu.CompilerParams(vmem_limit_bytes=VMEM_BYTES, **extra)


ANY = pl.BlockSpec(memory_space=pl.ANY)
VM = pl.BlockSpec(memory_space=pltpu.VMEM)


def exchange_scratch(n_sp, width, halo_types, chans):
    out = [pltpu.VMEM((8, chans), F32), pltpu.VMEM((n_sp, 8, chans), F32)]
    for ty in halo_types:
        out += [pltpu.VMEM((width, chans), ty), pltpu.VMEM((width, chans), ty)]
    count = n_sp - 1 + 2 * len(halo_types)
    return out + [pltpu.SemaphoreType.DMA((count,)), pltpu.SemaphoreType.DMA((count,))]


def exchange_greet(n_sp):
    at = Place()
    greet([at.rp(k, n_sp) for k in range(1, n_sp)])


def exchange(n_sp, width, scratch, edges):
    at = Place()
    mine, every = scratch[0], scratch[1]
    ssem, rsem = scratch[-2:]
    greeted(n_sp - 1)
    sent = []
    for e, ref in enumerate(edges):
        above, below = scratch[2 + 2 * e], scratch[3 + 2 * e]
        px = ref.shape[0]
        j = n_sp - 1 + 2 * e
        sent.append(remote(ref.at[px - width :], above, ssem.at[j], rsem.at[j], at.rp(1, n_sp)))
        sent.append(remote(ref.at[:width], below, ssem.at[j + 1], rsem.at[j + 1], at.rp(n_sp - 1, n_sp)))
    for k in range(1, n_sp):
        sent.append(remote(mine, every.at[at.s], ssem.at[k - 1], rsem.at[k - 1], at.rp(k, n_sp)))
    every[at.s] = mine[...]
    for cp in sent:
        cp.wait()


def channel_stats(mine, v):
    mean = jnp.sum(v, axis=0, keepdims=True) / v.shape[0]
    dev = v - mean
    mine[0:1, :] = mean
    mine[1:2, :] = jnp.sum(dev * dev, axis=0, keepdims=True)


def group_total(rows):
    c = rows.shape[1]
    size = c // GROUPS
    a = lax.broadcasted_iota(jnp.int32, (128, 128), 0)
    b = lax.broadcasted_iota(jnp.int32, (128, 128), 1)
    same = jnp.where(lax.bitwise_xor(a, b) < size, 1.0, 0.0).astype(BF16)
    high = rows.astype(BF16)
    rest = rows - high.astype(F32)
    mid = rest.astype(BF16)
    low = (rest - mid.astype(F32)).astype(BF16)
    parts = jnp.concatenate([high.astype(F32), mid.astype(F32), low.astype(F32)]).astype(BF16)
    total = jnp.concatenate(
        [dot(parts[:, j * 128 : (j + 1) * 128], same, 1, 0) for j in range(c // 128)], axis=1
    )
    n = rows.shape[0]
    return total[:n] + total[n : 2 * n] + total[2 * n :]


def combine_stats(every, px):
    n_sp, _, c = every.shape
    size = c // GROUPS
    means = [every[j, 0:1, :] for j in range(n_sp)]
    center_c = sum(means) / n_sp
    dev = sum(every[j, 1:2, :] for j in range(n_sp))
    dev = dev + px * sum((m - center_c) * (m - center_c) for m in means)
    center = group_total(jnp.broadcast_to(center_c, (8, c)))[0:1] / size
    off = center_c - center
    dev = dev + (px * n_sp) * (off * off)
    var = group_total(jnp.broadcast_to(dev, (8, c)))[0:1] / (px * n_sp * size)
    return center, lax.rsqrt(var + EPSILON)


def combine_sums(every):
    n_sp = every.shape[0]
    total = every[0]
    for j in range(1, n_sp):
        total = total + every[j]
    return total


def edge_flags(n_sp, s):
    return jnp.where(s > 0, 1.0, 0.0), jnp.where(s < n_sp - 1, 1.0, 0.0)


def shifted(dst, row, width, block):
    col = lax.broadcasted_iota(jnp.int32, block.shape, 0)
    r = slice(row * width, (row + 1) * width)
    dst[1, r, :] = block.astype(BF16)
    dst[0, r, :] = jnp.where(col == 0, 0.0, pltpu.roll(block, 1, 0)).astype(BF16)
    dst[2, r, :] = jnp.where(col == width - 1, 0.0, pltpu.roll(block, width - 1, 0)).astype(BF16)


def joined(w_ref, *lead):
    return jnp.concatenate([w_ref[(j,) + lead] for j in range(4)], axis=-1)


def split_small(whole, n_sp):
    c = whole.shape[1]
    cols, out = 3 * c // n_sp, c // n_sp
    chunk = cols + out
    return (
        jnp.concatenate([whole[j * chunk : j * chunk + cols] for j in range(n_sp)]),
        jnp.concatenate([whole[j * chunk + cols : (j + 1) * chunk] for j in range(n_sp)]),
    )


def conv_kernel(n_sp, width, refs_in, x, up, dn, every, rows, w, *rest):
    base = None
    if refs_in:
        base, rest = rest[0], rest[1:]
    out, act, stats, above, below, a3 = rest[:6]
    scratch = rest[6:]
    step = pl.program_id(0)
    px, c = out.shape
    height = px // width

    @pl.when(step == 0)
    def _():
        exchange_greet(n_sp)
        center, inverse = combine_stats(every, px)
        mul = inverse * rows[0:1, :] * rows[2:3, :]
        add = rows[1:2, :] * rows[2:3, :] + rows[3:4, :]
        has_up, has_dn = edge_flags(n_sp, lax.axis_index("sp"))
        for r in range(height + 2):
            if r == 0:
                v = up[...]
            elif r == height + 1:
                v = dn[...]
            else:
                v = x[(r - 1) * width : r * width, :]
            v = silu((v.astype(F32) - center) * mul + add)
            if r == 0:
                v = v * has_up
            elif r == height + 1:
                v = v * has_dn
            act[r * width : (r + 1) * width, :] = v.astype(BF16)
            shifted(a3, r, width, v)
        if base is None:
            out[...] = jnp.zeros_like(out)
        else:
            out[...] = base[...].astype(F32)

    i, j = lax.div(step, 3), lax.rem(step, 3)
    lhs = a3[j, pl.ds(pl.multiple_of(i * width, width), px), :]
    out[...] += dot(lhs, joined(w, 0), 1, 1)

    @pl.when(step == 8)
    def _():
        channel_stats(scratch[0], out[...])
        exchange(n_sp, width, scratch, [out])
        stats[...] = scratch[1][...]
        above[...] = scratch[2][...]
        below[...] = scratch[3][...]


def whole_spec(shape):
    return pl.BlockSpec(shape, lambda t: (0,) * len(shape))


def conv_call(x, up, dn, every, rows, w, base, n_sp, width, cid):
    px, c = x.shape
    padded = px + 2 * width
    ins = [x, up, dn, every, rows, w] + ([] if base is None else [base])
    in_specs = [whole_spec(v.shape) for v in ins]
    in_specs[5] = pl.BlockSpec((4, 1, c, 128), lambda t: (0, t, 0, 0))
    outs = [((px, c), F32), ((padded, c), BF16), ((n_sp, 8, c), F32), ((width, c), F32), ((width, c), F32)]
    return pl.pallas_call(
        functools.partial(conv_kernel, n_sp, width, base is not None),
        grid=(9,),
        in_specs=in_specs,
        out_specs=[whole_spec(s) for s, _ in outs],
        out_shape=[jax.ShapeDtypeStruct(s, ty) for s, ty in outs],
        scratch_shapes=[pltpu.VMEM((3, padded, c), BF16)] + exchange_scratch(n_sp, width, [F32], c),
        compiler_params=params(cid, 1),
        name="conv_forward",
    )(*ins)


def project_kernel(n_sp, res, every, rows, w_small, cot, normed, kv, qg):
    px, c = res.shape
    d = c // HEADS
    center, inverse = combine_stats(every, px)
    n = ((res[...] - center) * (inverse * rows[0:1, :]) + rows[1:2, :]).astype(BF16)
    normed[...] = n
    wq, wp = split_small(joined(w_small), n_sp)
    q = (dot(n, wq[:c], 1, 1).astype(BF16).astype(F32) * (d ** -0.5)).astype(BF16)
    k = dot(n, wq[c : 2 * c], 1, 1).astype(BF16)
    v = dot(n, wq[2 * c :], 1, 1).astype(BF16)
    g = dot(cot[...], wp, 1, 0).astype(BF16)
    for h in range(HEADS):
        cut = slice(h * d, (h + 1) * d)
        kv[h] = jnp.concatenate([k[:, cut], v[:, cut]], axis=1)
        qg[h] = jnp.concatenate([q[:, cut], g[:, cut]], axis=1)


def project_call(res, every, rows, w_small, cot, n_sp):
    px, c = res.shape
    big = jax.ShapeDtypeStruct((HEADS, px, 128), BF16)
    return pl.pallas_call(
        functools.partial(project_kernel, n_sp),
        out_shape=[jax.ShapeDtypeStruct((px, c), BF16), big, big],
        in_specs=[VM] * 5,
        out_specs=[VM] * 3,
        compiler_params=params(),
        name="project",
    )(res, every, rows, w_small, cot)


def attention_kernel(
    n_sp, BQ, BK, kv, qg, text, keep, od, dkv, dt,
    kv_r, qg_r, od_s, dkv_s, dt_s, k_s, v_s, s_s, e_s, dk_s, dv_s, lsem, ssem, rsem,
):
    at = Place()
    px = kv.shape[1]
    L, T = n_sp * px, text.shape[1]
    d = kv.shape[2] // 2
    line = [at.rp(k, n_sp) for k in range(1, n_sp)]
    greet(line)
    own = [
        pltpu.make_async_copy(kv.at[at.s], kv_r.at[at.s], lsem.at[0]),
        pltpu.make_async_copy(qg.at[at.s], qg_r.at[at.s], lsem.at[1]),
    ]
    for cp in own:
        cp.start()
    greeted(n_sp - 1)
    sent = [remote(kv.at[dev[1]], kv_r.at[at.s], ssem.at[0, k + 1], rsem.at[0, k + 1], dev) for k, dev in enumerate(line)]
    odd = lax.rem(at.s, 2)
    pair = lax.div(at.s, 2)
    ones = (lax.broadcasted_iota(jnp.int32, (1, d), 1) == 0).astype(BF16)
    picked = []
    for j in (pair, HEADS // 2 + pair):
        blk = text[j].astype(F32)
        picked.append(jnp.where(odd > 0, blk[:, d:], blk[:, :d]).astype(BF16))
    k_s[0:T, :] = picked[0]
    v_s[0:T, :] = jnp.concatenate([picked[1], jnp.broadcast_to(ones, (T, d))], axis=1)
    dk_s[...] = jnp.zeros_like(dk_s)
    dv_s[...] = jnp.zeros_like(dv_s)

    def take(j):
        rows = pl.ds(pl.multiple_of(T + j * px, px if T % px == 0 else T), px)
        k_s[rows, :] = kv_r[j][:, :d]
        v_s[rows, :] = jnp.concatenate([kv_r[j][:, d:], jnp.broadcast_to(ones, (px, d))], axis=1)

    for cp in own:
        cp.wait()
    take(at.s)
    for k in range(1, n_sp):
        sent[k - 1].wait_recv()
        take(lax.rem(at.s - k + n_sp, n_sp))
    sent += [remote(qg.at[dev[1]], qg_r.at[at.s], ssem.at[1, k + 1], rsem.at[1, k + 1], dev) for k, dev in enumerate(line)]

    blocks = [(0, T)] + [(T + j * BK, BK) for j in range(L // BK)]
    per = px // BQ
    scale = d ** -0.5

    def query_copy(k):
        return pltpu.make_async_remote_copy(
            src_ref=qg.at[at.s], dst_ref=qg_r.at[at.s], send_sem=ssem.at[1, k], recv_sem=rsem.at[1, k],
            device_id=(at.i, lax.rem(at.s + k, n_sp)), device_id_type=MESH,
        )

    def back_copy(k, o):
        return pltpu.make_async_remote_copy(
            src_ref=od_s.at[o], dst_ref=od.at[at.s], send_sem=ssem.at[2, k], recv_sem=rsem.at[2, k],
            device_id=(at.i, o), device_id_type=MESH,
        )

    def step(t, _):
        k, part = lax.div(t, per), lax.rem(t, per)
        o_dev = lax.rem(at.s - k + n_sp, n_sp)

        @pl.when(jnp.logical_and(part == 0, k > 0))
        def _():
            query_copy(k).wait_recv()

        r = pl.ds(pl.multiple_of(part * BQ, BQ), BQ)
        both = qg_r[o_dev, r, :]
        q, g = both[:, :d], both[:, d:]
        peak = None
        for st, n in blocks:
            s = dot(q, k_s[st : st + n, :], 1, 1)
            if st == 0:
                s = jnp.where(keep[...] > 0, s, MASKED)
            s_s[:, st : st + n] = s
            for j in range(n // 128):
                piece = s[:, 128 * j : 128 * j + 128]
                peak = piece if peak is None else jnp.maximum(peak, piece)
        peak = jnp.max(peak, axis=1, keepdims=True)
        o = jnp.zeros((BQ, 2 * d), F32)
        for st, n in blocks:
            e = jnp.exp(s_s[:, st : st + n] - peak).astype(BF16)
            e_s[:, st : st + n] = e
            o = o + dot(e, v_s[st : st + n, :], 1, 0)
        inverse = 1.0 / o[:, d : d + 1]
        o = o[:, :d] * inverse
        g = g.astype(F32) * inverse
        row = jnp.sum(o * g, axis=1, keepdims=True)
        g = g.astype(BF16)
        gt, qt = g.T, q.T
        dq = jnp.zeros((BQ, d), F32)
        for st, n in blocks:
            e = e_s[:, st : st + n]
            dp = dot(g, v_s[st : st + n, :d], 1, 1)
            ds = (e.astype(F32) * (dp - row)).astype(BF16)
            dq = dq + dot(ds, k_s[st : st + n, :], 1, 0)
            dv_s[:, st : st + n] += dot(gt, e, 1, 0)
            dk_s[:, st : st + n] += dot(qt, ds, 1, 0)
        od_s[o_dev, r, :] = jnp.concatenate([o, dq * scale], axis=1).astype(BF16)

        @pl.when(jnp.logical_and(part == per - 1, k > 0))
        def _():
            back_copy(k, o_dev).start()

        return 0

    lax.fori_loop(0, n_sp * per, step, 0)
    local = [pltpu.make_async_copy(od_s.at[at.s], od.at[at.s], lsem.at[2])]

    def gradients(st, n):
        return jnp.concatenate([dk_s[:, st : st + n], dv_s[:, st : st + n]], axis=0).astype(BF16).T

    for j in range(n_sp):
        dkv_s[j] = gradients(T + j * px, px)
    for k, dev in enumerate(line):
        sent.append(remote(dkv_s.at[dev[1]], dkv.at[at.s], ssem.at[3, k + 1], rsem.at[3, k + 1], dev))
    dt_s[...] = gradients(0, T)
    for k, dev in enumerate(line):
        sent.append(remote(dt_s, dt.at[at.s], ssem.at[4, k + 1], rsem.at[4, k + 1], dev))
    local.append(pltpu.make_async_copy(dkv_s.at[at.s], dkv.at[at.s], lsem.at[3]))
    local.append(pltpu.make_async_copy(dt_s, dt.at[at.s], lsem.at[4]))
    for cp in local:
        cp.start()
    for k in range(1, n_sp):
        back_copy(k, lax.rem(at.s - k + n_sp, n_sp)).wait()
    for cp in sent[n_sp - 1 : 2 * (n_sp - 1)]:
        cp.wait_send()
    for cp in sent[: n_sp - 1]:
        cp.wait_send()
    for cp in sent[2 * (n_sp - 1) :]:
        cp.wait()
    for cp in local:
        cp.wait()


def attention_call(kv, qg, text, keep, cid):
    n_sp, px, d2 = kv.shape
    T = text.shape[1]
    L = n_sp * px
    d = d2 // 2
    BQ, BK = 256, 1024
    outs = [(n_sp, px, d2), (n_sp, px, d2), (n_sp, T, d2)]
    vm = pltpu.VMEM
    return pl.pallas_call(
        functools.partial(attention_kernel, n_sp, BQ, BK),
        out_shape=[jax.ShapeDtypeStruct(s, BF16) for s in outs],
        in_specs=[ANY, ANY, VM, VM],
        out_specs=[ANY] * 3,
        scratch_shapes=[
            vm((n_sp, px, d2), BF16), vm((n_sp, px, d2), BF16), vm((n_sp, px, d2), BF16), vm((n_sp, px, d2), BF16),
            vm((T, d2), BF16), vm((T + L, d), BF16), vm((T + L, d2), BF16),
            vm((BQ, T + L), F32), vm((BQ, T + L), BF16), vm((d, T + L), F32), vm((d, T + L), F32),
            pltpu.SemaphoreType.DMA((5,)),
            pltpu.SemaphoreType.DMA((5, n_sp)),
            pltpu.SemaphoreType.DMA((5, n_sp)),
        ],
        compiler_params=params(cid),
        name="attention",
    )(kv, qg, text, keep)


class Mail:
    def __init__(self, ssem, rsem):
        self.ssem, self.rsem, self.sent = ssem, rsem, []

    def send(self, src, dst, dev):
        j = len(self.sent)
        cp = remote(src, dst, self.ssem.at[j], self.rsem.at[j], dev)
        self.sent.append(cp)
        return cp


def img_peers(at):
    return [(lax.rem(at.i + k, 4), at.s) for k in range(1, 4)]


HEAD_MAIL = 3 * 3 + 3 + 2 * 7 + 7 + 4


def head_kernel(nz, width, dims, *refs):
    na = len(dims)
    ins, refs = refs[: na - 1], refs[na - 1 :]
    x, cot, temb, cap, w_emb, w_cap, gains, biases, w_qkv, w_proj = refs[:10]
    outs, refs = refs[10 : 10 + na], refs[10 + na :]
    st0, xa, xb, ca, cb, rows, kv_all, cap_all, emb_all = refs[:9]
    (ssem, rsem, lsem, mine, every, h0, h1, h2, h3, aff_s, emb_s, cap_s, part, part_r, kv_s, kv_r, mod_s, mod_r,
     msend, mrecv, emb, affine, small) = refs[9:]
    ins = list(ins) + [small]
    n_sp = 2 * nz
    at = Place()
    line = [at.rp(k, n_sp) for k in range(1, n_sp)]
    grid = img_peers(at)
    greet(line + grid)
    mail = Mail(msend, mrecv)
    local = []
    sent = {}
    kinds = {}

    def view(a, ii, k, core, half=None):
        r = dims[a][1]
        sp = 2 * lax.rem(at.z - k + nz, nz) + core
        if half is None:
            return outs[a].at[ii, :, pl.ds(pl.multiple_of(sp * r, r), r), :]
        h = r // 2
        return outs[a].at[ii, :, pl.ds(pl.multiple_of(sp * r + half * h, h), h), :]

    def send(a, kind, src, dst, dev):
        j = kinds.setdefault(kind, len(kinds))
        sent[a, kind] = remote(src, dst, ssem.at[a, j], rsem.at[a, j], dev)

    def forward(a, kind, ref, dev):
        send(a, kind, ref, ref, dev)

    def first(a):
        own = view(a, at.i, 0, at.c)
        for k in range(1, nz):
            send(a, ("z", k), ins[a], own, at.zp(k, nz))
        send(a, ("x", 0), ins[a], own, at.xn)
        send(a, ("y", 0), ins[a], own, at.yn)
        send(a, ("s", 0), ins[a], own, at.sib)

    def second(a):
        for k in range(1, nz):
            sent[a, ("z", k)].wait_recv()
            got = view(a, at.i, k, at.c)
            forward(a, ("x", k), got, at.xn)
            forward(a, ("y", k), got, at.yn)
            forward(a, ("s", k), got, at.sib)

    def third(a):
        for k in range(nz):
            sent[a, ("x", k)].wait_recv()
            forward(a, ("da", k), view(a, at.ix, k, at.c, 0), at.yn)
            forward(a, ("sx", k), view(a, at.ix, k, at.c), at.sib)
            sent[a, ("y", k)].wait_recv()
            forward(a, ("db", k), view(a, at.iy, k, at.c, 1), at.xn)
            forward(a, ("sy", k), view(a, at.iy, k, at.c), at.sib)

    def fourth(a):
        for k in range(nz):
            sent[a, ("da", k)].wait_recv()
            forward(a, ("sa", k), view(a, at.id, k, at.c, 0), at.sib)
            sent[a, ("db", k)].wait_recv()
            forward(a, ("sb", k), view(a, at.id, k, at.c, 1), at.sib)

    cut = w_qkv.shape[0]
    small[0, :cut] = w_qkv[...]
    small[0, cut:] = w_proj[...]
    e = cap.shape[1] // 4
    embedded = silu(temb[...].astype(F32)).astype(BF16).astype(F32)
    for j in range(4):
        emb[j] = jnp.broadcast_to(embedded[:, j * e : (j + 1) * e], (8, e))
    affine[0:3] = gains[...].astype(F32)
    affine[3:6] = biases[...].astype(F32)
    channel_stats(mine, x[...].astype(F32))
    greeted(n_sp + 2)
    first(0)
    round1 = []
    for dev in grid:
        round1.append(mail.send(affine, aff_s.at[at.i], dev))
        round1.append(mail.send(emb.at[dev[0]], emb_s.at[at.i], dev))
        round1.append(mail.send(cap.at[:, pl.ds(pl.multiple_of(dev[0] * e, e), e)], cap_s.at[at.i], dev))
    own_cap = pltpu.make_async_copy(cap.at[:, pl.ds(pl.multiple_of(at.i * e, e), e)], cap_s.at[at.i], lsem.at[na])
    own_cap.start()
    aff_s[at.i] = affine[...]
    emb_s[at.i] = emb[at.i]
    px = x.shape[0]
    stat = []
    for ref, above, below in ((x, h0, h1), (cot, h2, h3)):
        stat.append(mail.send(ref.at[px - width :], above, line[0]))
        stat.append(mail.send(ref.at[:width], below, line[-1]))
    for dev in line:
        stat.append(mail.send(mine, every.at[at.s], dev))
    every[at.s] = mine[...]
    for a in range(na):
        cp = pltpu.make_async_copy(ins[a], view(a, at.i, 0, at.c), lsem.at[a])
        cp.start()
        local.append(cp)
    tokens = cap.shape[0]
    round2, round3 = [], []

    def extras(tick):
        if tick == 1:
            own_cap.wait()
            for cp in round1:
                cp.wait_recv()
            for j in range(4):
                part[j, :tokens] = dot(cap_s[j], w_cap[...], 1, 0)
                part[j, tokens:] = dot(emb_s[j].astype(BF16), w_emb[...], 1, 0)
            for dev in grid:
                round2.append(mail.send(part.at[dev[0]], part_r.at[at.i], dev))
            part_r[at.i] = part[at.i]
        if tick == 2:
            for cp in round2:
                cp.wait_recv()
            total = part_r[0] + part_r[1] + part_r[2] + part_r[3]
            kv_s[...] = total[:tokens].astype(BF16)
            mod_s[...] = total[tokens:]
            for dev in line:
                round3.append(mail.send(kv_s, kv_r.at[at.s], dev))
                round3.append(mail.send(mod_s, mod_r.at[at.s], dev))
            kv_r[at.s] = kv_s[...]
            mod_r[at.s] = mod_s[...]
        if tick == 4:
            for cp in round3 + stat:
                cp.wait_recv()
            kv_all[...] = kv_r[...]
            cap_all[...] = cap_s[...]
            emb_all[...] = jnp.concatenate([emb_s[j][0:1] for j in range(4)] + [jnp.zeros((4, e), F32)])
            st0[...] = every[...]
            for dst, src in ((xa, h0), (xb, h1), (ca, h2), (cb, h3)):
                dst[...] = src[...]
            aff = jnp.concatenate([aff_s[j] for j in range(4)], axis=1)
            mod = jnp.concatenate([mod_r[j][0:1] for j in range(n_sp)], axis=1)
            c = aff.shape[1]
            rows[...] = jnp.zeros_like(rows)
            for j in range(3):
                rows[j, 0:1] = aff[j : j + 1]
                rows[j, 1:2] = aff[3 + j : 4 + j]
                rows[j, 2:3] = 1.0 + mod[:, :c] if j == 1 else jnp.ones((1, c), F32)
            rows[1, 3:4] = mod[:, c:]

    stages = (first, second, third, fourth)
    for tick in range(1, na + 3):
        for a in range(na):
            stage = tick - a
            if 0 <= stage < 4 and (stage, a) != (0, 0):
                stages[stage](a)
        extras(tick)
    for cp in local:
        cp.wait()
    for (a, kind), cp in sent.items():
        if kind[0] in ("s", "sx", "sy", "sa", "sb"):
            cp.wait_recv()
        cp.wait_send()
    for cp in mail.sent:
        cp.wait_send()


def head_call(chunks, x, cot, temb, cap, w_emb, w_cap, gains, biases, w_qkv, w_proj, nz, width, cid):
    dims = [c.shape[:2] for c in chunks] + [(1, w_qkv.shape[0] + w_proj.shape[0])]
    na = len(dims)
    n_sp = 2 * nz
    copies = 3 * nz - 1 + 7 * nz
    px, c = x.shape
    tokens, wide = cap.shape
    e = wide // 4
    edge = ((width, c), BF16)
    outs = [
        ((n_sp, 8, c), F32), edge, edge, edge, edge, ((3, 8, c), F32), ((n_sp, tokens, 128), BF16),
        ((4, tokens, e), BF16), ((8, e), F32),
    ]
    return pl.pallas_call(
        functools.partial(head_kernel, nz, width, dims),
        out_shape=[jax.ShapeDtypeStruct((4, t, n_sp * r, 128), BF16) for t, r in dims]
        + [jax.ShapeDtypeStruct(s, ty) for s, ty in outs],
        in_specs=[ANY] * (na - 1) + [VM, VM, VM, ANY] + [VM] * 6,
        out_specs=[ANY] * na + [VM] * len(outs),
        scratch_shapes=[
            pltpu.SemaphoreType.DMA((na, copies)),
            pltpu.SemaphoreType.DMA((na, copies)),
            pltpu.SemaphoreType.DMA((na + 1,)),
            pltpu.VMEM((8, c), F32),
            pltpu.VMEM((n_sp, 8, c), F32),
            pltpu.VMEM((width, c), BF16), pltpu.VMEM((width, c), BF16),
            pltpu.VMEM((width, c), BF16), pltpu.VMEM((width, c), BF16),
            pltpu.VMEM((4, 8, 128), F32),
            pltpu.VMEM((4, 8, e), F32),
            pltpu.VMEM((4, tokens, e), BF16),
            pltpu.VMEM((4, tokens + 8, 128), F32),
            pltpu.VMEM((4, tokens + 8, 128), F32),
            pltpu.VMEM((tokens, 128), BF16),
            pltpu.VMEM((n_sp, tokens, 128), BF16),
            pltpu.VMEM((8, 128), F32),
            pltpu.VMEM((n_sp, 8, 128), F32),
            pltpu.SemaphoreType.DMA((HEAD_MAIL,)),
            pltpu.SemaphoreType.DMA((HEAD_MAIL,)),
            pltpu.VMEM((4, 8, e), F32),
            pltpu.VMEM((8, 128), F32),
            pltpu.VMEM((1,) + dims[-1][1:] + (128,), BF16),
        ],
        compiler_params=params(cid),
        name="gather_weights",
    )(*chunks, x, cot, temb, cap, w_emb, w_cap, gains, biases, w_qkv, w_proj)


class Reducer:
    NAMES = ("d", "sb", "da", "db", "rx", "ry", "r", "zr")

    def __init__(self, at, nz, arrays, ssem, rsem):
        self.at, self.nz, self.arrays = at, nz, arrays
        self.ssem, self.rsem = ssem, rsem
        self.sent, self.groups = {}, []

    @staticmethod
    def buffers(nz, t, r):
        return [
            pltpu.VMEM((2, 4, t, nz, r, 128), BF16),
            pltpu.VMEM((4, t, nz, r, 128), BF16),
            pltpu.VMEM((t, nz, r // 2, 128), BF16),
            pltpu.VMEM((t, nz, r // 2, 128), BF16),
            pltpu.VMEM((t, nz, r, 128), BF16),
            pltpu.VMEM((t, nz, r, 128), BF16),
            pltpu.VMEM((t, nz, r, 128), BF16),
            pltpu.VMEM((nz - 1, t, r, 128), BF16),
        ]

    def send(self, g, j, src, dst, dev):
        self.sent[g, j] = remote(src, dst, self.ssem.at[g, j], self.rsem.at[g, j], dev)

    def add(self, a, t0, t1):
        g = len(self.groups)
        self.groups.append((a, t0, t1))
        b = self.arrays[a][1]
        self.send(g, 0, b["d"].at[1 - self.at.c, :, t0:t1], b["sb"].at[:, t0:t1], self.at.sib)

    def run(self, stage, *groups):
        one = (self.stage1, self.stage2, self.stage3, self.stage4)[stage - 1]
        for g in groups:
            one(g, *self.groups[g])

    def stage1(self, g, a, t0, t1):
        b, at = self.arrays[a][1], self.at
        d, sb = b["d"], b["sb"]
        self.sent[g, 0].wait_recv()
        n = t1 - t0

        def add(j, _):
            ii, tt = lax.div(j, n), t0 + lax.rem(j, n)
            d[at.c, ii, tt] = (d[at.c, ii, tt].astype(F32) + sb[ii, tt].astype(F32)).astype(BF16)
            return 0

        lax.fori_loop(0, 4 * n, add, 0)
        h = d.shape[4] // 2
        self.send(g, 1, d.at[at.c, at.id, t0:t1, :, :h], b["da"].at[t0:t1], at.yn)
        self.send(g, 2, d.at[at.c, at.id, t0:t1, :, h:], b["db"].at[t0:t1], at.xn)

    def stage2(self, g, a, t0, t1):
        b, at = self.arrays[a][1], self.at
        d = b["d"]
        h = d.shape[4] // 2
        self.sent[g, 1].wait_recv()
        self.sent[g, 2].wait_recv()

        def add(tt, _):
            d[at.c, at.ix, tt, :, :h] = (
                d[at.c, at.ix, tt, :, :h].astype(F32) + b["da"][tt].astype(F32)
            ).astype(BF16)
            d[at.c, at.iy, tt, :, h:] = (
                d[at.c, at.iy, tt, :, h:].astype(F32) + b["db"][tt].astype(F32)
            ).astype(BF16)
            return 0

        lax.fori_loop(t0, t1, add, 0)
        self.send(g, 3, d.at[at.c, at.ix, t0:t1], b["rx"].at[t0:t1], at.xn)
        self.send(g, 4, d.at[at.c, at.iy, t0:t1], b["ry"].at[t0:t1], at.yn)

    def stage3(self, g, a, t0, t1):
        b, at = self.arrays[a][1], self.at
        self.sent[g, 3].wait_recv()
        self.sent[g, 4].wait_recv()

        def add(tt, _):
            total = b["d"][at.c, at.i, tt].astype(F32) + b["rx"][tt].astype(F32) + b["ry"][tt].astype(F32)
            b["r"][tt] = total.astype(BF16)
            return 0

        lax.fori_loop(t0, t1, add, 0)
        for k in range(1, self.nz):
            there = lax.rem(at.z + k, self.nz)
            self.send(g, 4 + k, b["r"].at[t0:t1, there], b["zr"].at[k - 1, t0:t1], at.zp(k, self.nz))

    def stage4(self, g, a, t0, t1):
        (out, b), at = self.arrays[a], self.at
        for k in range(1, self.nz):
            self.sent[g, 4 + k].wait_recv()

        def add(tt, _):
            total = (
                b["d"][at.c, at.i, tt, at.z].astype(F32)
                + b["rx"][tt, at.z].astype(F32)
                + b["ry"][tt, at.z].astype(F32)
            )
            for k in range(1, self.nz):
                total = total + b["zr"][k - 1, tt].astype(F32)
            out[tt] = total
            return 0

        lax.fori_loop(t0, t1, add, 0)

    def finish(self):
        for cp in self.sent.values():
            cp.wait_send()


BACK_MAIL = 6 + 14 + 6 + 3 + 7 + 9 + 9
BACK_GROUPS = 7
BIG = 10


def conv_taps(t0, t1, w, ring, rsem, one):
    slots = ring.shape[0]

    def step(tap, _):
        slot = lax.rem(tap, slots)
        pltpu.make_async_copy(w.at[:, tap], ring.at[slot], rsem.at[slot]).wait()
        one(tap, jnp.concatenate([ring[slot, j] for j in range(4)], axis=-1))

        @pl.when(tap + slots < 9)
        def _():
            pltpu.make_async_copy(w.at[:, tap + slots], ring.at[slot], rsem.at[slot]).start()

        return 0

    lax.fori_loop(t0, t1, step, 0)


def ring_start(w, ring, rsem):
    for j in range(ring.shape[0]):
        pltpu.make_async_copy(w.at[:, j], ring.at[j], rsem.at[j]).start()


def backward_kernel(nz, width, *refs):
    hbm, refs = refs[:BIG], refs[BIG:]
    w_in, w_out = refs[:2]
    (st0, st1, st2, rows, ca, cb, ra, rb, ha, hb, dt_all, cap_all, emb_all, w_emb, w_cap, temb) = refs[2:18]
    output, image_grad, s_in, s_out, s_small, g_temb, g_cap, g_wemb, g_wcap, g_aff = refs[18:28]
    refs = refs[28:]
    big, refs = refs[:BIG], refs[BIG:]
    bufs = [dict(zip(Reducer.NAMES, refs[8 * a : 8 * a + 8])) for a in range(3)]
    (bsem, gsend, grecv, msend, mrecv, ring, rsem, a3, g3, gt, acc, ng, pre_grad, res_grad,
     mine, every, na, nb, pa, pb, tg_s, tg_r, mod_s, mod_r,
     gc_s, gc_r, pe_s, pe_r, gs_s, gs_r, ps_s, ps_r, aff_s, aff_r) = refs[24:]
    n_sp = 2 * nz
    at = Place()
    line = [at.rp(k, n_sp) for k in range(1, n_sp)]
    grid = img_peers(at)
    greet(line + grid)
    loads = []
    for j in range(BIG):
        cp = pltpu.make_async_copy(hbm[j], big[j], bsem.at[j])
        cp.start()
        loads.append(cp)
    od, dkv, w_small, res, cot, normed, act1, hidden, act0, x = big
    ring_start(w_out, ring, rsem)
    mail = Mail(msend, mrecv)
    red = Reducer(at, nz, [(s_out, bufs[0]), (s_small, bufs[1]), (s_in, bufs[2])], gsend, grecv)
    px, c = res.shape
    height = px // width
    members = px * n_sp * (c // GROUPS)
    d = c // HEADS
    cols = 3 * c // n_sp

    def publish(j, rows01, edges):
        out = []
        for ref, above, below in edges:
            out.append(mail.send(ref.at[px - width :], above, line[0]))
            out.append(mail.send(ref.at[:width], below, line[-1]))
        mine[j] = jnp.zeros((8, c), F32)
        mine[j, 0:1] = rows01[0]
        mine[j, 1:2] = rows01[1]
        for dev in line:
            out.append(mail.send(mine.at[j], every.at[j, at.s], dev))
        every[j, at.s] = mine[j]
        return out

    for j in range(6):
        loads[j].wait()
    att = jnp.concatenate([od[h][:, :d] for h in range(HEADS)], axis=1)
    pg = jnp.concatenate(
        [od[h][:, d:] for h in range(HEADS)]
        + [dkv[h][:, :d] for h in range(HEADS)]
        + [dkv[h][:, d:] for h in range(HEADS)],
        axis=1,
    )
    wq, wp = split_small(joined(w_small), n_sp)
    ng[...] = dot(pg, wq, 1, 0)
    center2, inverse2 = combine_stats(st2, px)
    hat = (res[...] - center2) * inverse2
    u = ng[...]
    sums = (jnp.sum(u, axis=0, keepdims=True), jnp.sum(u * hat, axis=0, keepdims=True))
    greeted(n_sp + 2)
    round_2 = publish(2, sums, [(ng, na, nb)])
    gq = dot(pg, normed[...], 0, 0).astype(BF16)
    go = dot(cot[...], att, 0, 0).astype(BF16)
    small = bufs[1]["d"]
    for j in range(n_sp):
        for b in range(4):
            lanes = slice(b * 128, (b + 1) * 128)
            small[j % 2, b, 0, j // 2, :cols] = gq[j * cols : (j + 1) * cols, lanes]
            small[j % 2, b, 0, j // 2, cols:] = go[j * (c // n_sp) : (j + 1) * (c // n_sp), lanes]
    red.add(1, 0, 1)
    output[...] = (res[...] + dot(att, wp, 1, 1)).astype(BF16)

    first = 2 * lax.rem(at.s, nz)
    value = lax.div(at.s, nz)
    halves = []
    for j in range(2):
        blk = dt_all[first + j].astype(F32)
        halves.append(jnp.where(value > 0, blk[:, d:], blk[:, :d]))
    tg_s[...] = jnp.concatenate(halves, axis=1).astype(BF16)
    round_a = [mail.send(tg_s, tg_r.at[at.i], dev) for dev in grid]
    tg_r[at.i] = tg_s[...]

    has_up, has_dn = edge_flags(n_sp, at.s)

    def upstream(j, uu, ua, ub, center, inverse, yy, ya, yb, act, base, keep):
        total = combine_sums(every[j])
        mul = rows[j, 0:1] * rows[j, 2:3]
        back = group_total(total * mul) / members
        s1, s2 = back[0:1, :], back[1:2, :]
        for r in range(height + 2):
            cut = slice((r - 1) * width, r * width)
            top, end = r == 0, r == height + 1
            un = ua[...] if top else ub[...] if end else uu[cut, :]
            yn = ya[...] if top else yb[...] if end else yy[cut, :]
            g = inverse * (un * mul - s1 - (yn - center) * inverse * s2)
            if base:
                g = g + (base[1][...] if top else base[2][...] if end else base[0][cut, :]).astype(F32)
            if top:
                g = g * has_up
            elif end:
                g = g * has_dn
            elif keep is not None:
                keep[cut, :] = g
            shifted(g3, r, width, g.astype(BF16).astype(F32))
            shifted(a3, r, width, act[r * width : (r + 1) * width, :].astype(F32))
        gt[...] = g3[1, width : width + px, :].T
        return total

    def weight_taps(a, t0, t1):
        dst = bufs[a]["d"]

        def one(tap, _):
            i, j = lax.div(tap, 3), lax.rem(tap, 3)
            part = dot(gt[...], a3[j, pl.ds(pl.multiple_of(i * width, width), px), :], 1, 0).astype(BF16)
            r = c // n_sp
            for k in range(n_sp):
                for b in range(4):
                    dst[k % 2, b, tap, k // 2] = part[k * r : (k + 1) * r, b * 128 : (b + 1) * 128]
            return 0

        lax.fori_loop(t0, t1, one, 0)
        red.add(a, t0, t1)

    def input_taps(w):
        def one(tap, wt):
            i, j = lax.div(tap, 3), lax.rem(tap, 3)
            lhs = g3[2 - j, pl.ds(pl.multiple_of((2 - i) * width, width), px), :]
            acc[...] = dot(lhs, wt, 1, 0) + jnp.where(tap > 0, acc[...], 0.0)

        conv_taps(0, 9, w, ring, rsem, one)

    for cp in round_2:
        cp.wait_recv()
    loads[6].wait()
    t2 = upstream(2, ng, na, nb, center2, inverse2, res, ra, rb, act1, (cot, ca, cb), res_grad)
    red.run(1, 0)
    for tap in (0, 3, 6):
        weight_taps(0, tap, tap + 3)
    red.run(2, 0)
    input_taps(w_out)
    ring_start(w_in, ring, rsem)
    for j in range(7, BIG):
        loads[j].wait()
    center1, inverse1 = combine_stats(st1, px)
    hat = (hidden[...] - center1) * inverse1
    gain1, bias1, fac1 = rows[1, 0:1], rows[1, 1:2], rows[1, 2:3]
    v = acc[...] * silu_slope(hat * (gain1 * fac1) + (bias1 * fac1 + rows[1, 3:4]))
    pre_grad[...] = v
    sums = (jnp.sum(v, axis=0, keepdims=True), jnp.sum(v * hat, axis=0, keepdims=True))
    round_1 = publish(1, sums, [(pre_grad, pa, pb)])
    red.run(1, 1, 2, 3)
    red.run(3, 0)

    exact = lambda a, b, ca_, cb_: lax.dot_general(
        a, b, (((ca_,), (cb_,)), ((), ())), preferred_element_type=F32, precision=PRECISE
    )
    tokens = tg_s.shape[0]
    share = tokens // n_sp
    for cp in round_a:
        cp.wait_recv()
    flat_tg = tg_r[...].reshape(4 * tokens, 128)
    g_wcap[...] = dot(cap_all[...].reshape(4 * tokens, cap_all.shape[2]), flat_tg, 0, 0)
    gc_s[...] = dot(flat_tg, w_cap[...], 1, 1).astype(BF16).reshape(gc_s.shape)
    round_b = []
    for dev in line:
        cut = pl.ds(pl.multiple_of(dev[1] * share, share), share)
        round_b.append(mail.send(gc_s.at[:, cut, :], gc_r.at[at.s], dev))
    gc_r[at.s] = gc_s[:, pl.ds(pl.multiple_of(at.s * share, share), share), :]

    for cp in round_1:
        cp.wait_recv()
    t1 = upstream(1, pre_grad, pa, pb, center1, inverse1, hidden, ha, hb, act0, None, None)
    mod = jnp.concatenate([t1[1:2] * gain1 + t1[0:1] * bias1, t1[0:1]], axis=1)
    for j in range(n_sp):
        mod_s[j] = jnp.broadcast_to(mod[:, j * 128 : (j + 1) * 128], (8, 128))
    round_m = [mail.send(mod_s.at[at.s], mod_r.at[at.i], dev) for dev in grid]
    mod_r[at.i] = mod_s[at.s]
    red.run(2, 1)
    weight_taps(2, 0, 3)
    red.run(2, 2)
    weight_taps(2, 3, 6)
    red.run(2, 3)
    weight_taps(2, 6, 9)
    input_taps(w_in)

    center0, inverse0 = combine_stats(st0, px)
    hat = (x[...].astype(F32) - center0) * inverse0
    gain0 = rows[0, 0:1]
    v = acc[...] * silu_slope(hat * gain0 + rows[0, 1:2])
    acc[...] = v
    sums = (jnp.sum(v, axis=0, keepdims=True), jnp.sum(v * hat, axis=0, keepdims=True))
    round_0 = publish(0, sums, [])
    red.run(1, 4, 5, 6)
    red.run(4, 0)
    for cp in round_m:
        cp.wait_recv()
    mods = jnp.concatenate([mod_r[j][0:1] for j in range(4)] + [jnp.zeros((4, 128), F32)])
    emb_t = emb_all[...].T
    g_wemb[...] = sum(emb_t[:, j : j + 1] * mods[j : j + 1] for j in range(4))
    pe_s[...] = exact(mods, w_emb[...].astype(F32), 1, 1)
    round_p = [mail.send(pe_s, pe_r.at[at.s], dev) for dev in line]
    pe_r[at.s] = pe_s[...]
    for cp in round_0:
        cp.wait_recv()
    t0 = combine_sums(every[0])
    zero = jnp.zeros((2, c), F32)
    aff = jnp.concatenate([t0[1:2], t1[1:2] * fac1, t2[1:2], t0[0:1], t1[0:1] * fac1, t2[0:1], zero])
    for j in range(4):
        aff_s[j] = aff[:, j * 128 : (j + 1) * 128]
    round_e = [mail.send(aff_s.at[dev[0]], aff_r.at[at.i], dev) for dev in grid]
    aff_r[at.i] = aff_s[at.i]
    total = group_total(t0 * gain0) / members
    image_grad[...] = res_grad[...] + inverse0 * (acc[...] * gain0 - total[0:1] - hat * total[1:2])
    for g in (1, 2, 3):
        red.run(3, g)
        red.run(2, g + 3)
    for cp in round_b + round_p:
        cp.wait_recv()
    gc = gc_r[0].astype(F32)
    pe = pe_r[0]
    for j in range(1, n_sp):
        gc = gc + gc_r[j].astype(F32)
        pe = pe + pe_r[j]
    gs_s[...] = gc
    for j in range(4):
        ps_s[j] = jnp.broadcast_to(pe[j : j + 1], pe.shape)
    round_c = []
    for dev in grid:
        round_c.append(mail.send(gs_s.at[dev[0]], gs_r.at[at.i], dev))
        round_c.append(mail.send(ps_s.at[dev[0]], ps_r.at[at.i], dev))
    gs_r[at.i] = gs_s[at.i]
    ps_r[at.i] = ps_s[at.i]
    red.run(4, 1, 2, 3)
    red.run(3, 4, 5, 6)
    red.run(4, 4, 5, 6)
    red.finish()
    for cp in round_c + round_e:
        cp.wait_recv()
    g_cap[...] = jnp.concatenate([gs_r[j] for j in range(4)], axis=1)
    g_temb[...] = jnp.concatenate([ps_r[j] for j in range(4)], axis=1) * silu_slope(temb[...].astype(F32))
    g_aff[...] = aff_r[0] + aff_r[1] + aff_r[2] + aff_r[3]
    for cp in mail.sent:
        cp.wait_send()


def backward_call(big, w_in, w_out, small, nz, width, cid):
    px, c = big[3].shape
    n_sp = 2 * nz
    padded = px + 2 * width
    r = c // n_sp
    rs = big[2].shape[1] // n_sp
    dt_all, cap_all = small[10], small[11]
    tokens = dt_all.shape[1]
    e = cap_all.shape[2]
    share = tokens // n_sp
    outs = [
        ((px, c), BF16), ((px, c), F32), ((9, r, 128), F32), ((9, r, 128), F32), ((1, rs, 128), F32),
        ((8, 4 * e), F32), ((share, 4 * e), F32), ((e, 128), F32), ((e, 128), F32), ((8, 128), F32),
    ]
    vm = pltpu.VMEM
    return pl.pallas_call(
        functools.partial(backward_kernel, nz, width),
        out_shape=[jax.ShapeDtypeStruct(s, ty) for s, ty in outs],
        in_specs=[ANY] * (len(big) + 2) + [VM] * len(small),
        out_specs=[VM] * len(outs),
        scratch_shapes=[vm(v.shape, v.dtype) for v in big]
        + Reducer.buffers(nz, 9, r) + Reducer.buffers(nz, 1, rs) + Reducer.buffers(nz, 9, r)
        + [
            pltpu.SemaphoreType.DMA((len(big),)),
            pltpu.SemaphoreType.DMA((BACK_GROUPS, 4 + nz)),
            pltpu.SemaphoreType.DMA((BACK_GROUPS, 4 + nz)),
            pltpu.SemaphoreType.DMA((BACK_MAIL,)),
            pltpu.SemaphoreType.DMA((BACK_MAIL,)),
            vm((3, 4, c, 128), BF16),
            pltpu.SemaphoreType.DMA((3,)),
            vm((3, padded, c), BF16), vm((3, padded, c), BF16), vm((c, px), BF16),
            vm((px, c), F32), vm((px, c), F32), vm((px, c), F32), vm((px, c), F32),
            vm((3, 8, c), F32), vm((3, n_sp, 8, c), F32),
            vm((width, c), F32), vm((width, c), F32), vm((width, c), F32), vm((width, c), F32),
            vm((tokens, 128), BF16), vm((4, tokens, 128), BF16),
            vm((n_sp, 8, 128), F32), vm((4, 8, 128), F32),
            vm((4, tokens, e), BF16), vm((n_sp, 4, share, e), BF16),
            vm((8, e), F32), vm((n_sp, 8, e), F32),
            vm((4, share, e), F32), vm((4, share, e), F32),
            vm((4, 8, e), F32), vm((4, 8, e), F32),
            vm((4, 8, 128), F32), vm((4, 8, 128), F32),
        ],
        compiler_params=params(cid),
        name="backward",
    )(*big, w_in, w_out, *small)


def emit_kernel(cut, *refs):
    ins, outs, mids, loads, stores = refs[:10], refs[10:22], refs[22:31], refs[31], refs[32]
    output, image, s_in, s_out, s_small, g_temb, g_cap, g_wemb, g_wcap, g_aff = ins
    pairs = [
        (output, outs[0]), (image, outs[1]), (g_cap, outs[3]), (s_in, outs[4]), (s_out, outs[5]), (g_wemb, outs[6]),
        (s_small.at[0, :cut], outs[7]), (g_wcap, outs[8]), (s_small.at[0, cut:], outs[9]),
    ]
    copies = [pltpu.make_async_copy(src, mid, loads.at[j]) for j, ((src, _), mid) in enumerate(zip(pairs, mids))]
    for cp in copies:
        cp.start()
    backs = []
    for j, cp in enumerate(copies):
        cp.wait()
        backs.append(pltpu.make_async_copy(mids[j], pairs[j][1], stores.at[j]))
        backs[-1].start()
    outs[2][...] = g_temb[0:1, :]
    outs[10][...] = g_aff[0:3, :]
    outs[11][...] = g_aff[3:6, :]
    for cp in backs:
        cp.wait()


def emit_call(parts, cut):
    output, image, s_in, s_out, s_small, g_temb, g_cap, g_wemb, g_wcap, g_aff = parts
    rest = s_small.shape[1] - cut
    like = lambda v: jax.ShapeDtypeStruct(v.shape, v.dtype)
    f32 = lambda *s: jax.ShapeDtypeStruct(s, F32)
    shapes = [
        like(output), like(image), f32(1, g_temb.shape[1]), like(g_cap), like(s_in), like(s_out), like(g_wemb),
        f32(cut, 128), like(g_wcap), f32(rest, 128), f32(3, 128), f32(3, 128),
    ]
    in_specs = [ANY] * 10
    in_specs[5] = in_specs[9] = VM
    out_specs = [ANY] * 12
    out_specs[2] = out_specs[10] = out_specs[11] = VM
    return pl.pallas_call(
        functools.partial(emit_kernel, cut),
        out_shape=shapes,
        in_specs=in_specs,
        out_specs=out_specs,
        scratch_shapes=[pltpu.VMEM(shapes[j].shape, shapes[j].dtype) for j in (0, 1, 3, 4, 5, 6, 7, 8, 9)]
        + [pltpu.SemaphoreType.DMA((9,)), pltpu.SemaphoreType.DMA((9,))],
        compiler_params=params(),
        name="emit",
    )(*parts)


def fast_body(
    image_in, time_embed, caption, caption_mask, conv_in, conv_out, embed_proj, qkv_proj,
    caption_proj, out_proj, norm_gains, norm_biases, cotangent,
):
    n, height, width, c = image_in.shape
    n_img, n_sp = lax.axis_size("img"), lax.axis_size("sp")
    sp = lax.axis_index("sp")
    nz = n_sp // 2
    px = height * width
    d = c // HEADS
    x = image_in.reshape(px, c)
    cot = cotangent.reshape(px, c)

    flat = lambda w: w.transpose(1, 2, 3, 0).reshape(9, w.shape[3], w.shape[0])
    (w_in, w_out, w_small, st0, xa, xb, ca, cb, rows, kv_all, cap_all, emb_all) = head_call(
        [flat(conv_in), flat(conv_out)], x, cot, time_embed, caption[0], embed_proj, caption_proj,
        norm_gains, norm_biases, qkv_proj.T, out_proj.T, nz, width, 0,
    )
    w_small = w_small.reshape(4, -1, 128)

    hidden, act0, st1, ha, hb = conv_call(x, xa, xb, st0, rows[0], w_in, None, n_sp, width, 1)
    res, act1, st2, ra, rb = conv_call(hidden, ha, hb, st1, rows[1], w_out, x, n_sp, width, 2)
    normed, kv, qg = project_call(res, st2, rows[2], w_small, cot, n_sp)
    od, dkv, dt_all = attention_call(kv, qg, kv_all, caption_mask, 3)

    parts = backward_call(
        [od, dkv, w_small, res, cot, normed, act1, hidden, act0, x], w_in, w_out,
        [st0, st1, st2, rows, ca, cb, ra, rb, ha, hb, dt_all, cap_all, emb_all, embed_proj, caption_proj, time_embed],
        nz, width, 5,
    )
    output, image, g_temb, g_cap, s_in, s_out, g_wemb, g_qkv, g_wcap, g_out, g_gains, g_biases = emit_call(
        parts, qkv_proj.shape[1]
    )
    unflat = lambda g: g.reshape(3, 3, g.shape[1], 128).transpose(3, 0, 1, 2)
    return (
        output.reshape(image_in.shape), image.reshape(image_in.shape), g_temb, g_cap[None], unflat(s_in), unflat(s_out),
        g_wemb, g_qkv.T, g_wcap, g_out.T, g_gains, g_biases,
    )


def body(*args):
    image_in, qkv_proj = args[0], args[7]
    n, height, width, c = image_in.shape
    n_img, n_sp = lax.axis_size("img"), lax.axis_size("sp")
    fits = n == 1 and n_img == 4 and n_sp == HEADS and c == 512 and width == 64
    return fast_body(*args) if fits else plain_body(*args)


def solution(mesh):
    rows = P("img", "sp", None, None)
    kernel = P("img", None, None, "sp")
    flat = P("img", "sp")
    return jax.shard_map(
        body,
        mesh=mesh,
        in_specs=(
            rows, P("img", None), P("img", None, None), P("img", None), kernel, kernel,
            flat, flat, flat, flat, P(None, "img"), P(None, "img"), rows,
        ),
        out_specs=(
            rows, rows, P("img", None), P("img", "sp", None), kernel, kernel,
            flat, flat, flat, flat, P(None, "img"), P(None, "img"),
        ),
        check_vma=False,
    )
```

```python
import functools

import jax
import jax.numpy as jnp
from jax import lax
from jax.experimental import pallas as pl
from jax.experimental.pallas import tpu as pltpu
from jax.sharding import PartitionSpec as P

HEADS = 8
GROUPS = 32
EPSILON = 1e-05
PRECISE = lax.Precision.HIGHEST
MASKED = -1e30
BF16 = jnp.bfloat16
F32 = jnp.float32
MESH = pl.DeviceIdType.MESH
VMEM_BYTES = 60 * 1024 * 1024


def dot(a, b, ca, cb):
    return lax.dot_general(a, b, (((ca,), (cb,)), ((), ())), preferred_element_type=F32)


def silu(v):
    return v * jax.nn.sigmoid(v)


def silu_slope(v):
    s = jax.nn.sigmoid(v)
    return s * (1.0 + v * (1.0 - s))


def gather(x, axis, dim):
    return lax.all_gather(x, axis, axis=dim, tiled=True)


def scatter_sum(x, axis, dim):
    return lax.psum_scatter(x, axis, scatter_dimension=dim, tiled=True)


def swap(x, axis, split, concat):
    return lax.all_to_all(x, axis, split, concat, tiled=True)


def halo(x):
    count = lax.axis_size("sp")
    above = lax.ppermute(x[:, -1:], "sp", [(i, i + 1) for i in range(count - 1)])
    below = lax.ppermute(x[:, :1], "sp", [(i + 1, i) for i in range(count - 1)])
    return above, below


def group_sum(v):
    c = v.shape[-1]
    g = v.reshape(v.shape[:-1] + (GROUPS, c // GROUPS))
    s = jnp.sum(g, axis=-1, keepdims=True)
    return jnp.broadcast_to(s, g.shape).reshape(v.shape)


def norm_stats(x):
    n, r, w, c = x.shape
    cells = r * w * (c // GROUPS)
    parts = lax.axis_size("sp")
    mean = group_sum(jnp.sum(x, axis=(1, 2))) / cells
    dev = group_sum(jnp.sum(jnp.square(x - mean[:, None, None, :]), axis=(1, 2)))
    both = lax.all_gather(jnp.stack([mean, dev]), "sp")
    means, devs = both[:, 0], both[:, 1]
    center = jnp.mean(means, axis=0)
    var = (jnp.sum(devs, axis=0) + cells * jnp.sum(jnp.square(means - center), axis=0)) / (
        cells * parts
    )
    return center, lax.rsqrt(var + EPSILON)


def hat_of(x, center, inverse):
    return (x - center[:, None, None, :]) * inverse[:, None, None, :]


def norm_back(u, hat, inverse, gain, sum_u, sum_uh, members):
    s1 = group_sum(sum_u * gain) / members
    s2 = group_sum(sum_uh * gain) / members
    return inverse[:, None, None, :] * (
        u * gain - s1[:, None, None, :] - hat * s2[:, None, None, :]
    )


def pad_cols(x):
    return jnp.pad(x, ((0, 0), (0, 0), (1, 1), (0, 0)))


def conv(padded, weight_t, transposed):
    n, rp, wp, c = padded.shape
    r, w = rp - 2, wp - 2
    total = None
    for i in range(3):
        for j in range(3):
            a = padded[:, i : i + r, j : j + w].reshape(n * r * w, c)
            part = dot(a, weight_t[2 - i, 2 - j], 1, 0) if transposed else dot(a, weight_t[i, j], 1, 1)
            total = part if total is None else total + part
    return total.reshape(n, r, w, -1)


def conv_grad(padded, g):
    n, r, w, c = g.shape
    gf = g.reshape(n * r * w, c)
    rows = []
    for i in range(3):
        for j in range(3):
            a = padded[:, i : i + r, j : j + w].reshape(n * r * w, -1)
            rows.append(dot(gf, a, 0, 0))
    return jnp.stack(rows).reshape(3, 3, c, -1)


def to_pairs(x, images):
    n, px, h, d = x.shape
    y = x.transpose(0, 2, 1, 3).reshape(n * h, px, d)
    return swap(y, "sp", 0, 1)


def from_pairs(x, images):
    y = swap(x, "sp", 1, 0)
    return y.reshape(images, HEADS, y.shape[1], y.shape[2]).transpose(0, 2, 1, 3)


def attention_plain(q, k, v, g, tk, tv, keep, scale):
    p, length, d = q.shape
    block = min(512, length)
    keys = jnp.concatenate([tk, k], axis=1)
    values = jnp.concatenate([tv, v], axis=1)
    text = tk.shape[1]
    keep_all = jnp.concatenate([keep, jnp.ones((p, length), bool)], axis=1)

    def step(carry, blk):
        dk, dv = carry
        qb, gb = blk
        s = jnp.einsum("pqd,pkd->pqk", qb, keys, preferred_element_type=F32) * scale
        s = jnp.where(keep_all[:, None, :], s, MASKED)
        peak = jnp.max(s, axis=-1, keepdims=True)
        e = jnp.exp(s - peak)
        prob = e / jnp.sum(e, axis=-1, keepdims=True)
        pb = prob.astype(BF16)
        o = jnp.einsum("pqk,pkd->pqd", pb, values, preferred_element_type=F32)
        row = jnp.sum(o * gb.astype(F32), axis=-1, keepdims=True)
        dp = jnp.einsum("pqd,pkd->pqk", gb, values, preferred_element_type=F32)
        ds = (prob * (dp - row)).astype(BF16)
        dq = jnp.einsum("pqk,pkd->pqd", ds, keys, preferred_element_type=F32) * scale
        dk = dk + jnp.einsum("pqk,pqd->pkd", ds, qb, preferred_element_type=F32)
        dv = dv + jnp.einsum("pqk,pqd->pkd", pb, gb, preferred_element_type=F32)
        return (dk, dv), (o.astype(BF16), dq.astype(BF16))

    zeros = jnp.zeros((p, text + length, d), F32)
    cut = lambda t: t.reshape(p, length // block, block, d).swapaxes(0, 1)
    (dk, dv), (o, dq) = lax.scan(step, (zeros, zeros), (cut(q), cut(g)))
    join = lambda t: t.swapaxes(0, 1).reshape(p, length, d)
    dk = (dk * scale).astype(BF16)
    dv = dv.astype(BF16)
    return join(o), join(dq), dk[:, text:], dv[:, text:], dk[:, :text], dv[:, :text]


def plain_body(
    image_in, time_embed, caption, caption_mask, conv_in, conv_out, embed_proj, qkv_proj,
    caption_proj, out_proj, norm_gains, norm_biases, cotangent,
):
    n, rows, width, chans = image_in.shape
    n_img, n_sp = lax.axis_size("img"), lax.axis_size("sp")
    img, sp = lax.axis_index("img"), lax.axis_index("sp")
    px = rows * width
    members = px * n_sp * (chans // GROUPS)
    d = chans // HEADS
    scale = d ** -0.5
    pairs = n * HEADS // n_sp

    def whole(w):
        w = gather(w, "img", w.ndim - 1)
        return gather(w, "sp", w.ndim - 2)

    w_in = whole(conv_in.transpose(1, 2, 3, 0))
    w_out = whole(conv_out.transpose(1, 2, 3, 0))
    w_qkv = whole(qkv_proj.T)
    w_proj = whole(out_proj.T)
    affine = gather(jnp.concatenate([norm_gains, norm_biases]), "img", 1).astype(F32)
    gains, biases = affine[:3], affine[3:]

    embedded = silu(time_embed.astype(F32)).astype(BF16)
    emb_all = swap(embedded, "img", 1, 0)
    mod = scatter_sum(jnp.dot(emb_all, embed_proj, preferred_element_type=F32), "img", 0)
    mod = gather(mod, "sp", 1)
    scale_term, shift_term = mod[:, :chans], mod[:, chans:]
    cap_all = swap(caption, "img", 2, 0)
    cap_flat = cap_all.reshape(-1, cap_all.shape[2])
    kv = jnp.dot(cap_flat, caption_proj, preferred_element_type=F32)
    kv = scatter_sum(kv.reshape(cap_all.shape[0], cap_all.shape[1], -1), "img", 0).astype(BF16)
    kv = gather(kv, "sp", 2)
    text = kv.shape[1]
    kv_heads = kv.reshape(n, text, 2, HEADS, d).transpose(2, 0, 3, 1, 4).reshape(2, n * HEADS, text, d)
    mine = lax.dynamic_slice_in_dim(kv_heads, sp * pairs, pairs, 1)
    keep = jnp.repeat(caption_mask > 0, HEADS, axis=0)
    keep = lax.dynamic_slice_in_dim(keep, sp * pairs, pairs, 0)

    image_f = image_in.astype(F32)
    c0, i0 = norm_stats(image_f)
    hat0 = hat_of(image_f, c0, i0)
    first = hat0 * gains[0] + biases[0]
    act0 = silu(first).astype(BF16)
    above, below = halo(act0)
    pad0 = pad_cols(jnp.concatenate([above, act0, below], axis=1))
    hidden = conv(pad0, w_in, False)
    c1, i1 = norm_stats(hidden)
    hat1 = hat_of(hidden, c1, i1)
    second = hat1 * gains[1] + biases[1]
    pre = second * (1.0 + scale_term[:, None, None, :]) + shift_term[:, None, None, :]
    act1 = silu(pre).astype(BF16)
    above, below = halo(act1)
    pad1 = pad_cols(jnp.concatenate([above, act1, below], axis=1))
    residual = image_f + conv(pad1, w_out, False)
    c2, i2 = norm_stats(residual)
    hat2 = hat_of(residual, c2, i2)
    normed = (hat2 * gains[2] + biases[2]).astype(BF16).reshape(n * px, chans)
    qkv = dot(normed, w_qkv, 1, 1).astype(BF16)
    cot = cotangent.reshape(n * px, chans)
    g_att = dot(cot, w_proj, 1, 0).astype(BF16)
    four = jnp.concatenate([qkv, g_att], axis=1).reshape(n, px, 4, HEADS, d)
    packed = to_pairs(four.transpose(0, 1, 3, 2, 4).reshape(n, px, HEADS, 4 * d), n)
    q, k, v, g = (packed[..., j * d : (j + 1) * d] for j in range(4))
    o, dq, dk, dv, dtk, dtv = attention_plain(q, k, v, g, mine[0], mine[1], keep, scale)
    back = from_pairs(jnp.concatenate([o, dq, dk, dv], axis=-1), n)
    back = back.reshape(n * px, HEADS, 4, d).transpose(0, 2, 1, 3).reshape(n * px, 4 * chans)
    attended, proj_grad = back[:, :chans], back[:, chans:]
    output = residual + dot(attended, w_proj, 1, 1).reshape(image_in.shape)

    grad_out = dot(cot, attended, 0, 0)
    grad_qkv = dot(proj_grad, normed, 0, 0)
    normed_grad = dot(proj_grad, w_qkv, 1, 0).reshape(image_in.shape)

    def sums(u, hat):
        both = jnp.stack([jnp.sum(u, axis=(1, 2)), jnp.sum(u * hat, axis=(1, 2))])
        return lax.psum(both, "sp")

    su2, sh2 = sums(normed_grad, hat2)
    residual_grad = cotangent.astype(F32) + norm_back(
        normed_grad, hat2, i2, gains[2], su2, sh2, members
    )
    g2 = residual_grad.astype(BF16)
    above, below = halo(g2)
    gpad = pad_cols(jnp.concatenate([above, g2, below], axis=1))
    grad_conv_out = conv_grad(pad1, g2)
    pre_grad = conv(gpad, w_out, True) * silu_slope(pre)
    sa, sb = sums(pre_grad, hat1)
    fac = 1.0 + scale_term
    shift_grad = sa
    scale_grad = sb * gains[1] + sa * biases[1]
    u1 = pre_grad * fac[:, None, None, :]
    su1, sh1 = sa * fac, sb * fac
    g1 = norm_back(u1, hat1, i1, gains[1], su1, sh1, members).astype(BF16)
    above, below = halo(g1)
    gpad = pad_cols(jnp.concatenate([above, g1, below], axis=1))
    grad_conv_in = conv_grad(pad0, g1)
    u0 = conv(gpad, w_in, True) * silu_slope(first)
    su0, sh0 = sums(u0, hat0)
    grad_image = residual_grad + norm_back(u0, hat0, i0, gains[0], su0, sh0, members)

    mod_grad = jnp.concatenate([scale_grad, shift_grad], axis=1)
    cols = embed_proj.shape[1]
    mod_all = gather(mod_grad, "img", 0)
    mod_cols = lax.dynamic_slice_in_dim(mod_all, sp * cols, cols, 1)
    grad_embed_proj = jnp.einsum("ne,nd->ed", emb_all.astype(F32), mod_cols, precision=PRECISE)
    part = jnp.einsum("nd,ed->ne", mod_cols, embed_proj.astype(F32), precision=PRECISE)
    part = swap(lax.psum(part, "sp"), "img", 0, 1)
    grad_embed = part * silu_slope(time_embed.astype(F32))

    tg = gather(jnp.stack([dtk, dtv]), "sp", 1).reshape(2, n, HEADS, text, d)
    tg = tg.transpose(1, 3, 0, 2, 4).reshape(n, text, 2 * chans)
    cols = caption_proj.shape[1]
    tg = gather(lax.dynamic_slice_in_dim(tg, sp * cols, cols, 2), "img", 0).reshape(-1, cols)
    grad_caption_proj = dot(cap_flat, tg, 0, 0)
    gc = dot(tg, caption_proj, 1, 1).reshape(cap_all.shape)
    gc = scatter_sum(gc, "sp", 1)
    grad_caption = swap(gc, "img", 0, 2)

    grads = jnp.concatenate(
        [jnp.sum(t, axis=0)[None] for t in (sh0, sh1, sh2, su0, su1, su2)]
    )
    grads = scatter_sum(grads, "img", 1)

    def shared(w):
        w = scatter_sum(w, "sp", w.ndim - 2)
        return scatter_sum(w, "img", w.ndim - 1)

    return (
        output.astype(BF16),
        grad_image,
        grad_embed,
        grad_caption,
        shared(grad_conv_in).transpose(3, 0, 1, 2),
        shared(grad_conv_out).transpose(3, 0, 1, 2),
        grad_embed_proj,
        shared(grad_qkv).T,
        grad_caption_proj,
        shared(grad_out).T,
        grads[:3],
        grads[3:],
    )


class Place:
    def __init__(self):
        self.i = lax.axis_index("img")
        self.s = lax.axis_index("sp")
        self.z = lax.div(self.s, 2)
        self.c = lax.rem(self.s, 2)
        x = lax.rem(self.i, 2)
        y = lax.div(self.i, 2)
        self.ix = self.i + 1 - 2 * x
        self.iy = self.i + 2 - 4 * y
        self.id = 3 - self.i
        self.sib = (self.i, self.s + 1 - 2 * self.c)
        self.xn = (self.ix, self.s)
        self.yn = (self.iy, self.s)

    def zp(self, k, nz):
        return (self.i, 2 * lax.rem(self.z + k, nz) + self.c)

    def rp(self, k, n_sp):
        return (self.i, lax.rem(self.s + k, n_sp))


def greet(peers):
    bar = pltpu.get_barrier_semaphore()
    for p in peers:
        pl.semaphore_signal(bar, inc=1, device_id=p, device_id_type=MESH)


def greeted(count):
    pl.semaphore_wait(pltpu.get_barrier_semaphore(), count)


def remote(src, dst, ssem, rsem, dev):
    cp = pltpu.make_async_remote_copy(
        src_ref=src, dst_ref=dst, send_sem=ssem, recv_sem=rsem, device_id=dev, device_id_type=MESH
    )
    cp.start()
    return cp


def params(cid=None, grid=0):
    extra = {} if cid is None else {"collective_id": cid, "has_side_effects": True}
    if grid:
        extra["dimension_semantics"] = ("arbitrary",) * grid
    return pltpu.CompilerParams(vmem_limit_bytes=VMEM_BYTES, **extra)


ANY = pl.BlockSpec(memory_space=pl.ANY)
VM = pl.BlockSpec(memory_space=pltpu.VMEM)
def channel_stats(mine, v):
    mean = jnp.sum(v, axis=0, keepdims=True) / v.shape[0]
    dev = v - mean
    mine[0:1, :] = mean
    mine[1:2, :] = jnp.sum(dev * dev, axis=0, keepdims=True)


def group_total(rows):
    c = rows.shape[1]
    size = c // GROUPS
    a = lax.broadcasted_iota(jnp.int32, (128, 128), 0)
    b = lax.broadcasted_iota(jnp.int32, (128, 128), 1)
    same = jnp.where(lax.bitwise_xor(a, b) < size, 1.0, 0.0).astype(BF16)
    high = rows.astype(BF16)
    rest = rows - high.astype(F32)
    mid = rest.astype(BF16)
    low = (rest - mid.astype(F32)).astype(BF16)
    parts = jnp.concatenate([high.astype(F32), mid.astype(F32), low.astype(F32)]).astype(BF16)
    total = jnp.concatenate(
        [dot(parts[:, j * 128 : (j + 1) * 128], same, 1, 0) for j in range(c // 128)], axis=1
    )
    n = rows.shape[0]
    return total[:n] + total[n : 2 * n] + total[2 * n :]


def combine_stats(every, px):
    n_sp, _, c = every.shape
    size = c // GROUPS
    means = [every[j, 0:1, :] for j in range(n_sp)]
    center_c = sum(means) / n_sp
    dev = sum(every[j, 1:2, :] for j in range(n_sp))
    dev = dev + px * sum((m - center_c) * (m - center_c) for m in means)
    center = group_total(jnp.broadcast_to(center_c, (8, c)))[0:1] / size
    off = center_c - center
    dev = dev + (px * n_sp) * (off * off)
    var = group_total(jnp.broadcast_to(dev, (8, c)))[0:1] / (px * n_sp * size)
    return center, lax.rsqrt(var + EPSILON)


def combine_sums(every):
    n_sp = every.shape[0]
    total = every[0]
    for j in range(1, n_sp):
        total = total + every[j]
    return total


def edge_flags(n_sp, s):
    return jnp.where(s > 0, 1.0, 0.0), jnp.where(s < n_sp - 1, 1.0, 0.0)


def shifted(dst, row, width, block):
    col = lax.broadcasted_iota(jnp.int32, block.shape, 0)
    r = slice(row * width, (row + 1) * width)
    dst[1, r, :] = block.astype(BF16)
    dst[0, r, :] = jnp.where(col == 0, 0.0, pltpu.roll(block, 1, 0)).astype(BF16)
    dst[2, r, :] = jnp.where(col == width - 1, 0.0, pltpu.roll(block, width - 1, 0)).astype(BF16)


def joined(w_ref, *lead):
    return jnp.concatenate([w_ref[(j,) + lead] for j in range(4)], axis=-1)


def split_small(whole, n_sp):
    c = whole.shape[1]
    cols, out = 3 * c // n_sp, c // n_sp
    chunk = cols + out
    return (
        jnp.concatenate([whole[j * chunk : j * chunk + cols] for j in range(n_sp)]),
        jnp.concatenate([whole[j * chunk + cols : (j + 1) * chunk] for j in range(n_sp)]),
    )


def attention_kernel(
    n_sp, BQ, BK, kv, qg, text, keep, od, dkv, dt,
    kv_r, qg_r, od_s, dkv_s, dt_s, k_s, v_s, s_s, e_s, dk_s, dv_s, lsem, ssem, rsem,
):
    at = Place()
    px = kv.shape[1]
    L, T = n_sp * px, text.shape[1]
    d = kv.shape[2] // 2
    line = [at.rp(k, n_sp) for k in range(1, n_sp)]
    greet(line)
    own = [
        pltpu.make_async_copy(kv.at[at.s], kv_r.at[at.s], lsem.at[0]),
        pltpu.make_async_copy(qg.at[at.s], qg_r.at[at.s], lsem.at[1]),
    ]
    for cp in own:
        cp.start()
    greeted(n_sp - 1)
    sent = [remote(kv.at[dev[1]], kv_r.at[at.s], ssem.at[0, k + 1], rsem.at[0, k + 1], dev) for k, dev in enumerate(line)]
    odd = lax.rem(at.s, 2)
    pair = lax.div(at.s, 2)
    ones = (lax.broadcasted_iota(jnp.int32, (1, d), 1) == 0).astype(BF16)
    picked = []
    for j in (pair, HEADS // 2 + pair):
        blk = text[j].astype(F32)
        picked.append(jnp.where(odd > 0, blk[:, d:], blk[:, :d]).astype(BF16))
    k_s[0:T, :] = picked[0]
    v_s[0:T, :] = jnp.concatenate([picked[1], jnp.broadcast_to(ones, (T, d))], axis=1)
    dk_s[...] = jnp.zeros_like(dk_s)
    dv_s[...] = jnp.zeros_like(dv_s)

    def take(j):
        rows = pl.ds(pl.multiple_of(T + j * px, px if T % px == 0 else T), px)
        k_s[rows, :] = kv_r[j][:, :d]
        v_s[rows, :] = jnp.concatenate([kv_r[j][:, d:], jnp.broadcast_to(ones, (px, d))], axis=1)

    for cp in own:
        cp.wait()
    take(at.s)
    for k in range(1, n_sp):
        sent[k - 1].wait_recv()
        take(lax.rem(at.s - k + n_sp, n_sp))
    sent += [remote(qg.at[dev[1]], qg_r.at[at.s], ssem.at[1, k + 1], rsem.at[1, k + 1], dev) for k, dev in enumerate(line)]

    blocks = [(0, T)] + [(T + j * BK, BK) for j in range(L // BK)]
    per = px // BQ
    scale = d ** -0.5

    def query_copy(k):
        return pltpu.make_async_remote_copy(
            src_ref=qg.at[at.s], dst_ref=qg_r.at[at.s], send_sem=ssem.at[1, k], recv_sem=rsem.at[1, k],
            device_id=(at.i, lax.rem(at.s + k, n_sp)), device_id_type=MESH,
        )

    def back_copy(k, o):
        return pltpu.make_async_remote_copy(
            src_ref=od_s.at[o], dst_ref=od.at[at.s], send_sem=ssem.at[2, k], recv_sem=rsem.at[2, k],
            device_id=(at.i, o), device_id_type=MESH,
        )

    def step(t, _):
        k, part = lax.div(t, per), lax.rem(t, per)
        o_dev = lax.rem(at.s - k + n_sp, n_sp)

        @pl.when(jnp.logical_and(part == 0, k > 0))
        def _():
            query_copy(k).wait_recv()

        r = pl.ds(pl.multiple_of(part * BQ, BQ), BQ)
        both = qg_r[o_dev, r, :]
        q, g = both[:, :d], both[:, d:]
        peak = None
        for st, n in blocks:
            s = dot(q, k_s[st : st + n, :], 1, 1)
            if st == 0:
                s = jnp.where(keep[...] > 0, s, MASKED)
            s_s[:, st : st + n] = s
            for j in range(n // 128):
                piece = s[:, 128 * j : 128 * j + 128]
                peak = piece if peak is None else jnp.maximum(peak, piece)
        peak = jnp.max(peak, axis=1, keepdims=True)
        o = jnp.zeros((BQ, 2 * d), F32)
        for st, n in blocks:
            e = jnp.exp(s_s[:, st : st + n] - peak).astype(BF16)
            e_s[:, st : st + n] = e
            o = o + dot(e, v_s[st : st + n, :], 1, 0)
        inverse = 1.0 / o[:, d : d + 1]
        o = o[:, :d] * inverse
        g = g.astype(F32) * inverse
        row = jnp.sum(o * g, axis=1, keepdims=True)
        g = g.astype(BF16)
        gt, qt = g.T, q.T
        dq = jnp.zeros((BQ, d), F32)
        for st, n in blocks:
            e = e_s[:, st : st + n]
            dp = dot(g, v_s[st : st + n, :d], 1, 1)
            ds = (e.astype(F32) * (dp - row)).astype(BF16)
            dq = dq + dot(ds, k_s[st : st + n, :], 1, 0)
            dv_s[:, st : st + n] += dot(gt, e, 1, 0)
            dk_s[:, st : st + n] += dot(qt, ds, 1, 0)
        od_s[o_dev, r, :] = jnp.concatenate([o, dq * scale], axis=1).astype(BF16)

        @pl.when(jnp.logical_and(part == per - 1, k > 0))
        def _():
            back_copy(k, o_dev).start()

        return 0

    lax.fori_loop(0, n_sp * per, step, 0)
    local = [pltpu.make_async_copy(od_s.at[at.s], od.at[at.s], lsem.at[2])]

    def gradients(st, n):
        return jnp.concatenate([dk_s[:, st : st + n], dv_s[:, st : st + n]], axis=0).astype(BF16).T

    for j in range(n_sp):
        dkv_s[j] = gradients(T + j * px, px)
    for k, dev in enumerate(line):
        sent.append(remote(dkv_s.at[dev[1]], dkv.at[at.s], ssem.at[3, k + 1], rsem.at[3, k + 1], dev))
    dt_s[...] = gradients(0, T)
    for k, dev in enumerate(line):
        sent.append(remote(dt_s, dt.at[at.s], ssem.at[4, k + 1], rsem.at[4, k + 1], dev))
    local.append(pltpu.make_async_copy(dkv_s.at[at.s], dkv.at[at.s], lsem.at[3]))
    local.append(pltpu.make_async_copy(dt_s, dt.at[at.s], lsem.at[4]))
    for cp in local:
        cp.start()
    for k in range(1, n_sp):
        back_copy(k, lax.rem(at.s - k + n_sp, n_sp)).wait()
    for cp in sent[n_sp - 1 : 2 * (n_sp - 1)]:
        cp.wait_send()
    for cp in sent[: n_sp - 1]:
        cp.wait_send()
    for cp in sent[2 * (n_sp - 1) :]:
        cp.wait()
    for cp in local:
        cp.wait()


def attention_call(kv, qg, text, keep, cid):
    n_sp, px, d2 = kv.shape
    T = text.shape[1]
    L = n_sp * px
    d = d2 // 2
    BQ, BK = 256, 1024
    outs = [(n_sp, px, d2), (n_sp, px, d2), (n_sp, T, d2)]
    vm = pltpu.VMEM
    return pl.pallas_call(
        functools.partial(attention_kernel, n_sp, BQ, BK),
        out_shape=[jax.ShapeDtypeStruct(s, BF16) for s in outs],
        in_specs=[ANY, ANY, VM, VM],
        out_specs=[ANY] * 3,
        scratch_shapes=[
            vm((n_sp, px, d2), BF16), vm((n_sp, px, d2), BF16), vm((n_sp, px, d2), BF16), vm((n_sp, px, d2), BF16),
            vm((T, d2), BF16), vm((T + L, d), BF16), vm((T + L, d2), BF16),
            vm((BQ, T + L), F32), vm((BQ, T + L), BF16), vm((d, T + L), F32), vm((d, T + L), F32),
            pltpu.SemaphoreType.DMA((5,)),
            pltpu.SemaphoreType.DMA((5, n_sp)),
            pltpu.SemaphoreType.DMA((5, n_sp)),
        ],
        compiler_params=params(cid),
        name="attention",
    )(kv, qg, text, keep)


class Mail:
    def __init__(self, ssem, rsem):
        self.ssem, self.rsem, self.sent = ssem, rsem, []

    def send(self, src, dst, dev):
        j = len(self.sent)
        cp = remote(src, dst, self.ssem.at[j], self.rsem.at[j], dev)
        self.sent.append(cp)
        return cp


class Gather:
    def __init__(self, at, nz, ins, outs, dims, ssem, rsem):
        self.at, self.nz, self.ins, self.outs, self.dims = at, nz, ins, outs, dims
        self.ssem, self.rsem = ssem, rsem
        self.sent, self.kinds = {}, {}

    @staticmethod
    def copies(nz):
        return 3 * nz - 1 + 7 * nz

    def view(self, a, ii, k, core, half=None):
        at, nz, r = self.at, self.nz, self.dims[a][1]
        sp = 2 * lax.rem(at.z - k + nz, nz) + core
        if half is None:
            return self.outs[a].at[ii, :, pl.ds(pl.multiple_of(sp * r, r), r), :]
        h = r // 2
        return self.outs[a].at[ii, :, pl.ds(pl.multiple_of(sp * r + half * h, h), h), :]

    def send(self, a, kind, src, dst, dev):
        j = self.kinds.setdefault(kind, len(self.kinds))
        self.sent[a, kind] = remote(src, dst, self.ssem.at[a, j], self.rsem.at[a, j], dev)

    def forward(self, a, kind, ref, dev):
        self.send(a, kind, ref, ref, dev)

    def first(self, a):
        at = self.at
        own = self.view(a, at.i, 0, at.c)
        for k in range(1, self.nz):
            self.send(a, ("z", k), self.ins[a], own, at.zp(k, self.nz))
        self.send(a, ("x", 0), self.ins[a], own, at.xn)
        self.send(a, ("y", 0), self.ins[a], own, at.yn)
        self.send(a, ("s", 0), self.ins[a], own, at.sib)

    def second(self, a):
        at = self.at
        for k in range(1, self.nz):
            self.sent[a, ("z", k)].wait_recv()
            got = self.view(a, at.i, k, at.c)
            self.forward(a, ("x", k), got, at.xn)
            self.forward(a, ("y", k), got, at.yn)
            self.forward(a, ("s", k), got, at.sib)

    def third(self, a):
        at = self.at
        for k in range(self.nz):
            self.sent[a, ("x", k)].wait_recv()
            self.forward(a, ("da", k), self.view(a, at.ix, k, at.c, 0), at.yn)
            self.forward(a, ("sx", k), self.view(a, at.ix, k, at.c), at.sib)
            self.sent[a, ("y", k)].wait_recv()
            self.forward(a, ("db", k), self.view(a, at.iy, k, at.c, 1), at.xn)
            self.forward(a, ("sy", k), self.view(a, at.iy, k, at.c), at.sib)

    def fourth(self, a):
        at = self.at
        for k in range(self.nz):
            self.sent[a, ("da", k)].wait_recv()
            self.forward(a, ("sa", k), self.view(a, at.id, k, at.c, 0), at.sib)
            self.sent[a, ("db", k)].wait_recv()
            self.forward(a, ("sb", k), self.view(a, at.id, k, at.c, 1), at.sib)

    def complete(self, a):
        for (b, kind), cp in self.sent.items():
            if b == a and kind[0][0] == "s":
                cp.wait_recv()

    def finish(self):
        for cp in self.sent.values():
            cp.wait_send()


def img_peers(at):
    return [(lax.rem(at.i + k, 4), at.s) for k in range(1, 4)]


FORWARD_MAIL = 3 * 3 + 3 + 2 * 7 + 4 + 7 + 2 * (2 + 7)


def forward_kernel(nz, width, dims, *refs):
    na = len(dims)
    chunks, refs = refs[: na - 1], refs[na - 1 :]
    x, cot, temb, cap, w_emb, w_cap, gains, biases, w_qkv, w_proj = refs[:10]
    outs, refs = refs[10 : 10 + na], refs[10 + na :]
    hidden_o, act0_o, res_o, act1_o, normed, kv, qg = refs[:7]
    st0, st1, st2, rows, ca, cb, ra, rb, ha, hb, kv_all, cap_all, emb_all = refs[7:20]
    refs = refs[20:]
    weights, refs = refs[:na], refs[na:]
    (ssem, rsem, lsem, msend, mrecv, small, emb, affine, mine, every, xa, xb, ca_s, cb_s, ha_s, hb_s, ra_s, rb_s,
     aff_s, emb_s, cap_s, part, part_r, kv_s, kv_r, mod_s, mod_r, a3, act0, act1, hidden, res) = refs
    n_sp = 2 * nz
    at = Place()
    line = [at.rp(k, n_sp) for k in range(1, n_sp)]
    grid = img_peers(at)
    greet(line + grid)
    mail = Mail(msend, mrecv)
    got = Gather(at, nz, list(chunks) + [small], weights, dims, ssem, rsem)
    px, c = x.shape
    height = px // width
    d = c // HEADS
    tokens = cap.shape[0]
    e = cap.shape[1] // 4
    cut = w_qkv.shape[0]
    local = []

    def copy(src, dst):
        cp = pltpu.make_async_copy(src, dst, lsem.at[len(local)])
        cp.start()
        local.append(cp)
        return cp

    small[0, :cut] = w_qkv[...]
    small[0, cut:] = w_proj[...]
    embedded = silu(temb[...].astype(F32)).astype(BF16).astype(F32)
    for j in range(4):
        emb[j] = jnp.broadcast_to(embedded[:, j * e : (j + 1) * e], (8, e))
    affine[0:3] = gains[...].astype(F32)
    affine[3:6] = biases[...].astype(F32)
    mine[...] = jnp.zeros_like(mine)

    def publish(j, v, edges):
        channel_stats(mine.at[j], v)
        out = []
        for ref, above, below in edges:
            out.append(mail.send(ref.at[px - width :], above, line[0]))
            out.append(mail.send(ref.at[:width], below, line[-1]))
        for dev in line:
            out.append(mail.send(mine.at[j], every.at[j, at.s], dev))
        every[j, at.s] = mine[j]
        return out

    greeted(n_sp + 2)
    got.first(0)
    stat0 = publish(0, x[...].astype(F32), [(x, xa, xb), (cot, ca_s, cb_s)])
    round1 = []
    for dev in grid:
        round1.append(mail.send(affine, aff_s.at[at.i], dev))
        round1.append(mail.send(emb.at[dev[0]], emb_s.at[at.i], dev))
        round1.append(mail.send(cap.at[:, pl.ds(pl.multiple_of(dev[0] * e, e), e)], cap_s.at[at.i], dev))
    own_cap = copy(cap.at[:, pl.ds(pl.multiple_of(at.i * e, e), e)], cap_s.at[at.i])
    aff_s[at.i] = affine[...]
    emb_s[at.i] = emb[at.i]
    got.first(1)
    own = [copy(got.ins[a], got.view(a, at.i, 0, at.c)) for a in range(na)]
    got.second(0)
    got.first(2)
    got.third(0)
    got.second(1)

    own_cap.wait()
    for cp in round1:
        cp.wait_recv()
    for j in range(4):
        part[j, :tokens] = dot(cap_s[j], w_cap[...], 1, 0)
        part[j, tokens:] = dot(emb_s[j].astype(BF16), w_emb[...], 1, 0)
    round2 = [mail.send(part.at[dev[0]], part_r.at[at.i], dev) for dev in grid]
    part_r[at.i] = part[at.i]
    cap_all[...] = cap_s[...]
    emb_all[...] = jnp.concatenate([emb_s[j][0:1] for j in range(4)] + [jnp.zeros((4, e), F32)])
    aff = jnp.concatenate([aff_s[j] for j in range(4)], axis=1)
    rows[...] = jnp.zeros_like(rows)
    for j in range(3):
        rows[j, 0:1] = aff[j : j + 1]
        rows[j, 1:2] = aff[3 + j : 4 + j]
        rows[j, 2:3] = jnp.ones((1, c), F32)

    has_up, has_dn = edge_flags(n_sp, at.s)

    def activate(j, v, above, below, act):
        center, inverse = combine_stats(every.at[j], px)
        mul = inverse * rows[j, 0:1] * rows[j, 2:3]
        add = rows[j, 1:2] * rows[j, 2:3] + rows[j, 3:4]
        for r in range(height + 2):
            top, end = r == 0, r == height + 1
            t = above[...] if top else below[...] if end else v[(r - 1) * width : r * width, :]
            t = silu((t.astype(F32) - center) * mul + add)
            if top:
                t = t * has_up
            elif end:
                t = t * has_dn
            act[r * width : (r + 1) * width, :] = t.astype(BF16)
            shifted(a3, r, width, t)

    def taps(w, out, t0, t1, base):
        def one(tap, _):
            i, j = lax.div(tap, 3), lax.rem(tap, 3)
            lhs = a3[j, pl.ds(pl.multiple_of(i * width, width), px), :]
            first = 0.0 if base is None else base[...].astype(F32)
            out[...] = dot(lhs, joined(w, tap), 1, 1) + jnp.where(tap > 0, out[...], first)
            return 0

        lax.fori_loop(t0, t1, one, 0)

    for cp in stat0:
        cp.wait_recv()
    activate(0, x, xa, xb, act0)
    copy(act0, act0_o)
    got.fourth(0)
    for cp in own:
        cp.wait()
    got.complete(0)
    copy(weights[0], outs[0])
    taps(weights[0], hidden, 0, 3, None)
    got.second(2)
    taps(weights[0], hidden, 3, 6, None)
    got.third(1)
    taps(weights[0], hidden, 6, 9, None)
    stat1 = publish(1, hidden[...], [(hidden, ha_s, hb_s)])
    copy(hidden, hidden_o)
    for cp in round2:
        cp.wait_recv()
    total = part_r[0] + part_r[1] + part_r[2] + part_r[3]
    kv_s[...] = total[:tokens].astype(BF16)
    mod_s[...] = total[tokens:]
    round3 = []
    for dev in line:
        round3.append(mail.send(kv_s, kv_r.at[at.s], dev))
        round3.append(mail.send(mod_s, mod_r.at[at.s], dev))
    kv_r[at.s] = kv_s[...]
    mod_r[at.s] = mod_s[...]
    got.fourth(1)
    got.third(2)
    for cp in round3 + stat1:
        cp.wait_recv()
    kv_all[...] = kv_r[...]
    mod = jnp.concatenate([mod_r[j][0:1] for j in range(n_sp)], axis=1)
    rows[1, 2:3] = 1.0 + mod[:, :c]
    rows[1, 3:4] = mod[:, c:]

    activate(1, hidden, ha_s, hb_s, act1)
    copy(act1, act1_o)
    got.fourth(2)
    got.complete(1)
    copy(weights[1], outs[1])
    taps(weights[1], res, 0, 9, x)
    stat2 = publish(2, res[...], [(res, ra_s, rb_s)])
    copy(res, res_o)
    for dst, src in ((ca, ca_s), (cb, cb_s), (ha, ha_s), (hb, hb_s)):
        dst[...] = src[...]
    got.complete(2)
    copy(weights[2], outs[2])
    wq, wp = split_small(joined(weights[2], 0), n_sp)
    g = dot(cot[...], wp, 1, 0).astype(BF16)

    for cp in stat2:
        cp.wait_recv()
    center, inverse = combine_stats(every.at[2], px)
    n = ((res[...] - center) * (inverse * rows[2, 0:1]) + rows[2, 1:2]).astype(BF16)
    normed[...] = n
    k = dot(n, wq[c : 2 * c], 1, 1).astype(BF16)
    v = dot(n, wq[2 * c :], 1, 1).astype(BF16)
    q = (dot(n, wq[:c], 1, 1).astype(BF16).astype(F32) * (d ** -0.5)).astype(BF16)
    for h in range(HEADS):
        lanes = slice(h * d, (h + 1) * d)
        kv[h] = jnp.concatenate([k[:, lanes], v[:, lanes]], axis=1)
        qg[h] = jnp.concatenate([q[:, lanes], g[:, lanes]], axis=1)
    ra[...] = ra_s[...]
    rb[...] = rb_s[...]
    st0[...] = every[0]
    st1[...] = every[1]
    st2[...] = every[2]
    for cp in local[1 + na :]:
        cp.wait()
    got.finish()
    for cp in mail.sent:
        cp.wait_send()


def forward_call(chunks, x, cot, temb, cap, w_emb, w_cap, gains, biases, w_qkv, w_proj, nz, width, cid):
    dims = [c.shape[:2] for c in chunks] + [(1, w_qkv.shape[0] + w_proj.shape[0])]
    na = len(dims)
    n_sp = 2 * nz
    px, c = x.shape
    padded = px + 2 * width
    tokens, wide = cap.shape
    e = wide // 4
    d2 = 2 * c // HEADS
    big = [((4, t, n_sp * r, 128), BF16) for t, r in dims]
    edge16, edge32 = ((width, c), BF16), ((width, c), F32)
    stat = ((n_sp, 8, c), F32)
    outs = big + [
        ((px, c), F32), ((padded, c), BF16), ((px, c), F32), ((padded, c), BF16), ((px, c), BF16),
        ((HEADS, px, d2), BF16), ((HEADS, px, d2), BF16),
        stat, stat, stat, ((3, 8, c), F32), edge16, edge16, edge32, edge32, edge32, edge32,
        ((n_sp, tokens, 128), BF16), ((4, tokens, e), BF16), ((8, e), F32),
    ]
    vm = pltpu.VMEM
    return pl.pallas_call(
        functools.partial(forward_kernel, nz, width, dims),
        out_shape=[jax.ShapeDtypeStruct(s, ty) for s, ty in outs],
        in_specs=[ANY] * (na - 1) + [VM, VM, VM, ANY] + [VM] * 6,
        out_specs=[ANY] * (na + 4) + [VM] * (len(outs) - na - 4),
        scratch_shapes=[vm(s, ty) for s, ty in big]
        + [
            pltpu.SemaphoreType.DMA((na, Gather.copies(nz))),
            pltpu.SemaphoreType.DMA((na, Gather.copies(nz))),
            pltpu.SemaphoreType.DMA((2 * na + 5,)),
            pltpu.SemaphoreType.DMA((FORWARD_MAIL,)),
            pltpu.SemaphoreType.DMA((FORWARD_MAIL,)),
            vm((1, dims[-1][1], 128), BF16), vm((4, 8, e), F32), vm((8, 128), F32),
            vm((3, 8, c), F32), vm((3, n_sp, 8, c), F32),
        ]
        + [vm(*edge16)] * 4 + [vm(*edge32)] * 4
        + [
            vm((4, 8, 128), F32), vm((4, 8, e), F32), vm((4, tokens, e), BF16),
            vm((4, tokens + 8, 128), F32), vm((4, tokens + 8, 128), F32),
            vm((tokens, 128), BF16), vm((n_sp, tokens, 128), BF16), vm((8, 128), F32), vm((n_sp, 8, 128), F32),
            vm((3, padded, c), BF16), vm((padded, c), BF16), vm((padded, c), BF16), vm((px, c), F32), vm((px, c), F32),
        ],
        compiler_params=params(cid),
        name="forward",
    )(*chunks, x, cot, temb, cap, w_emb, w_cap, gains, biases, w_qkv, w_proj)


class Reducer:
    NAMES = ("d", "sb", "da", "db", "rx", "ry", "r", "zr")

    def __init__(self, at, nz, arrays, ssem, rsem):
        self.at, self.nz, self.arrays = at, nz, arrays
        self.ssem, self.rsem = ssem, rsem
        self.sent, self.groups = {}, []

    @staticmethod
    def buffers(nz, t, r):
        return [
            pltpu.VMEM((2, 4, t, nz, r, 128), BF16),
            pltpu.VMEM((4, t, nz, r, 128), BF16),
            pltpu.VMEM((t, nz, r // 2, 128), BF16),
            pltpu.VMEM((t, nz, r // 2, 128), BF16),
            pltpu.VMEM((t, nz, r, 128), BF16),
            pltpu.VMEM((t, nz, r, 128), BF16),
            pltpu.VMEM((t, nz, r, 128), BF16),
            pltpu.VMEM((nz - 1, t, r, 128), BF16),
        ]

    def send(self, g, j, src, dst, dev):
        self.sent[g, j] = remote(src, dst, self.ssem.at[g, j], self.rsem.at[g, j], dev)

    def add(self, a, t0, t1):
        g = len(self.groups)
        self.groups.append((a, t0, t1))
        b = self.arrays[a][1]
        self.send(g, 0, b["d"].at[1 - self.at.c, :, t0:t1], b["sb"].at[:, t0:t1], self.at.sib)

    def run(self, stage, *groups):
        one = (self.stage1, self.stage2, self.stage3, self.stage4)[stage - 1]
        for g in groups:
            one(g, *self.groups[g])

    def stage1(self, g, a, t0, t1):
        b, at = self.arrays[a][1], self.at
        d, sb = b["d"], b["sb"]
        self.sent[g, 0].wait_recv()
        n = t1 - t0

        def add(j, _):
            ii, tt = lax.div(j, n), t0 + lax.rem(j, n)
            d[at.c, ii, tt] = (d[at.c, ii, tt].astype(F32) + sb[ii, tt].astype(F32)).astype(BF16)
            return 0

        lax.fori_loop(0, 4 * n, add, 0)
        h = d.shape[4] // 2
        self.send(g, 1, d.at[at.c, at.id, t0:t1, :, :h], b["da"].at[t0:t1], at.yn)
        self.send(g, 2, d.at[at.c, at.id, t0:t1, :, h:], b["db"].at[t0:t1], at.xn)

    def stage2(self, g, a, t0, t1):
        b, at = self.arrays[a][1], self.at
        d = b["d"]
        h = d.shape[4] // 2
        self.sent[g, 1].wait_recv()
        self.sent[g, 2].wait_recv()

        def add(tt, _):
            d[at.c, at.ix, tt, :, :h] = (
                d[at.c, at.ix, tt, :, :h].astype(F32) + b["da"][tt].astype(F32)
            ).astype(BF16)
            d[at.c, at.iy, tt, :, h:] = (
                d[at.c, at.iy, tt, :, h:].astype(F32) + b["db"][tt].astype(F32)
            ).astype(BF16)
            return 0

        lax.fori_loop(t0, t1, add, 0)
        self.send(g, 3, d.at[at.c, at.ix, t0:t1], b["rx"].at[t0:t1], at.xn)
        self.send(g, 4, d.at[at.c, at.iy, t0:t1], b["ry"].at[t0:t1], at.yn)

    def stage3(self, g, a, t0, t1):
        b, at = self.arrays[a][1], self.at
        self.sent[g, 3].wait_recv()
        self.sent[g, 4].wait_recv()

        def add(tt, _):
            total = b["d"][at.c, at.i, tt].astype(F32) + b["rx"][tt].astype(F32) + b["ry"][tt].astype(F32)
            b["r"][tt] = total.astype(BF16)
            return 0

        lax.fori_loop(t0, t1, add, 0)
        for k in range(1, self.nz):
            there = lax.rem(at.z + k, self.nz)
            self.send(g, 4 + k, b["r"].at[t0:t1, there], b["zr"].at[k - 1, t0:t1], at.zp(k, self.nz))

    def stage4(self, g, a, t0, t1):
        (out, b), at = self.arrays[a], self.at
        for k in range(1, self.nz):
            self.sent[g, 4 + k].wait_recv()

        def add(tt, _):
            total = (
                b["d"][at.c, at.i, tt, at.z].astype(F32)
                + b["rx"][tt, at.z].astype(F32)
                + b["ry"][tt, at.z].astype(F32)
            )
            for k in range(1, self.nz):
                total = total + b["zr"][k - 1, tt].astype(F32)
            out[tt] = total
            return 0

        lax.fori_loop(t0, t1, add, 0)

    def finish(self):
        for cp in self.sent.values():
            cp.wait_send()


BACK_MAIL = 6 + 14 + 6 + 3 + 7 + 9 + 9
BACK_GROUPS = 7
BIG = 10


def conv_taps(t0, t1, w, ring, rsem, one):
    slots = ring.shape[0]

    def step(tap, _):
        slot = lax.rem(tap, slots)
        pltpu.make_async_copy(w.at[:, tap], ring.at[slot], rsem.at[slot]).wait()
        one(tap, jnp.concatenate([ring[slot, j] for j in range(4)], axis=-1))

        @pl.when(tap + slots < 9)
        def _():
            pltpu.make_async_copy(w.at[:, tap + slots], ring.at[slot], rsem.at[slot]).start()

        return 0

    lax.fori_loop(t0, t1, step, 0)


def ring_start(w, ring, rsem):
    for j in range(ring.shape[0]):
        pltpu.make_async_copy(w.at[:, j], ring.at[j], rsem.at[j]).start()


def backward_kernel(nz, width, *refs):
    hbm, refs = refs[:BIG], refs[BIG:]
    w_in, w_out = refs[:2]
    (st0, st1, st2, rows, ca, cb, ra, rb, ha, hb, dt_all, cap_all, emb_all, w_emb, w_cap, temb) = refs[2:18]
    output, image_grad, s_in, s_out, s_small, g_temb, g_cap, g_wemb, g_wcap, g_aff = refs[18:28]
    refs = refs[28:]
    big, refs = refs[:BIG], refs[BIG:]
    bufs = [dict(zip(Reducer.NAMES, refs[8 * a : 8 * a + 8])) for a in range(3)]
    (bsem, gsend, grecv, msend, mrecv, ring, rsem, a3, g3, gt, acc, ng, pre_grad, res_grad,
     mine, every, na, nb, pa, pb, tg_s, tg_r, mod_s, mod_r,
     gc_s, gc_r, pe_s, pe_r, gs_s, gs_r, ps_s, ps_r, aff_s, aff_r) = refs[24:]
    n_sp = 2 * nz
    at = Place()
    line = [at.rp(k, n_sp) for k in range(1, n_sp)]
    grid = img_peers(at)
    greet(line + grid)
    loads = []
    for j in range(BIG):
        cp = pltpu.make_async_copy(hbm[j], big[j], bsem.at[j])
        cp.start()
        loads.append(cp)
    od, dkv, w_small, res, cot, normed, act1, hidden, act0, x = big
    ring_start(w_out, ring, rsem)
    mail = Mail(msend, mrecv)
    red = Reducer(at, nz, [(s_out, bufs[0]), (s_small, bufs[1]), (s_in, bufs[2])], gsend, grecv)
    px, c = res.shape
    height = px // width
    members = px * n_sp * (c // GROUPS)
    d = c // HEADS
    cols = 3 * c // n_sp

    def publish(j, rows01, edges):
        out = []
        for ref, above, below in edges:
            out.append(mail.send(ref.at[px - width :], above, line[0]))
            out.append(mail.send(ref.at[:width], below, line[-1]))
        mine[j] = jnp.zeros((8, c), F32)
        mine[j, 0:1] = rows01[0]
        mine[j, 1:2] = rows01[1]
        for dev in line:
            out.append(mail.send(mine.at[j], every.at[j, at.s], dev))
        every[j, at.s] = mine[j]
        return out

    for j in range(6):
        loads[j].wait()
    att = jnp.concatenate([od[h][:, :d] for h in range(HEADS)], axis=1)
    pg = jnp.concatenate(
        [od[h][:, d:] for h in range(HEADS)]
        + [dkv[h][:, :d] for h in range(HEADS)]
        + [dkv[h][:, d:] for h in range(HEADS)],
        axis=1,
    )
    wq, wp = split_small(joined(w_small), n_sp)
    ng[...] = dot(pg, wq, 1, 0)
    center2, inverse2 = combine_stats(st2, px)
    hat = (res[...] - center2) * inverse2
    u = ng[...]
    sums = (jnp.sum(u, axis=0, keepdims=True), jnp.sum(u * hat, axis=0, keepdims=True))
    greeted(n_sp + 2)
    round_2 = publish(2, sums, [(ng, na, nb)])
    gq = dot(pg, normed[...], 0, 0).astype(BF16)
    go = dot(cot[...], att, 0, 0).astype(BF16)
    small = bufs[1]["d"]
    for j in range(n_sp):
        for b in range(4):
            lanes = slice(b * 128, (b + 1) * 128)
            small[j % 2, b, 0, j // 2, :cols] = gq[j * cols : (j + 1) * cols, lanes]
            small[j % 2, b, 0, j // 2, cols:] = go[j * (c // n_sp) : (j + 1) * (c // n_sp), lanes]
    red.add(1, 0, 1)
    output[...] = (res[...] + dot(att, wp, 1, 1)).astype(BF16)

    first = 2 * lax.rem(at.s, nz)
    value = lax.div(at.s, nz)
    halves = []
    for j in range(2):
        blk = dt_all[first + j].astype(F32)
        halves.append(jnp.where(value > 0, blk[:, d:], blk[:, :d]))
    tg_s[...] = jnp.concatenate(halves, axis=1).astype(BF16)
    round_a = [mail.send(tg_s, tg_r.at[at.i], dev) for dev in grid]
    tg_r[at.i] = tg_s[...]

    has_up, has_dn = edge_flags(n_sp, at.s)

    def upstream(j, uu, ua, ub, center, inverse, yy, ya, yb, act, base, keep):
        total = combine_sums(every[j])
        mul = rows[j, 0:1] * rows[j, 2:3]
        back = group_total(total * mul) / members
        s1, s2 = back[0:1, :], back[1:2, :]
        for r in range(height + 2):
            cut = slice((r - 1) * width, r * width)
            top, end = r == 0, r == height + 1
            un = ua[...] if top else ub[...] if end else uu[cut, :]
            yn = ya[...] if top else yb[...] if end else yy[cut, :]
            g = inverse * (un * mul - s1 - (yn - center) * inverse * s2)
            if base:
                g = g + (base[1][...] if top else base[2][...] if end else base[0][cut, :]).astype(F32)
            if top:
                g = g * has_up
            elif end:
                g = g * has_dn
            elif keep is not None:
                keep[cut, :] = g
            shifted(g3, r, width, g.astype(BF16).astype(F32))
            shifted(a3, r, width, act[r * width : (r + 1) * width, :].astype(F32))
        gt[...] = g3[1, width : width + px, :].T
        return total

    def weight_taps(a, t0, t1):
        dst = bufs[a]["d"]

        def one(tap, _):
            i, j = lax.div(tap, 3), lax.rem(tap, 3)
            part = dot(gt[...], a3[j, pl.ds(pl.multiple_of(i * width, width), px), :], 1, 0).astype(BF16)
            r = c // n_sp
            for k in range(n_sp):
                for b in range(4):
                    dst[k % 2, b, tap, k // 2] = part[k * r : (k + 1) * r, b * 128 : (b + 1) * 128]
            return 0

        lax.fori_loop(t0, t1, one, 0)
        red.add(a, t0, t1)

    def input_taps(w):
        def one(tap, wt):
            i, j = lax.div(tap, 3), lax.rem(tap, 3)
            lhs = g3[2 - j, pl.ds(pl.multiple_of((2 - i) * width, width), px), :]
            acc[...] = dot(lhs, wt, 1, 0) + jnp.where(tap > 0, acc[...], 0.0)

        conv_taps(0, 9, w, ring, rsem, one)

    for cp in round_2:
        cp.wait_recv()
    loads[6].wait()
    t2 = upstream(2, ng, na, nb, center2, inverse2, res, ra, rb, act1, (cot, ca, cb), res_grad)
    red.run(1, 0)
    for tap in (0, 3, 6):
        weight_taps(0, tap, tap + 3)
    red.run(2, 0)
    input_taps(w_out)
    ring_start(w_in, ring, rsem)
    for j in range(7, BIG):
        loads[j].wait()
    center1, inverse1 = combine_stats(st1, px)
    hat = (hidden[...] - center1) * inverse1
    gain1, bias1, fac1 = rows[1, 0:1], rows[1, 1:2], rows[1, 2:3]
    v = acc[...] * silu_slope(hat * (gain1 * fac1) + (bias1 * fac1 + rows[1, 3:4]))
    pre_grad[...] = v
    sums = (jnp.sum(v, axis=0, keepdims=True), jnp.sum(v * hat, axis=0, keepdims=True))
    round_1 = publish(1, sums, [(pre_grad, pa, pb)])
    red.run(1, 1, 2, 3)
    red.run(3, 0)

    exact = lambda a, b, ca_, cb_: lax.dot_general(
        a, b, (((ca_,), (cb_,)), ((), ())), preferred_element_type=F32, precision=PRECISE
    )
    tokens = tg_s.shape[0]
    share = tokens // n_sp
    for cp in round_a:
        cp.wait_recv()
    flat_tg = tg_r[...].reshape(4 * tokens, 128)
    g_wcap[...] = dot(cap_all[...].reshape(4 * tokens, cap_all.shape[2]), flat_tg, 0, 0)
    gc_s[...] = dot(flat_tg, w_cap[...], 1, 1).astype(BF16).reshape(gc_s.shape)
    round_b = []
    for dev in line:
        cut = pl.ds(pl.multiple_of(dev[1] * share, share), share)
        round_b.append(mail.send(gc_s.at[:, cut, :], gc_r.at[at.s], dev))
    gc_r[at.s] = gc_s[:, pl.ds(pl.multiple_of(at.s * share, share), share), :]

    for cp in round_1:
        cp.wait_recv()
    t1 = upstream(1, pre_grad, pa, pb, center1, inverse1, hidden, ha, hb, act0, None, None)
    mod = jnp.concatenate([t1[1:2] * gain1 + t1[0:1] * bias1, t1[0:1]], axis=1)
    for j in range(n_sp):
        mod_s[j] = jnp.broadcast_to(mod[:, j * 128 : (j + 1) * 128], (8, 128))
    round_m = [mail.send(mod_s.at[at.s], mod_r.at[at.i], dev) for dev in grid]
    mod_r[at.i] = mod_s[at.s]
    red.run(2, 1)
    weight_taps(2, 0, 3)
    red.run(2, 2)
    weight_taps(2, 3, 6)
    red.run(2, 3)
    weight_taps(2, 6, 9)
    input_taps(w_in)

    center0, inverse0 = combine_stats(st0, px)
    hat = (x[...].astype(F32) - center0) * inverse0
    gain0 = rows[0, 0:1]
    v = acc[...] * silu_slope(hat * gain0 + rows[0, 1:2])
    acc[...] = v
    sums = (jnp.sum(v, axis=0, keepdims=True), jnp.sum(v * hat, axis=0, keepdims=True))
    round_0 = publish(0, sums, [])
    red.run(1, 4, 5, 6)
    red.run(4, 0)
    for cp in round_m:
        cp.wait_recv()
    mods = jnp.concatenate([mod_r[j][0:1] for j in range(4)] + [jnp.zeros((4, 128), F32)])
    emb_t = emb_all[...].T
    g_wemb[...] = sum(emb_t[:, j : j + 1] * mods[j : j + 1] for j in range(4))
    pe_s[...] = exact(mods, w_emb[...].astype(F32), 1, 1)
    round_p = [mail.send(pe_s, pe_r.at[at.s], dev) for dev in line]
    pe_r[at.s] = pe_s[...]
    for cp in round_0:
        cp.wait_recv()
    t0 = combine_sums(every[0])
    zero = jnp.zeros((2, c), F32)
    aff = jnp.concatenate([t0[1:2], t1[1:2] * fac1, t2[1:2], t0[0:1], t1[0:1] * fac1, t2[0:1], zero])
    for j in range(4):
        aff_s[j] = aff[:, j * 128 : (j + 1) * 128]
    round_e = [mail.send(aff_s.at[dev[0]], aff_r.at[at.i], dev) for dev in grid]
    aff_r[at.i] = aff_s[at.i]
    total = group_total(t0 * gain0) / members
    image_grad[...] = res_grad[...] + inverse0 * (acc[...] * gain0 - total[0:1] - hat * total[1:2])
    for g in (1, 2, 3):
        red.run(3, g)
        red.run(2, g + 3)
    for cp in round_b + round_p:
        cp.wait_recv()
    gc = gc_r[0].astype(F32)
    pe = pe_r[0]
    for j in range(1, n_sp):
        gc = gc + gc_r[j].astype(F32)
        pe = pe + pe_r[j]
    gs_s[...] = gc
    for j in range(4):
        ps_s[j] = jnp.broadcast_to(pe[j : j + 1], pe.shape)
    round_c = []
    for dev in grid:
        round_c.append(mail.send(gs_s.at[dev[0]], gs_r.at[at.i], dev))
        round_c.append(mail.send(ps_s.at[dev[0]], ps_r.at[at.i], dev))
    gs_r[at.i] = gs_s[at.i]
    ps_r[at.i] = ps_s[at.i]
    red.run(4, 1, 2, 3)
    red.run(3, 4, 5, 6)
    red.run(4, 4, 5, 6)
    red.finish()
    for cp in round_c + round_e:
        cp.wait_recv()
    g_cap[...] = jnp.concatenate([gs_r[j] for j in range(4)], axis=1)
    g_temb[...] = jnp.concatenate([ps_r[j] for j in range(4)], axis=1) * silu_slope(temb[...].astype(F32))
    g_aff[...] = aff_r[0] + aff_r[1] + aff_r[2] + aff_r[3]
    for cp in mail.sent:
        cp.wait_send()


def backward_call(big, w_in, w_out, small, nz, width, cid):
    px, c = big[3].shape
    n_sp = 2 * nz
    padded = px + 2 * width
    r = c // n_sp
    rs = big[2].shape[1] // n_sp
    dt_all, cap_all = small[10], small[11]
    tokens = dt_all.shape[1]
    e = cap_all.shape[2]
    share = tokens // n_sp
    outs = [
        ((px, c), BF16), ((px, c), F32), ((9, r, 128), F32), ((9, r, 128), F32), ((1, rs, 128), F32),
        ((8, 4 * e), F32), ((share, 4 * e), F32), ((e, 128), F32), ((e, 128), F32), ((8, 128), F32),
    ]
    vm = pltpu.VMEM
    return pl.pallas_call(
        functools.partial(backward_kernel, nz, width),
        out_shape=[jax.ShapeDtypeStruct(s, ty) for s, ty in outs],
        in_specs=[ANY] * (len(big) + 2) + [VM] * len(small),
        out_specs=[VM] * len(outs),
        scratch_shapes=[vm(v.shape, v.dtype) for v in big]
        + Reducer.buffers(nz, 9, r) + Reducer.buffers(nz, 1, rs) + Reducer.buffers(nz, 9, r)
        + [
            pltpu.SemaphoreType.DMA((len(big),)),
            pltpu.SemaphoreType.DMA((BACK_GROUPS, 4 + nz)),
            pltpu.SemaphoreType.DMA((BACK_GROUPS, 4 + nz)),
            pltpu.SemaphoreType.DMA((BACK_MAIL,)),
            pltpu.SemaphoreType.DMA((BACK_MAIL,)),
            vm((3, 4, c, 128), BF16),
            pltpu.SemaphoreType.DMA((3,)),
            vm((3, padded, c), BF16), vm((3, padded, c), BF16), vm((c, px), BF16),
            vm((px, c), F32), vm((px, c), F32), vm((px, c), F32), vm((px, c), F32),
            vm((3, 8, c), F32), vm((3, n_sp, 8, c), F32),
            vm((width, c), F32), vm((width, c), F32), vm((width, c), F32), vm((width, c), F32),
            vm((tokens, 128), BF16), vm((4, tokens, 128), BF16),
            vm((n_sp, 8, 128), F32), vm((4, 8, 128), F32),
            vm((4, tokens, e), BF16), vm((n_sp, 4, share, e), BF16),
            vm((8, e), F32), vm((n_sp, 8, e), F32),
            vm((4, share, e), F32), vm((4, share, e), F32),
            vm((4, 8, e), F32), vm((4, 8, e), F32),
            vm((4, 8, 128), F32), vm((4, 8, 128), F32),
        ],
        compiler_params=params(cid),
        name="backward",
    )(*big, w_in, w_out, *small)


def emit_kernel(cut, *refs):
    ins, outs, mids, loads, stores = refs[:10], refs[10:22], refs[22:31], refs[31], refs[32]
    output, image, s_in, s_out, s_small, g_temb, g_cap, g_wemb, g_wcap, g_aff = ins
    pairs = [
        (output, outs[0]), (image, outs[1]), (g_cap, outs[3]), (s_in, outs[4]), (s_out, outs[5]), (g_wemb, outs[6]),
        (s_small.at[0, :cut], outs[7]), (g_wcap, outs[8]), (s_small.at[0, cut:], outs[9]),
    ]
    copies = [pltpu.make_async_copy(src, mid, loads.at[j]) for j, ((src, _), mid) in enumerate(zip(pairs, mids))]
    for cp in copies:
        cp.start()
    backs = []
    for j, cp in enumerate(copies):
        cp.wait()
        backs.append(pltpu.make_async_copy(mids[j], pairs[j][1], stores.at[j]))
        backs[-1].start()
    outs[2][...] = g_temb[0:1, :]
    outs[10][...] = g_aff[0:3, :]
    outs[11][...] = g_aff[3:6, :]
    for cp in backs:
        cp.wait()


def emit_call(parts, cut):
    output, image, s_in, s_out, s_small, g_temb, g_cap, g_wemb, g_wcap, g_aff = parts
    rest = s_small.shape[1] - cut
    like = lambda v: jax.ShapeDtypeStruct(v.shape, v.dtype)
    f32 = lambda *s: jax.ShapeDtypeStruct(s, F32)
    shapes = [
        like(output), like(image), f32(1, g_temb.shape[1]), like(g_cap), like(s_in), like(s_out), like(g_wemb),
        f32(cut, 128), like(g_wcap), f32(rest, 128), f32(3, 128), f32(3, 128),
    ]
    in_specs = [ANY] * 10
    in_specs[5] = in_specs[9] = VM
    out_specs = [ANY] * 12
    out_specs[2] = out_specs[10] = out_specs[11] = VM
    return pl.pallas_call(
        functools.partial(emit_kernel, cut),
        out_shape=shapes,
        in_specs=in_specs,
        out_specs=out_specs,
        scratch_shapes=[pltpu.VMEM(shapes[j].shape, shapes[j].dtype) for j in (0, 1, 3, 4, 5, 6, 7, 8, 9)]
        + [pltpu.SemaphoreType.DMA((9,)), pltpu.SemaphoreType.DMA((9,))],
        compiler_params=params(),
        name="emit",
    )(*parts)


def fast_body(
    image_in, time_embed, caption, caption_mask, conv_in, conv_out, embed_proj, qkv_proj,
    caption_proj, out_proj, norm_gains, norm_biases, cotangent,
):
    n, height, width, c = image_in.shape
    n_sp = lax.axis_size("sp")
    nz = n_sp // 2
    px = height * width
    x = image_in.reshape(px, c)
    cot = cotangent.reshape(px, c)

    flat = lambda w: w.transpose(1, 2, 3, 0).reshape(9, w.shape[3], w.shape[0])
    (w_in, w_out, w_small, hidden, act0, res, act1, normed, kv, qg,
     st0, st1, st2, rows, ca, cb, ra, rb, ha, hb, kv_all, cap_all, emb_all) = forward_call(
        [flat(conv_in), flat(conv_out)], x, cot, time_embed, caption[0], embed_proj, caption_proj,
        norm_gains, norm_biases, qkv_proj.T, out_proj.T, nz, width, 0,
    )
    w_small = w_small.reshape(4, -1, 128)
    od, dkv, dt_all = attention_call(kv, qg, kv_all, caption_mask, 1)

    parts = backward_call(
        [od, dkv, w_small, res, cot, normed, act1, hidden, act0, x], w_in, w_out,
        [st0, st1, st2, rows, ca, cb, ra, rb, ha, hb, dt_all, cap_all, emb_all, embed_proj, caption_proj, time_embed],
        nz, width, 2,
    )
    output, image, g_temb, g_cap, s_in, s_out, g_wemb, g_qkv, g_wcap, g_out, g_gains, g_biases = emit_call(
        parts, qkv_proj.shape[1]
    )
    unflat = lambda g: g.reshape(3, 3, g.shape[1], 128).transpose(3, 0, 1, 2)
    return (
        output.reshape(image_in.shape), image.reshape(image_in.shape), g_temb, g_cap[None], unflat(s_in), unflat(s_out),
        g_wemb, g_qkv.T, g_wcap, g_out.T, g_gains, g_biases,
    )


def body(*args):
    image_in, qkv_proj = args[0], args[7]
    n, height, width, c = image_in.shape
    n_img, n_sp = lax.axis_size("img"), lax.axis_size("sp")
    fits = n == 1 and n_img == 4 and n_sp == HEADS and c == 512 and width == 64
    return fast_body(*args) if fits else plain_body(*args)


def solution(mesh):
    rows = P("img", "sp", None, None)
    kernel = P("img", None, None, "sp")
    flat = P("img", "sp")
    return jax.shard_map(
        body,
        mesh=mesh,
        in_specs=(
            rows, P("img", None), P("img", None, None), P("img", None), kernel, kernel,
            flat, flat, flat, flat, P(None, "img"), P(None, "img"), rows,
        ),
        out_specs=(
            rows, rows, P("img", None), P("img", "sp", None), kernel, kernel,
            flat, flat, flat, flat, P(None, "img"), P(None, "img"),
        ),
        check_vma=False,
    )
```

```python
import functools

import jax
import jax.numpy as jnp
from jax import lax
from jax.experimental import pallas as pl
from jax.experimental.pallas import tpu as pltpu
from jax.sharding import PartitionSpec as P

HEADS = 8
GROUPS = 32
EPSILON = 1e-05
PRECISE = lax.Precision.HIGHEST
MASKED = -1e30
BF16 = jnp.bfloat16
F32 = jnp.float32
MESH = pl.DeviceIdType.MESH
VMEM_BYTES = 60 * 1024 * 1024


def dot(a, b, ca, cb):
    return lax.dot_general(a, b, (((ca,), (cb,)), ((), ())), preferred_element_type=F32)


def silu(v):
    return v * jax.nn.sigmoid(v)


def silu_slope(v):
    s = jax.nn.sigmoid(v)
    return s * (1.0 + v * (1.0 - s))


def gather(x, axis, dim):
    return lax.all_gather(x, axis, axis=dim, tiled=True)


def scatter_sum(x, axis, dim):
    return lax.psum_scatter(x, axis, scatter_dimension=dim, tiled=True)


def swap(x, axis, split, concat):
    return lax.all_to_all(x, axis, split, concat, tiled=True)


def halo(x):
    count = lax.axis_size("sp")
    above = lax.ppermute(x[:, -1:], "sp", [(i, i + 1) for i in range(count - 1)])
    below = lax.ppermute(x[:, :1], "sp", [(i + 1, i) for i in range(count - 1)])
    return above, below


def group_sum(v):
    c = v.shape[-1]
    g = v.reshape(v.shape[:-1] + (GROUPS, c // GROUPS))
    s = jnp.sum(g, axis=-1, keepdims=True)
    return jnp.broadcast_to(s, g.shape).reshape(v.shape)


def norm_stats(x):
    n, r, w, c = x.shape
    cells = r * w * (c // GROUPS)
    parts = lax.axis_size("sp")
    mean = group_sum(jnp.sum(x, axis=(1, 2))) / cells
    dev = group_sum(jnp.sum(jnp.square(x - mean[:, None, None, :]), axis=(1, 2)))
    both = lax.all_gather(jnp.stack([mean, dev]), "sp")
    means, devs = both[:, 0], both[:, 1]
    center = jnp.mean(means, axis=0)
    var = (jnp.sum(devs, axis=0) + cells * jnp.sum(jnp.square(means - center), axis=0)) / (
        cells * parts
    )
    return center, lax.rsqrt(var + EPSILON)


def hat_of(x, center, inverse):
    return (x - center[:, None, None, :]) * inverse[:, None, None, :]


def norm_back(u, hat, inverse, gain, sum_u, sum_uh, members):
    s1 = group_sum(sum_u * gain) / members
    s2 = group_sum(sum_uh * gain) / members
    return inverse[:, None, None, :] * (
        u * gain - s1[:, None, None, :] - hat * s2[:, None, None, :]
    )


def pad_cols(x):
    return jnp.pad(x, ((0, 0), (0, 0), (1, 1), (0, 0)))


def conv(padded, weight_t, transposed):
    n, rp, wp, c = padded.shape
    r, w = rp - 2, wp - 2
    total = None
    for i in range(3):
        for j in range(3):
            a = padded[:, i : i + r, j : j + w].reshape(n * r * w, c)
            part = dot(a, weight_t[2 - i, 2 - j], 1, 0) if transposed else dot(a, weight_t[i, j], 1, 1)
            total = part if total is None else total + part
    return total.reshape(n, r, w, -1)


def conv_grad(padded, g):
    n, r, w, c = g.shape
    gf = g.reshape(n * r * w, c)
    rows = []
    for i in range(3):
        for j in range(3):
            a = padded[:, i : i + r, j : j + w].reshape(n * r * w, -1)
            rows.append(dot(gf, a, 0, 0))
    return jnp.stack(rows).reshape(3, 3, c, -1)


def to_pairs(x, images):
    n, px, h, d = x.shape
    y = x.transpose(0, 2, 1, 3).reshape(n * h, px, d)
    return swap(y, "sp", 0, 1)


def from_pairs(x, images):
    y = swap(x, "sp", 1, 0)
    return y.reshape(images, HEADS, y.shape[1], y.shape[2]).transpose(0, 2, 1, 3)


def attention_plain(q, k, v, g, tk, tv, keep, scale):
    p, length, d = q.shape
    block = min(512, length)
    keys = jnp.concatenate([tk, k], axis=1)
    values = jnp.concatenate([tv, v], axis=1)
    text = tk.shape[1]
    keep_all = jnp.concatenate([keep, jnp.ones((p, length), bool)], axis=1)

    def step(carry, blk):
        dk, dv = carry
        qb, gb = blk
        s = jnp.einsum("pqd,pkd->pqk", qb, keys, preferred_element_type=F32) * scale
        s = jnp.where(keep_all[:, None, :], s, MASKED)
        peak = jnp.max(s, axis=-1, keepdims=True)
        e = jnp.exp(s - peak)
        prob = e / jnp.sum(e, axis=-1, keepdims=True)
        pb = prob.astype(BF16)
        o = jnp.einsum("pqk,pkd->pqd", pb, values, preferred_element_type=F32)
        row = jnp.sum(o * gb.astype(F32), axis=-1, keepdims=True)
        dp = jnp.einsum("pqd,pkd->pqk", gb, values, preferred_element_type=F32)
        ds = (prob * (dp - row)).astype(BF16)
        dq = jnp.einsum("pqk,pkd->pqd", ds, keys, preferred_element_type=F32) * scale
        dk = dk + jnp.einsum("pqk,pqd->pkd", ds, qb, preferred_element_type=F32)
        dv = dv + jnp.einsum("pqk,pqd->pkd", pb, gb, preferred_element_type=F32)
        return (dk, dv), (o.astype(BF16), dq.astype(BF16))

    zeros = jnp.zeros((p, text + length, d), F32)
    cut = lambda t: t.reshape(p, length // block, block, d).swapaxes(0, 1)
    (dk, dv), (o, dq) = lax.scan(step, (zeros, zeros), (cut(q), cut(g)))
    join = lambda t: t.swapaxes(0, 1).reshape(p, length, d)
    dk = (dk * scale).astype(BF16)
    dv = dv.astype(BF16)
    return join(o), join(dq), dk[:, text:], dv[:, text:], dk[:, :text], dv[:, :text]


def plain_body(
    image_in, time_embed, caption, caption_mask, conv_in, conv_out, embed_proj, qkv_proj,
    caption_proj, out_proj, norm_gains, norm_biases, cotangent,
):
    n, rows, width, chans = image_in.shape
    n_img, n_sp = lax.axis_size("img"), lax.axis_size("sp")
    img, sp = lax.axis_index("img"), lax.axis_index("sp")
    px = rows * width
    members = px * n_sp * (chans // GROUPS)
    d = chans // HEADS
    scale = d ** -0.5
    pairs = n * HEADS // n_sp

    def whole(w):
        w = gather(w, "img", w.ndim - 1)
        return gather(w, "sp", w.ndim - 2)

    w_in = whole(conv_in.transpose(1, 2, 3, 0))
    w_out = whole(conv_out.transpose(1, 2, 3, 0))
    w_qkv = whole(qkv_proj.T)
    w_proj = whole(out_proj.T)
    affine = gather(jnp.concatenate([norm_gains, norm_biases]), "img", 1).astype(F32)
    gains, biases = affine[:3], affine[3:]

    embedded = silu(time_embed.astype(F32)).astype(BF16)
    emb_all = swap(embedded, "img", 1, 0)
    mod = scatter_sum(jnp.dot(emb_all, embed_proj, preferred_element_type=F32), "img", 0)
    mod = gather(mod, "sp", 1)
    scale_term, shift_term = mod[:, :chans], mod[:, chans:]
    cap_all = swap(caption, "img", 2, 0)
    cap_flat = cap_all.reshape(-1, cap_all.shape[2])
    kv = jnp.dot(cap_flat, caption_proj, preferred_element_type=F32)
    kv = scatter_sum(kv.reshape(cap_all.shape[0], cap_all.shape[1], -1), "img", 0).astype(BF16)
    kv = gather(kv, "sp", 2)
    text = kv.shape[1]
    kv_heads = kv.reshape(n, text, 2, HEADS, d).transpose(2, 0, 3, 1, 4).reshape(2, n * HEADS, text, d)
    mine = lax.dynamic_slice_in_dim(kv_heads, sp * pairs, pairs, 1)
    keep = jnp.repeat(caption_mask > 0, HEADS, axis=0)
    keep = lax.dynamic_slice_in_dim(keep, sp * pairs, pairs, 0)

    image_f = image_in.astype(F32)
    c0, i0 = norm_stats(image_f)
    hat0 = hat_of(image_f, c0, i0)
    first = hat0 * gains[0] + biases[0]
    act0 = silu(first).astype(BF16)
    above, below = halo(act0)
    pad0 = pad_cols(jnp.concatenate([above, act0, below], axis=1))
    hidden = conv(pad0, w_in, False)
    c1, i1 = norm_stats(hidden)
    hat1 = hat_of(hidden, c1, i1)
    second = hat1 * gains[1] + biases[1]
    pre = second * (1.0 + scale_term[:, None, None, :]) + shift_term[:, None, None, :]
    act1 = silu(pre).astype(BF16)
    above, below = halo(act1)
    pad1 = pad_cols(jnp.concatenate([above, act1, below], axis=1))
    residual = image_f + conv(pad1, w_out, False)
    c2, i2 = norm_stats(residual)
    hat2 = hat_of(residual, c2, i2)
    normed = (hat2 * gains[2] + biases[2]).astype(BF16).reshape(n * px, chans)
    qkv = dot(normed, w_qkv, 1, 1).astype(BF16)
    cot = cotangent.reshape(n * px, chans)
    g_att = dot(cot, w_proj, 1, 0).astype(BF16)
    four = jnp.concatenate([qkv, g_att], axis=1).reshape(n, px, 4, HEADS, d)
    packed = to_pairs(four.transpose(0, 1, 3, 2, 4).reshape(n, px, HEADS, 4 * d), n)
    q, k, v, g = (packed[..., j * d : (j + 1) * d] for j in range(4))
    o, dq, dk, dv, dtk, dtv = attention_plain(q, k, v, g, mine[0], mine[1], keep, scale)
    back = from_pairs(jnp.concatenate([o, dq, dk, dv], axis=-1), n)
    back = back.reshape(n * px, HEADS, 4, d).transpose(0, 2, 1, 3).reshape(n * px, 4 * chans)
    attended, proj_grad = back[:, :chans], back[:, chans:]
    output = residual + dot(attended, w_proj, 1, 1).reshape(image_in.shape)

    grad_out = dot(cot, attended, 0, 0)
    grad_qkv = dot(proj_grad, normed, 0, 0)
    normed_grad = dot(proj_grad, w_qkv, 1, 0).reshape(image_in.shape)

    def sums(u, hat):
        both = jnp.stack([jnp.sum(u, axis=(1, 2)), jnp.sum(u * hat, axis=(1, 2))])
        return lax.psum(both, "sp")

    su2, sh2 = sums(normed_grad, hat2)
    residual_grad = cotangent.astype(F32) + norm_back(
        normed_grad, hat2, i2, gains[2], su2, sh2, members
    )
    g2 = residual_grad.astype(BF16)
    above, below = halo(g2)
    gpad = pad_cols(jnp.concatenate([above, g2, below], axis=1))
    grad_conv_out = conv_grad(pad1, g2)
    pre_grad = conv(gpad, w_out, True) * silu_slope(pre)
    sa, sb = sums(pre_grad, hat1)
    fac = 1.0 + scale_term
    shift_grad = sa
    scale_grad = sb * gains[1] + sa * biases[1]
    u1 = pre_grad * fac[:, None, None, :]
    su1, sh1 = sa * fac, sb * fac
    g1 = norm_back(u1, hat1, i1, gains[1], su1, sh1, members).astype(BF16)
    above, below = halo(g1)
    gpad = pad_cols(jnp.concatenate([above, g1, below], axis=1))
    grad_conv_in = conv_grad(pad0, g1)
    u0 = conv(gpad, w_in, True) * silu_slope(first)
    su0, sh0 = sums(u0, hat0)
    grad_image = residual_grad + norm_back(u0, hat0, i0, gains[0], su0, sh0, members)

    mod_grad = jnp.concatenate([scale_grad, shift_grad], axis=1)
    cols = embed_proj.shape[1]
    mod_all = gather(mod_grad, "img", 0)
    mod_cols = lax.dynamic_slice_in_dim(mod_all, sp * cols, cols, 1)
    grad_embed_proj = jnp.einsum("ne,nd->ed", emb_all.astype(F32), mod_cols, precision=PRECISE)
    part = jnp.einsum("nd,ed->ne", mod_cols, embed_proj.astype(F32), precision=PRECISE)
    part = swap(lax.psum(part, "sp"), "img", 0, 1)
    grad_embed = part * silu_slope(time_embed.astype(F32))

    tg = gather(jnp.stack([dtk, dtv]), "sp", 1).reshape(2, n, HEADS, text, d)
    tg = tg.transpose(1, 3, 0, 2, 4).reshape(n, text, 2 * chans)
    cols = caption_proj.shape[1]
    tg = gather(lax.dynamic_slice_in_dim(tg, sp * cols, cols, 2), "img", 0).reshape(-1, cols)
    grad_caption_proj = dot(cap_flat, tg, 0, 0)
    gc = dot(tg, caption_proj, 1, 1).reshape(cap_all.shape)
    gc = scatter_sum(gc, "sp", 1)
    grad_caption = swap(gc, "img", 0, 2)

    grads = jnp.concatenate(
        [jnp.sum(t, axis=0)[None] for t in (sh0, sh1, sh2, su0, su1, su2)]
    )
    grads = scatter_sum(grads, "img", 1)

    def shared(w):
        w = scatter_sum(w, "sp", w.ndim - 2)
        return scatter_sum(w, "img", w.ndim - 1)

    return (
        output.astype(BF16),
        grad_image,
        grad_embed,
        grad_caption,
        shared(grad_conv_in).transpose(3, 0, 1, 2),
        shared(grad_conv_out).transpose(3, 0, 1, 2),
        grad_embed_proj,
        shared(grad_qkv).T,
        grad_caption_proj,
        shared(grad_out).T,
        grads[:3],
        grads[3:],
    )


class Place:
    def __init__(self):
        self.i = lax.axis_index("img")
        self.s = lax.axis_index("sp")
        self.z = lax.div(self.s, 2)
        self.c = lax.rem(self.s, 2)
        x = lax.rem(self.i, 2)
        y = lax.div(self.i, 2)
        self.ix = self.i + 1 - 2 * x
        self.iy = self.i + 2 - 4 * y
        self.id = 3 - self.i
        self.sib = (self.i, self.s + 1 - 2 * self.c)
        self.xn = (self.ix, self.s)
        self.yn = (self.iy, self.s)

    def zp(self, k, nz):
        return (self.i, 2 * lax.rem(self.z + k, nz) + self.c)

    def rp(self, k, n_sp):
        return (self.i, lax.rem(self.s + k, n_sp))


def greet(peers):
    bar = pltpu.get_barrier_semaphore()
    for p in peers:
        pl.semaphore_signal(bar, inc=1, device_id=p, device_id_type=MESH)


def greeted(count):
    pl.semaphore_wait(pltpu.get_barrier_semaphore(), count)


def remote(src, dst, ssem, rsem, dev):
    cp = pltpu.make_async_remote_copy(
        src_ref=src, dst_ref=dst, send_sem=ssem, recv_sem=rsem, device_id=dev, device_id_type=MESH
    )
    cp.start()
    return cp


def params(cid=None, grid=0):
    extra = {} if cid is None else {"collective_id": cid, "has_side_effects": True}
    if grid:
        extra["dimension_semantics"] = ("arbitrary",) * grid
    return pltpu.CompilerParams(vmem_limit_bytes=VMEM_BYTES, **extra)


ANY = pl.BlockSpec(memory_space=pl.ANY)
VM = pl.BlockSpec(memory_space=pltpu.VMEM)
def channel_stats(mine, v):
    mean = jnp.sum(v, axis=0, keepdims=True) / v.shape[0]
    dev = v - mean
    mine[0:1, :] = mean
    mine[1:2, :] = jnp.sum(dev * dev, axis=0, keepdims=True)


def group_total(rows):
    c = rows.shape[1]
    size = c // GROUPS
    a = lax.broadcasted_iota(jnp.int32, (128, 128), 0)
    b = lax.broadcasted_iota(jnp.int32, (128, 128), 1)
    same = jnp.where(lax.bitwise_xor(a, b) < size, 1.0, 0.0).astype(BF16)
    high = rows.astype(BF16)
    rest = rows - high.astype(F32)
    mid = rest.astype(BF16)
    low = (rest - mid.astype(F32)).astype(BF16)
    parts = jnp.concatenate([high.astype(F32), mid.astype(F32), low.astype(F32)]).astype(BF16)
    total = jnp.concatenate(
        [dot(parts[:, j * 128 : (j + 1) * 128], same, 1, 0) for j in range(c // 128)], axis=1
    )
    n = rows.shape[0]
    return total[:n] + total[n : 2 * n] + total[2 * n :]


def combine_stats(every, px):
    n_sp, _, c = every.shape
    size = c // GROUPS
    means = [every[j, 0:1, :] for j in range(n_sp)]
    center_c = sum(means) / n_sp
    dev = sum(every[j, 1:2, :] for j in range(n_sp))
    dev = dev + px * sum((m - center_c) * (m - center_c) for m in means)
    center = group_total(jnp.broadcast_to(center_c, (8, c)))[0:1] / size
    off = center_c - center
    dev = dev + (px * n_sp) * (off * off)
    var = group_total(jnp.broadcast_to(dev, (8, c)))[0:1] / (px * n_sp * size)
    return center, lax.rsqrt(var + EPSILON)


def combine_sums(every):
    n_sp = every.shape[0]
    total = every[0]
    for j in range(1, n_sp):
        total = total + every[j]
    return total


def edge_flags(n_sp, s):
    return jnp.where(s > 0, 1.0, 0.0), jnp.where(s < n_sp - 1, 1.0, 0.0)


def shifted(dst, row, width, block):
    col = lax.broadcasted_iota(jnp.int32, block.shape, 0)
    r = slice(row * width, (row + 1) * width)
    dst[1, r, :] = block.astype(BF16)
    dst[0, r, :] = jnp.where(col == 0, 0.0, pltpu.roll(block, 1, 0)).astype(BF16)
    dst[2, r, :] = jnp.where(col == width - 1, 0.0, pltpu.roll(block, width - 1, 0)).astype(BF16)


def joined(w_ref, *lead):
    return jnp.concatenate([w_ref[(j,) + lead] for j in range(4)], axis=-1)


def three_parts(v):
    a = v.astype(BF16).astype(F32)
    b = (v - a).astype(BF16).astype(F32)
    return a, b, v - a - b


AHEAD = 2


def attention_kernel(
    n_sp, BK, kv, qin, gin, text, keep, of, qf, dkv, dt,
    kv_r, q_r, g_r, q_s, o_s, dq_o, dkv_s, dt_s, k_s, v_s, s_s, e_s, g_s, dq_s, peak_s, lsem, ssem, rsem,
):
    at = Place()
    nz = n_sp // 2
    px = kv.shape[1]
    L, T = n_sp * px, text.shape[1]
    d = kv.shape[2] // 2
    BQ = px // 2
    line = [at.rp(k, n_sp) for k in range(1, n_sp)]
    greet(line)
    own = [
        pltpu.make_async_copy(kv.at[at.s], kv_r.at[at.s], lsem.at[0]),
        pltpu.make_async_copy(qin.at[at.s], q_r.at[at.s], lsem.at[1]),
        pltpu.make_async_copy(gin, g_r, lsem.at[6]),
    ]
    for cp in own:
        cp.start()
    greeted(n_sp - 1)
    keys = [remote(kv.at[dev[1]], kv_r.at[at.s], ssem.at[0, k + 1], rsem.at[0, k + 1], dev) for k, dev in enumerate(line)]
    odd = lax.rem(at.s, 2)
    pair = lax.div(at.s, 2)
    ones = (lax.broadcasted_iota(jnp.int32, (1, d), 1) < 3).astype(F32).astype(BF16)
    picked = []
    for j in (pair, HEADS // 2 + pair):
        blk = text[j].astype(F32)
        picked.append(jnp.where(odd > 0, blk[:, d:], blk[:, :d]).astype(BF16))
    k_s[0:T, :] = picked[0]
    v_s[0:T, :] = jnp.concatenate([picked[1], jnp.broadcast_to(ones, (T, d))], axis=1)

    def rows_of(o, n=px, start=0):
        return pl.ds(pl.multiple_of(o * px + start, 128), n)

    def take(j):
        rows = rows_of(j, px, T)
        k_s[rows, :] = kv_r[j][:, :d]
        v_s[rows, :] = jnp.concatenate([kv_r[j][:, d:], jnp.broadcast_to(ones, (px, d))], axis=1)

    for cp in own:
        cp.wait()
    take(at.s)
    for k in range(1, n_sp):
        keys[k - 1].wait_recv()
        take(lax.rem(at.s - k + n_sp, n_sp))
    blocks = [(0, T)] + [(T + j * BK, BK) for j in range(L // BK)]
    scale = d ** -0.5

    def query_copy(k):
        return pltpu.make_async_remote_copy(
            src_ref=qin.at[lax.rem(at.s + k, n_sp)], dst_ref=q_r.at[at.s], send_sem=ssem.at[1, k],
            recv_sem=rsem.at[1, k], device_id=(at.i, lax.rem(at.s + k, n_sp)), device_id_type=MESH,
        )

    def back_copy(j, k, src, dst, o):
        return pltpu.make_async_remote_copy(
            src_ref=src.at[o], dst_ref=dst.at[at.s], send_sem=ssem.at[j, k], recv_sem=rsem.at[j, k],
            device_id=(at.i, o), device_id_type=MESH,
        )

    def scores(q, slot, st, n, peak):
        s = dot(q, k_s[st : st + n, :], 1, 1)
        if st == 0:
            s = jnp.where(keep[...] > 0, s, MASKED)
        s_s[slot, :, st : st + n] = s
        for j in range(n // 128):
            piece = s[:, 128 * j : 128 * j + 128]
            peak = piece if peak is None else jnp.maximum(peak, piece)
        return peak

    def query(o, part):
        return q_r[o][:, part * d : (part + 1) * d]

    def forward(o, part, o_next):
        nxt = query(o_next, 1 - part)
        g = g_r[o][:, part * d : (part + 1) * d]
        rows = rows_of(o, BQ, part * BQ)
        q_s[rows, :] = query(o, part)
        top = jnp.max(peak_s[part], axis=1, keepdims=True)
        out = jnp.zeros((BQ, 2 * d), F32)
        peak = None
        for st, n in blocks:
            peak = scores(nxt, 1 - part, st, n, peak)
            e = jnp.exp(s_s[part, :, st : st + n] - top).astype(BF16)
            e_s[rows, st : st + n] = e
            out = out + dot(e, v_s[st : st + n, :], 1, 0)
        peak_s[1 - part] = peak
        inverse = 1.0 / out[:, d : d + 1]
        out = out[:, :d] * inverse
        g = g.astype(F32) * inverse
        row = jnp.sum(out * g, axis=1, keepdims=True)
        lane = lax.broadcasted_iota(jnp.int32, (BQ, d), 1)
        extra = jnp.zeros((BQ, d), F32)
        for j, piece in enumerate(three_parts(-row)):
            extra = jnp.where(lane == j, piece, extra)
        g_s[rows, :] = jnp.concatenate([g, extra], axis=1).astype(BF16)
        o_s[o, :, part * d : (part + 1) * d] = out.astype(BF16)

    peak = None
    for st, n in blocks:
        peak = scores(query(at.s, 0), 0, st, n, peak)
    peak_s[0] = peak

    for k in range(1, AHEAD):
        query_copy(k).start()

    def owner(k, _):
        o = lax.rem(at.s - k + n_sp, n_sp)

        @pl.when(k + AHEAD < n_sp)
        def _():
            query_copy(k + AHEAD).start()

        forward(o, 0, o)

        @pl.when(k + 1 < n_sp)
        def _():
            query_copy(k + 1).wait_recv()

        forward(o, 1, lax.rem(at.s - k - 1 + n_sp, n_sp))

        @pl.when(k > 0)
        def _():
            back_copy(2, k, o_s, of, o).start()

        return 0

    lax.fori_loop(0, n_sp, owner, 0)
    local = [pltpu.make_async_copy(o_s.at[at.s], of.at[at.s], lsem.at[2])]

    def block(o, cols, kc, vc, dk, dv, fresh):
        rows = rows_of(o)
        g, q = g_s[rows, :], q_s[rows, :]
        e = e_s[rows, cols]
        ds = (e.astype(F32) * dot(g, vc, 1, 1)).astype(BF16)
        part = dot(ds, kc, 1, 0)
        dq_s[rows, :] = part if fresh else dq_s[rows, :] + part
        return dk + dot(q.T, ds, 1, 0), dv + dot(g[:, :d].T, e, 1, 0)

    def both(dk, dv):
        return jnp.concatenate([dk, dv], axis=0).astype(BF16).T

    def chunk(cols, n, fresh):
        kc, vc = k_s[cols, :], v_s[cols, :]
        zero = jnp.zeros((d, n), F32)
        dk, dv = lax.fori_loop(
            0, n_sp, lambda o, acc: block(o, cols, kc, vc, acc[0], acc[1], fresh), (zero, zero), unroll=4
        )
        return both(dk, dv)

    def chip_columns(z):
        return pl.ds(pl.multiple_of(T + z * (2 * px), 128), 2 * px)

    dt_s[...] = chunk(pl.ds(0, T), T, True)
    sent = [remote(dt_s, dt.at[at.s], ssem.at[5, k + 1], rsem.at[5, k + 1], dev) for k, dev in enumerate(line)]
    local.append(pltpu.make_async_copy(dt_s, dt.at[at.s], lsem.at[3]))

    def chip(k, _):
        z = lax.rem(at.z + k, nz)
        grads = chunk(chip_columns(z), 2 * px, False)
        for core in range(2):
            o = 2 * z + core
            dkv_s[o] = grads[core * px : (core + 1) * px]
            back_copy(4, lax.rem(o - at.s + n_sp, n_sp), dkv_s, dkv, o).start()
        return 0

    lax.fori_loop(1, nz, chip, 0)
    cols = chip_columns(at.z)
    kc, vc = k_s[cols, :], v_s[cols, :]
    zero = jnp.zeros((d, 2 * px), F32)

    def last(j, acc):
        o = 2 * lax.rem(at.z + 1 + lax.div(j, 2), nz) + lax.rem(j, 2)
        acc = block(o, cols, kc, vc, acc[0], acc[1], False)
        dq = (dq_s[rows_of(o), :] * scale).astype(BF16)
        dq_o[o] = jnp.concatenate([dq[:BQ], dq[BQ:]], axis=1)

        @pl.when(o != at.s)
        def _():
            back_copy(3, lax.rem(o - at.s + n_sp, n_sp), dq_o, qf, o).start()

        return acc

    grads = both(*lax.fori_loop(0, n_sp, last, (zero, zero)))
    for core in range(2):
        dkv_s[2 * at.z + core] = grads[core * px : (core + 1) * px]
    sib = at.sib[1]
    back_copy(4, lax.rem(sib - at.s + n_sp, n_sp), dkv_s, dkv, sib).start()
    local.append(pltpu.make_async_copy(dkv_s.at[at.s], dkv.at[at.s], lsem.at[4]))
    local.append(pltpu.make_async_copy(dq_o.at[at.s], qf.at[at.s], lsem.at[5]))
    for cp in local:
        cp.start()
    for k in range(1, n_sp):
        back_copy(2, k, o_s, of, lax.rem(at.s - k + n_sp, n_sp)).wait()
        o = lax.rem(at.s + k, n_sp)
        back_copy(4, k, dkv_s, dkv, o).wait()
        back_copy(3, k, dq_o, qf, o).wait()
    for k in range(1, n_sp):
        query_copy(k).wait_send()
    for cp in keys:
        cp.wait_send()
    for cp in sent:
        cp.wait()
    for cp in local:
        cp.wait()


def attention_call(kv, qin, gin, text, keep, cid):
    n_sp, px, d2 = kv.shape
    T = text.shape[1]
    L = n_sp * px
    d = d2 // 2
    outs = [(n_sp, px // 2, d2), (n_sp, px // 2, d2), (n_sp, px, d2), (n_sp, T, d2)]
    vm = pltpu.VMEM
    return pl.pallas_call(
        functools.partial(attention_kernel, n_sp, 1024),
        out_shape=[jax.ShapeDtypeStruct(s, BF16) for s in outs],
        in_specs=[ANY, ANY, ANY, VM, VM],
        out_specs=[ANY] * 4,
        scratch_shapes=[
            vm((n_sp, px, d2), BF16), vm((n_sp, px // 2, d2), BF16), vm((n_sp, px // 2, d2), BF16), vm((L, d), BF16),
            vm((n_sp, px // 2, d2), BF16),
            vm((n_sp, px // 2, d2), BF16), vm((n_sp, px, d2), BF16), vm((T, d2), BF16),
            vm((T + L, d), BF16), vm((T + L, d2), BF16), vm((2, px // 2, T + L), F32), vm((L, T + L), BF16),
            vm((L, d2), BF16), vm((L, d), F32), vm((2, px // 2, 128), F32),
            pltpu.SemaphoreType.DMA((7,)),
            pltpu.SemaphoreType.DMA((6, n_sp)),
            pltpu.SemaphoreType.DMA((6, n_sp)),
        ],
        compiler_params=params(cid),
        name="attention",
    )(kv, qin, gin, text, keep)


class Mail:
    def __init__(self, ssem, rsem):
        self.ssem, self.rsem, self.sent = ssem, rsem, []

    def send(self, src, dst, dev):
        j = len(self.sent)
        cp = remote(src, dst, self.ssem.at[j], self.rsem.at[j], dev)
        self.sent.append(cp)
        return cp


class Gather:
    def __init__(self, at, nz, ins, outs, dims, ssem, rsem):
        self.at, self.nz, self.ins, self.outs, self.dims = at, nz, ins, outs, dims
        self.ssem, self.rsem = ssem, rsem
        self.sent, self.kinds = {}, {}
        self.order = sorted(range(1, nz), key=lambda k: min(k, nz - k))

    @staticmethod
    def copies(nz):
        return 3 * nz - 1 + 7 * nz

    def view(self, a, ii, k, core, half=None):
        at, nz, r = self.at, self.nz, self.dims[a][1]
        sp = 2 * lax.rem(at.z - k + nz, nz) + core
        if half is None:
            return self.outs[a].at[ii, :, pl.ds(pl.multiple_of(sp * r, r), r), :]
        h = r // 2
        return self.outs[a].at[ii, :, pl.ds(pl.multiple_of(sp * r + half * h, h), h), :]

    def send(self, a, kind, src, dst, dev):
        j = self.kinds.setdefault(kind, len(self.kinds))
        self.sent[a, kind] = remote(src, dst, self.ssem.at[a, j], self.rsem.at[a, j], dev)

    def forward(self, a, kind, ref, dev):
        self.send(a, kind, ref, ref, dev)

    def near(self, a):
        at = self.at
        own = self.view(a, at.i, 0, at.c)
        self.send(a, ("x", 0), self.ins[a], own, at.xn)
        self.send(a, ("y", 0), self.ins[a], own, at.yn)
        self.send(a, ("s", 0), self.ins[a], own, at.sib)

    def along(self, a, ks):
        for k in ks:
            self.send(a, ("z", k), self.ins[a], self.view(a, self.at.i, 0, self.at.c), self.at.zp(k, self.nz))

    def second(self, a, ks=None):
        at = self.at
        for k in self.order if ks is None else ks:
            self.sent[a, ("z", k)].wait_recv()
            got = self.view(a, at.i, k, at.c)
            self.forward(a, ("x", k), got, at.xn)
            self.forward(a, ("y", k), got, at.yn)
            self.forward(a, ("s", k), got, at.sib)

    def third(self, a):
        at = self.at
        for k in [0] + self.order:
            self.sent[a, ("x", k)].wait_recv()
            self.forward(a, ("da", k), self.view(a, at.ix, k, at.c, 0), at.yn)
            self.forward(a, ("sx", k), self.view(a, at.ix, k, at.c), at.sib)
            self.sent[a, ("y", k)].wait_recv()
            self.forward(a, ("db", k), self.view(a, at.iy, k, at.c, 1), at.xn)
            self.forward(a, ("sy", k), self.view(a, at.iy, k, at.c), at.sib)

    def fourth(self, a):
        at = self.at
        for k in [0] + self.order:
            self.sent[a, ("da", k)].wait_recv()
            self.forward(a, ("sa", k), self.view(a, at.id, k, at.c, 0), at.sib)
            self.sent[a, ("db", k)].wait_recv()
            self.forward(a, ("sb", k), self.view(a, at.id, k, at.c, 1), at.sib)

    def complete(self, a):
        for (b, kind), cp in self.sent.items():
            if b == a and kind[0][0] == "s":
                cp.wait_recv()

    def finish(self):
        for cp in self.sent.values():
            cp.wait_send()


def img_peers(at):
    return [(lax.rem(at.i + k, 4), at.s) for k in range(1, 4)]


FORWARD_MAIL = 4 * 3 + 3 + 2 * 7 + 4 + 7 + 2 * (2 + 7) + 7


def forward_kernel(nz, width, dims, *refs):
    na = len(dims)
    chunks, refs = refs[:na], refs[na:]
    x, cot, temb, cap, w_emb, w_cap, gains, biases = refs[:8]
    outs, refs = refs[8 : 8 + na], refs[8 + na :]
    hidden_o, act0_o, res_o, act1_o, g_o, normed, kv, qf = refs[:8]
    st0, st1, st2, rows, ca, cb, ra, rb, ha, hb, kv_all, cap_all, emb_all = refs[8:21]
    refs = refs[21:]
    weights, refs = refs[:na], refs[na:]
    (ssem, rsem, lsem, msend, mrecv, g_s, emb, affine, mine, every, xa, xb, ca_s, cb_s, ha_s, hb_s, ra_s, rb_s,
     aff_s, emb_s, cap_s, part, part_r, kv_s, kv_r, mod_s, mod_r, a3, act0, act1, hidden, res) = refs
    n_sp = 2 * nz
    at = Place()
    line = [at.rp(k, n_sp) for k in range(1, n_sp)]
    grid = img_peers(at)
    greet(line + grid)
    mail = Mail(msend, mrecv)
    got = Gather(at, nz, chunks, weights, dims, ssem, rsem)
    PROJ, IN, OUT, QKV = range(4)
    px, c = x.shape
    height = px // width
    d = c // HEADS
    tokens = cap.shape[0]
    e = cap.shape[1] // 4
    half = px // 2
    local = []

    def copy(src, dst):
        cp = pltpu.make_async_copy(src, dst, lsem.at[len(local)])
        cp.start()
        local.append(cp)
        return cp

    embedded = silu(temb[...].astype(F32)).astype(BF16).astype(F32)
    for j in range(4):
        emb[j] = jnp.broadcast_to(embedded[:, j * e : (j + 1) * e], (8, e))
    affine[0:3] = gains[...].astype(F32)
    affine[3:6] = biases[...].astype(F32)
    mine[...] = jnp.zeros_like(mine)

    def publish(j, v, edges):
        channel_stats(mine.at[j], v)
        out = []
        for ref, above, below in edges:
            out.append(mail.send(ref.at[px - width :], above, line[0]))
            out.append(mail.send(ref.at[:width], below, line[-1]))
        for dev in line:
            out.append(mail.send(mine.at[j], every.at[j, at.s], dev))
        every[j, at.s] = mine[j]
        return out

    def fold(v):
        return jnp.concatenate([v[:half], v[half:]], axis=1)

    greeted(n_sp + 2)
    close, far = got.order[:2], got.order[2:]
    got.along(PROJ, got.order)
    got.near(PROJ)
    got.along(IN, close)
    got.near(IN)
    stat0 = publish(0, x[...].astype(F32), [(x, xa, xb), (cot, ca_s, cb_s)])
    round1 = []
    share = tokens // 2
    part_tokens = pl.ds(pl.multiple_of(at.c * share, share), share)
    for dev in grid:
        round1.append(mail.send(affine, aff_s.at[at.i], dev))
        round1.append(mail.send(emb.at[dev[0]], emb_s.at[at.i], dev))
        round1.append(
            mail.send(cap.at[part_tokens, pl.ds(pl.multiple_of(dev[0] * e, e), e)], cap_s.at[at.i, part_tokens], dev)
        )
    own_cap = copy(cap.at[:, pl.ds(pl.multiple_of(at.i * e, e), e)], cap_s.at[at.i])
    aff_s[at.i] = affine[...]
    emb_s[at.i] = emb[at.i]
    got.near(OUT)
    own = [copy(got.ins[a], got.view(a, at.i, 0, at.c)) for a in range(na)]
    got.second(PROJ)
    got.second(IN, close[:1])
    got.along(IN, far)
    got.second(IN, close[1:])
    got.third(PROJ)
    got.near(QKV)
    got.along(OUT, close)
    got.second(IN, far)
    got.along(OUT, far)
    got.fourth(PROJ)
    got.third(IN)
    for cp in own:
        cp.wait()
    got.complete(PROJ)
    g = dot(cot[...], joined(weights[PROJ], 0), 1, 0).astype(BF16)
    for h in range(HEADS):
        g_s[h] = fold(g[:, h * d : (h + 1) * d])
    copy(weights[PROJ], outs[PROJ])
    got.second(OUT)
    got.along(QKV, got.order)

    own_cap.wait()
    for cp in round1:
        cp.wait_recv()
    halves = []
    for dev in grid:
        here = cap_s.at[dev[0], part_tokens]
        halves.append(mail.send(here, here, at.sib))
    for cp in halves:
        cp.wait_recv()
    for j in range(4):
        part[j, :tokens] = dot(cap_s[j], w_cap[...], 1, 0)
        part[j, tokens:] = dot(emb_s[j].astype(BF16), w_emb[...], 1, 0)
    round2 = [mail.send(part.at[dev[0]], part_r.at[at.i], dev) for dev in grid]
    part_r[at.i] = part[at.i]
    cap_all[...] = cap_s[...]
    emb_all[...] = jnp.concatenate([emb_s[j][0:1] for j in range(4)] + [jnp.zeros((4, e), F32)])
    aff = jnp.concatenate([aff_s[j] for j in range(4)], axis=1)
    rows[...] = jnp.zeros_like(rows)
    for j in range(3):
        rows[j, 0:1] = aff[j : j + 1]
        rows[j, 1:2] = aff[3 + j : 4 + j]
        rows[j, 2:3] = jnp.ones((1, c), F32)

    has_up, has_dn = edge_flags(n_sp, at.s)

    def activate(j, v, above, below, act):
        center, inverse = combine_stats(every.at[j], px)
        mul = inverse * rows[j, 0:1] * rows[j, 2:3]
        add = rows[j, 1:2] * rows[j, 2:3] + rows[j, 3:4]
        for r in range(height + 2):
            top, end = r == 0, r == height + 1
            t = above[...] if top else below[...] if end else v[(r - 1) * width : r * width, :]
            t = silu((t.astype(F32) - center) * mul + add)
            if top:
                t = t * has_up
            elif end:
                t = t * has_dn
            act[r * width : (r + 1) * width, :] = t.astype(BF16)
            shifted(a3, r, width, t)

    def taps(w, out, t0, t1, base):
        def one(tap, _):
            i, j = lax.div(tap, 3), lax.rem(tap, 3)
            lhs = a3[j, pl.ds(pl.multiple_of(i * width, width), px), :]
            first = 0.0 if base is None else base[...].astype(F32)
            out[...] = dot(lhs, joined(w, tap), 1, 1) + jnp.where(tap > 0, out[...], first)
            return 0

        lax.fori_loop(t0, t1, one, 0)

    for cp in stat0:
        cp.wait_recv()
    activate(0, x, xa, xb, act0)
    copy(act0, act0_o)
    got.fourth(IN)
    got.complete(IN)
    copy(weights[IN], outs[IN])
    taps(weights[IN], hidden, 0, 3, None)
    got.second(QKV)
    round_g = [mail.send(g_s.at[dev[1]], g_o.at[at.s], dev) for dev in line]
    copy(g_s.at[at.s], g_o.at[at.s])
    taps(weights[IN], hidden, 3, 6, None)
    got.third(OUT)
    taps(weights[IN], hidden, 6, 9, None)
    stat1 = publish(1, hidden[...], [(hidden, ha_s, hb_s)])
    copy(hidden, hidden_o)
    for cp in round2:
        cp.wait_recv()
    total = part_r[0] + part_r[1] + part_r[2] + part_r[3]
    kv_s[...] = total[:tokens].astype(BF16)
    mod_s[...] = total[tokens:]
    round3 = []
    for dev in line:
        round3.append(mail.send(kv_s, kv_r.at[at.s], dev))
        round3.append(mail.send(mod_s, mod_r.at[at.s], dev))
    kv_r[at.s] = kv_s[...]
    mod_r[at.s] = mod_s[...]
    got.fourth(OUT)
    got.third(QKV)
    for cp in round3 + stat1:
        cp.wait_recv()
    kv_all[...] = kv_r[...]
    mod = jnp.concatenate([mod_r[j][0:1] for j in range(n_sp)], axis=1)
    rows[1, 2:3] = 1.0 + mod[:, :c]
    rows[1, 3:4] = mod[:, c:]

    activate(1, hidden, ha_s, hb_s, act1)
    copy(act1, act1_o)
    got.fourth(QKV)
    got.complete(OUT)
    copy(weights[OUT], outs[OUT])
    taps(weights[OUT], res, 0, 9, x)
    stat2 = publish(2, res[...], [(res, ra_s, rb_s)])
    copy(res, res_o)
    for dst, src in ((ca, ca_s), (cb, cb_s), (ha, ha_s), (hb, hb_s)):
        dst[...] = src[...]
    got.complete(QKV)
    copy(weights[QKV], outs[QKV])
    wq = joined(weights[QKV], 0)

    for cp in stat2:
        cp.wait_recv()
    center, inverse = combine_stats(every.at[2], px)
    n = ((res[...] - center) * (inverse * rows[2, 0:1]) + rows[2, 1:2]).astype(BF16)
    normed[...] = n
    k = dot(n, wq[c : 2 * c], 1, 1).astype(BF16)
    v = dot(n, wq[2 * c :], 1, 1).astype(BF16)
    q = (dot(n, wq[:c], 1, 1).astype(BF16).astype(F32) * (d ** -0.5)).astype(BF16)
    for h in range(HEADS):
        lanes = slice(h * d, (h + 1) * d)
        kv[h] = jnp.concatenate([k[:, lanes], v[:, lanes]], axis=1)
        qf[h] = fold(q[:, lanes])
    ra[...] = ra_s[...]
    rb[...] = rb_s[...]
    st0[...] = every[0]
    st1[...] = every[1]
    st2[...] = every[2]
    for cp in local[1 + na :]:
        cp.wait()
    got.finish()
    for cp in round_g:
        cp.wait_recv()
    for cp in mail.sent:
        cp.wait_send()


def forward_call(chunks, x, cot, temb, cap, w_emb, w_cap, gains, biases, nz, width, cid):
    dims = [c.shape[:2] for c in chunks]
    na = len(dims)
    n_sp = 2 * nz
    px, c = x.shape
    padded = px + 2 * width
    tokens, wide = cap.shape
    e = wide // 4
    d2 = 2 * c // HEADS
    big = [((4, t, n_sp * r, 128), BF16) for t, r in dims]
    edge16, edge32 = ((width, c), BF16), ((width, c), F32)
    stat = ((n_sp, 8, c), F32)
    outs = big + [
        ((px, c), F32), ((padded, c), BF16), ((px, c), F32), ((padded, c), BF16),
        ((n_sp, px // 2, d2), BF16), ((px, c), BF16), ((HEADS, px, d2), BF16), ((HEADS, px // 2, d2), BF16),
        stat, stat, stat, ((3, 8, c), F32), edge16, edge16, edge32, edge32, edge32, edge32,
        ((n_sp, tokens, 128), BF16), ((4, tokens, e), BF16), ((8, e), F32),
    ]
    vm = pltpu.VMEM
    return pl.pallas_call(
        functools.partial(forward_kernel, nz, width, dims),
        out_shape=[jax.ShapeDtypeStruct(s, ty) for s, ty in outs],
        in_specs=[ANY] * na + [VM, VM, VM, ANY] + [VM] * 4,
        out_specs=[ANY] * (na + 5) + [VM] * (len(outs) - na - 5),
        scratch_shapes=[vm(s, ty) for s, ty in big]
        + [
            pltpu.SemaphoreType.DMA((na, Gather.copies(nz))),
            pltpu.SemaphoreType.DMA((na, Gather.copies(nz))),
            pltpu.SemaphoreType.DMA((2 * na + 6,)),
            pltpu.SemaphoreType.DMA((FORWARD_MAIL,)),
            pltpu.SemaphoreType.DMA((FORWARD_MAIL,)),
            vm((HEADS, px // 2, d2), BF16), vm((4, 8, e), F32), vm((8, 128), F32),
            vm((3, 8, c), F32), vm((3, n_sp, 8, c), F32),
        ]
        + [vm(*edge16)] * 4 + [vm(*edge32)] * 4
        + [
            vm((4, 8, 128), F32), vm((4, 8, e), F32), vm((4, tokens, e), BF16),
            vm((4, tokens + 8, 128), F32), vm((4, tokens + 8, 128), F32),
            vm((tokens, 128), BF16), vm((n_sp, tokens, 128), BF16), vm((8, 128), F32), vm((n_sp, 8, 128), F32),
            vm((3, padded, c), BF16), vm((padded, c), BF16), vm((padded, c), BF16), vm((px, c), F32), vm((px, c), F32),
        ],
        compiler_params=params(cid),
        name="forward",
    )(*chunks, x, cot, temb, cap, w_emb, w_cap, gains, biases)


class Reducer:
    NAMES = ("d", "sb", "da", "db", "rx", "ry", "r", "zr")

    def __init__(self, at, nz, arrays, ssem, rsem):
        self.at, self.nz, self.arrays = at, nz, arrays
        self.ssem, self.rsem = ssem, rsem
        self.sent, self.groups = {}, []

    @staticmethod
    def buffers(nz, t, r):
        return [
            pltpu.VMEM((2, 4, t, nz, r, 128), BF16),
            pltpu.VMEM((4, t, nz, r, 128), BF16),
            pltpu.VMEM((t, nz, r // 2, 128), BF16),
            pltpu.VMEM((t, nz, r // 2, 128), BF16),
            pltpu.VMEM((t, nz, r, 128), BF16),
            pltpu.VMEM((t, nz, r, 128), BF16),
            pltpu.VMEM((t, nz, r, 128), BF16),
            pltpu.VMEM((nz - 1, t, r, 128), BF16),
        ]

    def send(self, g, j, src, dst, dev):
        self.sent[g, j] = remote(src, dst, self.ssem.at[g, j], self.rsem.at[g, j], dev)

    def add(self, a, t0, t1):
        g = len(self.groups)
        self.groups.append((a, t0, t1))
        b = self.arrays[a][1]
        self.send(g, 0, b["d"].at[1 - self.at.c, :, t0:t1], b["sb"].at[:, t0:t1], self.at.sib)

    def run(self, stage, *groups):
        one = (self.stage1, self.stage2, self.stage3, self.stage4)[stage - 1]
        for g in groups:
            one(g, *self.groups[g])

    def stage1(self, g, a, t0, t1):
        b, at = self.arrays[a][1], self.at
        d, sb = b["d"], b["sb"]
        self.sent[g, 0].wait_recv()
        n = t1 - t0

        def add(j, _):
            ii, tt = lax.div(j, n), t0 + lax.rem(j, n)
            d[at.c, ii, tt] = (d[at.c, ii, tt].astype(F32) + sb[ii, tt].astype(F32)).astype(BF16)
            return 0

        lax.fori_loop(0, 4 * n, add, 0)
        h = d.shape[4] // 2
        self.send(g, 1, d.at[at.c, at.id, t0:t1, :, :h], b["da"].at[t0:t1], at.yn)
        self.send(g, 2, d.at[at.c, at.id, t0:t1, :, h:], b["db"].at[t0:t1], at.xn)

    def stage2(self, g, a, t0, t1):
        b, at = self.arrays[a][1], self.at
        d = b["d"]
        h = d.shape[4] // 2
        self.sent[g, 1].wait_recv()
        self.sent[g, 2].wait_recv()

        def add(tt, _):
            d[at.c, at.ix, tt, :, :h] = (
                d[at.c, at.ix, tt, :, :h].astype(F32) + b["da"][tt].astype(F32)
            ).astype(BF16)
            d[at.c, at.iy, tt, :, h:] = (
                d[at.c, at.iy, tt, :, h:].astype(F32) + b["db"][tt].astype(F32)
            ).astype(BF16)
            return 0

        lax.fori_loop(t0, t1, add, 0)
        self.send(g, 3, d.at[at.c, at.ix, t0:t1], b["rx"].at[t0:t1], at.xn)
        self.send(g, 4, d.at[at.c, at.iy, t0:t1], b["ry"].at[t0:t1], at.yn)

    def stage3(self, g, a, t0, t1):
        b, at = self.arrays[a][1], self.at
        self.sent[g, 3].wait_recv()
        self.sent[g, 4].wait_recv()

        def add(tt, _):
            total = b["d"][at.c, at.i, tt].astype(F32) + b["rx"][tt].astype(F32) + b["ry"][tt].astype(F32)
            b["r"][tt] = total.astype(BF16)
            return 0

        lax.fori_loop(t0, t1, add, 0)
        for k in range(1, self.nz):
            there = lax.rem(at.z + k, self.nz)
            self.send(g, 4 + k, b["r"].at[t0:t1, there], b["zr"].at[k - 1, t0:t1], at.zp(k, self.nz))

    def stage4(self, g, a, t0, t1):
        (out, b), at = self.arrays[a], self.at
        for k in range(1, self.nz):
            self.sent[g, 4 + k].wait_recv()

        def add(tt, _):
            total = (
                b["d"][at.c, at.i, tt, at.z].astype(F32)
                + b["rx"][tt, at.z].astype(F32)
                + b["ry"][tt, at.z].astype(F32)
            )
            for k in range(1, self.nz):
                total = total + b["zr"][k - 1, tt].astype(F32)
            out[tt] = total
            return 0

        lax.fori_loop(t0, t1, add, 0)

    def finish(self):
        for cp in self.sent.values():
            cp.wait_send()


BACK_MAIL = 6 + 14 + 6 + 3 + 7 + 9 + 9
BACK_GROUPS = 7
BIG = 12


def conv_taps(t0, t1, w, ring, rsem, one):
    slots = ring.shape[0]

    def step(tap, _):
        slot = lax.rem(tap, slots)
        pltpu.make_async_copy(w.at[:, tap], ring.at[slot], rsem.at[slot]).wait()
        one(tap, jnp.concatenate([ring[slot, j] for j in range(4)], axis=-1))

        @pl.when(tap + slots < 9)
        def _():
            pltpu.make_async_copy(w.at[:, tap + slots], ring.at[slot], rsem.at[slot]).start()

        return 0

    lax.fori_loop(t0, t1, step, 0)


def ring_start(w, ring, rsem):
    for j in range(ring.shape[0]):
        pltpu.make_async_copy(w.at[:, j], ring.at[j], rsem.at[j]).start()


def backward_kernel(nz, width, *refs):
    hbm, refs = refs[:BIG], refs[BIG:]
    w_in, w_out = refs[:2]
    (st0, st1, st2, rows, ca, cb, ra, rb, ha, hb, dt_all, cap_all, emb_all, w_emb, w_cap, temb) = refs[2:18]
    output, image_grad, s_in, s_out, s_small, g_temb, g_cap, g_wemb, g_wcap, g_aff = refs[18:28]
    refs = refs[28:]
    big, refs = refs[:BIG], refs[BIG:]
    bufs = [dict(zip(Reducer.NAMES, refs[8 * a : 8 * a + 8])) for a in range(3)]
    (bsem, gsend, grecv, msend, mrecv, ring, rsem, a3, g3, gt, acc, ng, pre_grad, res_grad,
     mine, every, na, nb, pa, pb, tg_s, tg_r, mod_s, mod_r,
     gc_s, gc_r, pe_s, pe_r, gs_s, gs_r, ps_s, ps_r, aff_s, aff_r) = refs[24:]
    n_sp = 2 * nz
    at = Place()
    line = [at.rp(k, n_sp) for k in range(1, n_sp)]
    grid = img_peers(at)
    greet(line + grid)
    loads = []
    for j in range(BIG):
        cp = pltpu.make_async_copy(hbm[j], big[j], bsem.at[j])
        cp.start()
        loads.append(cp)
    of, qf, dkv, w_qkv, w_proj, res, cot, normed, act1, hidden, act0, x = big
    ring_start(w_out, ring, rsem)
    mail = Mail(msend, mrecv)
    red = Reducer(at, nz, [(s_out, bufs[0]), (s_small, bufs[1]), (s_in, bufs[2])], gsend, grecv)
    px, c = res.shape
    height = px // width
    members = px * n_sp * (c // GROUPS)
    d = c // HEADS
    cols = 3 * c // n_sp

    def publish(j, rows01, edges):
        out = []
        for ref, above, below in edges:
            out.append(mail.send(ref.at[px - width :], above, line[0]))
            out.append(mail.send(ref.at[:width], below, line[-1]))
        mine[j] = jnp.zeros((8, c), F32)
        mine[j, 0:1] = rows01[0]
        mine[j, 1:2] = rows01[1]
        for dev in line:
            out.append(mail.send(mine.at[j], every.at[j, at.s], dev))
        every[j, at.s] = mine[j]
        return out

    for j in range(8):
        loads[j].wait()
    unfold = lambda v: jnp.concatenate([v[:, :d], v[:, d:]], axis=0)
    att = jnp.concatenate([unfold(of[h]) for h in range(HEADS)], axis=1)
    pg = jnp.concatenate(
        [unfold(qf[h]) for h in range(HEADS)]
        + [dkv[h][:, :d] for h in range(HEADS)]
        + [dkv[h][:, d:] for h in range(HEADS)],
        axis=1,
    )
    wq, wp = joined(w_qkv), joined(w_proj)
    ng[...] = dot(pg, wq, 1, 0)
    center2, inverse2 = combine_stats(st2, px)
    hat = (res[...] - center2) * inverse2
    u = ng[...]
    sums = (jnp.sum(u, axis=0, keepdims=True), jnp.sum(u * hat, axis=0, keepdims=True))
    greeted(n_sp + 2)
    round_2 = publish(2, sums, [(ng, na, nb)])
    gq = dot(pg, normed[...], 0, 0).astype(BF16)
    go = dot(cot[...], att, 0, 0).astype(BF16)
    small = bufs[1]["d"]
    for j in range(n_sp):
        for b in range(4):
            lanes = slice(b * 128, (b + 1) * 128)
            small[j % 2, b, 0, j // 2, :cols] = gq[j * cols : (j + 1) * cols, lanes]
            small[j % 2, b, 0, j // 2, cols:] = go[j * (c // n_sp) : (j + 1) * (c // n_sp), lanes]
    red.add(1, 0, 1)
    output[...] = (res[...] + dot(att, wp, 1, 1)).astype(BF16)

    first = 2 * lax.rem(at.s, nz)
    value = lax.div(at.s, nz)
    halves = []
    for j in range(2):
        blk = dt_all[first + j].astype(F32)
        halves.append(jnp.where(value > 0, blk[:, d:], blk[:, :d]))
    tg_s[...] = jnp.concatenate(halves, axis=1).astype(BF16)
    round_a = [mail.send(tg_s, tg_r.at[at.i], dev) for dev in grid]
    tg_r[at.i] = tg_s[...]

    has_up, has_dn = edge_flags(n_sp, at.s)

    def upstream(j, uu, ua, ub, center, inverse, yy, ya, yb, act, base, keep):
        total = combine_sums(every[j])
        mul = rows[j, 0:1] * rows[j, 2:3]
        back = group_total(total * mul) / members
        s1, s2 = back[0:1, :], back[1:2, :]
        for r in range(height + 2):
            cut = slice((r - 1) * width, r * width)
            top, end = r == 0, r == height + 1
            un = ua[...] if top else ub[...] if end else uu[cut, :]
            yn = ya[...] if top else yb[...] if end else yy[cut, :]
            g = inverse * (un * mul - s1 - (yn - center) * inverse * s2)
            if base:
                g = g + (base[1][...] if top else base[2][...] if end else base[0][cut, :]).astype(F32)
            if top:
                g = g * has_up
            elif end:
                g = g * has_dn
            elif keep is not None:
                keep[cut, :] = g
            shifted(g3, r, width, g.astype(BF16).astype(F32))
            shifted(a3, r, width, act[r * width : (r + 1) * width, :].astype(F32))
        gt[...] = g3[1, width : width + px, :].T
        return total

    def weight_taps(a, t0, t1):
        dst = bufs[a]["d"]

        def one(tap, _):
            i, j = lax.div(tap, 3), lax.rem(tap, 3)
            part = dot(gt[...], a3[j, pl.ds(pl.multiple_of(i * width, width), px), :], 1, 0).astype(BF16)
            r = c // n_sp
            for k in range(n_sp):
                for b in range(4):
                    dst[k % 2, b, tap, k // 2] = part[k * r : (k + 1) * r, b * 128 : (b + 1) * 128]
            return 0

        lax.fori_loop(t0, t1, one, 0)
        red.add(a, t0, t1)

    def input_taps(w):
        def one(tap, wt):
            i, j = lax.div(tap, 3), lax.rem(tap, 3)
            lhs = g3[2 - j, pl.ds(pl.multiple_of((2 - i) * width, width), px), :]
            acc[...] = dot(lhs, wt, 1, 0) + jnp.where(tap > 0, acc[...], 0.0)

        conv_taps(0, 9, w, ring, rsem, one)

    for cp in round_2:
        cp.wait_recv()
    loads[8].wait()
    t2 = upstream(2, ng, na, nb, center2, inverse2, res, ra, rb, act1, (cot, ca, cb), res_grad)
    red.run(1, 0)
    for tap in (0, 3, 6):
        weight_taps(0, tap, tap + 3)
    red.run(2, 0)
    input_taps(w_out)
    ring_start(w_in, ring, rsem)
    for j in range(9, BIG):
        loads[j].wait()
    center1, inverse1 = combine_stats(st1, px)
    hat = (hidden[...] - center1) * inverse1
    gain1, bias1, fac1 = rows[1, 0:1], rows[1, 1:2], rows[1, 2:3]
    v = acc[...] * silu_slope(hat * (gain1 * fac1) + (bias1 * fac1 + rows[1, 3:4]))
    pre_grad[...] = v
    sums = (jnp.sum(v, axis=0, keepdims=True), jnp.sum(v * hat, axis=0, keepdims=True))
    round_1 = publish(1, sums, [(pre_grad, pa, pb)])
    red.run(1, 1, 2, 3)
    red.run(3, 0)

    exact = lambda a, b, ca_, cb_: lax.dot_general(
        a, b, (((ca_,), (cb_,)), ((), ())), preferred_element_type=F32, precision=PRECISE
    )
    tokens = tg_s.shape[0]
    share = tokens // n_sp
    for cp in round_a:
        cp.wait_recv()
    flat_tg = tg_r[...].reshape(4 * tokens, 128)
    g_wcap[...] = dot(cap_all[...].reshape(4 * tokens, cap_all.shape[2]), flat_tg, 0, 0)
    gc_s[...] = dot(flat_tg, w_cap[...], 1, 1).astype(BF16).reshape(gc_s.shape)
    round_b = []
    for dev in line:
        cut = pl.ds(pl.multiple_of(dev[1] * share, share), share)
        round_b.append(mail.send(gc_s.at[:, cut, :], gc_r.at[at.s], dev))
    gc_r[at.s] = gc_s[:, pl.ds(pl.multiple_of(at.s * share, share), share), :]

    for cp in round_1:
        cp.wait_recv()
    t1 = upstream(1, pre_grad, pa, pb, center1, inverse1, hidden, ha, hb, act0, None, None)
    mod = jnp.concatenate([t1[1:2] * gain1 + t1[0:1] * bias1, t1[0:1]], axis=1)
    for j in range(n_sp):
        mod_s[j] = jnp.broadcast_to(mod[:, j * 128 : (j + 1) * 128], (8, 128))
    round_m = [mail.send(mod_s.at[at.s], mod_r.at[at.i], dev) for dev in grid]
    mod_r[at.i] = mod_s[at.s]
    red.run(2, 1)
    weight_taps(2, 0, 3)
    red.run(2, 2)
    weight_taps(2, 3, 6)
    red.run(2, 3)
    weight_taps(2, 6, 9)
    input_taps(w_in)

    center0, inverse0 = combine_stats(st0, px)
    hat = (x[...].astype(F32) - center0) * inverse0
    gain0 = rows[0, 0:1]
    v = acc[...] * silu_slope(hat * gain0 + rows[0, 1:2])
    acc[...] = v
    sums = (jnp.sum(v, axis=0, keepdims=True), jnp.sum(v * hat, axis=0, keepdims=True))
    round_0 = publish(0, sums, [])
    red.run(1, 4, 5, 6)
    red.run(4, 0)
    for cp in round_m:
        cp.wait_recv()
    mods = jnp.concatenate([mod_r[j][0:1] for j in range(4)] + [jnp.zeros((4, 128), F32)])
    emb_t = emb_all[...].T
    g_wemb[...] = sum(emb_t[:, j : j + 1] * mods[j : j + 1] for j in range(4))
    pe_s[...] = exact(mods, w_emb[...].astype(F32), 1, 1)
    round_p = [mail.send(pe_s, pe_r.at[at.s], dev) for dev in line]
    pe_r[at.s] = pe_s[...]
    for cp in round_0:
        cp.wait_recv()
    t0 = combine_sums(every[0])
    zero = jnp.zeros((2, c), F32)
    aff = jnp.concatenate([t0[1:2], t1[1:2] * fac1, t2[1:2], t0[0:1], t1[0:1] * fac1, t2[0:1], zero])
    for j in range(4):
        aff_s[j] = aff[:, j * 128 : (j + 1) * 128]
    round_e = [mail.send(aff_s.at[dev[0]], aff_r.at[at.i], dev) for dev in grid]
    aff_r[at.i] = aff_s[at.i]
    total = group_total(t0 * gain0) / members
    image_grad[...] = res_grad[...] + inverse0 * (acc[...] * gain0 - total[0:1] - hat * total[1:2])
    for g in (1, 2, 3):
        red.run(3, g)
        red.run(2, g + 3)
    for cp in round_b + round_p:
        cp.wait_recv()
    gc = gc_r[0].astype(F32)
    pe = pe_r[0]
    for j in range(1, n_sp):
        gc = gc + gc_r[j].astype(F32)
        pe = pe + pe_r[j]
    gs_s[...] = gc
    for j in range(4):
        ps_s[j] = jnp.broadcast_to(pe[j : j + 1], pe.shape)
    round_c = []
    for dev in grid:
        round_c.append(mail.send(gs_s.at[dev[0]], gs_r.at[at.i], dev))
        round_c.append(mail.send(ps_s.at[dev[0]], ps_r.at[at.i], dev))
    gs_r[at.i] = gs_s[at.i]
    ps_r[at.i] = ps_s[at.i]
    red.run(4, 1, 2, 3)
    red.run(3, 4, 5, 6)
    red.run(4, 4, 5, 6)
    red.finish()
    for cp in round_c + round_e:
        cp.wait_recv()
    g_cap[...] = jnp.concatenate([gs_r[j] for j in range(4)], axis=1)
    g_temb[...] = jnp.concatenate([ps_r[j] for j in range(4)], axis=1) * silu_slope(temb[...].astype(F32))
    g_aff[...] = aff_r[0] + aff_r[1] + aff_r[2] + aff_r[3]
    for cp in mail.sent:
        cp.wait_send()


def backward_call(big, w_in, w_out, small, nz, width, cid):
    px, c = big[5].shape
    n_sp = 2 * nz
    padded = px + 2 * width
    r = c // n_sp
    rs = (big[3].shape[1] + big[4].shape[1]) // n_sp
    dt_all, cap_all = small[10], small[11]
    tokens = dt_all.shape[1]
    e = cap_all.shape[2]
    share = tokens // n_sp
    outs = [
        ((px, c), BF16), ((px, c), F32), ((9, r, 128), F32), ((9, r, 128), F32), ((1, rs, 128), F32),
        ((8, 4 * e), F32), ((share, 4 * e), F32), ((e, 128), F32), ((e, 128), F32), ((8, 128), F32),
    ]
    vm = pltpu.VMEM
    return pl.pallas_call(
        functools.partial(backward_kernel, nz, width),
        out_shape=[jax.ShapeDtypeStruct(s, ty) for s, ty in outs],
        in_specs=[ANY] * (len(big) + 2) + [VM] * len(small),
        out_specs=[VM] * len(outs),
        scratch_shapes=[vm(v.shape, v.dtype) for v in big]
        + Reducer.buffers(nz, 9, r) + Reducer.buffers(nz, 1, rs) + Reducer.buffers(nz, 9, r)
        + [
            pltpu.SemaphoreType.DMA((len(big),)),
            pltpu.SemaphoreType.DMA((BACK_GROUPS, 4 + nz)),
            pltpu.SemaphoreType.DMA((BACK_GROUPS, 4 + nz)),
            pltpu.SemaphoreType.DMA((BACK_MAIL,)),
            pltpu.SemaphoreType.DMA((BACK_MAIL,)),
            vm((3, 4, c, 128), BF16),
            pltpu.SemaphoreType.DMA((3,)),
            vm((3, padded, c), BF16), vm((3, padded, c), BF16), vm((c, px), BF16),
            vm((px, c), F32), vm((px, c), F32), vm((px, c), F32), vm((px, c), F32),
            vm((3, 8, c), F32), vm((3, n_sp, 8, c), F32),
            vm((width, c), F32), vm((width, c), F32), vm((width, c), F32), vm((width, c), F32),
            vm((tokens, 128), BF16), vm((4, tokens, 128), BF16),
            vm((n_sp, 8, 128), F32), vm((4, 8, 128), F32),
            vm((4, tokens, e), BF16), vm((n_sp, 4, share, e), BF16),
            vm((8, e), F32), vm((n_sp, 8, e), F32),
            vm((4, share, e), F32), vm((4, share, e), F32),
            vm((4, 8, e), F32), vm((4, 8, e), F32),
            vm((4, 8, 128), F32), vm((4, 8, 128), F32),
        ],
        compiler_params=params(cid),
        name="backward",
    )(*big, w_in, w_out, *small)


def emit_kernel(cut, *refs):
    ins, outs, mids, loads, stores = refs[:10], refs[10:22], refs[22:31], refs[31], refs[32]
    output, image, s_in, s_out, s_small, g_temb, g_cap, g_wemb, g_wcap, g_aff = ins
    pairs = [
        (output, outs[0]), (image, outs[1]), (g_cap, outs[3]), (s_in, outs[4]), (s_out, outs[5]), (g_wemb, outs[6]),
        (s_small.at[0, :cut], outs[7]), (g_wcap, outs[8]), (s_small.at[0, cut:], outs[9]),
    ]
    copies = [pltpu.make_async_copy(src, mid, loads.at[j]) for j, ((src, _), mid) in enumerate(zip(pairs, mids))]
    for cp in copies:
        cp.start()
    backs = []
    for j, cp in enumerate(copies):
        cp.wait()
        backs.append(pltpu.make_async_copy(mids[j], pairs[j][1], stores.at[j]))
        backs[-1].start()
    outs[2][...] = g_temb[0:1, :]
    outs[10][...] = g_aff[0:3, :]
    outs[11][...] = g_aff[3:6, :]
    for cp in backs:
        cp.wait()


def emit_call(parts, cut):
    output, image, s_in, s_out, s_small, g_temb, g_cap, g_wemb, g_wcap, g_aff = parts
    rest = s_small.shape[1] - cut
    like = lambda v: jax.ShapeDtypeStruct(v.shape, v.dtype)
    f32 = lambda *s: jax.ShapeDtypeStruct(s, F32)
    shapes = [
        like(output), like(image), f32(1, g_temb.shape[1]), like(g_cap), like(s_in), like(s_out), like(g_wemb),
        f32(cut, 128), like(g_wcap), f32(rest, 128), f32(3, 128), f32(3, 128),
    ]
    in_specs = [ANY] * 10
    in_specs[5] = in_specs[9] = VM
    out_specs = [ANY] * 12
    out_specs[2] = out_specs[10] = out_specs[11] = VM
    return pl.pallas_call(
        functools.partial(emit_kernel, cut),
        out_shape=shapes,
        in_specs=in_specs,
        out_specs=out_specs,
        scratch_shapes=[pltpu.VMEM(shapes[j].shape, shapes[j].dtype) for j in (0, 1, 3, 4, 5, 6, 7, 8, 9)]
        + [pltpu.SemaphoreType.DMA((9,)), pltpu.SemaphoreType.DMA((9,))],
        compiler_params=params(),
        name="emit",
    )(*parts)


def fast_body(
    image_in, time_embed, caption, caption_mask, conv_in, conv_out, embed_proj, qkv_proj,
    caption_proj, out_proj, norm_gains, norm_biases, cotangent,
):
    n, height, width, c = image_in.shape
    n_sp = lax.axis_size("sp")
    nz = n_sp // 2
    px = height * width
    x = image_in.reshape(px, c)
    cot = cotangent.reshape(px, c)

    flat = lambda w: w.transpose(1, 2, 3, 0).reshape(9, w.shape[3], w.shape[0])
    (w_proj, w_in, w_out, w_qkv, hidden, act0, res, act1, g, normed, kv, q,
     st0, st1, st2, rows, ca, cb, ra, rb, ha, hb, kv_all, cap_all, emb_all) = forward_call(
        [out_proj.T[None], flat(conv_in), flat(conv_out), qkv_proj.T[None]], x, cot, time_embed, caption[0], embed_proj, caption_proj,
        norm_gains, norm_biases, nz, width, 0,
    )
    w_proj, w_qkv = w_proj[:, 0], w_qkv[:, 0]
    of, qf, dkv, dt_all = attention_call(kv, q, g, kv_all, caption_mask, 1)

    parts = backward_call(
        [of, qf, dkv, w_qkv, w_proj, res, cot, normed, act1, hidden, act0, x], w_in, w_out,
        [st0, st1, st2, rows, ca, cb, ra, rb, ha, hb, dt_all, cap_all, emb_all, embed_proj, caption_proj, time_embed],
        nz, width, 2,
    )
    output, image, g_temb, g_cap, s_in, s_out, g_wemb, g_qkv, g_wcap, g_out, g_gains, g_biases = emit_call(
        parts, qkv_proj.shape[1]
    )
    unflat = lambda g: g.reshape(3, 3, g.shape[1], 128).transpose(3, 0, 1, 2)
    return (
        output.reshape(image_in.shape), image.reshape(image_in.shape), g_temb, g_cap[None], unflat(s_in), unflat(s_out),
        g_wemb, g_qkv.T, g_wcap, g_out.T, g_gains, g_biases,
    )


def body(*args):
    image_in, qkv_proj = args[0], args[7]
    n, height, width, c = image_in.shape
    n_img, n_sp = lax.axis_size("img"), lax.axis_size("sp")
    fits = n == 1 and n_img == 4 and n_sp == HEADS and c == 512 and width == 64
    return fast_body(*args) if fits else plain_body(*args)


def solution(mesh):
    rows = P("img", "sp", None, None)
    kernel = P("img", None, None, "sp")
    flat = P("img", "sp")
    return jax.shard_map(
        body,
        mesh=mesh,
        in_specs=(
            rows, P("img", None), P("img", None, None), P("img", None), kernel, kernel,
            flat, flat, flat, flat, P(None, "img"), P(None, "img"), rows,
        ),
        out_specs=(
            rows, rows, P("img", None), P("img", "sp", None), kernel, kernel,
            flat, flat, flat, flat, P(None, "img"), P(None, "img"),
        ),
        check_vma=False,
    )
```

```python
import functools

import jax
import jax.numpy as jnp
from jax import lax
from jax.experimental import pallas as pl
from jax.experimental.pallas import tpu as pltpu
from jax.sharding import PartitionSpec as P

HEADS = 8
GROUPS = 32
EPSILON = 1e-05
PRECISE = lax.Precision.HIGHEST
MASKED = -1e30
BF16 = jnp.bfloat16
F32 = jnp.float32
MESH = pl.DeviceIdType.MESH
VMEM_BYTES = 60 * 1024 * 1024


def dot(a, b, ca, cb):
    return lax.dot_general(a, b, (((ca,), (cb,)), ((), ())), preferred_element_type=F32)


def silu(v):
    return v * jax.nn.sigmoid(v)


def silu_slope(v):
    s = jax.nn.sigmoid(v)
    return s * (1.0 + v * (1.0 - s))


def gather(x, axis, dim):
    return lax.all_gather(x, axis, axis=dim, tiled=True)


def scatter_sum(x, axis, dim):
    return lax.psum_scatter(x, axis, scatter_dimension=dim, tiled=True)


def swap(x, axis, split, concat):
    return lax.all_to_all(x, axis, split, concat, tiled=True)


def halo(x):
    count = lax.axis_size("sp")
    above = lax.ppermute(x[:, -1:], "sp", [(i, i + 1) for i in range(count - 1)])
    below = lax.ppermute(x[:, :1], "sp", [(i + 1, i) for i in range(count - 1)])
    return above, below


def group_sum(v):
    c = v.shape[-1]
    g = v.reshape(v.shape[:-1] + (GROUPS, c // GROUPS))
    s = jnp.sum(g, axis=-1, keepdims=True)
    return jnp.broadcast_to(s, g.shape).reshape(v.shape)


def norm_stats(x):
    n, r, w, c = x.shape
    cells = r * w * (c // GROUPS)
    parts = lax.axis_size("sp")
    mean = group_sum(jnp.sum(x, axis=(1, 2))) / cells
    dev = group_sum(jnp.sum(jnp.square(x - mean[:, None, None, :]), axis=(1, 2)))
    both = lax.all_gather(jnp.stack([mean, dev]), "sp")
    means, devs = both[:, 0], both[:, 1]
    center = jnp.mean(means, axis=0)
    var = (jnp.sum(devs, axis=0) + cells * jnp.sum(jnp.square(means - center), axis=0)) / (
        cells * parts
    )
    return center, lax.rsqrt(var + EPSILON)


def hat_of(x, center, inverse):
    return (x - center[:, None, None, :]) * inverse[:, None, None, :]


def norm_back(u, hat, inverse, gain, sum_u, sum_uh, members):
    s1 = group_sum(sum_u * gain) / members
    s2 = group_sum(sum_uh * gain) / members
    return inverse[:, None, None, :] * (
        u * gain - s1[:, None, None, :] - hat * s2[:, None, None, :]
    )


def pad_cols(x):
    return jnp.pad(x, ((0, 0), (0, 0), (1, 1), (0, 0)))


def conv(padded, weight_t, transposed):
    n, rp, wp, c = padded.shape
    r, w = rp - 2, wp - 2
    total = None
    for i in range(3):
        for j in range(3):
            a = padded[:, i : i + r, j : j + w].reshape(n * r * w, c)
            part = dot(a, weight_t[2 - i, 2 - j], 1, 0) if transposed else dot(a, weight_t[i, j], 1, 1)
            total = part if total is None else total + part
    return total.reshape(n, r, w, -1)


def conv_grad(padded, g):
    n, r, w, c = g.shape
    gf = g.reshape(n * r * w, c)
    rows = []
    for i in range(3):
        for j in range(3):
            a = padded[:, i : i + r, j : j + w].reshape(n * r * w, -1)
            rows.append(dot(gf, a, 0, 0))
    return jnp.stack(rows).reshape(3, 3, c, -1)


def to_pairs(x, images):
    n, px, h, d = x.shape
    y = x.transpose(0, 2, 1, 3).reshape(n * h, px, d)
    return swap(y, "sp", 0, 1)


def from_pairs(x, images):
    y = swap(x, "sp", 1, 0)
    return y.reshape(images, HEADS, y.shape[1], y.shape[2]).transpose(0, 2, 1, 3)


def attention_plain(q, k, v, g, tk, tv, keep, scale):
    p, length, d = q.shape
    block = min(512, length)
    keys = jnp.concatenate([tk, k], axis=1)
    values = jnp.concatenate([tv, v], axis=1)
    text = tk.shape[1]
    keep_all = jnp.concatenate([keep, jnp.ones((p, length), bool)], axis=1)

    def step(carry, blk):
        dk, dv = carry
        qb, gb = blk
        s = jnp.einsum("pqd,pkd->pqk", qb, keys, preferred_element_type=F32) * scale
        s = jnp.where(keep_all[:, None, :], s, MASKED)
        peak = jnp.max(s, axis=-1, keepdims=True)
        e = jnp.exp(s - peak)
        prob = e / jnp.sum(e, axis=-1, keepdims=True)
        pb = prob.astype(BF16)
        o = jnp.einsum("pqk,pkd->pqd", pb, values, preferred_element_type=F32)
        row = jnp.sum(o * gb.astype(F32), axis=-1, keepdims=True)
        dp = jnp.einsum("pqd,pkd->pqk", gb, values, preferred_element_type=F32)
        ds = (prob * (dp - row)).astype(BF16)
        dq = jnp.einsum("pqk,pkd->pqd", ds, keys, preferred_element_type=F32) * scale
        dk = dk + jnp.einsum("pqk,pqd->pkd", ds, qb, preferred_element_type=F32)
        dv = dv + jnp.einsum("pqk,pqd->pkd", pb, gb, preferred_element_type=F32)
        return (dk, dv), (o.astype(BF16), dq.astype(BF16))

    zeros = jnp.zeros((p, text + length, d), F32)
    cut = lambda t: t.reshape(p, length // block, block, d).swapaxes(0, 1)
    (dk, dv), (o, dq) = lax.scan(step, (zeros, zeros), (cut(q), cut(g)))
    join = lambda t: t.swapaxes(0, 1).reshape(p, length, d)
    dk = (dk * scale).astype(BF16)
    dv = dv.astype(BF16)
    return join(o), join(dq), dk[:, text:], dv[:, text:], dk[:, :text], dv[:, :text]


def plain_body(
    image_in, time_embed, caption, caption_mask, conv_in, conv_out, embed_proj, qkv_proj,
    caption_proj, out_proj, norm_gains, norm_biases, cotangent,
):
    n, rows, width, chans = image_in.shape
    n_img, n_sp = lax.axis_size("img"), lax.axis_size("sp")
    img, sp = lax.axis_index("img"), lax.axis_index("sp")
    px = rows * width
    members = px * n_sp * (chans // GROUPS)
    d = chans // HEADS
    scale = d ** -0.5
    pairs = n * HEADS // n_sp

    def whole(w):
        w = gather(w, "img", w.ndim - 1)
        return gather(w, "sp", w.ndim - 2)

    w_in = whole(conv_in.transpose(1, 2, 3, 0))
    w_out = whole(conv_out.transpose(1, 2, 3, 0))
    w_qkv = whole(qkv_proj.T)
    w_proj = whole(out_proj.T)
    affine = gather(jnp.concatenate([norm_gains, norm_biases]), "img", 1).astype(F32)
    gains, biases = affine[:3], affine[3:]

    embedded = silu(time_embed.astype(F32)).astype(BF16)
    emb_all = swap(embedded, "img", 1, 0)
    mod = scatter_sum(jnp.dot(emb_all, embed_proj, preferred_element_type=F32), "img", 0)
    mod = gather(mod, "sp", 1)
    scale_term, shift_term = mod[:, :chans], mod[:, chans:]
    cap_all = swap(caption, "img", 2, 0)
    cap_flat = cap_all.reshape(-1, cap_all.shape[2])
    kv = jnp.dot(cap_flat, caption_proj, preferred_element_type=F32)
    kv = scatter_sum(kv.reshape(cap_all.shape[0], cap_all.shape[1], -1), "img", 0).astype(BF16)
    kv = gather(kv, "sp", 2)
    text = kv.shape[1]
    kv_heads = kv.reshape(n, text, 2, HEADS, d).transpose(2, 0, 3, 1, 4).reshape(2, n * HEADS, text, d)
    mine = lax.dynamic_slice_in_dim(kv_heads, sp * pairs, pairs, 1)
    keep = jnp.repeat(caption_mask > 0, HEADS, axis=0)
    keep = lax.dynamic_slice_in_dim(keep, sp * pairs, pairs, 0)

    image_f = image_in.astype(F32)
    c0, i0 = norm_stats(image_f)
    hat0 = hat_of(image_f, c0, i0)
    first = hat0 * gains[0] + biases[0]
    act0 = silu(first).astype(BF16)
    above, below = halo(act0)
    pad0 = pad_cols(jnp.concatenate([above, act0, below], axis=1))
    hidden = conv(pad0, w_in, False)
    c1, i1 = norm_stats(hidden)
    hat1 = hat_of(hidden, c1, i1)
    second = hat1 * gains[1] + biases[1]
    pre = second * (1.0 + scale_term[:, None, None, :]) + shift_term[:, None, None, :]
    act1 = silu(pre).astype(BF16)
    above, below = halo(act1)
    pad1 = pad_cols(jnp.concatenate([above, act1, below], axis=1))
    residual = image_f + conv(pad1, w_out, False)
    c2, i2 = norm_stats(residual)
    hat2 = hat_of(residual, c2, i2)
    normed = (hat2 * gains[2] + biases[2]).astype(BF16).reshape(n * px, chans)
    qkv = dot(normed, w_qkv, 1, 1).astype(BF16)
    cot = cotangent.reshape(n * px, chans)
    g_att = dot(cot, w_proj, 1, 0).astype(BF16)
    four = jnp.concatenate([qkv, g_att], axis=1).reshape(n, px, 4, HEADS, d)
    packed = to_pairs(four.transpose(0, 1, 3, 2, 4).reshape(n, px, HEADS, 4 * d), n)
    q, k, v, g = (packed[..., j * d : (j + 1) * d] for j in range(4))
    o, dq, dk, dv, dtk, dtv = attention_plain(q, k, v, g, mine[0], mine[1], keep, scale)
    back = from_pairs(jnp.concatenate([o, dq, dk, dv], axis=-1), n)
    back = back.reshape(n * px, HEADS, 4, d).transpose(0, 2, 1, 3).reshape(n * px, 4 * chans)
    attended, proj_grad = back[:, :chans], back[:, chans:]
    output = residual + dot(attended, w_proj, 1, 1).reshape(image_in.shape)

    grad_out = dot(cot, attended, 0, 0)
    grad_qkv = dot(proj_grad, normed, 0, 0)
    normed_grad = dot(proj_grad, w_qkv, 1, 0).reshape(image_in.shape)

    def sums(u, hat):
        both = jnp.stack([jnp.sum(u, axis=(1, 2)), jnp.sum(u * hat, axis=(1, 2))])
        return lax.psum(both, "sp")

    su2, sh2 = sums(normed_grad, hat2)
    residual_grad = cotangent.astype(F32) + norm_back(
        normed_grad, hat2, i2, gains[2], su2, sh2, members
    )
    g2 = residual_grad.astype(BF16)
    above, below = halo(g2)
    gpad = pad_cols(jnp.concatenate([above, g2, below], axis=1))
    grad_conv_out = conv_grad(pad1, g2)
    pre_grad = conv(gpad, w_out, True) * silu_slope(pre)
    sa, sb = sums(pre_grad, hat1)
    fac = 1.0 + scale_term
    shift_grad = sa
    scale_grad = sb * gains[1] + sa * biases[1]
    u1 = pre_grad * fac[:, None, None, :]
    su1, sh1 = sa * fac, sb * fac
    g1 = norm_back(u1, hat1, i1, gains[1], su1, sh1, members).astype(BF16)
    above, below = halo(g1)
    gpad = pad_cols(jnp.concatenate([above, g1, below], axis=1))
    grad_conv_in = conv_grad(pad0, g1)
    u0 = conv(gpad, w_in, True) * silu_slope(first)
    su0, sh0 = sums(u0, hat0)
    grad_image = residual_grad + norm_back(u0, hat0, i0, gains[0], su0, sh0, members)

    mod_grad = jnp.concatenate([scale_grad, shift_grad], axis=1)
    cols = embed_proj.shape[1]
    mod_all = gather(mod_grad, "img", 0)
    mod_cols = lax.dynamic_slice_in_dim(mod_all, sp * cols, cols, 1)
    grad_embed_proj = jnp.einsum("ne,nd->ed", emb_all.astype(F32), mod_cols, precision=PRECISE)
    part = jnp.einsum("nd,ed->ne", mod_cols, embed_proj.astype(F32), precision=PRECISE)
    part = swap(lax.psum(part, "sp"), "img", 0, 1)
    grad_embed = part * silu_slope(time_embed.astype(F32))

    tg = gather(jnp.stack([dtk, dtv]), "sp", 1).reshape(2, n, HEADS, text, d)
    tg = tg.transpose(1, 3, 0, 2, 4).reshape(n, text, 2 * chans)
    cols = caption_proj.shape[1]
    tg = gather(lax.dynamic_slice_in_dim(tg, sp * cols, cols, 2), "img", 0).reshape(-1, cols)
    grad_caption_proj = dot(cap_flat, tg, 0, 0)
    gc = dot(tg, caption_proj, 1, 1).reshape(cap_all.shape)
    gc = scatter_sum(gc, "sp", 1)
    grad_caption = swap(gc, "img", 0, 2)

    grads = jnp.concatenate(
        [jnp.sum(t, axis=0)[None] for t in (sh0, sh1, sh2, su0, su1, su2)]
    )
    grads = scatter_sum(grads, "img", 1)

    def shared(w):
        w = scatter_sum(w, "sp", w.ndim - 2)
        return scatter_sum(w, "img", w.ndim - 1)

    return (
        output.astype(BF16),
        grad_image,
        grad_embed,
        grad_caption,
        shared(grad_conv_in).transpose(3, 0, 1, 2),
        shared(grad_conv_out).transpose(3, 0, 1, 2),
        grad_embed_proj,
        shared(grad_qkv).T,
        grad_caption_proj,
        shared(grad_out).T,
        grads[:3],
        grads[3:],
    )


class Place:
    def __init__(self):
        self.i = lax.axis_index("img")
        self.s = lax.axis_index("sp")
        self.z = lax.div(self.s, 2)
        self.c = lax.rem(self.s, 2)
        x = lax.rem(self.i, 2)
        y = lax.div(self.i, 2)
        self.ix = self.i + 1 - 2 * x
        self.iy = self.i + 2 - 4 * y
        self.id = 3 - self.i
        self.sib = (self.i, self.s + 1 - 2 * self.c)
        self.xn = (self.ix, self.s)
        self.yn = (self.iy, self.s)

    def zp(self, k, nz):
        return (self.i, 2 * lax.rem(self.z + k, nz) + self.c)

    def rp(self, k, n_sp):
        return (self.i, lax.rem(self.s + k, n_sp))


def greet(peers):
    bar = pltpu.get_barrier_semaphore()
    for p in peers:
        pl.semaphore_signal(bar, inc=1, device_id=p, device_id_type=MESH)


def greeted(count):
    pl.semaphore_wait(pltpu.get_barrier_semaphore(), count)


def remote(src, dst, ssem, rsem, dev):
    cp = pltpu.make_async_remote_copy(
        src_ref=src, dst_ref=dst, send_sem=ssem, recv_sem=rsem, device_id=dev, device_id_type=MESH
    )
    cp.start()
    return cp


def params(cid=None, grid=0):
    extra = {} if cid is None else {"collective_id": cid, "has_side_effects": True}
    if grid:
        extra["dimension_semantics"] = ("arbitrary",) * grid
    return pltpu.CompilerParams(vmem_limit_bytes=VMEM_BYTES, **extra)


ANY = pl.BlockSpec(memory_space=pl.ANY)
VM = pl.BlockSpec(memory_space=pltpu.VMEM)
def channel_stats(v):
    mean = jnp.sum(v, axis=0, keepdims=True) / v.shape[0]
    dev = v - mean
    return mean, jnp.sum(dev * dev, axis=0, keepdims=True)


def put_rows(dst, pair):
    n = pair[0].shape[1] // 128
    for a, row in enumerate(pair):
        for j in range(n):
            dst[a * n + j : a * n + j + 1, :] = row[:, j * 128 : (j + 1) * 128]


def get_rows(block):
    n = block.shape[0] // 2
    return tuple(jnp.concatenate([block[a * n + j : a * n + j + 1] for j in range(n)], axis=1) for a in range(2))


def group_total(rows):
    c = rows.shape[1]
    size = 512 // GROUPS
    a = lax.broadcasted_iota(jnp.int32, (128, 128), 0)
    b = lax.broadcasted_iota(jnp.int32, (128, 128), 1)
    same = jnp.where(lax.bitwise_xor(a, b) < size, 1.0, 0.0).astype(BF16)
    high = rows.astype(BF16)
    rest = rows - high.astype(F32)
    mid = rest.astype(BF16)
    low = (rest - mid.astype(F32)).astype(BF16)
    parts = jnp.concatenate([high.astype(F32), mid.astype(F32), low.astype(F32)]).astype(BF16)
    total = jnp.concatenate(
        [dot(parts[:, j * 128 : (j + 1) * 128], same, 1, 0) for j in range(c // 128)], axis=1
    )
    n = rows.shape[0]
    return total[:n] + total[n : 2 * n] + total[2 * n :]


def combine_stats(every, px):
    n_sp, rows, lanes = every.shape
    half = rows // 2
    size = half * lanes // GROUPS
    means = [every[j, :half, :] for j in range(n_sp)]
    center_c = sum(means) / n_sp
    dev = sum(every[j, half:, :] for j in range(n_sp))
    dev = dev + px * sum((m - center_c) * (m - center_c) for m in means)
    spread = lambda v: group_total(jnp.concatenate([v, v]))[:half]
    center = spread(center_c) / size
    off = center_c - center
    var = spread(dev + (px * n_sp) * (off * off)) / (px * n_sp * size)
    return get_rows(jnp.concatenate([center, lax.rsqrt(var + EPSILON)]))


def combine_sums(every):
    total = every[0]
    for j in range(1, every.shape[0]):
        total = total + every[j]
    a, b = get_rows(total)
    return jnp.concatenate([a, b, jnp.zeros((6, a.shape[1]), F32)])


def edge_flags(n_sp, s):
    return jnp.where(s > 0, 1.0, 0.0), jnp.where(s < n_sp - 1, 1.0, 0.0)


def shifted(dst, row, width, block):
    col = lax.broadcasted_iota(jnp.int32, block.shape, 0)
    r = slice(row * width, (row + 1) * width)
    dst[1, r, :] = block.astype(BF16)
    dst[0, r, :] = jnp.where(col == 0, 0.0, pltpu.roll(block, 1, 0)).astype(BF16)
    dst[2, r, :] = jnp.where(col == width - 1, 0.0, pltpu.roll(block, width - 1, 0)).astype(BF16)


def joined(w_ref, *lead):
    return jnp.concatenate([w_ref[(j,) + lead] for j in range(4)], axis=-1)


def three_parts(v):
    a = v.astype(BF16).astype(F32)
    b = (v - a).astype(BF16).astype(F32)
    return a, b, v - a - b


AHEAD = 2


def attention_kernel(
    n_sp, BK, kv, qin, gin, text, keep, of, qf, dkv, dt,
    kv_r, q_r, g_r, q_s, o_s, dq_o, dkv_s, dt_s, k_s, v_s, s_s, e_s, g_s, dq_s, peak_s, lsem, ssem, rsem,
):
    at = Place()
    nz = n_sp // 2
    px = kv.shape[1]
    L, T = n_sp * px, text.shape[1]
    d = kv.shape[2] // 2
    BQ = px // 2
    line = [at.rp(k, n_sp) for k in range(1, n_sp)]
    greet(line)
    own = [
        pltpu.make_async_copy(kv.at[at.s], kv_r.at[at.s], lsem.at[0]),
        pltpu.make_async_copy(qin.at[at.s], q_r.at[at.s], lsem.at[1]),
        pltpu.make_async_copy(gin, g_r, lsem.at[6]),
    ]
    for cp in own:
        cp.start()
    greeted(n_sp - 1)
    keys = [remote(kv.at[dev[1]], kv_r.at[at.s], ssem.at[0, k + 1], rsem.at[0, k + 1], dev) for k, dev in enumerate(line)]
    odd = lax.rem(at.s, 2)
    pair = lax.div(at.s, 2)
    ones = (lax.broadcasted_iota(jnp.int32, (1, d), 1) < 3).astype(F32).astype(BF16)
    picked = []
    for j in (pair, HEADS // 2 + pair):
        blk = text[j].astype(F32)
        picked.append(jnp.where(odd > 0, blk[:, d:], blk[:, :d]).astype(BF16))
    k_s[0:T, :] = picked[0]
    v_s[0:T, :] = jnp.concatenate([picked[1], jnp.broadcast_to(ones, (T, d))], axis=1)

    def rows_of(o, n=px, start=0):
        return pl.ds(pl.multiple_of(o * px + start, 128), n)

    def take(j):
        rows = rows_of(j, px, T)
        k_s[rows, :] = kv_r[j][:, :d]
        v_s[rows, :] = jnp.concatenate([kv_r[j][:, d:], jnp.broadcast_to(ones, (px, d))], axis=1)

    for cp in own:
        cp.wait()
    take(at.s)
    for k in range(1, n_sp):
        keys[k - 1].wait_recv()
        take(lax.rem(at.s - k + n_sp, n_sp))
    blocks = [(0, T)] + [(T + j * BK, BK) for j in range(L // BK)]
    scale = d ** -0.5

    def query_copy(k):
        return pltpu.make_async_remote_copy(
            src_ref=qin.at[lax.rem(at.s + k, n_sp)], dst_ref=q_r.at[at.s], send_sem=ssem.at[1, k],
            recv_sem=rsem.at[1, k], device_id=(at.i, lax.rem(at.s + k, n_sp)), device_id_type=MESH,
        )

    def back_copy(j, k, src, dst, o):
        return pltpu.make_async_remote_copy(
            src_ref=src.at[o], dst_ref=dst.at[at.s], send_sem=ssem.at[j, k], recv_sem=rsem.at[j, k],
            device_id=(at.i, o), device_id_type=MESH,
        )

    def scores(q, slot, st, n, peak):
        s = dot(q, k_s[st : st + n, :], 1, 1)
        if st == 0:
            s = jnp.where(keep[...] > 0, s, MASKED)
        s_s[slot, :, st : st + n] = s
        for j in range(n // 128):
            piece = s[:, 128 * j : 128 * j + 128]
            peak = piece if peak is None else jnp.maximum(peak, piece)
        return peak

    def query(o, part):
        return q_r[o][:, part * d : (part + 1) * d]

    def forward(o, part, o_next):
        nxt = query(o_next, 1 - part)
        g = g_r[o][:, part * d : (part + 1) * d]
        rows = rows_of(o, BQ, part * BQ)
        q_s[rows, :] = query(o, part)
        top = jnp.max(peak_s[part], axis=1, keepdims=True)
        out = jnp.zeros((BQ, 2 * d), F32)
        peak = None
        for st, n in blocks:
            peak = scores(nxt, 1 - part, st, n, peak)
            e = jnp.exp(s_s[part, :, st : st + n] - top).astype(BF16)
            e_s[rows, st : st + n] = e
            out = out + dot(e, v_s[st : st + n, :], 1, 0)
        peak_s[1 - part] = peak
        inverse = 1.0 / out[:, d : d + 1]
        out = out[:, :d] * inverse
        g = g.astype(F32) * inverse
        row = jnp.sum(out * g, axis=1, keepdims=True)
        lane = lax.broadcasted_iota(jnp.int32, (BQ, d), 1)
        extra = jnp.zeros((BQ, d), F32)
        for j, piece in enumerate(three_parts(-row)):
            extra = jnp.where(lane == j, piece, extra)
        g_s[rows, :] = jnp.concatenate([g, extra], axis=1).astype(BF16)
        o_s[o, :, part * d : (part + 1) * d] = out.astype(BF16)

    peak = None
    for st, n in blocks:
        peak = scores(query(at.s, 0), 0, st, n, peak)
    peak_s[0] = peak

    for k in range(1, AHEAD):
        query_copy(k).start()

    def owner(k, _):
        o = lax.rem(at.s - k + n_sp, n_sp)

        @pl.when(k + AHEAD < n_sp)
        def _():
            query_copy(k + AHEAD).start()

        forward(o, 0, o)

        @pl.when(k + 1 < n_sp)
        def _():
            query_copy(k + 1).wait_recv()

        forward(o, 1, lax.rem(at.s - k - 1 + n_sp, n_sp))

        @pl.when(k > 0)
        def _():
            back_copy(2, k, o_s, of, o).start()

        return 0

    lax.fori_loop(0, n_sp, owner, 0)
    local = [pltpu.make_async_copy(o_s.at[at.s], of.at[at.s], lsem.at[2])]

    def block(o, cols, kc, vc, dk, dv, fresh):
        rows = rows_of(o)
        g, q = g_s[rows, :], q_s[rows, :]
        e = e_s[rows, cols]
        ds = (e.astype(F32) * dot(g, vc, 1, 1)).astype(BF16)
        part = dot(ds, kc, 1, 0)
        dq_s[rows, :] = part if fresh else dq_s[rows, :] + part
        return dk + dot(q.T, ds, 1, 0), dv + dot(g[:, :d].T, e, 1, 0)

    def both(dk, dv):
        return jnp.concatenate([dk, dv], axis=0).astype(BF16).T

    def chunk(cols, n, fresh):
        kc, vc = k_s[cols, :], v_s[cols, :]
        zero = jnp.zeros((d, n), F32)
        dk, dv = lax.fori_loop(
            0, n_sp, lambda o, acc: block(o, cols, kc, vc, acc[0], acc[1], fresh), (zero, zero), unroll=4
        )
        return both(dk, dv)

    def chip_columns(z):
        return pl.ds(pl.multiple_of(T + z * (2 * px), 128), 2 * px)

    dt_s[...] = chunk(pl.ds(0, T), T, True)
    sent = [remote(dt_s, dt.at[at.s], ssem.at[5, k + 1], rsem.at[5, k + 1], dev) for k, dev in enumerate(line)]
    local.append(pltpu.make_async_copy(dt_s, dt.at[at.s], lsem.at[3]))

    def chip(k, _):
        z = lax.rem(at.z + k, nz)
        grads = chunk(chip_columns(z), 2 * px, False)
        for core in range(2):
            o = 2 * z + core
            dkv_s[o] = grads[core * px : (core + 1) * px]
            back_copy(4, lax.rem(o - at.s + n_sp, n_sp), dkv_s, dkv, o).start()
        return 0

    lax.fori_loop(1, nz, chip, 0)
    cols = chip_columns(at.z)
    kc, vc = k_s[cols, :], v_s[cols, :]
    zero = jnp.zeros((d, 2 * px), F32)

    def last(j, acc):
        o = 2 * lax.rem(at.z + 1 + lax.div(j, 2), nz) + lax.rem(j, 2)
        acc = block(o, cols, kc, vc, acc[0], acc[1], False)
        dq = (dq_s[rows_of(o), :] * scale).astype(BF16)
        dq_o[o] = jnp.concatenate([dq[:BQ], dq[BQ:]], axis=1)

        @pl.when(o != at.s)
        def _():
            back_copy(3, lax.rem(o - at.s + n_sp, n_sp), dq_o, qf, o).start()

        return acc

    grads = both(*lax.fori_loop(0, n_sp, last, (zero, zero)))
    for core in range(2):
        dkv_s[2 * at.z + core] = grads[core * px : (core + 1) * px]
    sib = at.sib[1]
    back_copy(4, lax.rem(sib - at.s + n_sp, n_sp), dkv_s, dkv, sib).start()
    local.append(pltpu.make_async_copy(dkv_s.at[at.s], dkv.at[at.s], lsem.at[4]))
    local.append(pltpu.make_async_copy(dq_o.at[at.s], qf.at[at.s], lsem.at[5]))
    for cp in local:
        cp.start()
    for k in range(1, n_sp):
        back_copy(2, k, o_s, of, lax.rem(at.s - k + n_sp, n_sp)).wait()
        o = lax.rem(at.s + k, n_sp)
        back_copy(4, k, dkv_s, dkv, o).wait()
        back_copy(3, k, dq_o, qf, o).wait()
    for k in range(1, n_sp):
        query_copy(k).wait_send()
    for cp in keys:
        cp.wait_send()
    for cp in sent:
        cp.wait()
    for cp in local:
        cp.wait()


def attention_call(kv, qin, gin, text, keep, cid):
    n_sp, px, d2 = kv.shape
    T = text.shape[1]
    L = n_sp * px
    d = d2 // 2
    outs = [(n_sp, px // 2, d2), (n_sp, px // 2, d2), (n_sp, px, d2), (n_sp, T, d2)]
    vm = pltpu.VMEM
    return pl.pallas_call(
        functools.partial(attention_kernel, n_sp, 1024),
        out_shape=[jax.ShapeDtypeStruct(s, BF16) for s in outs],
        in_specs=[ANY, ANY, ANY, VM, VM],
        out_specs=[ANY] * 4,
        scratch_shapes=[
            vm((n_sp, px, d2), BF16), vm((n_sp, px // 2, d2), BF16), vm((n_sp, px // 2, d2), BF16), vm((L, d), BF16),
            vm((n_sp, px // 2, d2), BF16),
            vm((n_sp, px // 2, d2), BF16), vm((n_sp, px, d2), BF16), vm((T, d2), BF16),
            vm((T + L, d), BF16), vm((T + L, d2), BF16), vm((2, px // 2, T + L), F32), vm((L, T + L), BF16),
            vm((L, d2), BF16), vm((L, d), F32), vm((2, px // 2, 128), F32),
            pltpu.SemaphoreType.DMA((7,)),
            pltpu.SemaphoreType.DMA((6, n_sp)),
            pltpu.SemaphoreType.DMA((6, n_sp)),
        ],
        compiler_params=params(cid),
        name="attention",
    )(kv, qin, gin, text, keep)


class Mail:
    def __init__(self, ssem, rsem):
        self.ssem, self.rsem, self.sent = ssem, rsem, []

    def send(self, src, dst, dev):
        j = len(self.sent)
        cp = remote(src, dst, self.ssem.at[j], self.rsem.at[j], dev)
        self.sent.append(cp)
        return cp


class Gather:
    def __init__(self, at, nz, ins, outs, dims, ssem, rsem):
        self.at, self.nz, self.ins, self.outs, self.dims = at, nz, ins, outs, dims
        self.ssem, self.rsem = ssem, rsem
        self.sent, self.kinds = {}, {}
        self.order = sorted(range(1, nz), key=lambda k: min(k, nz - k))

    @staticmethod
    def copies(nz):
        return 3 * nz - 1 + 7 * nz

    def view(self, a, ii, k, core, half=None):
        at, nz, r = self.at, self.nz, self.dims[a][1]
        sp = 2 * lax.rem(at.z - k + nz, nz) + core
        if half is None:
            return self.outs[a].at[ii, :, pl.ds(pl.multiple_of(sp * r, r), r), :]
        h = r // 2
        return self.outs[a].at[ii, :, pl.ds(pl.multiple_of(sp * r + half * h, h), h), :]

    def send(self, a, kind, src, dst, dev):
        j = self.kinds.setdefault(kind, len(self.kinds))
        self.sent[a, kind] = remote(src, dst, self.ssem.at[a, j], self.rsem.at[a, j], dev)

    def forward(self, a, kind, ref, dev):
        self.send(a, kind, ref, ref, dev)

    def near(self, a):
        at = self.at
        own = self.view(a, at.i, 0, at.c)
        self.send(a, ("x", 0), self.ins[a], own, at.xn)
        self.send(a, ("y", 0), self.ins[a], own, at.yn)
        self.send(a, ("s", 0), self.ins[a], own, at.sib)

    def along(self, a, ks):
        for k in ks:
            self.send(a, ("z", k), self.ins[a], self.view(a, self.at.i, 0, self.at.c), self.at.zp(k, self.nz))

    def second(self, a, ks=None):
        at = self.at
        for k in self.order if ks is None else ks:
            self.sent[a, ("z", k)].wait_recv()
            got = self.view(a, at.i, k, at.c)
            self.forward(a, ("x", k), got, at.xn)
            self.forward(a, ("y", k), got, at.yn)
            self.forward(a, ("s", k), got, at.sib)

    def third(self, a):
        at = self.at
        for k in [0] + self.order:
            self.sent[a, ("x", k)].wait_recv()
            self.forward(a, ("da", k), self.view(a, at.ix, k, at.c, 0), at.yn)
            self.forward(a, ("sx", k), self.view(a, at.ix, k, at.c), at.sib)
            self.sent[a, ("y", k)].wait_recv()
            self.forward(a, ("db", k), self.view(a, at.iy, k, at.c, 1), at.xn)
            self.forward(a, ("sy", k), self.view(a, at.iy, k, at.c), at.sib)

    def fourth(self, a):
        at = self.at
        for k in [0] + self.order:
            self.sent[a, ("da", k)].wait_recv()
            self.forward(a, ("sa", k), self.view(a, at.id, k, at.c, 0), at.sib)
            self.sent[a, ("db", k)].wait_recv()
            self.forward(a, ("sb", k), self.view(a, at.id, k, at.c, 1), at.sib)

    def complete(self, a):
        for (b, kind), cp in self.sent.items():
            if b == a and kind[0][0] == "s":
                cp.wait_recv()

    def finish(self):
        for cp in self.sent.values():
            cp.wait_send()


def img_peers(at):
    return [(lax.rem(at.i + k, 4), at.s) for k in range(1, 4)]


FORWARD_MAIL = 4 * 3 + 3 + 2 * 7 + 4 + 7 + 2 * (2 + 7) + 7


def forward_kernel(nz, width, dims, *refs):
    na = len(dims)
    chunks, refs = refs[:na], refs[na:]
    x, cot, temb, cap, w_emb, w_cap, gains, biases = refs[:8]
    outs, refs = refs[8 : 8 + na], refs[8 + na :]
    hidden_o, a0_o, res_o, a1_o, g_o, normed, kv, qf = refs[:8]
    st0, st1, st2, rows, ca, cb, ra, rb, ha, hb, kv_all, cap_all, emb_all = refs[8:21]
    refs = refs[21:]
    weights, refs = refs[:na], refs[na:]
    (ssem, rsem, lsem, msend, mrecv, g_s, emb, affine, mine, every, edge_s, xa, xb, ca_s, cb_s, ha_s, hb_s, ra_s, rb_s,
     aff_s, emb_s, cap_s, part, part_r, kv_s, kv_r, mod_s, mod_r, acts, hidden, res) = refs
    n_sp = 2 * nz
    at = Place()
    line = [at.rp(k, n_sp) for k in range(1, n_sp)]
    grid = img_peers(at)
    greet(line + grid)
    mail = Mail(msend, mrecv)
    got = Gather(at, nz, chunks, weights, dims, ssem, rsem)
    PROJ, IN, OUT, QKV = range(4)
    px, c = x.shape
    height = px // width
    d = c // HEADS
    tokens = cap.shape[0]
    e = cap.shape[1] // 4
    half = px // 2
    local = []

    def copy(src, dst):
        cp = pltpu.make_async_copy(src, dst, lsem.at[len(local)])
        cp.start()
        local.append(cp)
        return cp

    embedded = silu(temb[...].astype(F32)).astype(BF16).astype(F32)
    for j in range(4):
        emb[j] = jnp.broadcast_to(embedded[:, j * e : (j + 1) * e], (8, e))
    affine[0:3] = gains[...].astype(F32)
    affine[3:6] = biases[...].astype(F32)

    def publish(j, v, edges):
        pair = channel_stats(v)
        put_rows(mine.at[j], pair)
        out = []
        for ref, above, below in edges:
            if ref is None:
                edge_s[j - 1, 0] = (v[px - width :] - pair[0]).astype(BF16)
                edge_s[j - 1, 1] = (v[:width] - pair[0]).astype(BF16)
                out.append(mail.send(edge_s.at[j - 1, 0], above, line[0]))
                out.append(mail.send(edge_s.at[j - 1, 1], below, line[-1]))
            else:
                out.append(mail.send(ref.at[px - width :], above, line[0]))
                out.append(mail.send(ref.at[:width], below, line[-1]))
        for dev in line:
            out.append(mail.send(mine.at[j], every.at[j, at.s], dev))
        every[j, at.s] = mine[j]
        return out

    def fold(v):
        return jnp.concatenate([v[:half], v[half:]], axis=1)

    greeted(n_sp + 2)
    close, far = got.order[:2], got.order[2:]
    got.along(PROJ, got.order)
    got.near(PROJ)
    got.along(IN, close)
    got.near(IN)
    stat0 = publish(0, x[...].astype(F32), [(x, xa, xb), (cot, ca_s, cb_s)])
    round1 = []
    share = tokens // 2
    part_tokens = pl.ds(pl.multiple_of(at.c * share, share), share)
    for dev in grid:
        round1.append(mail.send(affine, aff_s.at[at.i], dev))
        round1.append(mail.send(emb.at[dev[0]], emb_s.at[at.i], dev))
        round1.append(
            mail.send(cap.at[part_tokens, pl.ds(pl.multiple_of(dev[0] * e, e), e)], cap_s.at[at.i, part_tokens], dev)
        )
    own_cap = copy(cap.at[:, pl.ds(pl.multiple_of(at.i * e, e), e)], cap_s.at[at.i])
    aff_s[at.i] = affine[...]
    emb_s[at.i] = emb[at.i]
    got.near(OUT)
    own = [copy(got.ins[a], got.view(a, at.i, 0, at.c)) for a in range(na)]
    got.second(PROJ)
    got.second(IN, close[:1])
    got.along(IN, far)
    got.second(IN, close[1:])
    got.third(PROJ)
    got.near(QKV)
    got.along(OUT, close)
    got.second(IN, far)
    got.along(OUT, far)
    got.fourth(PROJ)
    got.third(IN)
    got.second(OUT)
    got.along(QKV, got.order)

    own_cap.wait()
    for cp in round1:
        cp.wait_recv()
    halves = []
    for dev in grid:
        here = cap_s.at[dev[0], part_tokens]
        halves.append(mail.send(here, here, at.sib))
    for cp in halves:
        cp.wait_recv()
    for j in range(4):
        part[j, :tokens] = dot(cap_s[j], w_cap[...], 1, 0)
        part[j, tokens:] = dot(emb_s[j].astype(BF16), w_emb[...], 1, 0)
    round2 = [mail.send(part.at[dev[0]], part_r.at[at.i], dev) for dev in grid]
    part_r[at.i] = part[at.i]
    cap_all[...] = cap_s[...]
    emb_all[...] = jnp.concatenate([emb_s[j][0:1] for j in range(4)] + [jnp.zeros((4, e), F32)])
    aff = jnp.concatenate([aff_s[j] for j in range(4)], axis=1)
    rows[...] = jnp.zeros_like(rows)
    for j in range(3):
        rows[j, 0:1] = aff[j : j + 1]
        rows[j, 1:2] = aff[3 + j : 4 + j]
        rows[j, 2:3] = jnp.ones((1, c), F32)

    has_up, has_dn = edge_flags(n_sp, at.s)

    def restore(j, above, below, above_o, below_o):
        for src, dst, dev in ((above, above_o, line[-1]), (below, below_o, line[0])):
            dst[...] = src[...].astype(F32) + get_rows(every[j, dev[1]])[0]

    def activate(j, v, above, below):
        center, inverse = combine_stats(every.at[j], px)
        mul = inverse * rows[j, 0:1] * rows[j, 2:3]
        add = rows[j, 1:2] * rows[j, 2:3] + rows[j, 3:4]
        for r in range(height + 2):
            top, end = r == 0, r == height + 1
            t = above[...] if top else below[...] if end else v[(r - 1) * width : r * width, :]
            t = silu((t.astype(F32) - center) * mul + add)
            if top:
                t = t * has_up
            elif end:
                t = t * has_dn
            shifted(acts.at[j], r, width, t)

    def taps(w, out, t0, t1, base):
        a3 = acts.at[0 if base is None else 1]

        def one(tap, _):
            i, j = lax.div(tap, 3), lax.rem(tap, 3)
            lhs = a3[j, pl.ds(pl.multiple_of(i * width, width), px), :]
            first = 0.0 if base is None else base[...].astype(F32)
            out[...] = dot(lhs, joined(w, tap), 1, 1) + jnp.where(tap > 0, out[...], first)
            return 0

        lax.fori_loop(t0, t1, one, 0)

    for cp in stat0:
        cp.wait_recv()
    activate(0, x, xa, xb)
    copy(acts.at[0], a0_o)
    got.fourth(IN)
    for cp in own:
        cp.wait()
    got.complete(IN)
    copy(weights[IN], outs[IN])
    taps(weights[IN], hidden, 0, 3, None)
    got.second(QKV)
    got.complete(PROJ)
    g = dot(cot[...], joined(weights[PROJ], 0), 1, 0).astype(BF16)
    for h in range(HEADS):
        g_s[h] = fold(g[:, h * d : (h + 1) * d])
    copy(weights[PROJ], outs[PROJ])
    round_g = [mail.send(g_s.at[dev[1]], g_o.at[at.s], dev) for dev in line]
    copy(g_s.at[at.s], g_o.at[at.s])
    taps(weights[IN], hidden, 3, 6, None)
    got.third(OUT)
    taps(weights[IN], hidden, 6, 9, None)
    stat1 = publish(1, hidden[...], [(None, ha_s, hb_s)])
    copy(hidden, hidden_o)
    for cp in round2:
        cp.wait_recv()
    total = part_r[0] + part_r[1] + part_r[2] + part_r[3]
    kv_s[...] = total[:tokens].astype(BF16)
    mod_s[...] = total[tokens:]
    round3 = []
    for dev in line:
        round3.append(mail.send(kv_s, kv_r.at[at.s], dev))
        round3.append(mail.send(mod_s, mod_r.at[at.s], dev))
    kv_r[at.s] = kv_s[...]
    mod_r[at.s] = mod_s[...]
    got.fourth(OUT)
    got.third(QKV)
    for cp in round3 + stat1:
        cp.wait_recv()
    kv_all[...] = kv_r[...]
    mod = jnp.concatenate([mod_r[j][0:1] for j in range(n_sp)], axis=1)
    rows[1, 2:3] = 1.0 + mod[:, :c]
    rows[1, 3:4] = mod[:, c:]

    restore(1, ha_s, hb_s, ha, hb)
    activate(1, hidden, ha, hb)
    copy(acts.at[1], a1_o)
    got.fourth(QKV)
    got.complete(OUT)
    copy(weights[OUT], outs[OUT])
    taps(weights[OUT], res, 0, 9, x)
    stat2 = publish(2, res[...], [(None, ra_s, rb_s)])
    copy(res, res_o)
    for dst, src in ((ca, ca_s), (cb, cb_s)):
        dst[...] = src[...]
    got.complete(QKV)
    copy(weights[QKV], outs[QKV])
    wq = joined(weights[QKV], 0)

    for cp in stat2:
        cp.wait_recv()
    center, inverse = combine_stats(every.at[2], px)
    n = ((res[...] - center) * (inverse * rows[2, 0:1]) + rows[2, 1:2]).astype(BF16)
    normed[...] = n
    k = dot(n, wq[c : 2 * c], 1, 1).astype(BF16)
    v = dot(n, wq[2 * c :], 1, 1).astype(BF16)
    q = (dot(n, wq[:c], 1, 1).astype(BF16).astype(F32) * (d ** -0.5)).astype(BF16)
    for h in range(HEADS):
        lanes = slice(h * d, (h + 1) * d)
        kv[h] = jnp.concatenate([k[:, lanes], v[:, lanes]], axis=1)
        qf[h] = fold(q[:, lanes])
    restore(2, ra_s, rb_s, ra, rb)
    st0[...] = every[0]
    st1[...] = every[1]
    st2[...] = every[2]
    for cp in local[1 + na :]:
        cp.wait()
    got.finish()
    for cp in round_g:
        cp.wait_recv()
    for cp in mail.sent:
        cp.wait_send()


def forward_call(chunks, x, cot, temb, cap, w_emb, w_cap, gains, biases, nz, width, cid):
    dims = [c.shape[:2] for c in chunks]
    na = len(dims)
    n_sp = 2 * nz
    px, c = x.shape
    padded = px + 2 * width
    tokens, wide = cap.shape
    e = wide // 4
    d2 = 2 * c // HEADS
    big = [((4, t, n_sp * r, 128), BF16) for t, r in dims]
    edge16, edge32 = ((width, c), BF16), ((width, c), F32)
    stat = ((n_sp, 8, c // 4), F32)
    outs = big + [
        ((px, c), F32), ((3, padded, c), BF16), ((px, c), F32), ((3, padded, c), BF16),
        ((n_sp, px // 2, d2), BF16), ((px, c), BF16), ((HEADS, px, d2), BF16), ((HEADS, px // 2, d2), BF16),
        stat, stat, stat, ((3, 8, c), F32), edge16, edge16, edge32, edge32, edge32, edge32,
        ((n_sp, tokens, 128), BF16), ((4, tokens, e), BF16), ((8, e), F32),
    ]
    vm = pltpu.VMEM
    return pl.pallas_call(
        functools.partial(forward_kernel, nz, width, dims),
        out_shape=[jax.ShapeDtypeStruct(s, ty) for s, ty in outs],
        in_specs=[ANY] * na + [VM, VM, VM, ANY] + [VM] * 4,
        out_specs=[ANY] * (na + 5) + [VM] * (len(outs) - na - 5),
        scratch_shapes=[vm(s, ty) for s, ty in big]
        + [
            pltpu.SemaphoreType.DMA((na, Gather.copies(nz))),
            pltpu.SemaphoreType.DMA((na, Gather.copies(nz))),
            pltpu.SemaphoreType.DMA((2 * na + 6,)),
            pltpu.SemaphoreType.DMA((FORWARD_MAIL,)),
            pltpu.SemaphoreType.DMA((FORWARD_MAIL,)),
            vm((HEADS, px // 2, d2), BF16), vm((4, 8, e), F32), vm((8, 128), F32),
            vm((3, 8, c // 4), F32), vm((3, n_sp, 8, c // 4), F32), vm((2, 2, width, c), BF16),
        ]
        + [vm(*edge16)] * 8
        + [
            vm((4, 8, 128), F32), vm((4, 8, e), F32), vm((4, tokens, e), BF16),
            vm((4, tokens + 8, 128), F32), vm((4, tokens + 8, 128), F32),
            vm((tokens, 128), BF16), vm((n_sp, tokens, 128), BF16), vm((8, 128), F32), vm((n_sp, 8, 128), F32),
            vm((2, 3, padded, c), BF16), vm((px, c), F32), vm((px, c), F32),
        ],
        compiler_params=params(cid),
        name="forward",
    )(*chunks, x, cot, temb, cap, w_emb, w_cap, gains, biases)


class Reducer:
    NAMES = ("d", "sb", "da", "db", "rx", "ry", "r", "zr")

    def __init__(self, at, nz, arrays, ssem, rsem):
        self.at, self.nz, self.arrays = at, nz, arrays
        self.ssem, self.rsem = ssem, rsem
        self.sent, self.groups = {}, []

    @staticmethod
    def buffers(nz, t, r):
        return [
            pltpu.VMEM((2, 4, t, nz, r, 128), BF16),
            pltpu.VMEM((4, t, nz, r, 128), BF16),
            pltpu.VMEM((t, nz, r // 2, 128), BF16),
            pltpu.VMEM((t, nz, r // 2, 128), BF16),
            pltpu.VMEM((t, nz, r, 128), BF16),
            pltpu.VMEM((t, nz, r, 128), BF16),
            pltpu.VMEM((t, nz, r, 128), BF16),
            pltpu.VMEM((nz - 1, t, r, 128), BF16),
        ]

    def send(self, g, j, src, dst, dev):
        self.sent[g, j] = remote(src, dst, self.ssem.at[g, j], self.rsem.at[g, j], dev)

    def add(self, a, t0, t1):
        g = len(self.groups)
        self.groups.append((a, t0, t1))
        b = self.arrays[a][1]
        self.send(g, 0, b["d"].at[1 - self.at.c, :, t0:t1], b["sb"].at[:, t0:t1], self.at.sib)

    def run(self, stage, *groups):
        one = (self.stage1, self.stage2, self.stage3, self.stage4)[stage - 1]
        for g in groups:
            one(g, *self.groups[g])

    def stage1(self, g, a, t0, t1):
        b, at = self.arrays[a][1], self.at
        d, sb = b["d"], b["sb"]
        self.sent[g, 0].wait_recv()
        n = t1 - t0

        def add(j, _):
            ii, tt = lax.div(j, n), t0 + lax.rem(j, n)
            d[at.c, ii, tt] = (d[at.c, ii, tt].astype(F32) + sb[ii, tt].astype(F32)).astype(BF16)
            return 0

        lax.fori_loop(0, 4 * n, add, 0)
        h = d.shape[4] // 2
        self.send(g, 1, d.at[at.c, at.id, t0:t1, :, :h], b["da"].at[t0:t1], at.yn)
        self.send(g, 2, d.at[at.c, at.id, t0:t1, :, h:], b["db"].at[t0:t1], at.xn)

    def stage2(self, g, a, t0, t1):
        b, at = self.arrays[a][1], self.at
        d = b["d"]
        h = d.shape[4] // 2
        self.sent[g, 1].wait_recv()
        self.sent[g, 2].wait_recv()

        def add(tt, _):
            d[at.c, at.ix, tt, :, :h] = (
                d[at.c, at.ix, tt, :, :h].astype(F32) + b["da"][tt].astype(F32)
            ).astype(BF16)
            d[at.c, at.iy, tt, :, h:] = (
                d[at.c, at.iy, tt, :, h:].astype(F32) + b["db"][tt].astype(F32)
            ).astype(BF16)
            return 0

        lax.fori_loop(t0, t1, add, 0)
        self.send(g, 3, d.at[at.c, at.ix, t0:t1], b["rx"].at[t0:t1], at.xn)
        self.send(g, 4, d.at[at.c, at.iy, t0:t1], b["ry"].at[t0:t1], at.yn)

    def stage3(self, g, a, t0, t1):
        b, at = self.arrays[a][1], self.at
        self.sent[g, 3].wait_recv()
        self.sent[g, 4].wait_recv()

        def add(tt, _):
            total = b["d"][at.c, at.i, tt].astype(F32) + b["rx"][tt].astype(F32) + b["ry"][tt].astype(F32)
            b["r"][tt] = total.astype(BF16)
            return 0

        lax.fori_loop(t0, t1, add, 0)
        for k in range(1, self.nz):
            there = lax.rem(at.z + k, self.nz)
            self.send(g, 4 + k, b["r"].at[t0:t1, there], b["zr"].at[k - 1, t0:t1], at.zp(k, self.nz))

    def stage4(self, g, a, t0, t1):
        (out, b), at = self.arrays[a], self.at
        for k in range(1, self.nz):
            self.sent[g, 4 + k].wait_recv()

        def add(tt, _):
            total = (
                b["d"][at.c, at.i, tt, at.z].astype(F32)
                + b["rx"][tt, at.z].astype(F32)
                + b["ry"][tt, at.z].astype(F32)
            )
            for k in range(1, self.nz):
                total = total + b["zr"][k - 1, tt].astype(F32)
            out[tt] = total
            return 0

        lax.fori_loop(t0, t1, add, 0)

    def finish(self):
        for cp in self.sent.values():
            cp.wait_send()


BACK_MAIL = 6 + 14 + 6 + 3 + 7 + 9 + 9
BACK_GROUPS = 7
BIG = 12


def conv_taps(t0, t1, w, ring, rsem, one):
    slots = ring.shape[0]

    def step(tap, _):
        slot = lax.rem(tap, slots)
        pltpu.make_async_copy(w.at[:, tap], ring.at[slot], rsem.at[slot]).wait()
        one(tap, jnp.concatenate([ring[slot, j] for j in range(4)], axis=-1))

        @pl.when(tap + slots < 9)
        def _():
            pltpu.make_async_copy(w.at[:, tap + slots], ring.at[slot], rsem.at[slot]).start()

        return 0

    lax.fori_loop(t0, t1, step, 0)


def ring_start(w, ring, rsem):
    for j in range(ring.shape[0]):
        pltpu.make_async_copy(w.at[:, j], ring.at[j], rsem.at[j]).start()


def backward_kernel(nz, width, *refs):
    hbm, refs = refs[:BIG], refs[BIG:]
    w_in, w_out = refs[:2]
    (st0, st1, st2, rows, ca, cb, ra, rb, ha, hb, dt_all, cap_all, emb_all, w_emb, w_cap, temb) = refs[2:18]
    output, image_grad, s_in, s_out, s_small, g_temb, g_cap, g_wemb, g_wcap, g_aff = refs[18:28]
    refs = refs[28:]
    big, refs = refs[:BIG], refs[BIG:]
    bufs = [dict(zip(Reducer.NAMES, refs[8 * a : 8 * a + 8])) for a in range(3)]
    (bsem, gsend, grecv, msend, mrecv, ring, rsem, g3, gt, acc, ng, pre_grad, res_grad,
     mine, every, edge_s, na, nb, pa, pb, tg_s, tg_r, mod_s, mod_r,
     gc_s, gc_r, pe_s, pe_r, gs_s, gs_r, ps_s, ps_r, aff_s, aff_r) = refs[24:]
    n_sp = 2 * nz
    at = Place()
    line = [at.rp(k, n_sp) for k in range(1, n_sp)]
    grid = img_peers(at)
    greet(line + grid)
    loads = []
    for j in range(BIG):
        cp = pltpu.make_async_copy(hbm[j], big[j], bsem.at[j])
        cp.start()
        loads.append(cp)
    of, qf, dkv, w_qkv, w_proj, res, cot, normed, a3_out, hidden, a3_in, x = big
    ring_start(w_out, ring, rsem)
    mail = Mail(msend, mrecv)
    red = Reducer(at, nz, [(s_out, bufs[0]), (s_small, bufs[1]), (s_in, bufs[2])], gsend, grecv)
    px, c = res.shape
    height = px // width
    members = px * n_sp * (c // GROUPS)
    d = c // HEADS
    cols = 3 * c // n_sp

    def publish(j, rows01, edges):
        out = []
        put_rows(mine.at[j], rows01)
        for ref, above, below in edges:
            mean = rows01[0] / px
            edge_s[j - 1, 0] = (ref[px - width :, :] - mean).astype(BF16)
            edge_s[j - 1, 1] = (ref[:width, :] - mean).astype(BF16)
            out.append(mail.send(edge_s.at[j - 1, 0], above, line[0]))
            out.append(mail.send(edge_s.at[j - 1, 1], below, line[-1]))
        for dev in line:
            out.append(mail.send(mine.at[j], every.at[j, at.s], dev))
        every[j, at.s] = mine[j]
        return out

    for j in range(8):
        loads[j].wait()
    unfold = lambda v: jnp.concatenate([v[:, :d], v[:, d:]], axis=0)
    att = jnp.concatenate([unfold(of[h]) for h in range(HEADS)], axis=1)
    pg = jnp.concatenate(
        [unfold(qf[h]) for h in range(HEADS)]
        + [dkv[h][:, :d] for h in range(HEADS)]
        + [dkv[h][:, d:] for h in range(HEADS)],
        axis=1,
    )
    wq, wp = joined(w_qkv), joined(w_proj)
    ng[...] = dot(pg, wq, 1, 0)
    center2, inverse2 = combine_stats(st2, px)
    hat = (res[...] - center2) * inverse2
    u = ng[...]
    sums = (jnp.sum(u, axis=0, keepdims=True), jnp.sum(u * hat, axis=0, keepdims=True))
    greeted(n_sp + 2)
    round_2 = publish(2, sums, [(ng, na, nb)])
    gq = dot(pg, normed[...], 0, 0).astype(BF16)
    go = dot(cot[...], att, 0, 0).astype(BF16)
    small = bufs[1]["d"]
    for j in range(n_sp):
        for b in range(4):
            lanes = slice(b * 128, (b + 1) * 128)
            small[j % 2, b, 0, j // 2, :cols] = gq[j * cols : (j + 1) * cols, lanes]
            small[j % 2, b, 0, j // 2, cols:] = go[j * (c // n_sp) : (j + 1) * (c // n_sp), lanes]
    red.add(1, 0, 1)
    output[...] = (res[...] + dot(att, wp, 1, 1)).astype(BF16)

    first = 2 * lax.rem(at.s, nz)
    value = lax.div(at.s, nz)
    halves = []
    for j in range(2):
        blk = dt_all[first + j].astype(F32)
        halves.append(jnp.where(value > 0, blk[:, d:], blk[:, :d]))
    tg_s[...] = jnp.concatenate(halves, axis=1).astype(BF16)
    round_a = [mail.send(tg_s, tg_r.at[at.i], dev) for dev in grid]
    tg_r[at.i] = tg_s[...]

    has_up, has_dn = edge_flags(n_sp, at.s)

    def upstream(j, uu, ua, ub, center, inverse, yy, ya, yb, base, keep):
        total = combine_sums(every[j])
        mul = rows[j, 0:1] * rows[j, 2:3]
        back = group_total(total * mul) / members
        s1, s2 = back[0:1, :], back[1:2, :]
        for r in range(height + 2):
            cut = slice((r - 1) * width, r * width)
            top, end = r == 0, r == height + 1
            if top or end:
                near = line[-1] if top else line[0]
                un = (ua if top else ub)[...].astype(F32) + get_rows(every[j, near[1]])[0] / px
            else:
                un = uu[cut, :]
            yn = ya[...] if top else yb[...] if end else yy[cut, :]
            g = inverse * (un * mul - s1 - (yn - center) * inverse * s2)
            if base:
                g = g + (base[1][...] if top else base[2][...] if end else base[0][cut, :]).astype(F32)
            if top:
                g = g * has_up
            elif end:
                g = g * has_dn
            elif keep is not None:
                keep[cut, :] = g
            shifted(g3, r, width, g.astype(BF16).astype(F32))
        gt[...] = g3[1, width : width + px, :].T
        return total

    def weight_taps(a, t0, t1):
        dst = bufs[a]["d"]
        a3 = a3_in if a == 2 else a3_out

        def one(tap, _):
            i, j = lax.div(tap, 3), lax.rem(tap, 3)
            part = dot(gt[...], a3[j, pl.ds(pl.multiple_of(i * width, width), px), :], 1, 0).astype(BF16)
            r = c // n_sp
            for k in range(n_sp):
                for b in range(4):
                    dst[k % 2, b, tap, k // 2] = part[k * r : (k + 1) * r, b * 128 : (b + 1) * 128]
            return 0

        lax.fori_loop(t0, t1, one, 0)
        red.add(a, t0, t1)

    def input_taps(w):
        def one(tap, wt):
            i, j = lax.div(tap, 3), lax.rem(tap, 3)
            lhs = g3[2 - j, pl.ds(pl.multiple_of((2 - i) * width, width), px), :]
            acc[...] = dot(lhs, wt, 1, 0) + jnp.where(tap > 0, acc[...], 0.0)

        conv_taps(0, 9, w, ring, rsem, one)

    for cp in round_2:
        cp.wait_recv()
    t2 = upstream(2, ng, na, nb, center2, inverse2, res, ra, rb, (cot, ca, cb), res_grad)
    red.run(1, 0)
    loads[8].wait()
    for tap in (0, 3, 6):
        weight_taps(0, tap, tap + 3)
    red.run(2, 0)
    input_taps(w_out)
    ring_start(w_in, ring, rsem)
    for j in range(9, BIG):
        loads[j].wait()
    center1, inverse1 = combine_stats(st1, px)
    hat = (hidden[...] - center1) * inverse1
    gain1, bias1, fac1 = rows[1, 0:1], rows[1, 1:2], rows[1, 2:3]
    v = acc[...] * silu_slope(hat * (gain1 * fac1) + (bias1 * fac1 + rows[1, 3:4]))
    pre_grad[...] = v
    sums = (jnp.sum(v, axis=0, keepdims=True), jnp.sum(v * hat, axis=0, keepdims=True))
    round_1 = publish(1, sums, [(pre_grad, pa, pb)])
    red.run(1, 1, 2, 3)
    red.run(3, 0)

    exact = lambda a, b, ca_, cb_: lax.dot_general(
        a, b, (((ca_,), (cb_,)), ((), ())), preferred_element_type=F32, precision=PRECISE
    )
    tokens = tg_s.shape[0]
    share = tokens // n_sp
    for cp in round_a:
        cp.wait_recv()
    flat_tg = tg_r[...].reshape(4 * tokens, 128)
    g_wcap[...] = dot(cap_all[...].reshape(4 * tokens, cap_all.shape[2]), flat_tg, 0, 0)
    gc_s[...] = dot(flat_tg, w_cap[...], 1, 1).astype(BF16).reshape(gc_s.shape)
    round_b = []
    for dev in line:
        cut = pl.ds(pl.multiple_of(dev[1] * share, share), share)
        round_b.append(mail.send(gc_s.at[:, cut, :], gc_r.at[at.s], dev))
    gc_r[at.s] = gc_s[:, pl.ds(pl.multiple_of(at.s * share, share), share), :]

    for cp in round_1:
        cp.wait_recv()
    t1 = upstream(1, pre_grad, pa, pb, center1, inverse1, hidden, ha, hb, None, None)
    mod = jnp.concatenate([t1[1:2] * gain1 + t1[0:1] * bias1, t1[0:1]], axis=1)
    for j in range(n_sp):
        mod_s[j] = jnp.broadcast_to(mod[:, j * 128 : (j + 1) * 128], (8, 128))
    round_m = [mail.send(mod_s.at[at.s], mod_r.at[at.i], dev) for dev in grid]
    mod_r[at.i] = mod_s[at.s]
    red.run(2, 1)
    weight_taps(2, 0, 3)
    red.run(2, 2)
    weight_taps(2, 3, 6)
    red.run(2, 3)
    weight_taps(2, 6, 9)
    red.run(1, 4, 5, 6)
    input_taps(w_in)

    center0, inverse0 = combine_stats(st0, px)
    hat = (x[...].astype(F32) - center0) * inverse0
    gain0 = rows[0, 0:1]
    v = acc[...] * silu_slope(hat * gain0 + rows[0, 1:2])
    acc[...] = v
    sums = (jnp.sum(v, axis=0, keepdims=True), jnp.sum(v * hat, axis=0, keepdims=True))
    round_0 = publish(0, sums, [])
    red.run(4, 0)
    red.run(3, 1)
    red.run(2, 4)
    for cp in round_m:
        cp.wait_recv()
    mods = jnp.concatenate([mod_r[j][0:1] for j in range(4)] + [jnp.zeros((4, 128), F32)])
    emb_t = emb_all[...].T
    g_wemb[...] = sum(emb_t[:, j : j + 1] * mods[j : j + 1] for j in range(4))
    pe_s[...] = exact(mods, w_emb[...].astype(F32), 1, 1)
    round_p = [mail.send(pe_s, pe_r.at[at.s], dev) for dev in line]
    pe_r[at.s] = pe_s[...]
    for cp in round_0:
        cp.wait_recv()
    t0 = combine_sums(every[0])
    zero = jnp.zeros((2, c), F32)
    aff = jnp.concatenate([t0[1:2], t1[1:2] * fac1, t2[1:2], t0[0:1], t1[0:1] * fac1, t2[0:1], zero])
    for j in range(4):
        aff_s[j] = aff[:, j * 128 : (j + 1) * 128]
    round_e = [mail.send(aff_s.at[dev[0]], aff_r.at[at.i], dev) for dev in grid]
    aff_r[at.i] = aff_s[at.i]
    total = group_total(t0 * gain0) / members
    image_grad[...] = res_grad[...] + inverse0 * (acc[...] * gain0 - total[0:1] - hat * total[1:2])
    for g in (2, 3):
        red.run(3, g)
        red.run(2, g + 3)
    for cp in round_b + round_p:
        cp.wait_recv()
    gc = gc_r[0].astype(F32)
    pe = pe_r[0]
    for j in range(1, n_sp):
        gc = gc + gc_r[j].astype(F32)
        pe = pe + pe_r[j]
    gs_s[...] = gc
    for j in range(4):
        ps_s[j] = jnp.broadcast_to(pe[j : j + 1], pe.shape)
    round_c = []
    for dev in grid:
        round_c.append(mail.send(gs_s.at[dev[0]], gs_r.at[at.i], dev))
        round_c.append(mail.send(ps_s.at[dev[0]], ps_r.at[at.i], dev))
    gs_r[at.i] = gs_s[at.i]
    ps_r[at.i] = ps_s[at.i]
    red.run(4, 1, 2, 3)
    red.run(3, 4, 5, 6)
    red.run(4, 4, 5, 6)
    red.finish()
    for cp in round_c + round_e:
        cp.wait_recv()
    g_cap[...] = jnp.concatenate([gs_r[j] for j in range(4)], axis=1)
    g_temb[...] = jnp.concatenate([ps_r[j] for j in range(4)], axis=1) * silu_slope(temb[...].astype(F32))
    g_aff[...] = aff_r[0] + aff_r[1] + aff_r[2] + aff_r[3]
    for cp in mail.sent:
        cp.wait_send()


def backward_call(big, w_in, w_out, small, nz, width, cid):
    px, c = big[5].shape
    n_sp = 2 * nz
    padded = px + 2 * width
    r = c // n_sp
    rs = (big[3].shape[1] + big[4].shape[1]) // n_sp
    dt_all, cap_all = small[10], small[11]
    tokens = dt_all.shape[1]
    e = cap_all.shape[2]
    share = tokens // n_sp
    outs = [
        ((px, c), BF16), ((px, c), F32), ((9, r, 128), F32), ((9, r, 128), F32), ((1, rs, 128), F32),
        ((8, 4 * e), F32), ((share, 4 * e), F32), ((e, 128), F32), ((e, 128), F32), ((8, 128), F32),
    ]
    vm = pltpu.VMEM
    return pl.pallas_call(
        functools.partial(backward_kernel, nz, width),
        out_shape=[jax.ShapeDtypeStruct(s, ty) for s, ty in outs],
        in_specs=[ANY] * (len(big) + 2) + [VM] * len(small),
        out_specs=[VM] * len(outs),
        scratch_shapes=[vm(v.shape, v.dtype) for v in big]
        + Reducer.buffers(nz, 9, r) + Reducer.buffers(nz, 1, rs) + Reducer.buffers(nz, 9, r)
        + [
            pltpu.SemaphoreType.DMA((len(big),)),
            pltpu.SemaphoreType.DMA((BACK_GROUPS, 4 + nz)),
            pltpu.SemaphoreType.DMA((BACK_GROUPS, 4 + nz)),
            pltpu.SemaphoreType.DMA((BACK_MAIL,)),
            pltpu.SemaphoreType.DMA((BACK_MAIL,)),
            vm((3, 4, c, 128), BF16),
            pltpu.SemaphoreType.DMA((3,)),
            vm((3, padded, c), BF16), vm((c, px), BF16),
            vm((px, c), F32), vm((px, c), F32), vm((px, c), F32), vm((px, c), F32),
            vm((3, 8, c // 4), F32), vm((3, n_sp, 8, c // 4), F32), vm((2, 2, width, c), BF16),
            vm((width, c), BF16), vm((width, c), BF16), vm((width, c), BF16), vm((width, c), BF16),
            vm((tokens, 128), BF16), vm((4, tokens, 128), BF16),
            vm((n_sp, 8, 128), F32), vm((4, 8, 128), F32),
            vm((4, tokens, e), BF16), vm((n_sp, 4, share, e), BF16),
            vm((8, e), F32), vm((n_sp, 8, e), F32),
            vm((4, share, e), F32), vm((4, share, e), F32),
            vm((4, 8, e), F32), vm((4, 8, e), F32),
            vm((4, 8, 128), F32), vm((4, 8, 128), F32),
        ],
        compiler_params=params(cid),
        name="backward",
    )(*big, w_in, w_out, *small)


def emit_kernel(cut, *refs):
    ins, outs, mids, loads, stores = refs[:10], refs[10:22], refs[22:31], refs[31], refs[32]
    output, image, s_in, s_out, s_small, g_temb, g_cap, g_wemb, g_wcap, g_aff = ins
    pairs = [
        (output, outs[0]), (image, outs[1]), (g_cap, outs[3]), (s_in, outs[4]), (s_out, outs[5]), (g_wemb, outs[6]),
        (s_small.at[0, :cut], outs[7]), (g_wcap, outs[8]), (s_small.at[0, cut:], outs[9]),
    ]
    copies = [pltpu.make_async_copy(src, mid, loads.at[j]) for j, ((src, _), mid) in enumerate(zip(pairs, mids))]
    for cp in copies:
        cp.start()
    backs = []
    for j, cp in enumerate(copies):
        cp.wait()
        backs.append(pltpu.make_async_copy(mids[j], pairs[j][1], stores.at[j]))
        backs[-1].start()
    outs[2][...] = g_temb[0:1, :]
    outs[10][...] = g_aff[0:3, :]
    outs[11][...] = g_aff[3:6, :]
    for cp in backs:
        cp.wait()


def emit_call(parts, cut):
    output, image, s_in, s_out, s_small, g_temb, g_cap, g_wemb, g_wcap, g_aff = parts
    rest = s_small.shape[1] - cut
    like = lambda v: jax.ShapeDtypeStruct(v.shape, v.dtype)
    f32 = lambda *s: jax.ShapeDtypeStruct(s, F32)
    shapes = [
        like(output), like(image), f32(1, g_temb.shape[1]), like(g_cap), like(s_in), like(s_out), like(g_wemb),
        f32(cut, 128), like(g_wcap), f32(rest, 128), f32(3, 128), f32(3, 128),
    ]
    in_specs = [ANY] * 10
    in_specs[5] = in_specs[9] = VM
    out_specs = [ANY] * 12
    out_specs[2] = out_specs[10] = out_specs[11] = VM
    return pl.pallas_call(
        functools.partial(emit_kernel, cut),
        out_shape=shapes,
        in_specs=in_specs,
        out_specs=out_specs,
        scratch_shapes=[pltpu.VMEM(shapes[j].shape, shapes[j].dtype) for j in (0, 1, 3, 4, 5, 6, 7, 8, 9)]
        + [pltpu.SemaphoreType.DMA((9,)), pltpu.SemaphoreType.DMA((9,))],
        compiler_params=params(),
        name="emit",
    )(*parts)


def fast_body(
    image_in, time_embed, caption, caption_mask, conv_in, conv_out, embed_proj, qkv_proj,
    caption_proj, out_proj, norm_gains, norm_biases, cotangent,
):
    n, height, width, c = image_in.shape
    n_sp = lax.axis_size("sp")
    nz = n_sp // 2
    px = height * width
    x = image_in.reshape(px, c)
    cot = cotangent.reshape(px, c)

    flat = lambda w: w.transpose(1, 2, 3, 0).reshape(9, w.shape[3], w.shape[0])
    (w_proj, w_in, w_out, w_qkv, hidden, a3_in, res, a3_out, g, normed, kv, q,
     st0, st1, st2, rows, ca, cb, ra, rb, ha, hb, kv_all, cap_all, emb_all) = forward_call(
        [out_proj.T[None], flat(conv_in), flat(conv_out), qkv_proj.T[None]], x, cot, time_embed, caption[0], embed_proj, caption_proj,
        norm_gains, norm_biases, nz, width, 0,
    )
    w_proj, w_qkv = w_proj[:, 0], w_qkv[:, 0]
    of, qf, dkv, dt_all = attention_call(kv, q, g, kv_all, caption_mask, 1)

    parts = backward_call(
        [of, qf, dkv, w_qkv, w_proj, res, cot, normed, a3_out, hidden, a3_in, x], w_in, w_out,
        [st0, st1, st2, rows, ca, cb, ra, rb, ha, hb, dt_all, cap_all, emb_all, embed_proj, caption_proj, time_embed],
        nz, width, 2,
    )
    output, image, g_temb, g_cap, s_in, s_out, g_wemb, g_qkv, g_wcap, g_out, g_gains, g_biases = emit_call(
        parts, qkv_proj.shape[1]
    )
    unflat = lambda g: g.reshape(3, 3, g.shape[1], 128).transpose(3, 0, 1, 2)
    return (
        output.reshape(image_in.shape), image.reshape(image_in.shape), g_temb, g_cap[None], unflat(s_in), unflat(s_out),
        g_wemb, g_qkv.T, g_wcap, g_out.T, g_gains, g_biases,
    )


def body(*args):
    image_in, qkv_proj = args[0], args[7]
    n, height, width, c = image_in.shape
    n_img, n_sp = lax.axis_size("img"), lax.axis_size("sp")
    fits = n == 1 and n_img == 4 and n_sp == HEADS and c == 512 and width == 64
    return fast_body(*args) if fits else plain_body(*args)


def solution(mesh):
    rows = P("img", "sp", None, None)
    kernel = P("img", None, None, "sp")
    flat = P("img", "sp")
    return jax.shard_map(
        body,
        mesh=mesh,
        in_specs=(
            rows, P("img", None), P("img", None, None), P("img", None), kernel, kernel,
            flat, flat, flat, flat, P(None, "img"), P(None, "img"), rows,
        ),
        out_specs=(
            rows, rows, P("img", None), P("img", "sp", None), kernel, kernel,
            flat, flat, flat, flat, P(None, "img"), P(None, "img"),
        ),
        check_vma=False,
    )
```

```python
import functools

import jax
import jax.numpy as jnp
from jax import lax
from jax.experimental import pallas as pl
from jax.experimental.pallas import tpu as pltpu
from jax.sharding import PartitionSpec as P

HEADS = 8
GROUPS = 32
EPSILON = 1e-05
PRECISE = lax.Precision.HIGHEST
MASKED = -1e30
BF16 = jnp.bfloat16
F32 = jnp.float32
MESH = pl.DeviceIdType.MESH
VMEM_BYTES = 60 * 1024 * 1024


def dot(a, b, ca, cb):
    return lax.dot_general(a, b, (((ca,), (cb,)), ((), ())), preferred_element_type=F32)


def silu(v):
    return v * jax.nn.sigmoid(v)


def silu_slope(v):
    s = jax.nn.sigmoid(v)
    return s * (1.0 + v * (1.0 - s))


def gather(x, axis, dim):
    return lax.all_gather(x, axis, axis=dim, tiled=True)


def scatter_sum(x, axis, dim):
    return lax.psum_scatter(x, axis, scatter_dimension=dim, tiled=True)


def swap(x, axis, split, concat):
    return lax.all_to_all(x, axis, split, concat, tiled=True)


def halo(x):
    count = lax.axis_size("sp")
    above = lax.ppermute(x[:, -1:], "sp", [(i, i + 1) for i in range(count - 1)])
    below = lax.ppermute(x[:, :1], "sp", [(i + 1, i) for i in range(count - 1)])
    return above, below


def group_sum(v):
    c = v.shape[-1]
    g = v.reshape(v.shape[:-1] + (GROUPS, c // GROUPS))
    s = jnp.sum(g, axis=-1, keepdims=True)
    return jnp.broadcast_to(s, g.shape).reshape(v.shape)


def norm_stats(x):
    n, r, w, c = x.shape
    cells = r * w * (c // GROUPS)
    parts = lax.axis_size("sp")
    mean = group_sum(jnp.sum(x, axis=(1, 2))) / cells
    dev = group_sum(jnp.sum(jnp.square(x - mean[:, None, None, :]), axis=(1, 2)))
    both = lax.all_gather(jnp.stack([mean, dev]), "sp")
    means, devs = both[:, 0], both[:, 1]
    center = jnp.mean(means, axis=0)
    var = (jnp.sum(devs, axis=0) + cells * jnp.sum(jnp.square(means - center), axis=0)) / (
        cells * parts
    )
    return center, lax.rsqrt(var + EPSILON)


def hat_of(x, center, inverse):
    return (x - center[:, None, None, :]) * inverse[:, None, None, :]


def norm_back(u, hat, inverse, gain, sum_u, sum_uh, members):
    s1 = group_sum(sum_u * gain) / members
    s2 = group_sum(sum_uh * gain) / members
    return inverse[:, None, None, :] * (
        u * gain - s1[:, None, None, :] - hat * s2[:, None, None, :]
    )


def pad_cols(x):
    return jnp.pad(x, ((0, 0), (0, 0), (1, 1), (0, 0)))


def conv(padded, weight_t, transposed):
    n, rp, wp, c = padded.shape
    r, w = rp - 2, wp - 2
    total = None
    for i in range(3):
        for j in range(3):
            a = padded[:, i : i + r, j : j + w].reshape(n * r * w, c)
            part = dot(a, weight_t[2 - i, 2 - j], 1, 0) if transposed else dot(a, weight_t[i, j], 1, 1)
            total = part if total is None else total + part
    return total.reshape(n, r, w, -1)


def conv_grad(padded, g):
    n, r, w, c = g.shape
    gf = g.reshape(n * r * w, c)
    rows = []
    for i in range(3):
        for j in range(3):
            a = padded[:, i : i + r, j : j + w].reshape(n * r * w, -1)
            rows.append(dot(gf, a, 0, 0))
    return jnp.stack(rows).reshape(3, 3, c, -1)


def to_pairs(x, images):
    n, px, h, d = x.shape
    y = x.transpose(0, 2, 1, 3).reshape(n * h, px, d)
    return swap(y, "sp", 0, 1)


def from_pairs(x, images):
    y = swap(x, "sp", 1, 0)
    return y.reshape(images, HEADS, y.shape[1], y.shape[2]).transpose(0, 2, 1, 3)


def attention_plain(q, k, v, g, tk, tv, keep, scale):
    p, length, d = q.shape
    block = min(512, length)
    keys = jnp.concatenate([tk, k], axis=1)
    values = jnp.concatenate([tv, v], axis=1)
    text = tk.shape[1]
    keep_all = jnp.concatenate([keep, jnp.ones((p, length), bool)], axis=1)

    def step(carry, blk):
        dk, dv = carry
        qb, gb = blk
        s = jnp.einsum("pqd,pkd->pqk", qb, keys, preferred_element_type=F32) * scale
        s = jnp.where(keep_all[:, None, :], s, MASKED)
        peak = jnp.max(s, axis=-1, keepdims=True)
        e = jnp.exp(s - peak)
        prob = e / jnp.sum(e, axis=-1, keepdims=True)
        pb = prob.astype(BF16)
        o = jnp.einsum("pqk,pkd->pqd", pb, values, preferred_element_type=F32)
        row = jnp.sum(o * gb.astype(F32), axis=-1, keepdims=True)
        dp = jnp.einsum("pqd,pkd->pqk", gb, values, preferred_element_type=F32)
        ds = (prob * (dp - row)).astype(BF16)
        dq = jnp.einsum("pqk,pkd->pqd", ds, keys, preferred_element_type=F32) * scale
        dk = dk + jnp.einsum("pqk,pqd->pkd", ds, qb, preferred_element_type=F32)
        dv = dv + jnp.einsum("pqk,pqd->pkd", pb, gb, preferred_element_type=F32)
        return (dk, dv), (o.astype(BF16), dq.astype(BF16))

    zeros = jnp.zeros((p, text + length, d), F32)
    cut = lambda t: t.reshape(p, length // block, block, d).swapaxes(0, 1)
    (dk, dv), (o, dq) = lax.scan(step, (zeros, zeros), (cut(q), cut(g)))
    join = lambda t: t.swapaxes(0, 1).reshape(p, length, d)
    dk = (dk * scale).astype(BF16)
    dv = dv.astype(BF16)
    return join(o), join(dq), dk[:, text:], dv[:, text:], dk[:, :text], dv[:, :text]


def plain_body(
    image_in, time_embed, caption, caption_mask, conv_in, conv_out, embed_proj, qkv_proj,
    caption_proj, out_proj, norm_gains, norm_biases, cotangent,
):
    n, rows, width, chans = image_in.shape
    n_img, n_sp = lax.axis_size("img"), lax.axis_size("sp")
    img, sp = lax.axis_index("img"), lax.axis_index("sp")
    px = rows * width
    members = px * n_sp * (chans // GROUPS)
    d = chans // HEADS
    scale = d ** -0.5
    pairs = n * HEADS // n_sp

    def whole(w):
        w = gather(w, "img", w.ndim - 1)
        return gather(w, "sp", w.ndim - 2)

    w_in = whole(conv_in.transpose(1, 2, 3, 0))
    w_out = whole(conv_out.transpose(1, 2, 3, 0))
    w_qkv = whole(qkv_proj.T)
    w_proj = whole(out_proj.T)
    affine = gather(jnp.concatenate([norm_gains, norm_biases]), "img", 1).astype(F32)
    gains, biases = affine[:3], affine[3:]

    embedded = silu(time_embed.astype(F32)).astype(BF16)
    emb_all = swap(embedded, "img", 1, 0)
    mod = scatter_sum(jnp.dot(emb_all, embed_proj, preferred_element_type=F32), "img", 0)
    mod = gather(mod, "sp", 1)
    scale_term, shift_term = mod[:, :chans], mod[:, chans:]
    cap_all = swap(caption, "img", 2, 0)
    cap_flat = cap_all.reshape(-1, cap_all.shape[2])
    kv = jnp.dot(cap_flat, caption_proj, preferred_element_type=F32)
    kv = scatter_sum(kv.reshape(cap_all.shape[0], cap_all.shape[1], -1), "img", 0).astype(BF16)
    kv = gather(kv, "sp", 2)
    text = kv.shape[1]
    kv_heads = kv.reshape(n, text, 2, HEADS, d).transpose(2, 0, 3, 1, 4).reshape(2, n * HEADS, text, d)
    mine = lax.dynamic_slice_in_dim(kv_heads, sp * pairs, pairs, 1)
    keep = jnp.repeat(caption_mask > 0, HEADS, axis=0)
    keep = lax.dynamic_slice_in_dim(keep, sp * pairs, pairs, 0)

    image_f = image_in.astype(F32)
    c0, i0 = norm_stats(image_f)
    hat0 = hat_of(image_f, c0, i0)
    first = hat0 * gains[0] + biases[0]
    act0 = silu(first).astype(BF16)
    above, below = halo(act0)
    pad0 = pad_cols(jnp.concatenate([above, act0, below], axis=1))
    hidden = conv(pad0, w_in, False)
    c1, i1 = norm_stats(hidden)
    hat1 = hat_of(hidden, c1, i1)
    second = hat1 * gains[1] + biases[1]
    pre = second * (1.0 + scale_term[:, None, None, :]) + shift_term[:, None, None, :]
    act1 = silu(pre).astype(BF16)
    above, below = halo(act1)
    pad1 = pad_cols(jnp.concatenate([above, act1, below], axis=1))
    residual = image_f + conv(pad1, w_out, False)
    c2, i2 = norm_stats(residual)
    hat2 = hat_of(residual, c2, i2)
    normed = (hat2 * gains[2] + biases[2]).astype(BF16).reshape(n * px, chans)
    qkv = dot(normed, w_qkv, 1, 1).astype(BF16)
    cot = cotangent.reshape(n * px, chans)
    g_att = dot(cot, w_proj, 1, 0).astype(BF16)
    four = jnp.concatenate([qkv, g_att], axis=1).reshape(n, px, 4, HEADS, d)
    packed = to_pairs(four.transpose(0, 1, 3, 2, 4).reshape(n, px, HEADS, 4 * d), n)
    q, k, v, g = (packed[..., j * d : (j + 1) * d] for j in range(4))
    o, dq, dk, dv, dtk, dtv = attention_plain(q, k, v, g, mine[0], mine[1], keep, scale)
    back = from_pairs(jnp.concatenate([o, dq, dk, dv], axis=-1), n)
    back = back.reshape(n * px, HEADS, 4, d).transpose(0, 2, 1, 3).reshape(n * px, 4 * chans)
    attended, proj_grad = back[:, :chans], back[:, chans:]
    output = residual + dot(attended, w_proj, 1, 1).reshape(image_in.shape)

    grad_out = dot(cot, attended, 0, 0)
    grad_qkv = dot(proj_grad, normed, 0, 0)
    normed_grad = dot(proj_grad, w_qkv, 1, 0).reshape(image_in.shape)

    def sums(u, hat):
        both = jnp.stack([jnp.sum(u, axis=(1, 2)), jnp.sum(u * hat, axis=(1, 2))])
        return lax.psum(both, "sp")

    su2, sh2 = sums(normed_grad, hat2)
    residual_grad = cotangent.astype(F32) + norm_back(
        normed_grad, hat2, i2, gains[2], su2, sh2, members
    )
    g2 = residual_grad.astype(BF16)
    above, below = halo(g2)
    gpad = pad_cols(jnp.concatenate([above, g2, below], axis=1))
    grad_conv_out = conv_grad(pad1, g2)
    pre_grad = conv(gpad, w_out, True) * silu_slope(pre)
    sa, sb = sums(pre_grad, hat1)
    fac = 1.0 + scale_term
    shift_grad = sa
    scale_grad = sb * gains[1] + sa * biases[1]
    u1 = pre_grad * fac[:, None, None, :]
    su1, sh1 = sa * fac, sb * fac
    g1 = norm_back(u1, hat1, i1, gains[1], su1, sh1, members).astype(BF16)
    above, below = halo(g1)
    gpad = pad_cols(jnp.concatenate([above, g1, below], axis=1))
    grad_conv_in = conv_grad(pad0, g1)
    u0 = conv(gpad, w_in, True) * silu_slope(first)
    su0, sh0 = sums(u0, hat0)
    grad_image = residual_grad + norm_back(u0, hat0, i0, gains[0], su0, sh0, members)

    mod_grad = jnp.concatenate([scale_grad, shift_grad], axis=1)
    cols = embed_proj.shape[1]
    mod_all = gather(mod_grad, "img", 0)
    mod_cols = lax.dynamic_slice_in_dim(mod_all, sp * cols, cols, 1)
    grad_embed_proj = jnp.einsum("ne,nd->ed", emb_all.astype(F32), mod_cols, precision=PRECISE)
    part = jnp.einsum("nd,ed->ne", mod_cols, embed_proj.astype(F32), precision=PRECISE)
    part = swap(lax.psum(part, "sp"), "img", 0, 1)
    grad_embed = part * silu_slope(time_embed.astype(F32))

    tg = gather(jnp.stack([dtk, dtv]), "sp", 1).reshape(2, n, HEADS, text, d)
    tg = tg.transpose(1, 3, 0, 2, 4).reshape(n, text, 2 * chans)
    cols = caption_proj.shape[1]
    tg = gather(lax.dynamic_slice_in_dim(tg, sp * cols, cols, 2), "img", 0).reshape(-1, cols)
    grad_caption_proj = dot(cap_flat, tg, 0, 0)
    gc = dot(tg, caption_proj, 1, 1).reshape(cap_all.shape)
    gc = scatter_sum(gc, "sp", 1)
    grad_caption = swap(gc, "img", 0, 2)

    grads = jnp.concatenate(
        [jnp.sum(t, axis=0)[None] for t in (sh0, sh1, sh2, su0, su1, su2)]
    )
    grads = scatter_sum(grads, "img", 1)

    def shared(w):
        w = scatter_sum(w, "sp", w.ndim - 2)
        return scatter_sum(w, "img", w.ndim - 1)

    return (
        output.astype(BF16),
        grad_image,
        grad_embed,
        grad_caption,
        shared(grad_conv_in).transpose(3, 0, 1, 2),
        shared(grad_conv_out).transpose(3, 0, 1, 2),
        grad_embed_proj,
        shared(grad_qkv).T,
        grad_caption_proj,
        shared(grad_out).T,
        grads[:3],
        grads[3:],
    )


class Place:
    def __init__(self):
        self.i = lax.axis_index("img")
        self.s = lax.axis_index("sp")
        self.z = lax.div(self.s, 2)
        self.c = lax.rem(self.s, 2)
        x = lax.rem(self.i, 2)
        y = lax.div(self.i, 2)
        self.ix = self.i + 1 - 2 * x
        self.iy = self.i + 2 - 4 * y
        self.id = 3 - self.i
        self.sib = (self.i, self.s + 1 - 2 * self.c)
        self.xn = (self.ix, self.s)
        self.yn = (self.iy, self.s)

    def zp(self, k, nz):
        return (self.i, 2 * lax.rem(self.z + k, nz) + self.c)

    def rp(self, k, n_sp):
        return (self.i, lax.rem(self.s + k, n_sp))


def greet(peers):
    bar = pltpu.get_barrier_semaphore()
    for p in peers:
        pl.semaphore_signal(bar, inc=1, device_id=p, device_id_type=MESH)


def greeted(count):
    pl.semaphore_wait(pltpu.get_barrier_semaphore(), count)


def remote(src, dst, ssem, rsem, dev):
    cp = pltpu.make_async_remote_copy(
        src_ref=src, dst_ref=dst, send_sem=ssem, recv_sem=rsem, device_id=dev, device_id_type=MESH
    )
    cp.start()
    return cp


def params(cid=None, grid=0):
    extra = {} if cid is None else {"collective_id": cid, "has_side_effects": True}
    if grid:
        extra["dimension_semantics"] = ("arbitrary",) * grid
    return pltpu.CompilerParams(vmem_limit_bytes=VMEM_BYTES, **extra)


ANY = pl.BlockSpec(memory_space=pl.ANY)
VM = pl.BlockSpec(memory_space=pltpu.VMEM)
def channel_stats(v):
    mean = jnp.sum(v, axis=0, keepdims=True) / v.shape[0]
    dev = v - mean
    return mean, jnp.sum(dev * dev, axis=0, keepdims=True)


def put_rows(dst, pair):
    n = pair[0].shape[1] // 128
    for a, row in enumerate(pair):
        for j in range(n):
            dst[a * n + j : a * n + j + 1, :] = row[:, j * 128 : (j + 1) * 128]


def get_rows(block):
    n = block.shape[0] // 2
    return tuple(jnp.concatenate([block[a * n + j : a * n + j + 1] for j in range(n)], axis=1) for a in range(2))


def group_total(rows):
    c = rows.shape[1]
    size = 512 // GROUPS
    a = lax.broadcasted_iota(jnp.int32, (128, 128), 0)
    b = lax.broadcasted_iota(jnp.int32, (128, 128), 1)
    same = jnp.where(lax.bitwise_xor(a, b) < size, 1.0, 0.0).astype(BF16)
    high = rows.astype(BF16)
    rest = rows - high.astype(F32)
    mid = rest.astype(BF16)
    low = (rest - mid.astype(F32)).astype(BF16)
    parts = jnp.concatenate([high.astype(F32), mid.astype(F32), low.astype(F32)]).astype(BF16)
    total = jnp.concatenate(
        [dot(parts[:, j * 128 : (j + 1) * 128], same, 1, 0) for j in range(c // 128)], axis=1
    )
    n = rows.shape[0]
    return total[:n] + total[n : 2 * n] + total[2 * n :]


def combine_stats(every, px):
    n_sp, rows, lanes = every.shape
    half = rows // 2
    size = half * lanes // GROUPS
    means = [every[j, :half, :] for j in range(n_sp)]
    center_c = sum(means) / n_sp
    dev = sum(every[j, half:, :] for j in range(n_sp))
    dev = dev + px * sum((m - center_c) * (m - center_c) for m in means)
    spread = lambda v: group_total(jnp.concatenate([v, v]))[:half]
    center = spread(center_c) / size
    off = center_c - center
    var = spread(dev + (px * n_sp) * (off * off)) / (px * n_sp * size)
    return get_rows(jnp.concatenate([center, lax.rsqrt(var + EPSILON)]))


def combine_sums(every):
    total = every[0]
    for j in range(1, every.shape[0]):
        total = total + every[j]
    a, b = get_rows(total)
    return jnp.concatenate([a, b, jnp.zeros((6, a.shape[1]), F32)])


def edge_flags(n_sp, s):
    return jnp.where(s > 0, 1.0, 0.0), jnp.where(s < n_sp - 1, 1.0, 0.0)


def shifted(dst, row, width, block):
    col = lax.broadcasted_iota(jnp.int32, block.shape, 0)
    r = slice(row * width, (row + 1) * width)
    dst[1, r, :] = block.astype(BF16)
    dst[0, r, :] = jnp.where(col == 0, 0.0, pltpu.roll(block, 1, 0)).astype(BF16)
    dst[2, r, :] = jnp.where(col == width - 1, 0.0, pltpu.roll(block, width - 1, 0)).astype(BF16)


def joined(w_ref, *lead):
    return jnp.concatenate([w_ref[(j,) + lead] for j in range(4)], axis=-1)


def three_parts(v):
    a = v.astype(BF16).astype(F32)
    b = (v - a).astype(BF16).astype(F32)
    return a, b, v - a - b


AHEAD = 3


def attention_kernel(
    n_sp, BK, kv, qin, gin, text, keep, of, qf, dkv, dt,
    kv_r, q_r, g_r, q_s, o_s, dq_o, dkv_s, dt_s, k_s, v_s, s_s, e_s, g_s, dq_s, peak_s, lsem, ssem, rsem,
):
    at = Place()
    nz = n_sp // 2
    px = kv.shape[1]
    L, T = n_sp * px, text.shape[1]
    d = kv.shape[2] // 2
    BQ = px // 2
    line = [at.rp(k, n_sp) for k in range(1, n_sp)]
    greet(line)
    own = [
        pltpu.make_async_copy(kv.at[at.s], kv_r.at[at.s], lsem.at[0]),
        pltpu.make_async_copy(qin.at[at.s], q_r.at[at.s], lsem.at[1]),
        pltpu.make_async_copy(gin, g_r, lsem.at[6]),
    ]
    for cp in own:
        cp.start()
    greeted(n_sp - 1)
    keys = [remote(kv.at[dev[1]], kv_r.at[at.s], ssem.at[0, k + 1], rsem.at[0, k + 1], dev) for k, dev in enumerate(line)]

    def source(k):
        return 2 * lax.rem(at.z - lax.div(k, 2) + nz, nz) + lax.rem(at.c + lax.rem(k, 2), 2)

    def target(k):
        return 2 * lax.rem(at.z + lax.div(k, 2), nz) + lax.rem(at.c + lax.rem(k, 2), 2)

    def query_copy(k):
        return pltpu.make_async_remote_copy(
            src_ref=qin.at[target(k)], dst_ref=q_r.at[at.s], send_sem=ssem.at[1, k], recv_sem=rsem.at[1, k],
            device_id=(at.i, target(k)), device_id_type=MESH,
        )

    odd = lax.rem(at.s, 2)
    pair = lax.div(at.s, 2)
    ones = (lax.broadcasted_iota(jnp.int32, (1, d), 1) < 3).astype(F32).astype(BF16)
    picked = []
    for j in (pair, HEADS // 2 + pair):
        blk = text[j].astype(F32)
        picked.append(jnp.where(odd > 0, blk[:, d:], blk[:, :d]).astype(BF16))
    k_s[0:T, :] = picked[0]
    v_s[0:T, :] = jnp.concatenate([picked[1], jnp.broadcast_to(ones, (T, d))], axis=1)

    def rows_of(o, n=px, start=0):
        return pl.ds(pl.multiple_of(o * px + start, 128), n)

    def take(j):
        rows = rows_of(j, px, T)
        k_s[rows, :] = kv_r[j][:, :d]
        v_s[rows, :] = jnp.concatenate([kv_r[j][:, d:], jnp.broadcast_to(ones, (px, d))], axis=1)

    for k in range(1, AHEAD):
        query_copy(k).start()
    for cp in own:
        cp.wait()
    take(at.s)
    for k in range(1, n_sp):
        keys[k - 1].wait_recv()
        take(lax.rem(at.s - k + n_sp, n_sp))
    blocks = [(0, T)] + [(T + j * BK, BK) for j in range(L // BK)]
    scale = d ** -0.5

    def back_copy(j, k, src, dst, o):
        return pltpu.make_async_remote_copy(
            src_ref=src.at[o], dst_ref=dst.at[at.s], send_sem=ssem.at[j, k], recv_sem=rsem.at[j, k],
            device_id=(at.i, o), device_id_type=MESH,
        )

    def scores(q, slot, st, n, peak):
        s = dot(q, k_s[st : st + n, :], 1, 1)
        if st == 0:
            s = jnp.where(keep[...] > 0, s, MASKED)
        s_s[slot, :, st : st + n] = s
        for j in range(n // 128):
            piece = s[:, 128 * j : 128 * j + 128]
            peak = piece if peak is None else jnp.maximum(peak, piece)
        return peak

    def query(o, part):
        return q_r[o][:, part * d : (part + 1) * d]

    def forward(o, part, o_next):
        nxt = query(o_next, 1 - part)
        g = g_r[o][:, part * d : (part + 1) * d]
        rows = rows_of(o, BQ, part * BQ)
        q_s[rows, :] = query(o, part)
        top = jnp.max(peak_s[part], axis=1, keepdims=True)
        out = jnp.zeros((BQ, 2 * d), F32)
        peak = None
        for st, n in blocks:
            peak = scores(nxt, 1 - part, st, n, peak)
            e = jnp.exp(s_s[part, :, st : st + n] - top).astype(BF16)
            e_s[rows, st : st + n] = e
            out = out + dot(e, v_s[st : st + n, :], 1, 0)
        peak_s[1 - part] = peak
        inverse = 1.0 / out[:, d : d + 1]
        out = out[:, :d] * inverse
        g = g.astype(F32) * inverse
        row = jnp.sum(out * g, axis=1, keepdims=True)
        lane = lax.broadcasted_iota(jnp.int32, (BQ, d), 1)
        extra = jnp.zeros((BQ, d), F32)
        for j, piece in enumerate(three_parts(-row)):
            extra = jnp.where(lane == j, piece, extra)
        g_s[rows, :] = jnp.concatenate([g, extra], axis=1).astype(BF16)
        o_s[o, :, part * d : (part + 1) * d] = out.astype(BF16)

    peak = None
    for st, n in blocks:
        peak = scores(query(at.s, 0), 0, st, n, peak)
    peak_s[0] = peak

    def owner(k, _):
        o = source(k)

        @pl.when(k + AHEAD < n_sp)
        def _():
            query_copy(k + AHEAD).start()

        forward(o, 0, o)

        @pl.when(k + 1 < n_sp)
        def _():
            query_copy(k + 1).wait_recv()

        forward(o, 1, source(lax.rem(k + 1, n_sp)))

        @pl.when(k > 0)
        def _():
            back_copy(2, k, o_s, of, o).start()

        return 0

    lax.fori_loop(0, n_sp, owner, 0)
    local = [pltpu.make_async_copy(o_s.at[at.s], of.at[at.s], lsem.at[2])]

    def block(o, cols, kc, vc, dk, dv, fresh):
        rows = rows_of(o)
        g, q = g_s[rows, :], q_s[rows, :]
        e = e_s[rows, cols]
        ds = (e.astype(F32) * dot(g, vc, 1, 1)).astype(BF16)
        part = dot(ds, kc, 1, 0)
        dq_s[rows, :] = part if fresh else dq_s[rows, :] + part
        return dk + dot(q.T, ds, 1, 0), dv + dot(g[:, :d].T, e, 1, 0)

    def both(dk, dv):
        return jnp.concatenate([dk, dv], axis=0).astype(BF16).T

    def chunk(cols, n, fresh):
        kc, vc = k_s[cols, :], v_s[cols, :]
        zero = jnp.zeros((d, n), F32)
        dk, dv = lax.fori_loop(
            0, n_sp, lambda o, acc: block(o, cols, kc, vc, acc[0], acc[1], fresh), (zero, zero), unroll=4
        )
        return both(dk, dv)

    def chip_columns(z):
        return pl.ds(pl.multiple_of(T + z * (2 * px), 128), 2 * px)

    dt_s[...] = chunk(pl.ds(0, T), T, True)
    sent = [remote(dt_s, dt.at[at.s], ssem.at[5, k + 1], rsem.at[5, k + 1], dev) for k, dev in enumerate(line)]
    local.append(pltpu.make_async_copy(dt_s, dt.at[at.s], lsem.at[3]))

    def chip(k, _):
        z = lax.rem(at.z + k, nz)
        grads = chunk(chip_columns(z), 2 * px, False)
        for core in range(2):
            o = 2 * z + core
            dkv_s[o] = grads[core * px : (core + 1) * px]
            back_copy(4, lax.rem(o - at.s + n_sp, n_sp), dkv_s, dkv, o).start()
        return 0

    lax.fori_loop(1, nz, chip, 0)
    cols = chip_columns(at.z)
    kc, vc = k_s[cols, :], v_s[cols, :]
    zero = jnp.zeros((d, 2 * px), F32)

    def last(j, acc):
        o = 2 * lax.rem(at.z + 1 + lax.div(j, 2), nz) + lax.rem(j, 2)
        acc = block(o, cols, kc, vc, acc[0], acc[1], False)
        dq = (dq_s[rows_of(o), :] * scale).astype(BF16)
        dq_o[o] = jnp.concatenate([dq[:BQ], dq[BQ:]], axis=1)

        @pl.when(o != at.s)
        def _():
            back_copy(3, lax.rem(o - at.s + n_sp, n_sp), dq_o, qf, o).start()

        return acc

    grads = both(*lax.fori_loop(0, n_sp, last, (zero, zero)))
    for core in range(2):
        dkv_s[2 * at.z + core] = grads[core * px : (core + 1) * px]
    sib = at.sib[1]
    back_copy(4, lax.rem(sib - at.s + n_sp, n_sp), dkv_s, dkv, sib).start()
    local.append(pltpu.make_async_copy(dkv_s.at[at.s], dkv.at[at.s], lsem.at[4]))
    local.append(pltpu.make_async_copy(dq_o.at[at.s], qf.at[at.s], lsem.at[5]))
    for cp in local:
        cp.start()
    for k in range(1, n_sp):
        back_copy(2, k, o_s, of, source(k)).wait()
        o = lax.rem(at.s + k, n_sp)
        back_copy(4, k, dkv_s, dkv, o).wait()
        back_copy(3, k, dq_o, qf, o).wait()
    for k in range(1, n_sp):
        query_copy(k).wait_send()
    for cp in keys:
        cp.wait_send()
    for cp in sent:
        cp.wait()
    for cp in local:
        cp.wait()


def attention_call(kv, qin, gin, text, keep, cid):
    n_sp, px, d2 = kv.shape
    T = text.shape[1]
    L = n_sp * px
    d = d2 // 2
    outs = [(n_sp, px // 2, d2), (n_sp, px // 2, d2), (n_sp, px, d2), (n_sp, T, d2)]
    vm = pltpu.VMEM
    return pl.pallas_call(
        functools.partial(attention_kernel, n_sp, 1024),
        out_shape=[jax.ShapeDtypeStruct(s, BF16) for s in outs],
        in_specs=[ANY, ANY, ANY, VM, VM],
        out_specs=[ANY] * 4,
        scratch_shapes=[
            vm((n_sp, px, d2), BF16), vm((n_sp, px // 2, d2), BF16), vm((n_sp, px // 2, d2), BF16), vm((L, d), BF16),
            vm((n_sp, px // 2, d2), BF16),
            vm((n_sp, px // 2, d2), BF16), vm((n_sp, px, d2), BF16), vm((T, d2), BF16),
            vm((T + L, d), BF16), vm((T + L, d2), BF16), vm((2, px // 2, T + L), F32), vm((L, T + L), BF16),
            vm((L, d2), BF16), vm((L, d), F32), vm((2, px // 2, 128), F32),
            pltpu.SemaphoreType.DMA((7,)),
            pltpu.SemaphoreType.DMA((6, n_sp)),
            pltpu.SemaphoreType.DMA((6, n_sp)),
        ],
        compiler_params=params(cid),
        name="attention",
    )(kv, qin, gin, text, keep)


class Mail:
    def __init__(self, ssem, rsem):
        self.ssem, self.rsem, self.sent = ssem, rsem, []

    def send(self, src, dst, dev):
        j = len(self.sent)
        cp = remote(src, dst, self.ssem.at[j], self.rsem.at[j], dev)
        self.sent.append(cp)
        return cp


class Gather:
    def __init__(self, at, nz, ins, outs, dims, ssem, rsem):
        self.at, self.nz, self.ins, self.outs, self.dims = at, nz, ins, outs, dims
        self.ssem, self.rsem = ssem, rsem
        self.sent, self.kinds = {}, {}
        self.order = sorted(range(1, nz), key=lambda k: min(k, nz - k))

    @staticmethod
    def copies(nz):
        return 3 * nz - 1 + 7 * nz

    def view(self, a, ii, k, core, half=None):
        at, nz, r = self.at, self.nz, self.dims[a][1]
        sp = 2 * lax.rem(at.z - k + nz, nz) + core
        if half is None:
            return self.outs[a].at[ii, :, pl.ds(pl.multiple_of(sp * r, r), r), :]
        h = r // 2
        return self.outs[a].at[ii, :, pl.ds(pl.multiple_of(sp * r + half * h, h), h), :]

    def send(self, a, kind, src, dst, dev):
        j = self.kinds.setdefault(kind, len(self.kinds))
        self.sent[a, kind] = remote(src, dst, self.ssem.at[a, j], self.rsem.at[a, j], dev)

    def forward(self, a, kind, ref, dev):
        self.send(a, kind, ref, ref, dev)

    def near(self, a):
        at = self.at
        own = self.view(a, at.i, 0, at.c)
        self.send(a, ("x", 0), self.ins[a], own, at.xn)
        self.send(a, ("y", 0), self.ins[a], own, at.yn)
        self.send(a, ("s", 0), self.ins[a], own, at.sib)

    def along(self, a, ks):
        for k in ks:
            self.send(a, ("z", k), self.ins[a], self.view(a, self.at.i, 0, self.at.c), self.at.zp(k, self.nz))

    def second(self, a, ks=None):
        at = self.at
        for k in self.order if ks is None else ks:
            self.sent[a, ("z", k)].wait_recv()
            got = self.view(a, at.i, k, at.c)
            self.forward(a, ("x", k), got, at.xn)
            self.forward(a, ("y", k), got, at.yn)
            self.forward(a, ("s", k), got, at.sib)

    def third(self, a):
        at = self.at
        for k in [0] + self.order:
            self.sent[a, ("x", k)].wait_recv()
            self.forward(a, ("da", k), self.view(a, at.ix, k, at.c, 0), at.yn)
            self.forward(a, ("sx", k), self.view(a, at.ix, k, at.c), at.sib)
            self.sent[a, ("y", k)].wait_recv()
            self.forward(a, ("db", k), self.view(a, at.iy, k, at.c, 1), at.xn)
            self.forward(a, ("sy", k), self.view(a, at.iy, k, at.c), at.sib)

    def fourth(self, a):
        at = self.at
        for k in [0] + self.order:
            self.sent[a, ("da", k)].wait_recv()
            self.forward(a, ("sa", k), self.view(a, at.id, k, at.c, 0), at.sib)
            self.sent[a, ("db", k)].wait_recv()
            self.forward(a, ("sb", k), self.view(a, at.id, k, at.c, 1), at.sib)

    def complete(self, a):
        for (b, kind), cp in self.sent.items():
            if b == a and kind[0][0] == "s":
                cp.wait_recv()

    def finish(self):
        for cp in self.sent.values():
            cp.wait_send()


def img_peers(at):
    return [(lax.rem(at.i + k, 4), at.s) for k in range(1, 4)]


FORWARD_MAIL = 4 * 3 + 3 + 2 * 7 + 4 + 7 + 2 * (2 + 7) + 7


def forward_kernel(nz, width, dims, *refs):
    na = len(dims)
    chunks, refs = refs[:na], refs[na:]
    x, cot, temb, cap, w_emb, w_cap, gains, biases = refs[:8]
    outs, refs = refs[8 : 8 + na], refs[8 + na :]
    hidden_o, a0_o, res_o, a1_o, g_o, normed, kv, qf = refs[:8]
    st0, st1, st2, rows, ca, cb, ra, rb, ha, hb, kv_all, cap_all, emb_all = refs[8:21]
    refs = refs[21:]
    weights, refs = refs[:na], refs[na:]
    (ssem, rsem, lsem, msend, mrecv, g_s, emb, affine, mine, every, edge_s, xa, xb, ca_s, cb_s, ha_s, hb_s, ra_s, rb_s,
     aff_s, emb_s, cap_s, part, part_r, kv_s, kv_r, mod_s, mod_r, acts, hidden, res) = refs
    n_sp = 2 * nz
    at = Place()
    line = [at.rp(k, n_sp) for k in range(1, n_sp)]
    grid = img_peers(at)
    greet(line + grid)
    mail = Mail(msend, mrecv)
    got = Gather(at, nz, chunks, weights, dims, ssem, rsem)
    PROJ, IN, OUT, QKV = range(4)
    px, c = x.shape
    height = px // width
    d = c // HEADS
    tokens = cap.shape[0]
    e = cap.shape[1] // 4
    half = px // 2
    local = []

    def copy(src, dst):
        cp = pltpu.make_async_copy(src, dst, lsem.at[len(local)])
        cp.start()
        local.append(cp)
        return cp

    embedded = silu(temb[...].astype(F32)).astype(BF16).astype(F32)
    for j in range(4):
        emb[j] = jnp.broadcast_to(embedded[:, j * e : (j + 1) * e], (8, e))
    affine[0:3] = gains[...].astype(F32)
    affine[3:6] = biases[...].astype(F32)

    def publish(j, v, edges):
        pair = channel_stats(v)
        put_rows(mine.at[j], pair)
        out = []
        for ref, above, below in edges:
            if ref is None:
                edge_s[j - 1, 0] = (v[px - width :] - pair[0]).astype(BF16)
                edge_s[j - 1, 1] = (v[:width] - pair[0]).astype(BF16)
                out.append(mail.send(edge_s.at[j - 1, 0], above, line[0]))
                out.append(mail.send(edge_s.at[j - 1, 1], below, line[-1]))
            else:
                out.append(mail.send(ref.at[px - width :], above, line[0]))
                out.append(mail.send(ref.at[:width], below, line[-1]))
        for dev in line:
            out.append(mail.send(mine.at[j], every.at[j, at.s], dev))
        every[j, at.s] = mine[j]
        return out

    def fold(v):
        return jnp.concatenate([v[:half], v[half:]], axis=1)

    greeted(n_sp + 2)
    close, far = got.order[:2], got.order[2:]
    got.along(PROJ, got.order)
    got.near(PROJ)
    got.along(IN, close)
    got.near(IN)
    stat0 = publish(0, x[...].astype(F32), [(x, xa, xb), (cot, ca_s, cb_s)])
    round1 = []
    share = tokens // 2
    part_tokens = pl.ds(pl.multiple_of(at.c * share, share), share)
    for dev in grid:
        round1.append(mail.send(affine, aff_s.at[at.i], dev))
        round1.append(mail.send(emb.at[dev[0]], emb_s.at[at.i], dev))
        round1.append(
            mail.send(cap.at[part_tokens, pl.ds(pl.multiple_of(dev[0] * e, e), e)], cap_s.at[at.i, part_tokens], dev)
        )
    own_cap = copy(cap.at[:, pl.ds(pl.multiple_of(at.i * e, e), e)], cap_s.at[at.i])
    aff_s[at.i] = affine[...]
    emb_s[at.i] = emb[at.i]
    got.near(OUT)
    own = [copy(got.ins[a], got.view(a, at.i, 0, at.c)) for a in range(na)]
    got.second(PROJ)
    got.second(IN, close[:1])
    got.along(IN, far)
    got.second(IN, close[1:])
    got.third(PROJ)
    got.along(OUT, close)
    got.second(IN, far)
    got.along(OUT, far)
    got.fourth(PROJ)
    got.third(IN)
    got.second(OUT)
    got.along(QKV, got.order)

    own_cap.wait()
    for cp in round1:
        cp.wait_recv()
    halves = []
    for dev in grid:
        here = cap_s.at[dev[0], part_tokens]
        halves.append(mail.send(here, here, at.sib))
    for cp in halves:
        cp.wait_recv()
    for j in range(4):
        part[j, :tokens] = dot(cap_s[j], w_cap[...], 1, 0)
        part[j, tokens:] = dot(emb_s[j].astype(BF16), w_emb[...], 1, 0)
    round2 = [mail.send(part.at[dev[0]], part_r.at[at.i], dev) for dev in grid]
    part_r[at.i] = part[at.i]
    cap_all[...] = cap_s[...]
    emb_all[...] = jnp.concatenate([emb_s[j][0:1] for j in range(4)] + [jnp.zeros((4, e), F32)])
    aff = jnp.concatenate([aff_s[j] for j in range(4)], axis=1)
    rows[...] = jnp.zeros_like(rows)
    for j in range(3):
        rows[j, 0:1] = aff[j : j + 1]
        rows[j, 1:2] = aff[3 + j : 4 + j]
        rows[j, 2:3] = jnp.ones((1, c), F32)

    has_up, has_dn = edge_flags(n_sp, at.s)

    def restore(j, above, below, above_o, below_o):
        for src, dst, dev in ((above, above_o, line[-1]), (below, below_o, line[0])):
            dst[...] = src[...].astype(F32) + get_rows(every[j, dev[1]])[0]

    def activate(j, v, above, below):
        center, inverse = combine_stats(every.at[j], px)
        mul = inverse * rows[j, 0:1] * rows[j, 2:3]
        add = rows[j, 1:2] * rows[j, 2:3] + rows[j, 3:4]
        for r in range(height + 2):
            top, end = r == 0, r == height + 1
            t = above[...] if top else below[...] if end else v[(r - 1) * width : r * width, :]
            t = silu((t.astype(F32) - center) * mul + add)
            if top:
                t = t * has_up
            elif end:
                t = t * has_dn
            shifted(acts.at[j], r, width, t)

    def taps(w, out, t0, t1, base):
        a3 = acts.at[0 if base is None else 1]

        def one(tap, _):
            i, j = lax.div(tap, 3), lax.rem(tap, 3)
            lhs = a3[j, pl.ds(pl.multiple_of(i * width, width), px), :]
            first = 0.0 if base is None else base[...].astype(F32)
            out[...] = dot(lhs, joined(w, tap), 1, 1) + jnp.where(tap > 0, out[...], first)
            return 0

        lax.fori_loop(t0, t1, one, 0)

    for cp in stat0:
        cp.wait_recv()
    activate(0, x, xa, xb)
    copy(acts.at[0], a0_o)
    got.fourth(IN)
    for cp in own:
        cp.wait()
    got.complete(IN)
    copy(weights[IN], outs[IN])
    taps(weights[IN], hidden, 0, 3, None)
    got.complete(PROJ)
    g = dot(cot[...], joined(weights[PROJ], 0), 1, 0).astype(BF16)
    for h in range(HEADS):
        g_s[h] = fold(g[:, h * d : (h + 1) * d])
    copy(weights[PROJ], outs[PROJ])
    round_g = [mail.send(g_s.at[dev[1]], g_o.at[at.s], dev) for dev in line]
    copy(g_s.at[at.s], g_o.at[at.s])
    taps(weights[IN], hidden, 3, 6, None)
    got.third(OUT)
    taps(weights[IN], hidden, 6, 9, None)
    stat1 = publish(1, hidden[...], [(None, ha_s, hb_s)])
    copy(hidden, hidden_o)
    for cp in round2:
        cp.wait_recv()
    total = part_r[0] + part_r[1] + part_r[2] + part_r[3]
    kv_s[...] = total[:tokens].astype(BF16)
    mod_s[...] = total[tokens:]
    round3 = []
    for dev in line:
        round3.append(mail.send(kv_s, kv_r.at[at.s], dev))
        round3.append(mail.send(mod_s, mod_r.at[at.s], dev))
    kv_r[at.s] = kv_s[...]
    mod_r[at.s] = mod_s[...]
    got.near(QKV)
    got.second(QKV)
    got.fourth(OUT)
    got.third(QKV)
    for cp in round3 + stat1:
        cp.wait_recv()
    kv_all[...] = kv_r[...]
    mod = jnp.concatenate([mod_r[j][0:1] for j in range(n_sp)], axis=1)
    rows[1, 2:3] = 1.0 + mod[:, :c]
    rows[1, 3:4] = mod[:, c:]

    restore(1, ha_s, hb_s, ha, hb)
    activate(1, hidden, ha, hb)
    copy(acts.at[1], a1_o)
    got.fourth(QKV)
    got.complete(OUT)
    copy(weights[OUT], outs[OUT])
    taps(weights[OUT], res, 0, 9, x)
    stat2 = publish(2, res[...], [(None, ra_s, rb_s)])
    copy(res, res_o)
    for dst, src in ((ca, ca_s), (cb, cb_s)):
        dst[...] = src[...]
    got.complete(QKV)
    copy(weights[QKV], outs[QKV])
    wq = joined(weights[QKV], 0)

    for cp in stat2:
        cp.wait_recv()
    center, inverse = combine_stats(every.at[2], px)
    n = ((res[...] - center) * (inverse * rows[2, 0:1]) + rows[2, 1:2]).astype(BF16)
    normed[...] = n
    k = dot(n, wq[c : 2 * c], 1, 1).astype(BF16)
    v = dot(n, wq[2 * c :], 1, 1).astype(BF16)
    q = (dot(n, wq[:c], 1, 1).astype(BF16).astype(F32) * (d ** -0.5)).astype(BF16)
    for h in range(HEADS):
        lanes = slice(h * d, (h + 1) * d)
        kv[h] = jnp.concatenate([k[:, lanes], v[:, lanes]], axis=1)
        qf[h] = fold(q[:, lanes])
    restore(2, ra_s, rb_s, ra, rb)
    st0[...] = every[0]
    st1[...] = every[1]
    st2[...] = every[2]
    for cp in local[1 + na :]:
        cp.wait()
    got.finish()
    for cp in round_g:
        cp.wait_recv()
    for cp in mail.sent:
        cp.wait_send()


def forward_call(chunks, x, cot, temb, cap, w_emb, w_cap, gains, biases, nz, width, cid):
    dims = [c.shape[:2] for c in chunks]
    na = len(dims)
    n_sp = 2 * nz
    px, c = x.shape
    padded = px + 2 * width
    tokens, wide = cap.shape
    e = wide // 4
    d2 = 2 * c // HEADS
    big = [((4, t, n_sp * r, 128), BF16) for t, r in dims]
    edge16, edge32 = ((width, c), BF16), ((width, c), F32)
    stat = ((n_sp, 8, c // 4), F32)
    outs = big + [
        ((px, c), F32), ((3, padded, c), BF16), ((px, c), F32), ((3, padded, c), BF16),
        ((n_sp, px // 2, d2), BF16), ((px, c), BF16), ((HEADS, px, d2), BF16), ((HEADS, px // 2, d2), BF16),
        stat, stat, stat, ((3, 8, c), F32), edge16, edge16, edge32, edge32, edge32, edge32,
        ((n_sp, tokens, 128), BF16), ((4, tokens, e), BF16), ((8, e), F32),
    ]
    vm = pltpu.VMEM
    return pl.pallas_call(
        functools.partial(forward_kernel, nz, width, dims),
        out_shape=[jax.ShapeDtypeStruct(s, ty) for s, ty in outs],
        in_specs=[ANY] * na + [VM, VM, VM, ANY] + [VM] * 4,
        out_specs=[ANY] * (na + 5) + [VM] * (len(outs) - na - 5),
        scratch_shapes=[vm(s, ty) for s, ty in big]
        + [
            pltpu.SemaphoreType.DMA((na, Gather.copies(nz))),
            pltpu.SemaphoreType.DMA((na, Gather.copies(nz))),
            pltpu.SemaphoreType.DMA((2 * na + 6,)),
            pltpu.SemaphoreType.DMA((FORWARD_MAIL,)),
            pltpu.SemaphoreType.DMA((FORWARD_MAIL,)),
            vm((HEADS, px // 2, d2), BF16), vm((4, 8, e), F32), vm((8, 128), F32),
            vm((3, 8, c // 4), F32), vm((3, n_sp, 8, c // 4), F32), vm((2, 2, width, c), BF16),
        ]
        + [vm(*edge16)] * 8
        + [
            vm((4, 8, 128), F32), vm((4, 8, e), F32), vm((4, tokens, e), BF16),
            vm((4, tokens + 8, 128), F32), vm((4, tokens + 8, 128), F32),
            vm((tokens, 128), BF16), vm((n_sp, tokens, 128), BF16), vm((8, 128), F32), vm((n_sp, 8, 128), F32),
            vm((2, 3, padded, c), BF16), vm((px, c), F32), vm((px, c), F32),
        ],
        compiler_params=params(cid),
        name="forward",
    )(*chunks, x, cot, temb, cap, w_emb, w_cap, gains, biases)


class Reducer:
    NAMES = ("d", "sb", "da", "db", "rx", "ry", "r", "zr")

    def __init__(self, at, nz, arrays, ssem, rsem):
        self.at, self.nz, self.arrays = at, nz, arrays
        self.ssem, self.rsem = ssem, rsem
        self.sent, self.groups = {}, []

    @staticmethod
    def buffers(nz, t, r):
        return [
            pltpu.VMEM((2, 4, t, nz, r, 128), BF16),
            pltpu.VMEM((4, t, nz, r, 128), BF16),
            pltpu.VMEM((t, nz, r // 2, 128), BF16),
            pltpu.VMEM((t, nz, r // 2, 128), BF16),
            pltpu.VMEM((t, nz, r, 128), BF16),
            pltpu.VMEM((t, nz, r, 128), BF16),
            pltpu.VMEM((t, nz, r, 128), BF16),
            pltpu.VMEM((nz - 1, t, r, 128), BF16),
        ]

    def send(self, g, j, src, dst, dev):
        self.sent[g, j] = remote(src, dst, self.ssem.at[g, j], self.rsem.at[g, j], dev)

    def add(self, a, t0, t1):
        g = len(self.groups)
        self.groups.append((a, t0, t1))
        b = self.arrays[a][1]
        self.send(g, 0, b["d"].at[1 - self.at.c, :, t0:t1], b["sb"].at[:, t0:t1], self.at.sib)

    def run(self, stage, *groups):
        one = (self.stage1, self.stage2, self.stage3, self.stage4)[stage - 1]
        for g in groups:
            one(g, *self.groups[g])

    def stage1(self, g, a, t0, t1):
        b, at = self.arrays[a][1], self.at
        d, sb = b["d"], b["sb"]
        self.sent[g, 0].wait_recv()
        n = t1 - t0

        def add(j, _):
            ii, tt = lax.div(j, n), t0 + lax.rem(j, n)
            d[at.c, ii, tt] = (d[at.c, ii, tt].astype(F32) + sb[ii, tt].astype(F32)).astype(BF16)
            return 0

        lax.fori_loop(0, 4 * n, add, 0)
        h = d.shape[4] // 2
        self.send(g, 1, d.at[at.c, at.id, t0:t1, :, :h], b["da"].at[t0:t1], at.yn)
        self.send(g, 2, d.at[at.c, at.id, t0:t1, :, h:], b["db"].at[t0:t1], at.xn)

    def stage2(self, g, a, t0, t1):
        b, at = self.arrays[a][1], self.at
        d = b["d"]
        h = d.shape[4] // 2
        self.sent[g, 1].wait_recv()
        self.sent[g, 2].wait_recv()

        def add(tt, _):
            d[at.c, at.ix, tt, :, :h] = (
                d[at.c, at.ix, tt, :, :h].astype(F32) + b["da"][tt].astype(F32)
            ).astype(BF16)
            d[at.c, at.iy, tt, :, h:] = (
                d[at.c, at.iy, tt, :, h:].astype(F32) + b["db"][tt].astype(F32)
            ).astype(BF16)
            return 0

        lax.fori_loop(t0, t1, add, 0)
        self.send(g, 3, d.at[at.c, at.ix, t0:t1], b["rx"].at[t0:t1], at.xn)
        self.send(g, 4, d.at[at.c, at.iy, t0:t1], b["ry"].at[t0:t1], at.yn)

    def stage3(self, g, a, t0, t1):
        b, at = self.arrays[a][1], self.at
        self.sent[g, 3].wait_recv()
        self.sent[g, 4].wait_recv()

        def add(tt, _):
            total = b["d"][at.c, at.i, tt].astype(F32) + b["rx"][tt].astype(F32) + b["ry"][tt].astype(F32)
            b["r"][tt] = total.astype(BF16)
            return 0

        lax.fori_loop(t0, t1, add, 0)
        for k in range(1, self.nz):
            there = lax.rem(at.z + k, self.nz)
            self.send(g, 4 + k, b["r"].at[t0:t1, there], b["zr"].at[k - 1, t0:t1], at.zp(k, self.nz))

    def stage4(self, g, a, t0, t1):
        (out, b), at = self.arrays[a], self.at
        for k in range(1, self.nz):
            self.sent[g, 4 + k].wait_recv()

        def add(tt, _):
            total = (
                b["d"][at.c, at.i, tt, at.z].astype(F32)
                + b["rx"][tt, at.z].astype(F32)
                + b["ry"][tt, at.z].astype(F32)
            )
            for k in range(1, self.nz):
                total = total + b["zr"][k - 1, tt].astype(F32)
            out[tt] = total
            return 0

        lax.fori_loop(t0, t1, add, 0)

    def finish(self):
        for cp in self.sent.values():
            cp.wait_send()


BACK_MAIL = 6 + 14 + 6 + 3 + 7 + 9 + 9
BACK_GROUPS = 7
BIG = 12


def conv_taps(t0, t1, w, ring, rsem, one):
    slots = ring.shape[0]

    def step(tap, _):
        slot = lax.rem(tap, slots)
        pltpu.make_async_copy(w.at[:, tap], ring.at[slot], rsem.at[slot]).wait()
        one(tap, jnp.concatenate([ring[slot, j] for j in range(4)], axis=-1))

        @pl.when(tap + slots < 9)
        def _():
            pltpu.make_async_copy(w.at[:, tap + slots], ring.at[slot], rsem.at[slot]).start()

        return 0

    lax.fori_loop(t0, t1, step, 0)


def ring_start(w, ring, rsem):
    for j in range(ring.shape[0]):
        pltpu.make_async_copy(w.at[:, j], ring.at[j], rsem.at[j]).start()


def backward_kernel(nz, width, *refs):
    hbm, refs = refs[:BIG], refs[BIG:]
    w_in, w_out = refs[:2]
    (st0, st1, st2, rows, ca, cb, ra, rb, ha, hb, dt_all, cap_all, emb_all, w_emb, w_cap, temb) = refs[2:18]
    output, image_grad, s_in, s_out, s_small, g_temb, g_cap, g_wemb, g_wcap, g_aff = refs[18:28]
    refs = refs[28:]
    big, refs = refs[:BIG], refs[BIG:]
    bufs = [dict(zip(Reducer.NAMES, refs[8 * a : 8 * a + 8])) for a in range(3)]
    (bsem, gsend, grecv, msend, mrecv, ring, rsem, g3, gt, acc, ng, pre_grad, res_grad,
     mine, every, edge_s, na, nb, pa, pb, tg_s, tg_r, mod_s, mod_r,
     gc_s, gc_r, pe_s, pe_r, gs_s, gs_r, ps_s, ps_r, aff_s, aff_r) = refs[24:]
    n_sp = 2 * nz
    at = Place()
    line = [at.rp(k, n_sp) for k in range(1, n_sp)]
    grid = img_peers(at)
    greet(line + grid)
    loads = []
    for j in range(BIG):
        cp = pltpu.make_async_copy(hbm[j], big[j], bsem.at[j])
        cp.start()
        loads.append(cp)
    of, qf, dkv, w_qkv, w_proj, res, cot, normed, a3_out, hidden, a3_in, x = big
    ring_start(w_out, ring, rsem)
    mail = Mail(msend, mrecv)
    red = Reducer(at, nz, [(s_out, bufs[0]), (s_small, bufs[1]), (s_in, bufs[2])], gsend, grecv)
    px, c = res.shape
    height = px // width
    members = px * n_sp * (c // GROUPS)
    d = c // HEADS
    cols = 3 * c // n_sp

    def publish(j, rows01, edges):
        out = []
        put_rows(mine.at[j], rows01)
        for ref, above, below in edges:
            mean = rows01[0] / px
            edge_s[j - 1, 0] = (ref[px - width :, :] - mean).astype(BF16)
            edge_s[j - 1, 1] = (ref[:width, :] - mean).astype(BF16)
            out.append(mail.send(edge_s.at[j - 1, 0], above, line[0]))
            out.append(mail.send(edge_s.at[j - 1, 1], below, line[-1]))
        for dev in line:
            out.append(mail.send(mine.at[j], every.at[j, at.s], dev))
        every[j, at.s] = mine[j]
        return out

    for j in range(8):
        loads[j].wait()
    unfold = lambda v: jnp.concatenate([v[:, :d], v[:, d:]], axis=0)
    att = jnp.concatenate([unfold(of[h]) for h in range(HEADS)], axis=1)
    pg = jnp.concatenate(
        [unfold(qf[h]) for h in range(HEADS)]
        + [dkv[h][:, :d] for h in range(HEADS)]
        + [dkv[h][:, d:] for h in range(HEADS)],
        axis=1,
    )
    wq, wp = joined(w_qkv), joined(w_proj)
    ng[...] = dot(pg, wq, 1, 0)
    center2, inverse2 = combine_stats(st2, px)
    hat = (res[...] - center2) * inverse2
    u = ng[...]
    sums = (jnp.sum(u, axis=0, keepdims=True), jnp.sum(u * hat, axis=0, keepdims=True))
    greeted(n_sp + 2)
    round_2 = publish(2, sums, [(ng, na, nb)])
    gq = dot(pg, normed[...], 0, 0).astype(BF16)
    go = dot(cot[...], att, 0, 0).astype(BF16)
    small = bufs[1]["d"]
    for j in range(n_sp):
        for b in range(4):
            lanes = slice(b * 128, (b + 1) * 128)
            small[j % 2, b, 0, j // 2, :cols] = gq[j * cols : (j + 1) * cols, lanes]
            small[j % 2, b, 0, j // 2, cols:] = go[j * (c // n_sp) : (j + 1) * (c // n_sp), lanes]
    red.add(1, 0, 1)
    output[...] = (res[...] + dot(att, wp, 1, 1)).astype(BF16)

    first = 2 * lax.rem(at.s, nz)
    value = lax.div(at.s, nz)
    halves = []
    for j in range(2):
        blk = dt_all[first + j].astype(F32)
        halves.append(jnp.where(value > 0, blk[:, d:], blk[:, :d]))
    tg_s[...] = jnp.concatenate(halves, axis=1).astype(BF16)
    round_a = [mail.send(tg_s, tg_r.at[at.i], dev) for dev in grid]
    tg_r[at.i] = tg_s[...]

    has_up, has_dn = edge_flags(n_sp, at.s)

    def upstream(j, uu, ua, ub, center, inverse, yy, ya, yb, base, keep):
        total = combine_sums(every[j])
        mul = rows[j, 0:1] * rows[j, 2:3]
        back = group_total(total * mul) / members
        s1, s2 = back[0:1, :], back[1:2, :]
        for r in range(height + 2):
            cut = slice((r - 1) * width, r * width)
            top, end = r == 0, r == height + 1
            if top or end:
                near = line[-1] if top else line[0]
                un = (ua if top else ub)[...].astype(F32) + get_rows(every[j, near[1]])[0] / px
            else:
                un = uu[cut, :]
            yn = ya[...] if top else yb[...] if end else yy[cut, :]
            g = inverse * (un * mul - s1 - (yn - center) * inverse * s2)
            if base:
                g = g + (base[1][...] if top else base[2][...] if end else base[0][cut, :]).astype(F32)
            if top:
                g = g * has_up
            elif end:
                g = g * has_dn
            elif keep is not None:
                keep[cut, :] = g
            shifted(g3, r, width, g.astype(BF16).astype(F32))
        gt[...] = g3[1, width : width + px, :].T
        return total

    def weight_taps(a, t0, t1):
        dst = bufs[a]["d"]
        a3 = a3_in if a == 2 else a3_out

        def one(tap, _):
            i, j = lax.div(tap, 3), lax.rem(tap, 3)
            part = dot(gt[...], a3[j, pl.ds(pl.multiple_of(i * width, width), px), :], 1, 0).astype(BF16)
            r = c // n_sp
            for k in range(n_sp):
                for b in range(4):
                    dst[k % 2, b, tap, k // 2] = part[k * r : (k + 1) * r, b * 128 : (b + 1) * 128]
            return 0

        lax.fori_loop(t0, t1, one, 0)
        red.add(a, t0, t1)

    def input_taps(w):
        def one(tap, wt):
            i, j = lax.div(tap, 3), lax.rem(tap, 3)
            lhs = g3[2 - j, pl.ds(pl.multiple_of((2 - i) * width, width), px), :]
            acc[...] = dot(lhs, wt, 1, 0) + jnp.where(tap > 0, acc[...], 0.0)

        conv_taps(0, 9, w, ring, rsem, one)

    for cp in round_2:
        cp.wait_recv()
    t2 = upstream(2, ng, na, nb, center2, inverse2, res, ra, rb, (cot, ca, cb), res_grad)
    red.run(1, 0)
    loads[8].wait()
    for tap in (0, 3, 6):
        weight_taps(0, tap, tap + 3)
    red.run(2, 0)
    input_taps(w_out)
    ring_start(w_in, ring, rsem)
    for j in range(9, BIG):
        loads[j].wait()
    center1, inverse1 = combine_stats(st1, px)
    hat = (hidden[...] - center1) * inverse1
    gain1, bias1, fac1 = rows[1, 0:1], rows[1, 1:2], rows[1, 2:3]
    v = acc[...] * silu_slope(hat * (gain1 * fac1) + (bias1 * fac1 + rows[1, 3:4]))
    pre_grad[...] = v
    sums = (jnp.sum(v, axis=0, keepdims=True), jnp.sum(v * hat, axis=0, keepdims=True))
    round_1 = publish(1, sums, [(pre_grad, pa, pb)])
    red.run(1, 1, 2, 3)
    red.run(3, 0)

    exact = lambda a, b, ca_, cb_: lax.dot_general(
        a, b, (((ca_,), (cb_,)), ((), ())), preferred_element_type=F32, precision=PRECISE
    )
    tokens = tg_s.shape[0]
    share = tokens // n_sp
    for cp in round_a:
        cp.wait_recv()
    flat_tg = tg_r[...].reshape(4 * tokens, 128)
    g_wcap[...] = dot(cap_all[...].reshape(4 * tokens, cap_all.shape[2]), flat_tg, 0, 0)
    gc_s[...] = dot(flat_tg, w_cap[...], 1, 1).astype(BF16).reshape(gc_s.shape)
    round_b = []
    for dev in line:
        cut = pl.ds(pl.multiple_of(dev[1] * share, share), share)
        round_b.append(mail.send(gc_s.at[:, cut, :], gc_r.at[at.s], dev))
    gc_r[at.s] = gc_s[:, pl.ds(pl.multiple_of(at.s * share, share), share), :]

    for cp in round_1:
        cp.wait_recv()
    t1 = upstream(1, pre_grad, pa, pb, center1, inverse1, hidden, ha, hb, None, None)
    mod = jnp.concatenate([t1[1:2] * gain1 + t1[0:1] * bias1, t1[0:1]], axis=1)
    for j in range(n_sp):
        mod_s[j] = jnp.broadcast_to(mod[:, j * 128 : (j + 1) * 128], (8, 128))
    round_m = [mail.send(mod_s.at[at.s], mod_r.at[at.i], dev) for dev in grid]
    mod_r[at.i] = mod_s[at.s]
    red.run(2, 1)
    weight_taps(2, 0, 3)
    red.run(2, 2)
    weight_taps(2, 3, 6)
    red.run(2, 3)
    weight_taps(2, 6, 9)
    red.run(1, 4, 5, 6)
    input_taps(w_in)

    center0, inverse0 = combine_stats(st0, px)
    hat = (x[...].astype(F32) - center0) * inverse0
    gain0 = rows[0, 0:1]
    v = acc[...] * silu_slope(hat * gain0 + rows[0, 1:2])
    acc[...] = v
    sums = (jnp.sum(v, axis=0, keepdims=True), jnp.sum(v * hat, axis=0, keepdims=True))
    round_0 = publish(0, sums, [])
    red.run(4, 0)
    red.run(3, 1)
    red.run(2, 4)
    for cp in round_m:
        cp.wait_recv()
    mods = jnp.concatenate([mod_r[j][0:1] for j in range(4)] + [jnp.zeros((4, 128), F32)])
    emb_t = emb_all[...].T
    g_wemb[...] = sum(emb_t[:, j : j + 1] * mods[j : j + 1] for j in range(4))
    pe_s[...] = exact(mods, w_emb[...].astype(F32), 1, 1)
    round_p = [mail.send(pe_s, pe_r.at[at.s], dev) for dev in line]
    pe_r[at.s] = pe_s[...]
    for cp in round_0:
        cp.wait_recv()
    t0 = combine_sums(every[0])
    zero = jnp.zeros((2, c), F32)
    aff = jnp.concatenate([t0[1:2], t1[1:2] * fac1, t2[1:2], t0[0:1], t1[0:1] * fac1, t2[0:1], zero])
    for j in range(4):
        aff_s[j] = aff[:, j * 128 : (j + 1) * 128]
    round_e = [mail.send(aff_s.at[dev[0]], aff_r.at[at.i], dev) for dev in grid]
    aff_r[at.i] = aff_s[at.i]
    total = group_total(t0 * gain0) / members
    image_grad[...] = res_grad[...] + inverse0 * (acc[...] * gain0 - total[0:1] - hat * total[1:2])
    for g in (2, 3):
        red.run(3, g)
        red.run(2, g + 3)
    for cp in round_b + round_p:
        cp.wait_recv()
    gc = gc_r[0].astype(F32)
    pe = pe_r[0]
    for j in range(1, n_sp):
        gc = gc + gc_r[j].astype(F32)
        pe = pe + pe_r[j]
    gs_s[...] = gc
    for j in range(4):
        ps_s[j] = jnp.broadcast_to(pe[j : j + 1], pe.shape)
    round_c = []
    for dev in grid:
        round_c.append(mail.send(gs_s.at[dev[0]], gs_r.at[at.i], dev))
        round_c.append(mail.send(ps_s.at[dev[0]], ps_r.at[at.i], dev))
    gs_r[at.i] = gs_s[at.i]
    ps_r[at.i] = ps_s[at.i]
    red.run(4, 1, 2, 3)
    red.run(3, 4, 5, 6)
    red.run(4, 4, 5, 6)
    red.finish()
    for cp in round_c + round_e:
        cp.wait_recv()
    g_cap[...] = jnp.concatenate([gs_r[j] for j in range(4)], axis=1)
    g_temb[...] = jnp.concatenate([ps_r[j] for j in range(4)], axis=1) * silu_slope(temb[...].astype(F32))
    g_aff[...] = aff_r[0] + aff_r[1] + aff_r[2] + aff_r[3]
    for cp in mail.sent:
        cp.wait_send()


def backward_call(big, w_in, w_out, small, nz, width, cid):
    px, c = big[5].shape
    n_sp = 2 * nz
    padded = px + 2 * width
    r = c // n_sp
    rs = (big[3].shape[1] + big[4].shape[1]) // n_sp
    dt_all, cap_all = small[10], small[11]
    tokens = dt_all.shape[1]
    e = cap_all.shape[2]
    share = tokens // n_sp
    outs = [
        ((px, c), BF16), ((px, c), F32), ((9, r, 128), F32), ((9, r, 128), F32), ((1, rs, 128), F32),
        ((8, 4 * e), F32), ((share, 4 * e), F32), ((e, 128), F32), ((e, 128), F32), ((8, 128), F32),
    ]
    vm = pltpu.VMEM
    return pl.pallas_call(
        functools.partial(backward_kernel, nz, width),
        out_shape=[jax.ShapeDtypeStruct(s, ty) for s, ty in outs],
        in_specs=[ANY] * (len(big) + 2) + [VM] * len(small),
        out_specs=[VM] * len(outs),
        scratch_shapes=[vm(v.shape, v.dtype) for v in big]
        + Reducer.buffers(nz, 9, r) + Reducer.buffers(nz, 1, rs) + Reducer.buffers(nz, 9, r)
        + [
            pltpu.SemaphoreType.DMA((len(big),)),
            pltpu.SemaphoreType.DMA((BACK_GROUPS, 4 + nz)),
            pltpu.SemaphoreType.DMA((BACK_GROUPS, 4 + nz)),
            pltpu.SemaphoreType.DMA((BACK_MAIL,)),
            pltpu.SemaphoreType.DMA((BACK_MAIL,)),
            vm((3, 4, c, 128), BF16),
            pltpu.SemaphoreType.DMA((3,)),
            vm((3, padded, c), BF16), vm((c, px), BF16),
            vm((px, c), F32), vm((px, c), F32), vm((px, c), F32), vm((px, c), F32),
            vm((3, 8, c // 4), F32), vm((3, n_sp, 8, c // 4), F32), vm((2, 2, width, c), BF16),
            vm((width, c), BF16), vm((width, c), BF16), vm((width, c), BF16), vm((width, c), BF16),
            vm((tokens, 128), BF16), vm((4, tokens, 128), BF16),
            vm((n_sp, 8, 128), F32), vm((4, 8, 128), F32),
            vm((4, tokens, e), BF16), vm((n_sp, 4, share, e), BF16),
            vm((8, e), F32), vm((n_sp, 8, e), F32),
            vm((4, share, e), F32), vm((4, share, e), F32),
            vm((4, 8, e), F32), vm((4, 8, e), F32),
            vm((4, 8, 128), F32), vm((4, 8, 128), F32),
        ],
        compiler_params=params(cid),
        name="backward",
    )(*big, w_in, w_out, *small)


def emit_kernel(cut, *refs):
    ins, outs, mids, loads, stores = refs[:10], refs[10:22], refs[22:31], refs[31], refs[32]
    output, image, s_in, s_out, s_small, g_temb, g_cap, g_wemb, g_wcap, g_aff = ins
    pairs = [
        (output, outs[0]), (image, outs[1]), (g_cap, outs[3]), (s_in, outs[4]), (s_out, outs[5]), (g_wemb, outs[6]),
        (s_small.at[0, :cut], outs[7]), (g_wcap, outs[8]), (s_small.at[0, cut:], outs[9]),
    ]
    copies = [pltpu.make_async_copy(src, mid, loads.at[j]) for j, ((src, _), mid) in enumerate(zip(pairs, mids))]
    for cp in copies:
        cp.start()
    backs = []
    for j, cp in enumerate(copies):
        cp.wait()
        backs.append(pltpu.make_async_copy(mids[j], pairs[j][1], stores.at[j]))
        backs[-1].start()
    outs[2][...] = g_temb[0:1, :]
    outs[10][...] = g_aff[0:3, :]
    outs[11][...] = g_aff[3:6, :]
    for cp in backs:
        cp.wait()


def emit_call(parts, cut):
    output, image, s_in, s_out, s_small, g_temb, g_cap, g_wemb, g_wcap, g_aff = parts
    rest = s_small.shape[1] - cut
    like = lambda v: jax.ShapeDtypeStruct(v.shape, v.dtype)
    f32 = lambda *s: jax.ShapeDtypeStruct(s, F32)
    shapes = [
        like(output), like(image), f32(1, g_temb.shape[1]), like(g_cap), like(s_in), like(s_out), like(g_wemb),
        f32(cut, 128), like(g_wcap), f32(rest, 128), f32(3, 128), f32(3, 128),
    ]
    in_specs = [ANY] * 10
    in_specs[5] = in_specs[9] = VM
    out_specs = [ANY] * 12
    out_specs[2] = out_specs[10] = out_specs[11] = VM
    return pl.pallas_call(
        functools.partial(emit_kernel, cut),
        out_shape=shapes,
        in_specs=in_specs,
        out_specs=out_specs,
        scratch_shapes=[pltpu.VMEM(shapes[j].shape, shapes[j].dtype) for j in (0, 1, 3, 4, 5, 6, 7, 8, 9)]
        + [pltpu.SemaphoreType.DMA((9,)), pltpu.SemaphoreType.DMA((9,))],
        compiler_params=params(),
        name="emit",
    )(*parts)


def fast_body(
    image_in, time_embed, caption, caption_mask, conv_in, conv_out, embed_proj, qkv_proj,
    caption_proj, out_proj, norm_gains, norm_biases, cotangent,
):
    n, height, width, c = image_in.shape
    n_sp = lax.axis_size("sp")
    nz = n_sp // 2
    px = height * width
    x = image_in.reshape(px, c)
    cot = cotangent.reshape(px, c)

    flat = lambda w: w.transpose(1, 2, 3, 0).reshape(9, w.shape[3], w.shape[0])
    (w_proj, w_in, w_out, w_qkv, hidden, a3_in, res, a3_out, g, normed, kv, q,
     st0, st1, st2, rows, ca, cb, ra, rb, ha, hb, kv_all, cap_all, emb_all) = forward_call(
        [out_proj.T[None], flat(conv_in), flat(conv_out), qkv_proj.T[None]], x, cot, time_embed, caption[0], embed_proj, caption_proj,
        norm_gains, norm_biases, nz, width, 0,
    )
    w_proj, w_qkv = w_proj[:, 0], w_qkv[:, 0]
    of, qf, dkv, dt_all = attention_call(kv, q, g, kv_all, caption_mask, 1)

    parts = backward_call(
        [of, qf, dkv, w_qkv, w_proj, res, cot, normed, a3_out, hidden, a3_in, x], w_in, w_out,
        [st0, st1, st2, rows, ca, cb, ra, rb, ha, hb, dt_all, cap_all, emb_all, embed_proj, caption_proj, time_embed],
        nz, width, 2,
    )
    output, image, g_temb, g_cap, s_in, s_out, g_wemb, g_qkv, g_wcap, g_out, g_gains, g_biases = emit_call(
        parts, qkv_proj.shape[1]
    )
    unflat = lambda g: g.reshape(3, 3, g.shape[1], 128).transpose(3, 0, 1, 2)
    return (
        output.reshape(image_in.shape), image.reshape(image_in.shape), g_temb, g_cap[None], unflat(s_in), unflat(s_out),
        g_wemb, g_qkv.T, g_wcap, g_out.T, g_gains, g_biases,
    )


def body(*args):
    image_in, qkv_proj = args[0], args[7]
    n, height, width, c = image_in.shape
    n_img, n_sp = lax.axis_size("img"), lax.axis_size("sp")
    fits = n == 1 and n_img == 4 and n_sp == HEADS and c == 512 and width == 64
    return fast_body(*args) if fits else plain_body(*args)


def solution(mesh):
    rows = P("img", "sp", None, None)
    kernel = P("img", None, None, "sp")
    flat = P("img", "sp")
    return jax.shard_map(
        body,
        mesh=mesh,
        in_specs=(
            rows, P("img", None), P("img", None, None), P("img", None), kernel, kernel,
            flat, flat, flat, flat, P(None, "img"), P(None, "img"), rows,
        ),
        out_specs=(
            rows, rows, P("img", None), P("img", "sp", None), kernel, kernel,
            flat, flat, flat, flat, P(None, "img"), P(None, "img"),
        ),
        check_vma=False,
    )
```

```python
import functools

import jax
import jax.numpy as jnp
from jax import lax
from jax.experimental import pallas as pl
from jax.experimental.pallas import tpu as pltpu
from jax.sharding import PartitionSpec as P

HEADS = 8
GROUPS = 32
EPSILON = 1e-05
PRECISE = lax.Precision.HIGHEST
MASKED = -1e30
BF16 = jnp.bfloat16
F32 = jnp.float32
MESH = pl.DeviceIdType.MESH
VMEM_BYTES = 60 * 1024 * 1024


def dot(a, b, ca, cb):
    return lax.dot_general(a, b, (((ca,), (cb,)), ((), ())), preferred_element_type=F32)


def silu(v):
    return v * jax.nn.sigmoid(v)


def silu_slope(v):
    s = jax.nn.sigmoid(v)
    return s * (1.0 + v * (1.0 - s))


def gather(x, axis, dim):
    return lax.all_gather(x, axis, axis=dim, tiled=True)


def scatter_sum(x, axis, dim):
    return lax.psum_scatter(x, axis, scatter_dimension=dim, tiled=True)


def swap(x, axis, split, concat):
    return lax.all_to_all(x, axis, split, concat, tiled=True)


def halo(x):
    count = lax.axis_size("sp")
    above = lax.ppermute(x[:, -1:], "sp", [(i, i + 1) for i in range(count - 1)])
    below = lax.ppermute(x[:, :1], "sp", [(i + 1, i) for i in range(count - 1)])
    return above, below


def group_sum(v):
    c = v.shape[-1]
    g = v.reshape(v.shape[:-1] + (GROUPS, c // GROUPS))
    s = jnp.sum(g, axis=-1, keepdims=True)
    return jnp.broadcast_to(s, g.shape).reshape(v.shape)


def norm_stats(x):
    n, r, w, c = x.shape
    cells = r * w * (c // GROUPS)
    parts = lax.axis_size("sp")
    mean = group_sum(jnp.sum(x, axis=(1, 2))) / cells
    dev = group_sum(jnp.sum(jnp.square(x - mean[:, None, None, :]), axis=(1, 2)))
    both = lax.all_gather(jnp.stack([mean, dev]), "sp")
    means, devs = both[:, 0], both[:, 1]
    center = jnp.mean(means, axis=0)
    var = (jnp.sum(devs, axis=0) + cells * jnp.sum(jnp.square(means - center), axis=0)) / (
        cells * parts
    )
    return center, lax.rsqrt(var + EPSILON)


def hat_of(x, center, inverse):
    return (x - center[:, None, None, :]) * inverse[:, None, None, :]


def norm_back(u, hat, inverse, gain, sum_u, sum_uh, members):
    s1 = group_sum(sum_u * gain) / members
    s2 = group_sum(sum_uh * gain) / members
    return inverse[:, None, None, :] * (
        u * gain - s1[:, None, None, :] - hat * s2[:, None, None, :]
    )


def pad_cols(x):
    return jnp.pad(x, ((0, 0), (0, 0), (1, 1), (0, 0)))


def conv(padded, weight_t, transposed):
    n, rp, wp, c = padded.shape
    r, w = rp - 2, wp - 2
    total = None
    for i in range(3):
        for j in range(3):
            a = padded[:, i : i + r, j : j + w].reshape(n * r * w, c)
            part = dot(a, weight_t[2 - i, 2 - j], 1, 0) if transposed else dot(a, weight_t[i, j], 1, 1)
            total = part if total is None else total + part
    return total.reshape(n, r, w, -1)


def conv_grad(padded, g):
    n, r, w, c = g.shape
    gf = g.reshape(n * r * w, c)
    rows = []
    for i in range(3):
        for j in range(3):
            a = padded[:, i : i + r, j : j + w].reshape(n * r * w, -1)
            rows.append(dot(gf, a, 0, 0))
    return jnp.stack(rows).reshape(3, 3, c, -1)


def to_pairs(x, images):
    n, px, h, d = x.shape
    y = x.transpose(0, 2, 1, 3).reshape(n * h, px, d)
    return swap(y, "sp", 0, 1)


def from_pairs(x, images):
    y = swap(x, "sp", 1, 0)
    return y.reshape(images, HEADS, y.shape[1], y.shape[2]).transpose(0, 2, 1, 3)


def attention_plain(q, k, v, g, tk, tv, keep, scale):
    p, length, d = q.shape
    block = min(512, length)
    keys = jnp.concatenate([tk, k], axis=1)
    values = jnp.concatenate([tv, v], axis=1)
    text = tk.shape[1]
    keep_all = jnp.concatenate([keep, jnp.ones((p, length), bool)], axis=1)

    def step(carry, blk):
        dk, dv = carry
        qb, gb = blk
        s = jnp.einsum("pqd,pkd->pqk", qb, keys, preferred_element_type=F32) * scale
        s = jnp.where(keep_all[:, None, :], s, MASKED)
        peak = jnp.max(s, axis=-1, keepdims=True)
        e = jnp.exp(s - peak)
        prob = e / jnp.sum(e, axis=-1, keepdims=True)
        pb = prob.astype(BF16)
        o = jnp.einsum("pqk,pkd->pqd", pb, values, preferred_element_type=F32)
        row = jnp.sum(o * gb.astype(F32), axis=-1, keepdims=True)
        dp = jnp.einsum("pqd,pkd->pqk", gb, values, preferred_element_type=F32)
        ds = (prob * (dp - row)).astype(BF16)
        dq = jnp.einsum("pqk,pkd->pqd", ds, keys, preferred_element_type=F32) * scale
        dk = dk + jnp.einsum("pqk,pqd->pkd", ds, qb, preferred_element_type=F32)
        dv = dv + jnp.einsum("pqk,pqd->pkd", pb, gb, preferred_element_type=F32)
        return (dk, dv), (o.astype(BF16), dq.astype(BF16))

    zeros = jnp.zeros((p, text + length, d), F32)
    cut = lambda t: t.reshape(p, length // block, block, d).swapaxes(0, 1)
    (dk, dv), (o, dq) = lax.scan(step, (zeros, zeros), (cut(q), cut(g)))
    join = lambda t: t.swapaxes(0, 1).reshape(p, length, d)
    dk = (dk * scale).astype(BF16)
    dv = dv.astype(BF16)
    return join(o), join(dq), dk[:, text:], dv[:, text:], dk[:, :text], dv[:, :text]


def plain_body(
    image_in, time_embed, caption, caption_mask, conv_in, conv_out, embed_proj, qkv_proj,
    caption_proj, out_proj, norm_gains, norm_biases, cotangent,
):
    n, rows, width, chans = image_in.shape
    n_img, n_sp = lax.axis_size("img"), lax.axis_size("sp")
    img, sp = lax.axis_index("img"), lax.axis_index("sp")
    px = rows * width
    members = px * n_sp * (chans // GROUPS)
    d = chans // HEADS
    scale = d ** -0.5
    pairs = n * HEADS // n_sp

    def whole(w):
        w = gather(w, "img", w.ndim - 1)
        return gather(w, "sp", w.ndim - 2)

    w_in = whole(conv_in.transpose(1, 2, 3, 0))
    w_out = whole(conv_out.transpose(1, 2, 3, 0))
    w_qkv = whole(qkv_proj.T)
    w_proj = whole(out_proj.T)
    affine = gather(jnp.concatenate([norm_gains, norm_biases]), "img", 1).astype(F32)
    gains, biases = affine[:3], affine[3:]

    embedded = silu(time_embed.astype(F32)).astype(BF16)
    emb_all = swap(embedded, "img", 1, 0)
    mod = scatter_sum(jnp.dot(emb_all, embed_proj, preferred_element_type=F32), "img", 0)
    mod = gather(mod, "sp", 1)
    scale_term, shift_term = mod[:, :chans], mod[:, chans:]
    cap_all = swap(caption, "img", 2, 0)
    cap_flat = cap_all.reshape(-1, cap_all.shape[2])
    kv = jnp.dot(cap_flat, caption_proj, preferred_element_type=F32)
    kv = scatter_sum(kv.reshape(cap_all.shape[0], cap_all.shape[1], -1), "img", 0).astype(BF16)
    kv = gather(kv, "sp", 2)
    text = kv.shape[1]
    kv_heads = kv.reshape(n, text, 2, HEADS, d).transpose(2, 0, 3, 1, 4).reshape(2, n * HEADS, text, d)
    mine = lax.dynamic_slice_in_dim(kv_heads, sp * pairs, pairs, 1)
    keep = jnp.repeat(caption_mask > 0, HEADS, axis=0)
    keep = lax.dynamic_slice_in_dim(keep, sp * pairs, pairs, 0)

    image_f = image_in.astype(F32)
    c0, i0 = norm_stats(image_f)
    hat0 = hat_of(image_f, c0, i0)
    first = hat0 * gains[0] + biases[0]
    act0 = silu(first).astype(BF16)
    above, below = halo(act0)
    pad0 = pad_cols(jnp.concatenate([above, act0, below], axis=1))
    hidden = conv(pad0, w_in, False)
    c1, i1 = norm_stats(hidden)
    hat1 = hat_of(hidden, c1, i1)
    second = hat1 * gains[1] + biases[1]
    pre = second * (1.0 + scale_term[:, None, None, :]) + shift_term[:, None, None, :]
    act1 = silu(pre).astype(BF16)
    above, below = halo(act1)
    pad1 = pad_cols(jnp.concatenate([above, act1, below], axis=1))
    residual = image_f + conv(pad1, w_out, False)
    c2, i2 = norm_stats(residual)
    hat2 = hat_of(residual, c2, i2)
    normed = (hat2 * gains[2] + biases[2]).astype(BF16).reshape(n * px, chans)
    qkv = dot(normed, w_qkv, 1, 1).astype(BF16)
    cot = cotangent.reshape(n * px, chans)
    g_att = dot(cot, w_proj, 1, 0).astype(BF16)
    four = jnp.concatenate([qkv, g_att], axis=1).reshape(n, px, 4, HEADS, d)
    packed = to_pairs(four.transpose(0, 1, 3, 2, 4).reshape(n, px, HEADS, 4 * d), n)
    q, k, v, g = (packed[..., j * d : (j + 1) * d] for j in range(4))
    o, dq, dk, dv, dtk, dtv = attention_plain(q, k, v, g, mine[0], mine[1], keep, scale)
    back = from_pairs(jnp.concatenate([o, dq, dk, dv], axis=-1), n)
    back = back.reshape(n * px, HEADS, 4, d).transpose(0, 2, 1, 3).reshape(n * px, 4 * chans)
    attended, proj_grad = back[:, :chans], back[:, chans:]
    output = residual + dot(attended, w_proj, 1, 1).reshape(image_in.shape)

    grad_out = dot(cot, attended, 0, 0)
    grad_qkv = dot(proj_grad, normed, 0, 0)
    normed_grad = dot(proj_grad, w_qkv, 1, 0).reshape(image_in.shape)

    def sums(u, hat):
        both = jnp.stack([jnp.sum(u, axis=(1, 2)), jnp.sum(u * hat, axis=(1, 2))])
        return lax.psum(both, "sp")

    su2, sh2 = sums(normed_grad, hat2)
    residual_grad = cotangent.astype(F32) + norm_back(
        normed_grad, hat2, i2, gains[2], su2, sh2, members
    )
    g2 = residual_grad.astype(BF16)
    above, below = halo(g2)
    gpad = pad_cols(jnp.concatenate([above, g2, below], axis=1))
    grad_conv_out = conv_grad(pad1, g2)
    pre_grad = conv(gpad, w_out, True) * silu_slope(pre)
    sa, sb = sums(pre_grad, hat1)
    fac = 1.0 + scale_term
    shift_grad = sa
    scale_grad = sb * gains[1] + sa * biases[1]
    u1 = pre_grad * fac[:, None, None, :]
    su1, sh1 = sa * fac, sb * fac
    g1 = norm_back(u1, hat1, i1, gains[1], su1, sh1, members).astype(BF16)
    above, below = halo(g1)
    gpad = pad_cols(jnp.concatenate([above, g1, below], axis=1))
    grad_conv_in = conv_grad(pad0, g1)
    u0 = conv(gpad, w_in, True) * silu_slope(first)
    su0, sh0 = sums(u0, hat0)
    grad_image = residual_grad + norm_back(u0, hat0, i0, gains[0], su0, sh0, members)

    mod_grad = jnp.concatenate([scale_grad, shift_grad], axis=1)
    cols = embed_proj.shape[1]
    mod_all = gather(mod_grad, "img", 0)
    mod_cols = lax.dynamic_slice_in_dim(mod_all, sp * cols, cols, 1)
    grad_embed_proj = jnp.einsum("ne,nd->ed", emb_all.astype(F32), mod_cols, precision=PRECISE)
    part = jnp.einsum("nd,ed->ne", mod_cols, embed_proj.astype(F32), precision=PRECISE)
    part = swap(lax.psum(part, "sp"), "img", 0, 1)
    grad_embed = part * silu_slope(time_embed.astype(F32))

    tg = gather(jnp.stack([dtk, dtv]), "sp", 1).reshape(2, n, HEADS, text, d)
    tg = tg.transpose(1, 3, 0, 2, 4).reshape(n, text, 2 * chans)
    cols = caption_proj.shape[1]
    tg = gather(lax.dynamic_slice_in_dim(tg, sp * cols, cols, 2), "img", 0).reshape(-1, cols)
    grad_caption_proj = dot(cap_flat, tg, 0, 0)
    gc = dot(tg, caption_proj, 1, 1).reshape(cap_all.shape)
    gc = scatter_sum(gc, "sp", 1)
    grad_caption = swap(gc, "img", 0, 2)

    grads = jnp.concatenate(
        [jnp.sum(t, axis=0)[None] for t in (sh0, sh1, sh2, su0, su1, su2)]
    )
    grads = scatter_sum(grads, "img", 1)

    def shared(w):
        w = scatter_sum(w, "sp", w.ndim - 2)
        return scatter_sum(w, "img", w.ndim - 1)

    return (
        output.astype(BF16),
        grad_image,
        grad_embed,
        grad_caption,
        shared(grad_conv_in).transpose(3, 0, 1, 2),
        shared(grad_conv_out).transpose(3, 0, 1, 2),
        grad_embed_proj,
        shared(grad_qkv).T,
        grad_caption_proj,
        shared(grad_out).T,
        grads[:3],
        grads[3:],
    )


class Place:
    def __init__(self):
        self.i = lax.axis_index("img")
        self.s = lax.axis_index("sp")
        self.z = lax.div(self.s, 2)
        self.c = lax.rem(self.s, 2)
        x = lax.rem(self.i, 2)
        y = lax.div(self.i, 2)
        self.ix = self.i + 1 - 2 * x
        self.iy = self.i + 2 - 4 * y
        self.id = 3 - self.i
        self.sib = (self.i, self.s + 1 - 2 * self.c)
        self.xn = (self.ix, self.s)
        self.yn = (self.iy, self.s)

    def zp(self, k, nz):
        return (self.i, 2 * lax.rem(self.z + k, nz) + self.c)

    def rp(self, k, n_sp):
        return (self.i, lax.rem(self.s + k, n_sp))


def greet(peers):
    bar = pltpu.get_barrier_semaphore()
    for p in peers:
        pl.semaphore_signal(bar, inc=1, device_id=p, device_id_type=MESH)


def greeted(count):
    pl.semaphore_wait(pltpu.get_barrier_semaphore(), count)


def remote(src, dst, ssem, rsem, dev):
    cp = pltpu.make_async_remote_copy(
        src_ref=src, dst_ref=dst, send_sem=ssem, recv_sem=rsem, device_id=dev, device_id_type=MESH
    )
    cp.start()
    return cp


def params(cid=None, grid=0):
    extra = {} if cid is None else {"collective_id": cid, "has_side_effects": True}
    if grid:
        extra["dimension_semantics"] = ("arbitrary",) * grid
    return pltpu.CompilerParams(vmem_limit_bytes=VMEM_BYTES, **extra)


ANY = pl.BlockSpec(memory_space=pl.ANY)
VM = pl.BlockSpec(memory_space=pltpu.VMEM)
def channel_stats(v):
    mean = jnp.sum(v, axis=0, keepdims=True) / v.shape[0]
    dev = v - mean
    return mean, jnp.sum(dev * dev, axis=0, keepdims=True)


def put_rows(dst, pair):
    n = pair[0].shape[1] // 128
    for a, row in enumerate(pair):
        for j in range(n):
            dst[a * n + j : a * n + j + 1, :] = row[:, j * 128 : (j + 1) * 128]


def get_rows(block):
    n = block.shape[0] // 2
    return tuple(jnp.concatenate([block[a * n + j : a * n + j + 1] for j in range(n)], axis=1) for a in range(2))


def group_total(rows):
    c = rows.shape[1]
    size = 512 // GROUPS
    a = lax.broadcasted_iota(jnp.int32, (128, 128), 0)
    b = lax.broadcasted_iota(jnp.int32, (128, 128), 1)
    same = jnp.where(lax.bitwise_xor(a, b) < size, 1.0, 0.0).astype(BF16)
    high = rows.astype(BF16)
    rest = rows - high.astype(F32)
    mid = rest.astype(BF16)
    low = (rest - mid.astype(F32)).astype(BF16)
    parts = jnp.concatenate([high.astype(F32), mid.astype(F32), low.astype(F32)]).astype(BF16)
    total = jnp.concatenate(
        [dot(parts[:, j * 128 : (j + 1) * 128], same, 1, 0) for j in range(c // 128)], axis=1
    )
    n = rows.shape[0]
    return total[:n] + total[n : 2 * n] + total[2 * n :]


def combine_stats(every, px):
    n_sp, rows, lanes = every.shape
    half = rows // 2
    size = half * lanes // GROUPS
    means = [every[j, :half, :] for j in range(n_sp)]
    center_c = sum(means) / n_sp
    dev = sum(every[j, half:, :] for j in range(n_sp))
    dev = dev + px * sum((m - center_c) * (m - center_c) for m in means)
    spread = lambda v: group_total(jnp.concatenate([v, v]))[:half]
    center = spread(center_c) / size
    off = center_c - center
    var = spread(dev + (px * n_sp) * (off * off)) / (px * n_sp * size)
    return get_rows(jnp.concatenate([center, lax.rsqrt(var + EPSILON)]))


def combine_sums(every):
    total = every[0]
    for j in range(1, every.shape[0]):
        total = total + every[j]
    a, b = get_rows(total)
    return jnp.concatenate([a, b, jnp.zeros((6, a.shape[1]), F32)])


def edge_flags(n_sp, s):
    return jnp.where(s > 0, 1.0, 0.0), jnp.where(s < n_sp - 1, 1.0, 0.0)


def shifted(dst, row, width, block):
    col = lax.broadcasted_iota(jnp.int32, block.shape, 0)
    r = slice(row * width, (row + 1) * width)
    dst[1, r, :] = block.astype(BF16)
    dst[0, r, :] = jnp.where(col == 0, 0.0, pltpu.roll(block, 1, 0)).astype(BF16)
    dst[2, r, :] = jnp.where(col == width - 1, 0.0, pltpu.roll(block, width - 1, 0)).astype(BF16)


def joined(w_ref, *lead):
    return jnp.concatenate([w_ref[(j,) + lead] for j in range(4)], axis=-1)


def three_parts(v):
    a = v.astype(BF16).astype(F32)
    b = (v - a).astype(BF16).astype(F32)
    return a, b, v - a - b


AHEAD = 3


def attention_kernel(
    n_sp, BK, kv, qin, gin, text, keep, of, qf, dkv, dt,
    kv_r, q_r, g_r, q_s, o_s, dq_o, dkv_s, dt_s, k_s, v_s, s_s, e_s, g_s, dq_s, peak_s, lsem, ssem, rsem,
):
    at = Place()
    nz = n_sp // 2
    px = kv.shape[1]
    L, T = n_sp * px, text.shape[1]
    d = kv.shape[2] // 2
    BQ = px // 2
    line = [at.rp(k, n_sp) for k in range(1, n_sp)]
    greet(line)
    own = [
        pltpu.make_async_copy(kv.at[at.s], kv_r.at[at.s], lsem.at[0]),
        pltpu.make_async_copy(qin.at[at.s], q_r.at[at.s], lsem.at[1]),
        pltpu.make_async_copy(gin, g_r, lsem.at[6]),
    ]
    for cp in own:
        cp.start()
    greeted(n_sp - 1)
    keys = [remote(kv.at[dev[1]], kv_r.at[at.s], ssem.at[0, k + 1], rsem.at[0, k + 1], dev) for k, dev in enumerate(line)]

    def source(k):
        return 2 * lax.rem(at.z - lax.div(k, 2) + nz, nz) + lax.rem(at.c + lax.rem(k, 2), 2)

    def target(k):
        return 2 * lax.rem(at.z + lax.div(k, 2), nz) + lax.rem(at.c + lax.rem(k, 2), 2)

    def query_copy(k):
        return pltpu.make_async_remote_copy(
            src_ref=qin.at[target(k)], dst_ref=q_r.at[at.s], send_sem=ssem.at[1, k], recv_sem=rsem.at[1, k],
            device_id=(at.i, target(k)), device_id_type=MESH,
        )

    odd = lax.rem(at.s, 2)
    pair = lax.div(at.s, 2)
    ones = (lax.broadcasted_iota(jnp.int32, (1, d), 1) < 3).astype(F32).astype(BF16)
    picked = []
    for j in (pair, HEADS // 2 + pair):
        blk = text[j].astype(F32)
        picked.append(jnp.where(odd > 0, blk[:, d:], blk[:, :d]).astype(BF16))
    k_s[0:T, :] = picked[0]
    v_s[0:T, :] = jnp.concatenate([picked[1], jnp.broadcast_to(ones, (T, d))], axis=1)

    def rows_of(o, n=px, start=0):
        return pl.ds(pl.multiple_of(o * px + start, 128), n)

    def take(j):
        rows = rows_of(j, px, T)
        k_s[rows, :] = kv_r[j][:, :d]
        v_s[rows, :] = jnp.concatenate([kv_r[j][:, d:], jnp.broadcast_to(ones, (px, d))], axis=1)

    for k in range(1, AHEAD):
        query_copy(k).start()
    for cp in own:
        cp.wait()
    take(at.s)
    for k in range(1, n_sp):
        keys[k - 1].wait_recv()
        take(lax.rem(at.s - k + n_sp, n_sp))
    blocks = [(0, T)] + [(T + j * BK, BK) for j in range(L // BK)]
    scale = d ** -0.5

    def back_copy(j, k, src, dst, o):
        return pltpu.make_async_remote_copy(
            src_ref=src.at[o], dst_ref=dst.at[at.s], send_sem=ssem.at[j, k], recv_sem=rsem.at[j, k],
            device_id=(at.i, o), device_id_type=MESH,
        )

    def scores(q, slot, st, n, peak):
        s = dot(q, k_s[st : st + n, :], 1, 1)
        if st == 0:
            s = jnp.where(keep[...] > 0, s, MASKED)
        s_s[slot, :, st : st + n] = s
        for j in range(n // 128):
            piece = s[:, 128 * j : 128 * j + 128]
            peak = piece if peak is None else jnp.maximum(peak, piece)
        return peak

    def query(o, part):
        return q_r[o][:, part * d : (part + 1) * d]

    def forward(o, part, o_next):
        nxt = query(o_next, 1 - part)
        g = g_r[o][:, part * d : (part + 1) * d]
        rows = rows_of(o, BQ, part * BQ)
        q_s[rows, :] = query(o, part)
        top = jnp.max(peak_s[part], axis=1, keepdims=True)
        out = jnp.zeros((BQ, 2 * d), F32)
        peak = None
        for st, n in blocks:
            peak = scores(nxt, 1 - part, st, n, peak)
            e = jnp.exp(s_s[part, :, st : st + n] - top).astype(BF16)
            e_s[rows, st : st + n] = e
            out = out + dot(e, v_s[st : st + n, :], 1, 0)
        peak_s[1 - part] = peak
        inverse = 1.0 / out[:, d : d + 1]
        out = out[:, :d] * inverse
        g = g.astype(F32) * inverse
        row = jnp.sum(out * g, axis=1, keepdims=True)
        lane = lax.broadcasted_iota(jnp.int32, (BQ, d), 1)
        extra = jnp.zeros((BQ, d), F32)
        for j, piece in enumerate(three_parts(-row)):
            extra = jnp.where(lane == j, piece, extra)
        g_s[rows, :] = jnp.concatenate([g, extra], axis=1).astype(BF16)
        o_s[o, :, part * d : (part + 1) * d] = out.astype(BF16)

    peak = None
    for st, n in blocks:
        peak = scores(query(at.s, 0), 0, st, n, peak)
    peak_s[0] = peak

    def owner(k, _):
        o = source(k)

        @pl.when(k + AHEAD < n_sp)
        def _():
            query_copy(k + AHEAD).start()

        forward(o, 0, o)

        @pl.when(k + 1 < n_sp)
        def _():
            query_copy(k + 1).wait_recv()

        forward(o, 1, source(lax.rem(k + 1, n_sp)))

        @pl.when(k > 0)
        def _():
            back_copy(2, k, o_s, of, o).start()

        return 0

    lax.fori_loop(0, n_sp, owner, 0)
    local = [pltpu.make_async_copy(o_s.at[at.s], of.at[at.s], lsem.at[2])]

    def block(o, cols, kc, vc, dk, dv, fresh):
        rows = rows_of(o)
        g, q = g_s[rows, :], q_s[rows, :]
        e = e_s[rows, cols]
        ds = (e.astype(F32) * dot(g, vc, 1, 1)).astype(BF16)
        part = dot(ds, kc, 1, 0)
        dq_s[rows, :] = part if fresh else dq_s[rows, :] + part
        return dk + dot(q.T, ds, 1, 0), dv + dot(g[:, :d].T, e, 1, 0)

    def both(dk, dv):
        return jnp.concatenate([dk, dv], axis=0).astype(BF16).T

    def chunk(cols, n, fresh):
        kc, vc = k_s[cols, :], v_s[cols, :]
        zero = jnp.zeros((d, n), F32)
        dk, dv = lax.fori_loop(
            0, n_sp, lambda o, acc: block(o, cols, kc, vc, acc[0], acc[1], fresh), (zero, zero), unroll=8
        )
        return both(dk, dv)

    def chip_columns(z):
        return pl.ds(pl.multiple_of(T + z * (2 * px), 128), 2 * px)

    dt_s[...] = chunk(pl.ds(0, T), T, True)
    sent = [remote(dt_s, dt.at[at.s], ssem.at[5, k + 1], rsem.at[5, k + 1], dev) for k, dev in enumerate(line)]
    local.append(pltpu.make_async_copy(dt_s, dt.at[at.s], lsem.at[3]))

    def chip(k, _):
        z = lax.rem(at.z + k, nz)
        grads = chunk(chip_columns(z), 2 * px, False)
        for core in range(2):
            o = 2 * z + core
            dkv_s[o] = grads[core * px : (core + 1) * px]
            back_copy(4, lax.rem(o - at.s + n_sp, n_sp), dkv_s, dkv, o).start()
        return 0

    lax.fori_loop(1, nz, chip, 0)
    cols = chip_columns(at.z)
    kc, vc = k_s[cols, :], v_s[cols, :]
    zero = jnp.zeros((d, 2 * px), F32)

    def last(j, acc):
        o = 2 * lax.rem(at.z + 1 + lax.div(j, 2), nz) + lax.rem(j, 2)
        acc = block(o, cols, kc, vc, acc[0], acc[1], False)
        dq = (dq_s[rows_of(o), :] * scale).astype(BF16)
        dq_o[o] = jnp.concatenate([dq[:BQ], dq[BQ:]], axis=1)

        @pl.when(o != at.s)
        def _():
            back_copy(3, lax.rem(o - at.s + n_sp, n_sp), dq_o, qf, o).start()

        return acc

    grads = both(*lax.fori_loop(0, n_sp, last, (zero, zero), unroll=2))
    for core in range(2):
        dkv_s[2 * at.z + core] = grads[core * px : (core + 1) * px]
    sib = at.sib[1]
    back_copy(4, lax.rem(sib - at.s + n_sp, n_sp), dkv_s, dkv, sib).start()
    local.append(pltpu.make_async_copy(dkv_s.at[at.s], dkv.at[at.s], lsem.at[4]))
    local.append(pltpu.make_async_copy(dq_o.at[at.s], qf.at[at.s], lsem.at[5]))
    for cp in local:
        cp.start()
    for k in range(1, n_sp):
        back_copy(2, k, o_s, of, source(k)).wait()
        o = lax.rem(at.s + k, n_sp)
        back_copy(4, k, dkv_s, dkv, o).wait()
        back_copy(3, k, dq_o, qf, o).wait()
    for k in range(1, n_sp):
        query_copy(k).wait_send()
    for cp in keys:
        cp.wait_send()
    for cp in sent:
        cp.wait()
    for cp in local:
        cp.wait()


def attention_call(kv, qin, gin, text, keep, cid):
    n_sp, px, d2 = kv.shape
    T = text.shape[1]
    L = n_sp * px
    d = d2 // 2
    outs = [(n_sp, px // 2, d2), (n_sp, px // 2, d2), (n_sp, px, d2), (n_sp, T, d2)]
    vm = pltpu.VMEM
    return pl.pallas_call(
        functools.partial(attention_kernel, n_sp, 1024),
        out_shape=[jax.ShapeDtypeStruct(s, BF16) for s in outs],
        in_specs=[ANY, ANY, ANY, VM, VM],
        out_specs=[ANY] * 4,
        scratch_shapes=[
            vm((n_sp, px, d2), BF16), vm((n_sp, px // 2, d2), BF16), vm((n_sp, px // 2, d2), BF16), vm((L, d), BF16),
            vm((n_sp, px // 2, d2), BF16),
            vm((n_sp, px // 2, d2), BF16), vm((n_sp, px, d2), BF16), vm((T, d2), BF16),
            vm((T + L, d), BF16), vm((T + L, d2), BF16), vm((2, px // 2, T + L), F32), vm((L, T + L), BF16),
            vm((L, d2), BF16), vm((L, d), F32), vm((2, px // 2, 128), F32),
            pltpu.SemaphoreType.DMA((7,)),
            pltpu.SemaphoreType.DMA((6, n_sp)),
            pltpu.SemaphoreType.DMA((6, n_sp)),
        ],
        compiler_params=params(cid),
        name="attention",
    )(kv, qin, gin, text, keep)


class Mail:
    def __init__(self, ssem, rsem):
        self.ssem, self.rsem, self.sent = ssem, rsem, []

    def send(self, src, dst, dev):
        j = len(self.sent)
        cp = remote(src, dst, self.ssem.at[j], self.rsem.at[j], dev)
        self.sent.append(cp)
        return cp


class Gather:
    def __init__(self, at, nz, ins, outs, dims, ssem, rsem):
        self.at, self.nz, self.ins, self.outs, self.dims = at, nz, ins, outs, dims
        self.ssem, self.rsem = ssem, rsem
        self.sent, self.kinds = {}, {}
        self.order = sorted(range(1, nz), key=lambda k: min(k, nz - k))

    @staticmethod
    def copies(nz):
        return 3 * nz - 1 + 7 * nz

    def view(self, a, ii, k, core, half=None):
        at, nz, r = self.at, self.nz, self.dims[a][1]
        sp = 2 * lax.rem(at.z - k + nz, nz) + core
        if half is None:
            return self.outs[a].at[ii, :, pl.ds(pl.multiple_of(sp * r, r), r), :]
        h = r // 2
        return self.outs[a].at[ii, :, pl.ds(pl.multiple_of(sp * r + half * h, h), h), :]

    def send(self, a, kind, src, dst, dev):
        j = self.kinds.setdefault(kind, len(self.kinds))
        self.sent[a, kind] = remote(src, dst, self.ssem.at[a, j], self.rsem.at[a, j], dev)

    def forward(self, a, kind, ref, dev):
        self.send(a, kind, ref, ref, dev)

    def near(self, a):
        at = self.at
        own = self.view(a, at.i, 0, at.c)
        self.send(a, ("x", 0), self.ins[a], own, at.xn)
        self.send(a, ("y", 0), self.ins[a], own, at.yn)
        self.send(a, ("s", 0), self.ins[a], own, at.sib)

    def along(self, a, ks):
        for k in ks:
            self.send(a, ("z", k), self.ins[a], self.view(a, self.at.i, 0, self.at.c), self.at.zp(k, self.nz))

    def second(self, a, ks=None):
        at = self.at
        for k in self.order if ks is None else ks:
            self.sent[a, ("z", k)].wait_recv()
            got = self.view(a, at.i, k, at.c)
            self.forward(a, ("x", k), got, at.xn)
            self.forward(a, ("y", k), got, at.yn)
            self.forward(a, ("s", k), got, at.sib)

    def third(self, a):
        at = self.at
        for k in [0] + self.order:
            self.sent[a, ("x", k)].wait_recv()
            self.forward(a, ("da", k), self.view(a, at.ix, k, at.c, 0), at.yn)
            self.forward(a, ("sx", k), self.view(a, at.ix, k, at.c), at.sib)
            self.sent[a, ("y", k)].wait_recv()
            self.forward(a, ("db", k), self.view(a, at.iy, k, at.c, 1), at.xn)
            self.forward(a, ("sy", k), self.view(a, at.iy, k, at.c), at.sib)

    def fourth(self, a):
        at = self.at
        for k in [0] + self.order:
            self.sent[a, ("da", k)].wait_recv()
            self.forward(a, ("sa", k), self.view(a, at.id, k, at.c, 0), at.sib)
            self.sent[a, ("db", k)].wait_recv()
            self.forward(a, ("sb", k), self.view(a, at.id, k, at.c, 1), at.sib)

    def complete(self, a):
        for (b, kind), cp in self.sent.items():
            if b == a and kind[0][0] == "s":
                cp.wait_recv()

    def finish(self):
        for cp in self.sent.values():
            cp.wait_send()


def img_peers(at):
    return [(lax.rem(at.i + k, 4), at.s) for k in range(1, 4)]


FORWARD_MAIL = 4 * 3 + 3 + 2 * 7 + 4 + 7 + 2 * (2 + 7) + 7


def forward_kernel(nz, width, dims, *refs):
    na = len(dims)
    chunks, refs = refs[:na], refs[na:]
    x, cot, temb, cap, w_emb, w_cap, gains, biases = refs[:8]
    outs, refs = refs[8 : 8 + na], refs[8 + na :]
    hidden_o, a0_o, res_o, a1_o, g_o, normed_o, kv_o, qf_o = refs[:8]
    st0, st1, st2, rows, ca, cb, ra, rb, ha, hb, kv_all, cap_all, emb_all = refs[8:21]
    refs = refs[21:]
    weights, refs = refs[:na], refs[na:]
    (ssem, rsem, lsem, msend, mrecv, g_s, emb, affine, mine, every, edge_s, xa, xb, ca_s, cb_s, ha_s, hb_s, ra_s, rb_s,
     aff_s, emb_s, cap_s, part, part_r, kv_s, kv_r, mod_s, mod_r, acts, hidden, res, normed, kv, qf) = refs
    n_sp = 2 * nz
    at = Place()
    line = [at.rp(k, n_sp) for k in range(1, n_sp)]
    grid = img_peers(at)
    greet(line + grid)
    mail = Mail(msend, mrecv)
    got = Gather(at, nz, chunks, weights, dims, ssem, rsem)
    PROJ, IN, OUT, QKV = range(4)
    px, c = x.shape
    height = px // width
    d = c // HEADS
    tokens = cap.shape[0]
    e = cap.shape[1] // 4
    half = px // 2
    local = []

    def copy(src, dst):
        cp = pltpu.make_async_copy(src, dst, lsem.at[len(local)])
        cp.start()
        local.append(cp)
        return cp

    embedded = silu(temb[...].astype(F32)).astype(BF16).astype(F32)
    for j in range(4):
        emb[j] = jnp.broadcast_to(embedded[:, j * e : (j + 1) * e], (8, e))
    affine[0:3] = gains[...].astype(F32)
    affine[3:6] = biases[...].astype(F32)

    def publish(j, v, edges):
        pair = channel_stats(v)
        put_rows(mine.at[j], pair)
        out = []
        for ref, above, below in edges:
            if ref is None:
                edge_s[j - 1, 0] = (v[px - width :] - pair[0]).astype(BF16)
                edge_s[j - 1, 1] = (v[:width] - pair[0]).astype(BF16)
                out.append(mail.send(edge_s.at[j - 1, 0], above, line[0]))
                out.append(mail.send(edge_s.at[j - 1, 1], below, line[-1]))
            else:
                out.append(mail.send(ref.at[px - width :], above, line[0]))
                out.append(mail.send(ref.at[:width], below, line[-1]))
        for dev in line:
            out.append(mail.send(mine.at[j], every.at[j, at.s], dev))
        every[j, at.s] = mine[j]
        return out

    def fold(v):
        return jnp.concatenate([v[:half], v[half:]], axis=1)

    greeted(n_sp + 2)
    close, far = got.order[:2], got.order[2:]
    got.along(PROJ, got.order)
    got.near(PROJ)
    got.along(IN, close)
    got.near(IN)
    stat0 = publish(0, x[...].astype(F32), [(x, xa, xb), (cot, ca_s, cb_s)])
    round1 = []
    share = tokens // 2
    part_tokens = pl.ds(pl.multiple_of(at.c * share, share), share)
    for dev in grid:
        round1.append(mail.send(affine, aff_s.at[at.i], dev))
        round1.append(mail.send(emb.at[dev[0]], emb_s.at[at.i], dev))
        round1.append(
            mail.send(cap.at[part_tokens, pl.ds(pl.multiple_of(dev[0] * e, e), e)], cap_s.at[at.i, part_tokens], dev)
        )
    own_cap = copy(cap.at[:, pl.ds(pl.multiple_of(at.i * e, e), e)], cap_s.at[at.i])
    aff_s[at.i] = affine[...]
    emb_s[at.i] = emb[at.i]
    got.near(OUT)
    own = [copy(got.ins[a], got.view(a, at.i, 0, at.c)) for a in range(na)]
    got.second(PROJ)
    got.second(IN, close[:1])
    got.along(IN, far)
    got.second(IN, close[1:])
    got.third(PROJ)
    got.along(OUT, close)
    got.second(IN, far)
    got.along(OUT, far)
    got.fourth(PROJ)
    got.third(IN)
    got.second(OUT)
    got.along(QKV, got.order)

    own_cap.wait()
    for cp in round1:
        cp.wait_recv()
    halves = []
    for dev in grid:
        here = cap_s.at[dev[0], part_tokens]
        halves.append(mail.send(here, here, at.sib))
    for cp in halves:
        cp.wait_recv()
    for j in range(4):
        part[j, :tokens] = dot(cap_s[j], w_cap[...], 1, 0)
        part[j, tokens:] = dot(emb_s[j].astype(BF16), w_emb[...], 1, 0)
    round2 = [mail.send(part.at[dev[0]], part_r.at[at.i], dev) for dev in grid]
    part_r[at.i] = part[at.i]
    cap_all[...] = cap_s[...]
    emb_all[...] = jnp.concatenate([emb_s[j][0:1] for j in range(4)] + [jnp.zeros((4, e), F32)])
    aff = jnp.concatenate([aff_s[j] for j in range(4)], axis=1)
    rows[...] = jnp.zeros_like(rows)
    for j in range(3):
        rows[j, 0:1] = aff[j : j + 1]
        rows[j, 1:2] = aff[3 + j : 4 + j]
        rows[j, 2:3] = jnp.ones((1, c), F32)

    has_up, has_dn = edge_flags(n_sp, at.s)

    def restore(j, above, below, above_o, below_o):
        for src, dst, dev in ((above, above_o, line[-1]), (below, below_o, line[0])):
            dst[...] = src[...].astype(F32) + get_rows(every[j, dev[1]])[0]

    def activate(j, v, above, below):
        center, inverse = combine_stats(every.at[j], px)
        mul = inverse * rows[j, 0:1] * rows[j, 2:3]
        add = rows[j, 1:2] * rows[j, 2:3] + rows[j, 3:4]
        for r in range(height + 2):
            top, end = r == 0, r == height + 1
            t = above[...] if top else below[...] if end else v[(r - 1) * width : r * width, :]
            t = silu((t.astype(F32) - center) * mul + add)
            if top:
                t = t * has_up
            elif end:
                t = t * has_dn
            shifted(acts.at[j], r, width, t)

    def taps(w, out, t0, t1, base):
        a3 = acts.at[0 if base is None else 1]

        def one(tap, _):
            i, j = lax.div(tap, 3), lax.rem(tap, 3)
            lhs = a3[j, pl.ds(pl.multiple_of(i * width, width), px), :]
            first = 0.0 if base is None else base[...].astype(F32)
            out[...] = dot(lhs, joined(w, tap), 1, 1) + jnp.where(tap > 0, out[...], first)
            return 0

        lax.fori_loop(t0, t1, one, 0)

    for cp in stat0:
        cp.wait_recv()
    activate(0, x, xa, xb)
    copy(acts.at[0], a0_o)
    got.fourth(IN)
    for cp in own:
        cp.wait()
    got.complete(IN)
    copy(weights[IN], outs[IN])
    taps(weights[IN], hidden, 0, 3, None)
    got.complete(PROJ)
    g = dot(cot[...], joined(weights[PROJ], 0), 1, 0).astype(BF16)
    for h in range(HEADS):
        g_s[h] = fold(g[:, h * d : (h + 1) * d])
    copy(weights[PROJ], outs[PROJ])
    round_g = [mail.send(g_s.at[dev[1]], g_o.at[at.s], dev) for dev in line]
    copy(g_s.at[at.s], g_o.at[at.s])
    taps(weights[IN], hidden, 3, 6, None)
    got.third(OUT)
    taps(weights[IN], hidden, 6, 9, None)
    stat1 = publish(1, hidden[...], [(None, ha_s, hb_s)])
    copy(hidden, hidden_o)
    for cp in round2:
        cp.wait_recv()
    total = part_r[0] + part_r[1] + part_r[2] + part_r[3]
    kv_s[...] = total[:tokens].astype(BF16)
    mod_s[...] = total[tokens:]
    round3 = []
    for dev in line:
        round3.append(mail.send(kv_s, kv_r.at[at.s], dev))
        round3.append(mail.send(mod_s, mod_r.at[at.s], dev))
    kv_r[at.s] = kv_s[...]
    mod_r[at.s] = mod_s[...]
    got.near(QKV)
    got.second(QKV)
    got.fourth(OUT)
    got.third(QKV)
    for cp in round3 + stat1:
        cp.wait_recv()
    kv_all[...] = kv_r[...]
    mod = jnp.concatenate([mod_r[j][0:1] for j in range(n_sp)], axis=1)
    rows[1, 2:3] = 1.0 + mod[:, :c]
    rows[1, 3:4] = mod[:, c:]

    restore(1, ha_s, hb_s, ha, hb)
    activate(1, hidden, ha, hb)
    copy(acts.at[1], a1_o)
    got.fourth(QKV)
    got.complete(OUT)
    copy(weights[OUT], outs[OUT])
    taps(weights[OUT], res, 0, 9, x)
    stat2 = publish(2, res[...], [(None, ra_s, rb_s)])
    copy(res, res_o)
    for dst, src in ((ca, ca_s), (cb, cb_s)):
        dst[...] = src[...]
    got.complete(QKV)
    copy(weights[QKV], outs[QKV])
    wq = joined(weights[QKV], 0)

    for cp in stat2:
        cp.wait_recv()
    center, inverse = combine_stats(every.at[2], px)
    n = ((res[...] - center) * (inverse * rows[2, 0:1]) + rows[2, 1:2]).astype(BF16)
    normed[...] = n
    k = dot(n, wq[c : 2 * c], 1, 1).astype(BF16)
    v = dot(n, wq[2 * c :], 1, 1).astype(BF16)
    q = (dot(n, wq[:c], 1, 1).astype(BF16).astype(F32) * (d ** -0.5)).astype(BF16)
    for h in range(HEADS):
        lanes = slice(h * d, (h + 1) * d)
        kv[h] = jnp.concatenate([k[:, lanes], v[:, lanes]], axis=1)
    copy(kv, kv_o)
    for h in range(HEADS):
        qf[h] = fold(q[:, h * d : (h + 1) * d])
    copy(qf, qf_o)
    copy(normed, normed_o)
    restore(2, ra_s, rb_s, ra, rb)
    st0[...] = every[0]
    st1[...] = every[1]
    st2[...] = every[2]
    for cp in local[1 + na :]:
        cp.wait()
    got.finish()
    for cp in round_g:
        cp.wait_recv()
    for cp in mail.sent:
        cp.wait_send()


def forward_call(chunks, x, cot, temb, cap, w_emb, w_cap, gains, biases, nz, width, cid):
    dims = [c.shape[:2] for c in chunks]
    na = len(dims)
    n_sp = 2 * nz
    px, c = x.shape
    padded = px + 2 * width
    tokens, wide = cap.shape
    e = wide // 4
    d2 = 2 * c // HEADS
    big = [((4, t, n_sp * r, 128), BF16) for t, r in dims]
    edge16, edge32 = ((width, c), BF16), ((width, c), F32)
    stat = ((n_sp, 8, c // 4), F32)
    outs = big + [
        ((px, c), F32), ((3, padded, c), BF16), ((px, c), F32), ((3, padded, c), BF16),
        ((n_sp, px // 2, d2), BF16), ((px, c), BF16), ((HEADS, px, d2), BF16), ((HEADS, px // 2, d2), BF16),
        stat, stat, stat, ((3, 8, c), F32), edge16, edge16, edge32, edge32, edge32, edge32,
        ((n_sp, tokens, 128), BF16), ((4, tokens, e), BF16), ((8, e), F32),
    ]
    vm = pltpu.VMEM
    return pl.pallas_call(
        functools.partial(forward_kernel, nz, width, dims),
        out_shape=[jax.ShapeDtypeStruct(s, ty) for s, ty in outs],
        in_specs=[ANY] * na + [VM, VM, VM, ANY] + [VM] * 4,
        out_specs=[ANY] * (na + 8) + [VM] * (len(outs) - na - 8),
        scratch_shapes=[vm(s, ty) for s, ty in big]
        + [
            pltpu.SemaphoreType.DMA((na, Gather.copies(nz))),
            pltpu.SemaphoreType.DMA((na, Gather.copies(nz))),
            pltpu.SemaphoreType.DMA((2 * na + 9,)),
            pltpu.SemaphoreType.DMA((FORWARD_MAIL,)),
            pltpu.SemaphoreType.DMA((FORWARD_MAIL,)),
            vm((HEADS, px // 2, d2), BF16), vm((4, 8, e), F32), vm((8, 128), F32),
            vm((3, 8, c // 4), F32), vm((3, n_sp, 8, c // 4), F32), vm((2, 2, width, c), BF16),
        ]
        + [vm(*edge16)] * 8
        + [
            vm((4, 8, 128), F32), vm((4, 8, e), F32), vm((4, tokens, e), BF16),
            vm((4, tokens + 8, 128), F32), vm((4, tokens + 8, 128), F32),
            vm((tokens, 128), BF16), vm((n_sp, tokens, 128), BF16), vm((8, 128), F32), vm((n_sp, 8, 128), F32),
            vm((2, 3, padded, c), BF16), vm((px, c), F32), vm((px, c), F32),
            vm((px, c), BF16), vm((HEADS, px, d2), BF16), vm((HEADS, px // 2, d2), BF16),
        ],
        compiler_params=params(cid),
        name="forward",
    )(*chunks, x, cot, temb, cap, w_emb, w_cap, gains, biases)


class Reducer:
    NAMES = ("d", "sb", "da", "db", "rx", "ry", "r", "zr")

    def __init__(self, at, nz, arrays, ssem, rsem):
        self.at, self.nz, self.arrays = at, nz, arrays
        self.ssem, self.rsem = ssem, rsem
        self.sent, self.groups = {}, []

    @staticmethod
    def buffers(nz, t, r):
        return [
            pltpu.VMEM((2, 4, t, nz, r, 128), BF16),
            pltpu.VMEM((4, t, nz, r, 128), BF16),
            pltpu.VMEM((t, nz, r // 2, 128), BF16),
            pltpu.VMEM((t, nz, r // 2, 128), BF16),
            pltpu.VMEM((t, nz, r, 128), BF16),
            pltpu.VMEM((t, nz, r, 128), BF16),
            pltpu.VMEM((t, nz, r, 128), BF16),
            pltpu.VMEM((nz - 1, t, r, 128), BF16),
        ]

    def send(self, g, j, src, dst, dev):
        self.sent[g, j] = remote(src, dst, self.ssem.at[g, j], self.rsem.at[g, j], dev)

    def add(self, a, t0, t1):
        g = len(self.groups)
        self.groups.append((a, t0, t1))
        b = self.arrays[a][1]
        self.send(g, 0, b["d"].at[1 - self.at.c, :, t0:t1], b["sb"].at[:, t0:t1], self.at.sib)

    def run(self, stage, *groups):
        one = (self.stage1, self.stage2, self.stage3, self.stage4)[stage - 1]
        for g in groups:
            one(g, *self.groups[g])

    def stage1(self, g, a, t0, t1):
        b, at = self.arrays[a][1], self.at
        d, sb = b["d"], b["sb"]
        self.sent[g, 0].wait_recv()
        n = t1 - t0

        def add(j, _):
            ii, tt = lax.div(j, n), t0 + lax.rem(j, n)
            d[at.c, ii, tt] = (d[at.c, ii, tt].astype(F32) + sb[ii, tt].astype(F32)).astype(BF16)
            return 0

        lax.fori_loop(0, 4 * n, add, 0)
        h = d.shape[4] // 2
        self.send(g, 1, d.at[at.c, at.id, t0:t1, :, :h], b["da"].at[t0:t1], at.yn)
        self.send(g, 2, d.at[at.c, at.id, t0:t1, :, h:], b["db"].at[t0:t1], at.xn)

    def stage2(self, g, a, t0, t1):
        b, at = self.arrays[a][1], self.at
        d = b["d"]
        h = d.shape[4] // 2
        self.sent[g, 1].wait_recv()
        self.sent[g, 2].wait_recv()

        def add(tt, _):
            d[at.c, at.ix, tt, :, :h] = (
                d[at.c, at.ix, tt, :, :h].astype(F32) + b["da"][tt].astype(F32)
            ).astype(BF16)
            d[at.c, at.iy, tt, :, h:] = (
                d[at.c, at.iy, tt, :, h:].astype(F32) + b["db"][tt].astype(F32)
            ).astype(BF16)
            return 0

        lax.fori_loop(t0, t1, add, 0)
        self.send(g, 3, d.at[at.c, at.ix, t0:t1], b["rx"].at[t0:t1], at.xn)
        self.send(g, 4, d.at[at.c, at.iy, t0:t1], b["ry"].at[t0:t1], at.yn)

    def stage3(self, g, a, t0, t1):
        b, at = self.arrays[a][1], self.at
        self.sent[g, 3].wait_recv()
        self.sent[g, 4].wait_recv()

        def add(tt, _):
            total = b["d"][at.c, at.i, tt].astype(F32) + b["rx"][tt].astype(F32) + b["ry"][tt].astype(F32)
            b["r"][tt] = total.astype(BF16)
            return 0

        lax.fori_loop(t0, t1, add, 0)
        for k in range(1, self.nz):
            there = lax.rem(at.z + k, self.nz)
            self.send(g, 4 + k, b["r"].at[t0:t1, there], b["zr"].at[k - 1, t0:t1], at.zp(k, self.nz))

    def stage4(self, g, a, t0, t1):
        (out, b), at = self.arrays[a], self.at
        for k in range(1, self.nz):
            self.sent[g, 4 + k].wait_recv()

        def add(tt, _):
            total = (
                b["d"][at.c, at.i, tt, at.z].astype(F32)
                + b["rx"][tt, at.z].astype(F32)
                + b["ry"][tt, at.z].astype(F32)
            )
            for k in range(1, self.nz):
                total = total + b["zr"][k - 1, tt].astype(F32)
            out[tt] = total
            return 0

        lax.fori_loop(t0, t1, add, 0)

    def finish(self):
        for cp in self.sent.values():
            cp.wait_send()


BACK_MAIL = 6 + 14 + 6 + 3 + 7 + 9 + 9
BACK_GROUPS = 7
BIG = 12


def conv_taps(t0, t1, w, ring, rsem, one):
    slots = ring.shape[0]

    def step(tap, _):
        slot = lax.rem(tap, slots)
        pltpu.make_async_copy(w.at[:, tap], ring.at[slot], rsem.at[slot]).wait()
        one(tap, jnp.concatenate([ring[slot, j] for j in range(4)], axis=-1))

        @pl.when(tap + slots < 9)
        def _():
            pltpu.make_async_copy(w.at[:, tap + slots], ring.at[slot], rsem.at[slot]).start()

        return 0

    lax.fori_loop(t0, t1, step, 0)


def ring_start(w, ring, rsem):
    for j in range(ring.shape[0]):
        pltpu.make_async_copy(w.at[:, j], ring.at[j], rsem.at[j]).start()


def backward_kernel(nz, width, *refs):
    hbm, refs = refs[:BIG], refs[BIG:]
    w_in, w_out = refs[:2]
    (st0, st1, st2, rows, ca, cb, ra, rb, ha, hb, dt_all, cap_all, emb_all, w_emb, w_cap, temb) = refs[2:18]
    output_o, image_o, s_in, s_out, s_small, g_temb, g_cap, g_wemb, g_wcap, g_aff = refs[18:28]
    refs = refs[28:]
    big, refs = refs[:BIG], refs[BIG:]
    bufs = [dict(zip(Reducer.NAMES, refs[8 * a : 8 * a + 8])) for a in range(3)]
    (bsem, gsend, grecv, msend, mrecv, ring, rsem, g3, gt, acc, ng, pre_grad, res_grad,
     mine, every, edge_s, na, nb, pa, pb, tg_s, tg_r, mod_s, mod_r,
     gc_s, gc_r, pe_s, pe_r, gs_s, gs_r, ps_s, ps_r, aff_s, aff_r, output, image_grad, osem) = refs[24:]
    n_sp = 2 * nz
    at = Place()
    line = [at.rp(k, n_sp) for k in range(1, n_sp)]
    grid = img_peers(at)
    greet(line + grid)
    loads = []
    for j in range(BIG):
        loads.append(pltpu.make_async_copy(hbm[j], big[j], bsem.at[j]))
    for cp in loads[:8]:
        cp.start()
    of, qf, dkv, w_qkv, w_proj, res, cot, normed, a3_out, hidden, a3_in, x = big
    mail = Mail(msend, mrecv)
    red = Reducer(at, nz, [(s_out, bufs[0]), (s_small, bufs[1]), (s_in, bufs[2])], gsend, grecv)
    px, c = res.shape
    height = px // width
    members = px * n_sp * (c // GROUPS)
    d = c // HEADS
    cols = 3 * c // n_sp

    def publish(j, rows01, edges):
        out = []
        put_rows(mine.at[j], rows01)
        for ref, above, below in edges:
            mean = rows01[0] / px
            edge_s[j - 1, 0] = (ref[px - width :, :] - mean).astype(BF16)
            edge_s[j - 1, 1] = (ref[:width, :] - mean).astype(BF16)
            out.append(mail.send(edge_s.at[j - 1, 0], above, line[0]))
            out.append(mail.send(edge_s.at[j - 1, 1], below, line[-1]))
        for dev in line:
            out.append(mail.send(mine.at[j], every.at[j, at.s], dev))
        every[j, at.s] = mine[j]
        return out

    for j in range(8):
        loads[j].wait()
    for cp in loads[8:]:
        cp.start()
    ring_start(w_out, ring, rsem)
    unfold = lambda v: jnp.concatenate([v[:, :d], v[:, d:]], axis=0)
    att = jnp.concatenate([unfold(of[h]) for h in range(HEADS)], axis=1)
    pg = jnp.concatenate(
        [unfold(qf[h]) for h in range(HEADS)]
        + [dkv[h][:, :d] for h in range(HEADS)]
        + [dkv[h][:, d:] for h in range(HEADS)],
        axis=1,
    )
    wq, wp = joined(w_qkv), joined(w_proj)
    ng[...] = dot(pg, wq, 1, 0)
    center2, inverse2 = combine_stats(st2, px)
    hat = (res[...] - center2) * inverse2
    u = ng[...]
    sums = (jnp.sum(u, axis=0, keepdims=True), jnp.sum(u * hat, axis=0, keepdims=True))
    greeted(n_sp + 2)
    round_2 = publish(2, sums, [(ng, na, nb)])
    gq = dot(pg, normed[...], 0, 0).astype(BF16)
    go = dot(cot[...], att, 0, 0).astype(BF16)
    small = bufs[1]["d"]
    for j in range(n_sp):
        for b in range(4):
            lanes = slice(b * 128, (b + 1) * 128)
            small[j % 2, b, 0, j // 2, :cols] = gq[j * cols : (j + 1) * cols, lanes]
            small[j % 2, b, 0, j // 2, cols:] = go[j * (c // n_sp) : (j + 1) * (c // n_sp), lanes]
    red.add(1, 0, 1)
    output[...] = (res[...] + dot(att, wp, 1, 1)).astype(BF16)
    handed = [pltpu.make_async_copy(output, output_o, osem.at[0]), pltpu.make_async_copy(image_grad, image_o, osem.at[1])]
    handed[0].start()

    first = 2 * lax.rem(at.s, nz)
    value = lax.div(at.s, nz)
    halves = []
    for j in range(2):
        blk = dt_all[first + j].astype(F32)
        halves.append(jnp.where(value > 0, blk[:, d:], blk[:, :d]))
    tg_s[...] = jnp.concatenate(halves, axis=1).astype(BF16)
    round_a = [mail.send(tg_s, tg_r.at[at.i], dev) for dev in grid]
    tg_r[at.i] = tg_s[...]

    has_up, has_dn = edge_flags(n_sp, at.s)

    def upstream(j, uu, ua, ub, center, inverse, yy, ya, yb, base, keep):
        total = combine_sums(every[j])
        mul = rows[j, 0:1] * rows[j, 2:3]
        back = group_total(total * mul) / members
        s1, s2 = back[0:1, :], back[1:2, :]
        for r in range(height + 2):
            cut = slice((r - 1) * width, r * width)
            top, end = r == 0, r == height + 1
            if top or end:
                near = line[-1] if top else line[0]
                un = (ua if top else ub)[...].astype(F32) + get_rows(every[j, near[1]])[0] / px
            else:
                un = uu[cut, :]
            yn = ya[...] if top else yb[...] if end else yy[cut, :]
            g = inverse * (un * mul - s1 - (yn - center) * inverse * s2)
            if base:
                g = g + (base[1][...] if top else base[2][...] if end else base[0][cut, :]).astype(F32)
            if top:
                g = g * has_up
            elif end:
                g = g * has_dn
            elif keep is not None:
                keep[cut, :] = g
            shifted(g3, r, width, g.astype(BF16).astype(F32))
        gt[...] = g3[1, width : width + px, :].T
        return total

    def weight_taps(a, t0, t1):
        dst = bufs[a]["d"]
        a3 = a3_in if a == 2 else a3_out

        def one(tap, _):
            i, j = lax.div(tap, 3), lax.rem(tap, 3)
            part = dot(gt[...], a3[j, pl.ds(pl.multiple_of(i * width, width), px), :], 1, 0).astype(BF16)
            r = c // n_sp
            for k in range(n_sp):
                for b in range(4):
                    dst[k % 2, b, tap, k // 2] = part[k * r : (k + 1) * r, b * 128 : (b + 1) * 128]
            return 0

        lax.fori_loop(t0, t1, one, 0)
        red.add(a, t0, t1)

    def input_taps(w):
        def one(tap, wt):
            i, j = lax.div(tap, 3), lax.rem(tap, 3)
            lhs = g3[2 - j, pl.ds(pl.multiple_of((2 - i) * width, width), px), :]
            acc[...] = dot(lhs, wt, 1, 0) + jnp.where(tap > 0, acc[...], 0.0)

        conv_taps(0, 9, w, ring, rsem, one)

    for cp in round_2:
        cp.wait_recv()
    t2 = upstream(2, ng, na, nb, center2, inverse2, res, ra, rb, (cot, ca, cb), res_grad)
    red.run(1, 0)
    loads[8].wait()
    for tap in (0, 3, 6):
        weight_taps(0, tap, tap + 3)
    red.run(2, 0)
    input_taps(w_out)
    ring_start(w_in, ring, rsem)
    for j in range(9, BIG):
        loads[j].wait()
    center1, inverse1 = combine_stats(st1, px)
    hat = (hidden[...] - center1) * inverse1
    gain1, bias1, fac1 = rows[1, 0:1], rows[1, 1:2], rows[1, 2:3]
    v = acc[...] * silu_slope(hat * (gain1 * fac1) + (bias1 * fac1 + rows[1, 3:4]))
    pre_grad[...] = v
    sums = (jnp.sum(v, axis=0, keepdims=True), jnp.sum(v * hat, axis=0, keepdims=True))
    round_1 = publish(1, sums, [(pre_grad, pa, pb)])
    red.run(1, 1, 2, 3)
    red.run(3, 0)

    exact = lambda a, b, ca_, cb_: lax.dot_general(
        a, b, (((ca_,), (cb_,)), ((), ())), preferred_element_type=F32, precision=PRECISE
    )
    tokens = tg_s.shape[0]
    share = tokens // n_sp
    for cp in round_a:
        cp.wait_recv()
    flat_tg = tg_r[...].reshape(4 * tokens, 128)
    g_wcap[...] = dot(cap_all[...].reshape(4 * tokens, cap_all.shape[2]), flat_tg, 0, 0)
    gc_s[...] = dot(flat_tg, w_cap[...], 1, 1).astype(BF16).reshape(gc_s.shape)
    round_b = []
    for dev in line:
        cut = pl.ds(pl.multiple_of(dev[1] * share, share), share)
        round_b.append(mail.send(gc_s.at[:, cut, :], gc_r.at[at.s], dev))
    gc_r[at.s] = gc_s[:, pl.ds(pl.multiple_of(at.s * share, share), share), :]

    for cp in round_1:
        cp.wait_recv()
    t1 = upstream(1, pre_grad, pa, pb, center1, inverse1, hidden, ha, hb, None, None)
    mod = jnp.concatenate([t1[1:2] * gain1 + t1[0:1] * bias1, t1[0:1]], axis=1)
    for j in range(n_sp):
        mod_s[j] = jnp.broadcast_to(mod[:, j * 128 : (j + 1) * 128], (8, 128))
    round_m = [mail.send(mod_s.at[at.s], mod_r.at[at.i], dev) for dev in grid]
    mod_r[at.i] = mod_s[at.s]
    red.run(2, 1)
    weight_taps(2, 0, 3)
    red.run(2, 2)
    weight_taps(2, 3, 6)
    red.run(2, 3)
    weight_taps(2, 6, 9)
    red.run(1, 4, 5, 6)
    input_taps(w_in)

    center0, inverse0 = combine_stats(st0, px)
    hat = (x[...].astype(F32) - center0) * inverse0
    gain0 = rows[0, 0:1]
    v = acc[...] * silu_slope(hat * gain0 + rows[0, 1:2])
    acc[...] = v
    sums = (jnp.sum(v, axis=0, keepdims=True), jnp.sum(v * hat, axis=0, keepdims=True))
    round_0 = publish(0, sums, [])
    red.run(4, 0)
    red.run(3, 1)
    red.run(2, 4)
    for cp in round_m:
        cp.wait_recv()
    mods = jnp.concatenate([mod_r[j][0:1] for j in range(4)] + [jnp.zeros((4, 128), F32)])
    emb_t = emb_all[...].T
    g_wemb[...] = sum(emb_t[:, j : j + 1] * mods[j : j + 1] for j in range(4))
    pe_s[...] = exact(mods, w_emb[...].astype(F32), 1, 1)
    round_p = [mail.send(pe_s, pe_r.at[at.s], dev) for dev in line]
    pe_r[at.s] = pe_s[...]
    for cp in round_0:
        cp.wait_recv()
    t0 = combine_sums(every[0])
    zero = jnp.zeros((2, c), F32)
    aff = jnp.concatenate([t0[1:2], t1[1:2] * fac1, t2[1:2], t0[0:1], t1[0:1] * fac1, t2[0:1], zero])
    for j in range(4):
        aff_s[j] = aff[:, j * 128 : (j + 1) * 128]
    round_e = [mail.send(aff_s.at[dev[0]], aff_r.at[at.i], dev) for dev in grid]
    aff_r[at.i] = aff_s[at.i]
    total = group_total(t0 * gain0) / members
    image_grad[...] = res_grad[...] + inverse0 * (acc[...] * gain0 - total[0:1] - hat * total[1:2])
    handed[1].start()
    for g in (2, 3):
        red.run(3, g)
        red.run(2, g + 3)
    for cp in round_b + round_p:
        cp.wait_recv()
    gc = gc_r[0].astype(F32)
    pe = pe_r[0]
    for j in range(1, n_sp):
        gc = gc + gc_r[j].astype(F32)
        pe = pe + pe_r[j]
    gs_s[...] = gc
    for j in range(4):
        ps_s[j] = jnp.broadcast_to(pe[j : j + 1], pe.shape)
    round_c = []
    for dev in grid:
        round_c.append(mail.send(gs_s.at[dev[0]], gs_r.at[at.i], dev))
        round_c.append(mail.send(ps_s.at[dev[0]], ps_r.at[at.i], dev))
    gs_r[at.i] = gs_s[at.i]
    ps_r[at.i] = ps_s[at.i]
    red.run(4, 1, 2, 3)
    red.run(3, 4, 5, 6)
    red.run(4, 4, 5, 6)
    red.finish()
    for cp in round_c + round_e:
        cp.wait_recv()
    g_cap[...] = jnp.concatenate([gs_r[j] for j in range(4)], axis=1)
    g_temb[...] = jnp.concatenate([ps_r[j] for j in range(4)], axis=1) * silu_slope(temb[...].astype(F32))
    g_aff[...] = aff_r[0] + aff_r[1] + aff_r[2] + aff_r[3]
    for cp in handed:
        cp.wait()
    for cp in mail.sent:
        cp.wait_send()


def backward_call(big, w_in, w_out, small, nz, width, cid):
    px, c = big[5].shape
    n_sp = 2 * nz
    padded = px + 2 * width
    r = c // n_sp
    rs = (big[3].shape[1] + big[4].shape[1]) // n_sp
    dt_all, cap_all = small[10], small[11]
    tokens = dt_all.shape[1]
    e = cap_all.shape[2]
    share = tokens // n_sp
    outs = [
        ((px, c), BF16), ((px, c), F32), ((9, r, 128), F32), ((9, r, 128), F32), ((1, rs, 128), F32),
        ((8, 4 * e), F32), ((share, 4 * e), F32), ((e, 128), F32), ((e, 128), F32), ((8, 128), F32),
    ]
    vm = pltpu.VMEM
    return pl.pallas_call(
        functools.partial(backward_kernel, nz, width),
        out_shape=[jax.ShapeDtypeStruct(s, ty) for s, ty in outs],
        in_specs=[ANY] * (len(big) + 2) + [VM] * len(small),
        out_specs=[ANY] * 2 + [VM] * (len(outs) - 2),
        scratch_shapes=[vm(v.shape, v.dtype) for v in big]
        + Reducer.buffers(nz, 9, r) + Reducer.buffers(nz, 1, rs) + Reducer.buffers(nz, 9, r)
        + [
            pltpu.SemaphoreType.DMA((len(big),)),
            pltpu.SemaphoreType.DMA((BACK_GROUPS, 4 + nz)),
            pltpu.SemaphoreType.DMA((BACK_GROUPS, 4 + nz)),
            pltpu.SemaphoreType.DMA((BACK_MAIL,)),
            pltpu.SemaphoreType.DMA((BACK_MAIL,)),
            vm((3, 4, c, 128), BF16),
            pltpu.SemaphoreType.DMA((3,)),
            vm((3, padded, c), BF16), vm((c, px), BF16),
            vm((px, c), F32), vm((px, c), F32), vm((px, c), F32), vm((px, c), F32),
            vm((3, 8, c // 4), F32), vm((3, n_sp, 8, c // 4), F32), vm((2, 2, width, c), BF16),
            vm((width, c), BF16), vm((width, c), BF16), vm((width, c), BF16), vm((width, c), BF16),
            vm((tokens, 128), BF16), vm((4, tokens, 128), BF16),
            vm((n_sp, 8, 128), F32), vm((4, 8, 128), F32),
            vm((4, tokens, e), BF16), vm((n_sp, 4, share, e), BF16),
            vm((8, e), F32), vm((n_sp, 8, e), F32),
            vm((4, share, e), F32), vm((4, share, e), F32),
            vm((4, 8, e), F32), vm((4, 8, e), F32),
            vm((4, 8, 128), F32), vm((4, 8, 128), F32),
            vm((px, c), BF16), vm((px, c), F32), pltpu.SemaphoreType.DMA((2,)),
        ],
        compiler_params=params(cid),
        name="backward",
    )(*big, w_in, w_out, *small)


def emit_kernel(cut, *refs):
    ins, outs, mids, loads, stores = refs[:10], refs[10:22], refs[22:31], refs[31], refs[32]
    output, image, s_in, s_out, s_small, g_temb, g_cap, g_wemb, g_wcap, g_aff = ins
    pairs = [
        (output, outs[0]), (image, outs[1]), (g_cap, outs[3]), (s_in, outs[4]), (s_out, outs[5]), (g_wemb, outs[6]),
        (s_small.at[0, :cut], outs[7]), (g_wcap, outs[8]), (s_small.at[0, cut:], outs[9]),
    ]
    copies = [pltpu.make_async_copy(src, mid, loads.at[j]) for j, ((src, _), mid) in enumerate(zip(pairs, mids))]
    for cp in copies:
        cp.start()
    backs = []
    for j, cp in enumerate(copies):
        cp.wait()
        backs.append(pltpu.make_async_copy(mids[j], pairs[j][1], stores.at[j]))
        backs[-1].start()
    outs[2][...] = g_temb[0:1, :]
    outs[10][...] = g_aff[0:3, :]
    outs[11][...] = g_aff[3:6, :]
    for cp in backs:
        cp.wait()


def emit_call(parts, cut):
    output, image, s_in, s_out, s_small, g_temb, g_cap, g_wemb, g_wcap, g_aff = parts
    rest = s_small.shape[1] - cut
    like = lambda v: jax.ShapeDtypeStruct(v.shape, v.dtype)
    f32 = lambda *s: jax.ShapeDtypeStruct(s, F32)
    shapes = [
        like(output), like(image), f32(1, g_temb.shape[1]), like(g_cap), like(s_in), like(s_out), like(g_wemb),
        f32(cut, 128), like(g_wcap), f32(rest, 128), f32(3, 128), f32(3, 128),
    ]
    in_specs = [ANY] * 10
    in_specs[5] = in_specs[9] = VM
    out_specs = [ANY] * 12
    out_specs[2] = out_specs[10] = out_specs[11] = VM
    return pl.pallas_call(
        functools.partial(emit_kernel, cut),
        out_shape=shapes,
        in_specs=in_specs,
        out_specs=out_specs,
        scratch_shapes=[pltpu.VMEM(shapes[j].shape, shapes[j].dtype) for j in (0, 1, 3, 4, 5, 6, 7, 8, 9)]
        + [pltpu.SemaphoreType.DMA((9,)), pltpu.SemaphoreType.DMA((9,))],
        compiler_params=params(),
        name="emit",
    )(*parts)


def fast_body(
    image_in, time_embed, caption, caption_mask, conv_in, conv_out, embed_proj, qkv_proj,
    caption_proj, out_proj, norm_gains, norm_biases, cotangent,
):
    n, height, width, c = image_in.shape
    n_sp = lax.axis_size("sp")
    nz = n_sp // 2
    px = height * width
    x = image_in.reshape(px, c)
    cot = cotangent.reshape(px, c)

    flat = lambda w: w.transpose(1, 2, 3, 0).reshape(9, w.shape[3], w.shape[0])
    (w_proj, w_in, w_out, w_qkv, hidden, a3_in, res, a3_out, g, normed, kv, q,
     st0, st1, st2, rows, ca, cb, ra, rb, ha, hb, kv_all, cap_all, emb_all) = forward_call(
        [out_proj.T[None], flat(conv_in), flat(conv_out), qkv_proj.T[None]], x, cot, time_embed, caption[0], embed_proj, caption_proj,
        norm_gains, norm_biases, nz, width, 0,
    )
    w_proj, w_qkv = w_proj[:, 0], w_qkv[:, 0]
    of, qf, dkv, dt_all = attention_call(kv, q, g, kv_all, caption_mask, 1)

    parts = backward_call(
        [of, qf, dkv, w_qkv, w_proj, res, cot, normed, a3_out, hidden, a3_in, x], w_in, w_out,
        [st0, st1, st2, rows, ca, cb, ra, rb, ha, hb, dt_all, cap_all, emb_all, embed_proj, caption_proj, time_embed],
        nz, width, 2,
    )
    output, image, g_temb, g_cap, s_in, s_out, g_wemb, g_qkv, g_wcap, g_out, g_gains, g_biases = emit_call(
        parts, qkv_proj.shape[1]
    )
    unflat = lambda g: g.reshape(3, 3, g.shape[1], 128).transpose(3, 0, 1, 2)
    return (
        output.reshape(image_in.shape), image.reshape(image_in.shape), g_temb, g_cap[None], unflat(s_in), unflat(s_out),
        g_wemb, g_qkv.T, g_wcap, g_out.T, g_gains, g_biases,
    )


def body(*args):
    image_in, qkv_proj = args[0], args[7]
    n, height, width, c = image_in.shape
    n_img, n_sp = lax.axis_size("img"), lax.axis_size("sp")
    fits = n == 1 and n_img == 4 and n_sp == HEADS and c == 512 and width == 64
    return fast_body(*args) if fits else plain_body(*args)


def solution(mesh):
    rows = P("img", "sp", None, None)
    kernel = P("img", None, None, "sp")
    flat = P("img", "sp")
    return jax.shard_map(
        body,
        mesh=mesh,
        in_specs=(
            rows, P("img", None), P("img", None, None), P("img", None), kernel, kernel,
            flat, flat, flat, flat, P(None, "img"), P(None, "img"), rows,
        ),
        out_specs=(
            rows, rows, P("img", None), P("img", "sp", None), kernel, kernel,
            flat, flat, flat, flat, P(None, "img"), P(None, "img"),
        ),
        check_vma=False,
    )
```

```python
import functools

import jax
import jax.numpy as jnp
from jax import lax
from jax.experimental import pallas as pl
from jax.experimental.pallas import tpu as pltpu
from jax.sharding import PartitionSpec as P

HEADS = 8
GROUPS = 32
EPSILON = 1e-05
PRECISE = lax.Precision.HIGHEST
MASKED = -1e30
BF16 = jnp.bfloat16
F32 = jnp.float32
MESH = pl.DeviceIdType.MESH
VMEM_BYTES = 60 * 1024 * 1024


def dot(a, b, ca, cb):
    return lax.dot_general(a, b, (((ca,), (cb,)), ((), ())), preferred_element_type=F32)


def silu(v):
    return v * jax.nn.sigmoid(v)


def silu_slope(v):
    s = jax.nn.sigmoid(v)
    return s * (1.0 + v * (1.0 - s))


def gather(x, axis, dim):
    return lax.all_gather(x, axis, axis=dim, tiled=True)


def scatter_sum(x, axis, dim):
    return lax.psum_scatter(x, axis, scatter_dimension=dim, tiled=True)


def swap(x, axis, split, concat):
    return lax.all_to_all(x, axis, split, concat, tiled=True)


def halo(x):
    count = lax.axis_size("sp")
    above = lax.ppermute(x[:, -1:], "sp", [(i, i + 1) for i in range(count - 1)])
    below = lax.ppermute(x[:, :1], "sp", [(i + 1, i) for i in range(count - 1)])
    return above, below


def group_sum(v):
    c = v.shape[-1]
    g = v.reshape(v.shape[:-1] + (GROUPS, c // GROUPS))
    s = jnp.sum(g, axis=-1, keepdims=True)
    return jnp.broadcast_to(s, g.shape).reshape(v.shape)


def norm_stats(x):
    n, r, w, c = x.shape
    cells = r * w * (c // GROUPS)
    parts = lax.axis_size("sp")
    mean = group_sum(jnp.sum(x, axis=(1, 2))) / cells
    dev = group_sum(jnp.sum(jnp.square(x - mean[:, None, None, :]), axis=(1, 2)))
    both = lax.all_gather(jnp.stack([mean, dev]), "sp")
    means, devs = both[:, 0], both[:, 1]
    center = jnp.mean(means, axis=0)
    var = (jnp.sum(devs, axis=0) + cells * jnp.sum(jnp.square(means - center), axis=0)) / (
        cells * parts
    )
    return center, lax.rsqrt(var + EPSILON)


def hat_of(x, center, inverse):
    return (x - center[:, None, None, :]) * inverse[:, None, None, :]


def norm_back(u, hat, inverse, gain, sum_u, sum_uh, members):
    s1 = group_sum(sum_u * gain) / members
    s2 = group_sum(sum_uh * gain) / members
    return inverse[:, None, None, :] * (
        u * gain - s1[:, None, None, :] - hat * s2[:, None, None, :]
    )


def pad_cols(x):
    return jnp.pad(x, ((0, 0), (0, 0), (1, 1), (0, 0)))


def conv(padded, weight_t, transposed):
    n, rp, wp, c = padded.shape
    r, w = rp - 2, wp - 2
    total = None
    for i in range(3):
        for j in range(3):
            a = padded[:, i : i + r, j : j + w].reshape(n * r * w, c)
            part = dot(a, weight_t[2 - i, 2 - j], 1, 0) if transposed else dot(a, weight_t[i, j], 1, 1)
            total = part if total is None else total + part
    return total.reshape(n, r, w, -1)


def conv_grad(padded, g):
    n, r, w, c = g.shape
    gf = g.reshape(n * r * w, c)
    rows = []
    for i in range(3):
        for j in range(3):
            a = padded[:, i : i + r, j : j + w].reshape(n * r * w, -1)
            rows.append(dot(gf, a, 0, 0))
    return jnp.stack(rows).reshape(3, 3, c, -1)


def to_pairs(x, images):
    n, px, h, d = x.shape
    y = x.transpose(0, 2, 1, 3).reshape(n * h, px, d)
    return swap(y, "sp", 0, 1)


def from_pairs(x, images):
    y = swap(x, "sp", 1, 0)
    return y.reshape(images, HEADS, y.shape[1], y.shape[2]).transpose(0, 2, 1, 3)


def attention_plain(q, k, v, g, tk, tv, keep, scale):
    p, length, d = q.shape
    block = min(512, length)
    keys = jnp.concatenate([tk, k], axis=1)
    values = jnp.concatenate([tv, v], axis=1)
    text = tk.shape[1]
    keep_all = jnp.concatenate([keep, jnp.ones((p, length), bool)], axis=1)

    def step(carry, blk):
        dk, dv = carry
        qb, gb = blk
        s = jnp.einsum("pqd,pkd->pqk", qb, keys, preferred_element_type=F32) * scale
        s = jnp.where(keep_all[:, None, :], s, MASKED)
        peak = jnp.max(s, axis=-1, keepdims=True)
        e = jnp.exp(s - peak)
        prob = e / jnp.sum(e, axis=-1, keepdims=True)
        pb = prob.astype(BF16)
        o = jnp.einsum("pqk,pkd->pqd", pb, values, preferred_element_type=F32)
        row = jnp.sum(o * gb.astype(F32), axis=-1, keepdims=True)
        dp = jnp.einsum("pqd,pkd->pqk", gb, values, preferred_element_type=F32)
        ds = (prob * (dp - row)).astype(BF16)
        dq = jnp.einsum("pqk,pkd->pqd", ds, keys, preferred_element_type=F32) * scale
        dk = dk + jnp.einsum("pqk,pqd->pkd", ds, qb, preferred_element_type=F32)
        dv = dv + jnp.einsum("pqk,pqd->pkd", pb, gb, preferred_element_type=F32)
        return (dk, dv), (o.astype(BF16), dq.astype(BF16))

    zeros = jnp.zeros((p, text + length, d), F32)
    cut = lambda t: t.reshape(p, length // block, block, d).swapaxes(0, 1)
    (dk, dv), (o, dq) = lax.scan(step, (zeros, zeros), (cut(q), cut(g)))
    join = lambda t: t.swapaxes(0, 1).reshape(p, length, d)
    dk = (dk * scale).astype(BF16)
    dv = dv.astype(BF16)
    return join(o), join(dq), dk[:, text:], dv[:, text:], dk[:, :text], dv[:, :text]


def plain_body(
    image_in, time_embed, caption, caption_mask, conv_in, conv_out, embed_proj, qkv_proj,
    caption_proj, out_proj, norm_gains, norm_biases, cotangent,
):
    n, rows, width, chans = image_in.shape
    n_img, n_sp = lax.axis_size("img"), lax.axis_size("sp")
    img, sp = lax.axis_index("img"), lax.axis_index("sp")
    px = rows * width
    members = px * n_sp * (chans // GROUPS)
    d = chans // HEADS
    scale = d ** -0.5
    pairs = n * HEADS // n_sp

    def whole(w):
        w = gather(w, "img", w.ndim - 1)
        return gather(w, "sp", w.ndim - 2)

    w_in = whole(conv_in.transpose(1, 2, 3, 0))
    w_out = whole(conv_out.transpose(1, 2, 3, 0))
    w_qkv = whole(qkv_proj.T)
    w_proj = whole(out_proj.T)
    affine = gather(jnp.concatenate([norm_gains, norm_biases]), "img", 1).astype(F32)
    gains, biases = affine[:3], affine[3:]

    embedded = silu(time_embed.astype(F32)).astype(BF16)
    emb_all = swap(embedded, "img", 1, 0)
    mod = scatter_sum(jnp.dot(emb_all, embed_proj, preferred_element_type=F32), "img", 0)
    mod = gather(mod, "sp", 1)
    scale_term, shift_term = mod[:, :chans], mod[:, chans:]
    cap_all = swap(caption, "img", 2, 0)
    cap_flat = cap_all.reshape(-1, cap_all.shape[2])
    kv = jnp.dot(cap_flat, caption_proj, preferred_element_type=F32)
    kv = scatter_sum(kv.reshape(cap_all.shape[0], cap_all.shape[1], -1), "img", 0).astype(BF16)
    kv = gather(kv, "sp", 2)
    text = kv.shape[1]
    kv_heads = kv.reshape(n, text, 2, HEADS, d).transpose(2, 0, 3, 1, 4).reshape(2, n * HEADS, text, d)
    mine = lax.dynamic_slice_in_dim(kv_heads, sp * pairs, pairs, 1)
    keep = jnp.repeat(caption_mask > 0, HEADS, axis=0)
    keep = lax.dynamic_slice_in_dim(keep, sp * pairs, pairs, 0)

    image_f = image_in.astype(F32)
    c0, i0 = norm_stats(image_f)
    hat0 = hat_of(image_f, c0, i0)
    first = hat0 * gains[0] + biases[0]
    act0 = silu(first).astype(BF16)
    above, below = halo(act0)
    pad0 = pad_cols(jnp.concatenate([above, act0, below], axis=1))
    hidden = conv(pad0, w_in, False)
    c1, i1 = norm_stats(hidden)
    hat1 = hat_of(hidden, c1, i1)
    second = hat1 * gains[1] + biases[1]
    pre = second * (1.0 + scale_term[:, None, None, :]) + shift_term[:, None, None, :]
    act1 = silu(pre).astype(BF16)
    above, below = halo(act1)
    pad1 = pad_cols(jnp.concatenate([above, act1, below], axis=1))
    residual = image_f + conv(pad1, w_out, False)
    c2, i2 = norm_stats(residual)
    hat2 = hat_of(residual, c2, i2)
    normed = (hat2 * gains[2] + biases[2]).astype(BF16).reshape(n * px, chans)
    qkv = dot(normed, w_qkv, 1, 1).astype(BF16)
    cot = cotangent.reshape(n * px, chans)
    g_att = dot(cot, w_proj, 1, 0).astype(BF16)
    four = jnp.concatenate([qkv, g_att], axis=1).reshape(n, px, 4, HEADS, d)
    packed = to_pairs(four.transpose(0, 1, 3, 2, 4).reshape(n, px, HEADS, 4 * d), n)
    q, k, v, g = (packed[..., j * d : (j + 1) * d] for j in range(4))
    o, dq, dk, dv, dtk, dtv = attention_plain(q, k, v, g, mine[0], mine[1], keep, scale)
    back = from_pairs(jnp.concatenate([o, dq, dk, dv], axis=-1), n)
    back = back.reshape(n * px, HEADS, 4, d).transpose(0, 2, 1, 3).reshape(n * px, 4 * chans)
    attended, proj_grad = back[:, :chans], back[:, chans:]
    output = residual + dot(attended, w_proj, 1, 1).reshape(image_in.shape)

    grad_out = dot(cot, attended, 0, 0)
    grad_qkv = dot(proj_grad, normed, 0, 0)
    normed_grad = dot(proj_grad, w_qkv, 1, 0).reshape(image_in.shape)

    def sums(u, hat):
        both = jnp.stack([jnp.sum(u, axis=(1, 2)), jnp.sum(u * hat, axis=(1, 2))])
        return lax.psum(both, "sp")

    su2, sh2 = sums(normed_grad, hat2)
    residual_grad = cotangent.astype(F32) + norm_back(
        normed_grad, hat2, i2, gains[2], su2, sh2, members
    )
    g2 = residual_grad.astype(BF16)
    above, below = halo(g2)
    gpad = pad_cols(jnp.concatenate([above, g2, below], axis=1))
    grad_conv_out = conv_grad(pad1, g2)
    pre_grad = conv(gpad, w_out, True) * silu_slope(pre)
    sa, sb = sums(pre_grad, hat1)
    fac = 1.0 + scale_term
    shift_grad = sa
    scale_grad = sb * gains[1] + sa * biases[1]
    u1 = pre_grad * fac[:, None, None, :]
    su1, sh1 = sa * fac, sb * fac
    g1 = norm_back(u1, hat1, i1, gains[1], su1, sh1, members).astype(BF16)
    above, below = halo(g1)
    gpad = pad_cols(jnp.concatenate([above, g1, below], axis=1))
    grad_conv_in = conv_grad(pad0, g1)
    u0 = conv(gpad, w_in, True) * silu_slope(first)
    su0, sh0 = sums(u0, hat0)
    grad_image = residual_grad + norm_back(u0, hat0, i0, gains[0], su0, sh0, members)

    mod_grad = jnp.concatenate([scale_grad, shift_grad], axis=1)
    cols = embed_proj.shape[1]
    mod_all = gather(mod_grad, "img", 0)
    mod_cols = lax.dynamic_slice_in_dim(mod_all, sp * cols, cols, 1)
    grad_embed_proj = jnp.einsum("ne,nd->ed", emb_all.astype(F32), mod_cols, precision=PRECISE)
    part = jnp.einsum("nd,ed->ne", mod_cols, embed_proj.astype(F32), precision=PRECISE)
    part = swap(lax.psum(part, "sp"), "img", 0, 1)
    grad_embed = part * silu_slope(time_embed.astype(F32))

    tg = gather(jnp.stack([dtk, dtv]), "sp", 1).reshape(2, n, HEADS, text, d)
    tg = tg.transpose(1, 3, 0, 2, 4).reshape(n, text, 2 * chans)
    cols = caption_proj.shape[1]
    tg = gather(lax.dynamic_slice_in_dim(tg, sp * cols, cols, 2), "img", 0).reshape(-1, cols)
    grad_caption_proj = dot(cap_flat, tg, 0, 0)
    gc = dot(tg, caption_proj, 1, 1).reshape(cap_all.shape)
    gc = scatter_sum(gc, "sp", 1)
    grad_caption = swap(gc, "img", 0, 2)

    grads = jnp.concatenate(
        [jnp.sum(t, axis=0)[None] for t in (sh0, sh1, sh2, su0, su1, su2)]
    )
    grads = scatter_sum(grads, "img", 1)

    def shared(w):
        w = scatter_sum(w, "sp", w.ndim - 2)
        return scatter_sum(w, "img", w.ndim - 1)

    return (
        output.astype(BF16),
        grad_image,
        grad_embed,
        grad_caption,
        shared(grad_conv_in).transpose(3, 0, 1, 2),
        shared(grad_conv_out).transpose(3, 0, 1, 2),
        grad_embed_proj,
        shared(grad_qkv).T,
        grad_caption_proj,
        shared(grad_out).T,
        grads[:3],
        grads[3:],
    )


class Place:
    def __init__(self):
        self.i = lax.axis_index("img")
        self.s = lax.axis_index("sp")
        self.z = lax.div(self.s, 2)
        self.c = lax.rem(self.s, 2)
        x = lax.rem(self.i, 2)
        y = lax.div(self.i, 2)
        self.ix = self.i + 1 - 2 * x
        self.iy = self.i + 2 - 4 * y
        self.id = 3 - self.i
        self.sib = (self.i, self.s + 1 - 2 * self.c)
        self.xn = (self.ix, self.s)
        self.yn = (self.iy, self.s)

    def zp(self, k, nz):
        return (self.i, 2 * lax.rem(self.z + k, nz) + self.c)

    def rp(self, k, n_sp):
        return (self.i, lax.rem(self.s + k, n_sp))


def greet(peers):
    bar = pltpu.get_barrier_semaphore()
    for p in peers:
        pl.semaphore_signal(bar, inc=1, device_id=p, device_id_type=MESH)


def greeted(count):
    pl.semaphore_wait(pltpu.get_barrier_semaphore(), count)


def remote(src, dst, ssem, rsem, dev):
    cp = pltpu.make_async_remote_copy(
        src_ref=src, dst_ref=dst, send_sem=ssem, recv_sem=rsem, device_id=dev, device_id_type=MESH
    )
    cp.start()
    return cp


def params(cid=None, grid=0):
    extra = {} if cid is None else {"collective_id": cid, "has_side_effects": True}
    if grid:
        extra["dimension_semantics"] = ("arbitrary",) * grid
    return pltpu.CompilerParams(vmem_limit_bytes=VMEM_BYTES, **extra)


ANY = pl.BlockSpec(memory_space=pl.ANY)
VM = pl.BlockSpec(memory_space=pltpu.VMEM)
def channel_stats(v):
    mean = jnp.sum(v, axis=0, keepdims=True) / v.shape[0]
    dev = v - mean
    return mean, jnp.sum(dev * dev, axis=0, keepdims=True)


def put_rows(dst, pair):
    n = pair[0].shape[1] // 128
    for a, row in enumerate(pair):
        for j in range(n):
            dst[a * n + j : a * n + j + 1, :] = row[:, j * 128 : (j + 1) * 128]


def get_rows(block):
    n = block.shape[0] // 2
    return tuple(jnp.concatenate([block[a * n + j : a * n + j + 1] for j in range(n)], axis=1) for a in range(2))


def group_total(rows):
    c = rows.shape[1]
    size = 512 // GROUPS
    a = lax.broadcasted_iota(jnp.int32, (128, 128), 0)
    b = lax.broadcasted_iota(jnp.int32, (128, 128), 1)
    same = jnp.where(lax.bitwise_xor(a, b) < size, 1.0, 0.0).astype(BF16)
    high = rows.astype(BF16)
    rest = rows - high.astype(F32)
    mid = rest.astype(BF16)
    low = (rest - mid.astype(F32)).astype(BF16)
    parts = jnp.concatenate([high.astype(F32), mid.astype(F32), low.astype(F32)]).astype(BF16)
    total = jnp.concatenate(
        [dot(parts[:, j * 128 : (j + 1) * 128], same, 1, 0) for j in range(c // 128)], axis=1
    )
    n = rows.shape[0]
    return total[:n] + total[n : 2 * n] + total[2 * n :]


def combine_stats(every, px):
    n_sp, rows, lanes = every.shape
    half = rows // 2
    size = half * lanes // GROUPS
    means = [every[j, :half, :] for j in range(n_sp)]
    center_c = sum(means) / n_sp
    dev = sum(every[j, half:, :] for j in range(n_sp))
    dev = dev + px * sum((m - center_c) * (m - center_c) for m in means)
    spread = lambda v: group_total(jnp.concatenate([v, v]))[:half]
    center = spread(center_c) / size
    off = center_c - center
    var = spread(dev + (px * n_sp) * (off * off)) / (px * n_sp * size)
    return get_rows(jnp.concatenate([center, lax.rsqrt(var + EPSILON)]))


def combine_sums(every):
    total = every[0]
    for j in range(1, every.shape[0]):
        total = total + every[j]
    a, b = get_rows(total)
    return jnp.concatenate([a, b, jnp.zeros((6, a.shape[1]), F32)])


def edge_flags(n_sp, s):
    return jnp.where(s > 0, 1.0, 0.0), jnp.where(s < n_sp - 1, 1.0, 0.0)


def shifted(dst, row, width, block):
    col = lax.broadcasted_iota(jnp.int32, block.shape, 0)
    r = slice(row * width, (row + 1) * width)
    dst[1, r, :] = block.astype(BF16)
    dst[0, r, :] = jnp.where(col == 0, 0.0, pltpu.roll(block, 1, 0)).astype(BF16)
    dst[2, r, :] = jnp.where(col == width - 1, 0.0, pltpu.roll(block, width - 1, 0)).astype(BF16)


def joined(w_ref, *lead):
    return jnp.concatenate([w_ref[(j,) + lead] for j in range(4)], axis=-1)


def three_parts(v):
    a = v.astype(BF16).astype(F32)
    b = (v - a).astype(BF16).astype(F32)
    return a, b, v - a - b


AHEAD = 3


def attention_kernel(
    n_sp, BK, kv, qin, gin, text, keep, of, qf, dkv, dt,
    kv_r, q_r, g_r, q_s, o_s, dq_o, dkv_s, dt_s, k_s, v_s, s_s, e_s, g_s, dq_s, peak_s, lsem, ssem, rsem,
):
    at = Place()
    nz = n_sp // 2
    px = kv.shape[1]
    L, T = n_sp * px, text.shape[1]
    d = kv.shape[2] // 2
    BQ = px // 2
    line = [at.rp(k, n_sp) for k in range(1, n_sp)]
    greet(line)
    own = [
        pltpu.make_async_copy(kv.at[at.s], kv_r.at[at.s], lsem.at[0]),
        pltpu.make_async_copy(qin.at[at.s], q_r.at[at.s], lsem.at[1]),
        pltpu.make_async_copy(gin, g_r, lsem.at[6]),
    ]
    for cp in own:
        cp.start()
    greeted(n_sp - 1)
    keys = [remote(kv.at[dev[1]], kv_r.at[at.s], ssem.at[0, k + 1], rsem.at[0, k + 1], dev) for k, dev in enumerate(line)]

    def source(k):
        return 2 * lax.rem(at.z - lax.div(k, 2) + nz, nz) + lax.rem(at.c + lax.rem(k, 2), 2)

    def target(k):
        return 2 * lax.rem(at.z + lax.div(k, 2), nz) + lax.rem(at.c + lax.rem(k, 2), 2)

    def query_copy(k):
        return pltpu.make_async_remote_copy(
            src_ref=qin.at[target(k)], dst_ref=q_r.at[at.s], send_sem=ssem.at[1, k], recv_sem=rsem.at[1, k],
            device_id=(at.i, target(k)), device_id_type=MESH,
        )

    odd = lax.rem(at.s, 2)
    pair = lax.div(at.s, 2)
    ones = (lax.broadcasted_iota(jnp.int32, (1, d), 1) < 3).astype(F32).astype(BF16)
    picked = []
    for j in (pair, HEADS // 2 + pair):
        blk = text[j].astype(F32)
        picked.append(jnp.where(odd > 0, blk[:, d:], blk[:, :d]).astype(BF16))
    k_s[0:T, :] = picked[0]
    v_s[0:T, :] = jnp.concatenate([picked[1], jnp.broadcast_to(ones, (T, d))], axis=1)

    def rows_of(o, n=px, start=0):
        return pl.ds(pl.multiple_of(o * px + start, 128), n)

    def take(j):
        rows = rows_of(j, px, T)
        k_s[rows, :] = kv_r[j][:, :d]
        v_s[rows, :] = jnp.concatenate([kv_r[j][:, d:], jnp.broadcast_to(ones, (px, d))], axis=1)

    for k in range(1, AHEAD):
        query_copy(k).start()
    for cp in own:
        cp.wait()
    take(at.s)
    for k in range(1, n_sp):
        keys[k - 1].wait_recv()
        take(lax.rem(at.s - k + n_sp, n_sp))
    blocks = [(0, T)] + [(T + j * BK, BK) for j in range(L // BK)]
    scale = d ** -0.5

    def back_copy(j, k, src, dst, o):
        return pltpu.make_async_remote_copy(
            src_ref=src.at[o], dst_ref=dst.at[at.s], send_sem=ssem.at[j, k], recv_sem=rsem.at[j, k],
            device_id=(at.i, o), device_id_type=MESH,
        )

    def scores(q, slot, st, n, peak):
        s = dot(q, k_s[st : st + n, :], 1, 1)
        if st == 0:
            s = jnp.where(keep[...] > 0, s, MASKED)
        s_s[slot, :, st : st + n] = s
        for j in range(n // 128):
            piece = s[:, 128 * j : 128 * j + 128]
            peak = piece if peak is None else jnp.maximum(peak, piece)
        return peak

    def query(o, part):
        return q_r[o][:, part * d : (part + 1) * d]

    def forward(o, part, o_next):
        nxt = query(o_next, 1 - part)
        g = g_r[o][:, part * d : (part + 1) * d]
        rows = rows_of(o, BQ, part * BQ)
        q_s[rows, :] = query(o, part)
        top = jnp.max(peak_s[part], axis=1, keepdims=True)
        out = jnp.zeros((BQ, 2 * d), F32)
        peak = None
        for st, n in blocks:
            peak = scores(nxt, 1 - part, st, n, peak)
            e = jnp.exp(s_s[part, :, st : st + n] - top).astype(BF16)
            e_s[rows, st : st + n] = e
            out = out + dot(e, v_s[st : st + n, :], 1, 0)
        peak_s[1 - part] = peak
        inverse = 1.0 / out[:, d : d + 1]
        out = out[:, :d] * inverse
        g = g.astype(F32) * inverse
        row = jnp.sum(out * g, axis=1, keepdims=True)
        lane = lax.broadcasted_iota(jnp.int32, (BQ, d), 1)
        extra = jnp.zeros((BQ, d), F32)
        for j, piece in enumerate(three_parts(-row)):
            extra = jnp.where(lane == j, piece, extra)
        g_s[rows, :] = jnp.concatenate([g, extra], axis=1).astype(BF16)
        o_s[o, :, part * d : (part + 1) * d] = out.astype(BF16)

    peak = None
    for st, n in blocks:
        peak = scores(query(at.s, 0), 0, st, n, peak)
    peak_s[0] = peak

    def owner(k, _):
        o = source(k)

        @pl.when(k + AHEAD < n_sp)
        def _():
            query_copy(k + AHEAD).start()

        forward(o, 0, o)

        @pl.when(k + 1 < n_sp)
        def _():
            query_copy(k + 1).wait_recv()

        forward(o, 1, source(lax.rem(k + 1, n_sp)))

        @pl.when(k > 0)
        def _():
            back_copy(2, k, o_s, of, o).start()

        return 0

    lax.fori_loop(0, n_sp, owner, 0)
    local = [pltpu.make_async_copy(o_s.at[at.s], of.at[at.s], lsem.at[2])]

    def block(o, cols, kc, vc, dk, dv, fresh):
        rows = rows_of(o)
        g, q = g_s[rows, :], q_s[rows, :]
        e = e_s[rows, cols]
        ds = (e.astype(F32) * dot(g, vc, 1, 1)).astype(BF16)
        part = dot(ds, kc, 1, 0)
        dq_s[rows, :] = part if fresh else dq_s[rows, :] + part
        return dk + dot(q.T, ds, 1, 0), dv + dot(g[:, :d].T, e, 1, 0)

    def both(dk, dv):
        return jnp.concatenate([dk, dv], axis=0).astype(BF16).T

    def chunk(cols, n, fresh):
        kc, vc = k_s[cols, :], v_s[cols, :]
        zero = jnp.zeros((d, n), F32)
        dk, dv = lax.fori_loop(
            0, n_sp, lambda o, acc: block(o, cols, kc, vc, acc[0], acc[1], fresh), (zero, zero), unroll=8
        )
        return both(dk, dv)

    def chip_columns(z):
        return pl.ds(pl.multiple_of(T + z * (2 * px), 128), 2 * px)

    dt_s[...] = chunk(pl.ds(0, T), T, True)
    sent = [remote(dt_s, dt.at[at.s], ssem.at[5, k + 1], rsem.at[5, k + 1], dev) for k, dev in enumerate(line)]
    local.append(pltpu.make_async_copy(dt_s, dt.at[at.s], lsem.at[3]))

    def chip(k, _):
        z = lax.rem(at.z + k, nz)
        grads = chunk(chip_columns(z), 2 * px, False)
        for core in range(2):
            o = 2 * z + core
            dkv_s[o] = grads[core * px : (core + 1) * px]
            back_copy(4, lax.rem(o - at.s + n_sp, n_sp), dkv_s, dkv, o).start()
        return 0

    lax.fori_loop(1, nz, chip, 0)
    cols = chip_columns(at.z)
    kc, vc = k_s[cols, :], v_s[cols, :]
    zero = jnp.zeros((d, 2 * px), F32)

    def last(j, acc):
        o = 2 * lax.rem(at.z + 1 + lax.div(j, 2), nz) + lax.rem(j, 2)
        acc = block(o, cols, kc, vc, acc[0], acc[1], False)
        dq = (dq_s[rows_of(o), :] * scale).astype(BF16)
        dq_o[o] = jnp.concatenate([dq[:BQ], dq[BQ:]], axis=1)

        @pl.when(o != at.s)
        def _():
            back_copy(3, lax.rem(o - at.s + n_sp, n_sp), dq_o, qf, o).start()

        return acc

    grads = both(*lax.fori_loop(0, n_sp, last, (zero, zero), unroll=2))
    for core in range(2):
        dkv_s[2 * at.z + core] = grads[core * px : (core + 1) * px]
    sib = at.sib[1]
    back_copy(4, lax.rem(sib - at.s + n_sp, n_sp), dkv_s, dkv, sib).start()
    local.append(pltpu.make_async_copy(dkv_s.at[at.s], dkv.at[at.s], lsem.at[4]))
    local.append(pltpu.make_async_copy(dq_o.at[at.s], qf.at[at.s], lsem.at[5]))
    for cp in local:
        cp.start()
    for k in range(1, n_sp):
        back_copy(2, k, o_s, of, source(k)).wait()
        o = lax.rem(at.s + k, n_sp)
        back_copy(4, k, dkv_s, dkv, o).wait()
        back_copy(3, k, dq_o, qf, o).wait()
    for k in range(1, n_sp):
        query_copy(k).wait_send()
    for cp in keys:
        cp.wait_send()
    for cp in sent:
        cp.wait()
    for cp in local:
        cp.wait()


def attention_call(kv, qin, gin, text, keep, cid):
    n_sp, px, d2 = kv.shape
    T = text.shape[1]
    L = n_sp * px
    d = d2 // 2
    outs = [(n_sp, px // 2, d2), (n_sp, px // 2, d2), (n_sp, px, d2), (n_sp, T, d2)]
    vm = pltpu.VMEM
    return pl.pallas_call(
        functools.partial(attention_kernel, n_sp, 1024),
        out_shape=[jax.ShapeDtypeStruct(s, BF16) for s in outs],
        in_specs=[ANY, ANY, ANY, VM, VM],
        out_specs=[ANY] * 4,
        scratch_shapes=[
            vm((n_sp, px, d2), BF16), vm((n_sp, px // 2, d2), BF16), vm((n_sp, px // 2, d2), BF16), vm((L, d), BF16),
            vm((n_sp, px // 2, d2), BF16),
            vm((n_sp, px // 2, d2), BF16), vm((n_sp, px, d2), BF16), vm((T, d2), BF16),
            vm((T + L, d), BF16), vm((T + L, d2), BF16), vm((2, px // 2, T + L), F32), vm((L, T + L), BF16),
            vm((L, d2), BF16), vm((L, d), F32), vm((2, px // 2, 128), F32),
            pltpu.SemaphoreType.DMA((7,)),
            pltpu.SemaphoreType.DMA((6, n_sp)),
            pltpu.SemaphoreType.DMA((6, n_sp)),
        ],
        compiler_params=params(cid),
        name="attention",
    )(kv, qin, gin, text, keep)


class Mail:
    def __init__(self, ssem, rsem):
        self.ssem, self.rsem, self.sent = ssem, rsem, []

    def send(self, src, dst, dev):
        j = len(self.sent)
        cp = remote(src, dst, self.ssem.at[j], self.rsem.at[j], dev)
        self.sent.append(cp)
        return cp


class Gather:
    def __init__(self, at, nz, ins, outs, dims, ssem, rsem):
        self.at, self.nz, self.ins, self.outs, self.dims = at, nz, ins, outs, dims
        self.ssem, self.rsem = ssem, rsem
        self.sent, self.kinds = {}, {}
        self.order = sorted(range(1, nz), key=lambda k: min(k, nz - k))

    @staticmethod
    def copies(nz):
        return 3 * nz - 1 + 7 * nz

    def view(self, a, ii, k, core, half=None):
        at, nz, r = self.at, self.nz, self.dims[a][1]
        sp = 2 * lax.rem(at.z - k + nz, nz) + core
        if half is None:
            return self.outs[a].at[ii, :, pl.ds(pl.multiple_of(sp * r, r), r), :]
        h = r // 2
        return self.outs[a].at[ii, :, pl.ds(pl.multiple_of(sp * r + half * h, h), h), :]

    def send(self, a, kind, src, dst, dev):
        j = self.kinds.setdefault(kind, len(self.kinds))
        self.sent[a, kind] = remote(src, dst, self.ssem.at[a, j], self.rsem.at[a, j], dev)

    def forward(self, a, kind, ref, dev):
        self.send(a, kind, ref, ref, dev)

    def near(self, a):
        at = self.at
        own = self.view(a, at.i, 0, at.c)
        self.send(a, ("x", 0), self.ins[a], own, at.xn)
        self.send(a, ("y", 0), self.ins[a], own, at.yn)
        self.send(a, ("s", 0), self.ins[a], own, at.sib)

    def along(self, a, ks):
        for k in ks:
            self.send(a, ("z", k), self.ins[a], self.view(a, self.at.i, 0, self.at.c), self.at.zp(k, self.nz))

    def second(self, a, ks=None):
        at = self.at
        for k in self.order if ks is None else ks:
            self.sent[a, ("z", k)].wait_recv()
            got = self.view(a, at.i, k, at.c)
            self.forward(a, ("x", k), got, at.xn)
            self.forward(a, ("y", k), got, at.yn)
            self.forward(a, ("s", k), got, at.sib)

    def third(self, a):
        at = self.at
        for k in [0] + self.order:
            self.sent[a, ("x", k)].wait_recv()
            self.forward(a, ("da", k), self.view(a, at.ix, k, at.c, 0), at.yn)
            self.forward(a, ("sx", k), self.view(a, at.ix, k, at.c), at.sib)
            self.sent[a, ("y", k)].wait_recv()
            self.forward(a, ("db", k), self.view(a, at.iy, k, at.c, 1), at.xn)
            self.forward(a, ("sy", k), self.view(a, at.iy, k, at.c), at.sib)

    def fourth(self, a):
        at = self.at
        for k in [0] + self.order:
            self.sent[a, ("da", k)].wait_recv()
            self.forward(a, ("sa", k), self.view(a, at.id, k, at.c, 0), at.sib)
            self.sent[a, ("db", k)].wait_recv()
            self.forward(a, ("sb", k), self.view(a, at.id, k, at.c, 1), at.sib)

    def complete(self, a):
        for (b, kind), cp in self.sent.items():
            if b == a and kind[0][0] == "s":
                cp.wait_recv()

    def finish(self):
        for cp in self.sent.values():
            cp.wait_send()


def img_peers(at):
    return [(lax.rem(at.i + k, 4), at.s) for k in range(1, 4)]


FORWARD_MAIL = 4 * 3 + 3 + 2 * 7 + 4 + 7 + 2 * (2 + 7) + 7


def forward_kernel(nz, width, dims, *refs):
    na = len(dims)
    chunks, refs = refs[:na], refs[na:]
    x, cot, temb, cap, w_emb, w_cap, gains, biases = refs[:8]
    outs, refs = refs[8 : 8 + na], refs[8 + na :]
    hidden_o, a0_o, res_o, a1_o, g_o, normed_o, kv_o, qf_o = refs[:8]
    st0, st1, st2, rows, ca, cb, ra, rb, ha, hb, kv_all, cap_all, emb_all = refs[8:21]
    refs = refs[21:]
    weights, refs = refs[:na], refs[na:]
    (ssem, rsem, lsem, msend, mrecv, g_s, emb, affine, mine, every, edge_s, xa, xb, ca_s, cb_s, ha_s, hb_s, ra_s, rb_s,
     aff_s, emb_s, cap_s, part, part_r, kv_s, kv_r, mod_s, mod_r, acts, hidden, res, normed, kv, qf) = refs
    n_sp = 2 * nz
    at = Place()
    line = [at.rp(k, n_sp) for k in range(1, n_sp)]
    grid = img_peers(at)
    greet(line + grid)
    mail = Mail(msend, mrecv)
    got = Gather(at, nz, chunks, weights, dims, ssem, rsem)
    PROJ, IN, OUT, QKV = range(4)
    px, c = x.shape
    height = px // width
    d = c // HEADS
    tokens = cap.shape[0]
    e = cap.shape[1] // 4
    half = px // 2
    local = []

    def copy(src, dst):
        cp = pltpu.make_async_copy(src, dst, lsem.at[len(local)])
        cp.start()
        local.append(cp)
        return cp

    embedded = silu(temb[...].astype(F32)).astype(BF16).astype(F32)
    for j in range(4):
        emb[j] = jnp.broadcast_to(embedded[:, j * e : (j + 1) * e], (8, e))
    affine[0:3] = gains[...].astype(F32)
    affine[3:6] = biases[...].astype(F32)

    def publish(j, v, edges):
        pair = channel_stats(v)
        put_rows(mine.at[j], pair)
        out = [mail.send(mine.at[j], every.at[j, at.s], dev) for dev in line]
        for ref, above, below in edges:
            if ref is None:
                edge_s[j - 1, 0] = (v[px - width :] - pair[0]).astype(BF16)
                edge_s[j - 1, 1] = (v[:width] - pair[0]).astype(BF16)
                out.append(mail.send(edge_s.at[j - 1, 0], above, line[0]))
                out.append(mail.send(edge_s.at[j - 1, 1], below, line[-1]))
            else:
                out.append(mail.send(ref.at[px - width :], above, line[0]))
                out.append(mail.send(ref.at[:width], below, line[-1]))
        every[j, at.s] = mine[j]
        return out

    def fold(v):
        return jnp.concatenate([v[:half], v[half:]], axis=1)

    greeted(n_sp + 2)
    close, far = got.order[:2], got.order[2:]
    got.along(PROJ, got.order)
    got.near(PROJ)
    got.along(IN, close)
    got.near(IN)
    stat0 = publish(0, x[...].astype(F32), [(x, xa, xb), (cot, ca_s, cb_s)])
    round1 = []
    share = tokens // 2
    part_tokens = pl.ds(pl.multiple_of(at.c * share, share), share)
    for dev in grid:
        round1.append(mail.send(affine, aff_s.at[at.i], dev))
        round1.append(mail.send(emb.at[dev[0]], emb_s.at[at.i], dev))
        round1.append(
            mail.send(cap.at[part_tokens, pl.ds(pl.multiple_of(dev[0] * e, e), e)], cap_s.at[at.i, part_tokens], dev)
        )
    own_cap = copy(cap.at[:, pl.ds(pl.multiple_of(at.i * e, e), e)], cap_s.at[at.i])
    aff_s[at.i] = affine[...]
    emb_s[at.i] = emb[at.i]
    got.near(OUT)
    own = [copy(got.ins[a], got.view(a, at.i, 0, at.c)) for a in range(na)]
    got.second(PROJ)
    got.second(IN, close[:1])
    got.along(IN, far)
    got.second(IN, close[1:])
    got.third(PROJ)
    got.along(OUT, close)
    got.second(IN, far)
    got.along(OUT, far)
    got.fourth(PROJ)
    got.third(IN)
    got.second(OUT)
    got.along(QKV, got.order)

    own_cap.wait()
    for cp in round1:
        cp.wait_recv()
    halves = []
    for dev in grid:
        here = cap_s.at[dev[0], part_tokens]
        halves.append(mail.send(here, here, at.sib))
    for cp in halves:
        cp.wait_recv()
    for j in range(4):
        part[j, :tokens] = dot(cap_s[j], w_cap[...], 1, 0)
        part[j, tokens:] = dot(emb_s[j].astype(BF16), w_emb[...], 1, 0)
    round2 = [mail.send(part.at[dev[0]], part_r.at[at.i], dev) for dev in grid]
    part_r[at.i] = part[at.i]
    cap_all[...] = cap_s[...]
    emb_all[...] = jnp.concatenate([emb_s[j][0:1] for j in range(4)] + [jnp.zeros((4, e), F32)])
    aff = jnp.concatenate([aff_s[j] for j in range(4)], axis=1)
    rows[...] = jnp.zeros_like(rows)
    for j in range(3):
        rows[j, 0:1] = aff[j : j + 1]
        rows[j, 1:2] = aff[3 + j : 4 + j]
        rows[j, 2:3] = jnp.ones((1, c), F32)

    has_up, has_dn = edge_flags(n_sp, at.s)

    def restore(j, above, below, above_o, below_o):
        for src, dst, dev in ((above, above_o, line[-1]), (below, below_o, line[0])):
            dst[...] = src[...].astype(F32) + get_rows(every[j, dev[1]])[0]

    def activate(j, v, above, below):
        center, inverse = combine_stats(every.at[j], px)
        mul = inverse * rows[j, 0:1] * rows[j, 2:3]
        add = rows[j, 1:2] * rows[j, 2:3] + rows[j, 3:4]
        for r in range(height + 2):
            top, end = r == 0, r == height + 1
            t = above[...] if top else below[...] if end else v[(r - 1) * width : r * width, :]
            t = silu((t.astype(F32) - center) * mul + add)
            if top:
                t = t * has_up
            elif end:
                t = t * has_dn
            shifted(acts.at[j], r, width, t)

    def taps(w, out, t0, t1, base):
        a3 = acts.at[0 if base is None else 1]

        def one(tap, _):
            i, j = lax.div(tap, 3), lax.rem(tap, 3)
            lhs = a3[j, pl.ds(pl.multiple_of(i * width, width), px), :]
            first = 0.0 if base is None else base[...].astype(F32)
            out[...] = dot(lhs, joined(w, tap), 1, 1) + jnp.where(tap > 0, out[...], first)
            return 0

        lax.fori_loop(t0, t1, one, 0)

    for cp in stat0:
        cp.wait_recv()
    activate(0, x, xa, xb)
    copy(acts.at[0], a0_o)
    got.fourth(IN)
    for cp in own:
        cp.wait()
    got.complete(IN)
    copy(weights[IN], outs[IN])
    taps(weights[IN], hidden, 0, 3, None)
    got.complete(PROJ)
    g = dot(cot[...], joined(weights[PROJ], 0), 1, 0).astype(BF16)
    for h in range(HEADS):
        g_s[h] = fold(g[:, h * d : (h + 1) * d])
    copy(weights[PROJ], outs[PROJ])
    round_g = [mail.send(g_s.at[dev[1]], g_o.at[at.s], dev) for dev in line]
    copy(g_s.at[at.s], g_o.at[at.s])
    taps(weights[IN], hidden, 3, 6, None)
    got.third(OUT)
    taps(weights[IN], hidden, 6, 9, None)
    stat1 = publish(1, hidden[...], [(None, ha_s, hb_s)])
    copy(hidden, hidden_o)
    for cp in round2:
        cp.wait_recv()
    total = part_r[0] + part_r[1] + part_r[2] + part_r[3]
    kv_s[...] = total[:tokens].astype(BF16)
    mod_s[...] = total[tokens:]
    round3 = []
    for dev in line:
        round3.append(mail.send(mod_s, mod_r.at[at.s], dev))
    kv_r[at.s] = kv_s[...]
    mod_r[at.s] = mod_s[...]
    got.near(QKV)
    got.second(QKV)
    got.fourth(OUT)
    got.third(QKV)
    for cp in round3 + stat1:
        cp.wait_recv()
    round_k = [mail.send(kv_s, kv_r.at[at.s], dev) for dev in line]
    mod = jnp.concatenate([mod_r[j][0:1] for j in range(n_sp)], axis=1)
    rows[1, 2:3] = 1.0 + mod[:, :c]
    rows[1, 3:4] = mod[:, c:]

    restore(1, ha_s, hb_s, ha, hb)
    activate(1, hidden, ha, hb)
    copy(acts.at[1], a1_o)
    got.fourth(QKV)
    got.complete(OUT)
    copy(weights[OUT], outs[OUT])
    taps(weights[OUT], res, 0, 9, x)
    stat2 = publish(2, res[...], [(None, ra_s, rb_s)])
    copy(res, res_o)
    for dst, src in ((ca, ca_s), (cb, cb_s)):
        dst[...] = src[...]
    got.complete(QKV)
    copy(weights[QKV], outs[QKV])
    wq = joined(weights[QKV], 0)

    for cp in stat2[: n_sp - 1]:
        cp.wait_recv()
    center, inverse = combine_stats(every.at[2], px)
    n = ((res[...] - center) * (inverse * rows[2, 0:1]) + rows[2, 1:2]).astype(BF16)
    normed[...] = n
    k = dot(n, wq[c : 2 * c], 1, 1).astype(BF16)
    v = dot(n, wq[2 * c :], 1, 1).astype(BF16)
    q = (dot(n, wq[:c], 1, 1).astype(BF16).astype(F32) * (d ** -0.5)).astype(BF16)
    for h in range(HEADS):
        lanes = slice(h * d, (h + 1) * d)
        kv[h] = jnp.concatenate([k[:, lanes], v[:, lanes]], axis=1)
    copy(kv, kv_o)
    for h in range(HEADS):
        qf[h] = fold(q[:, h * d : (h + 1) * d])
    copy(qf, qf_o)
    copy(normed, normed_o)
    for cp in stat2[n_sp - 1 :] + round_k:
        cp.wait_recv()
    kv_all[...] = kv_r[...]
    restore(2, ra_s, rb_s, ra, rb)
    st0[...] = every[0]
    st1[...] = every[1]
    st2[...] = every[2]
    for cp in local[1 + na :]:
        cp.wait()
    got.finish()
    for cp in round_g:
        cp.wait_recv()
    for cp in mail.sent:
        cp.wait_send()


def forward_call(chunks, x, cot, temb, cap, w_emb, w_cap, gains, biases, nz, width, cid):
    dims = [c.shape[:2] for c in chunks]
    na = len(dims)
    n_sp = 2 * nz
    px, c = x.shape
    padded = px + 2 * width
    tokens, wide = cap.shape
    e = wide // 4
    d2 = 2 * c // HEADS
    big = [((4, t, n_sp * r, 128), BF16) for t, r in dims]
    edge16, edge32 = ((width, c), BF16), ((width, c), F32)
    stat = ((n_sp, 8, c // 4), F32)
    outs = big + [
        ((px, c), F32), ((3, padded, c), BF16), ((px, c), F32), ((3, padded, c), BF16),
        ((n_sp, px // 2, d2), BF16), ((px, c), BF16), ((HEADS, px, d2), BF16), ((HEADS, px // 2, d2), BF16),
        stat, stat, stat, ((3, 8, c), F32), edge16, edge16, edge32, edge32, edge32, edge32,
        ((n_sp, tokens, 128), BF16), ((4, tokens, e), BF16), ((8, e), F32),
    ]
    vm = pltpu.VMEM
    return pl.pallas_call(
        functools.partial(forward_kernel, nz, width, dims),
        out_shape=[jax.ShapeDtypeStruct(s, ty) for s, ty in outs],
        in_specs=[ANY] * na + [VM, VM, VM, ANY] + [VM] * 4,
        out_specs=[ANY] * (na + 8) + [VM] * (len(outs) - na - 8),
        scratch_shapes=[vm(s, ty) for s, ty in big]
        + [
            pltpu.SemaphoreType.DMA((na, Gather.copies(nz))),
            pltpu.SemaphoreType.DMA((na, Gather.copies(nz))),
            pltpu.SemaphoreType.DMA((2 * na + 9,)),
            pltpu.SemaphoreType.DMA((FORWARD_MAIL,)),
            pltpu.SemaphoreType.DMA((FORWARD_MAIL,)),
            vm((HEADS, px // 2, d2), BF16), vm((4, 8, e), F32), vm((8, 128), F32),
            vm((3, 8, c // 4), F32), vm((3, n_sp, 8, c // 4), F32), vm((2, 2, width, c), BF16),
        ]
        + [vm(*edge16)] * 8
        + [
            vm((4, 8, 128), F32), vm((4, 8, e), F32), vm((4, tokens, e), BF16),
            vm((4, tokens + 8, 128), F32), vm((4, tokens + 8, 128), F32),
            vm((tokens, 128), BF16), vm((n_sp, tokens, 128), BF16), vm((8, 128), F32), vm((n_sp, 8, 128), F32),
            vm((2, 3, padded, c), BF16), vm((px, c), F32), vm((px, c), F32),
            vm((px, c), BF16), vm((HEADS, px, d2), BF16), vm((HEADS, px // 2, d2), BF16),
        ],
        compiler_params=params(cid),
        name="forward",
    )(*chunks, x, cot, temb, cap, w_emb, w_cap, gains, biases)


class Reducer:
    NAMES = ("d", "sb", "da", "db", "rx", "ry", "r", "zr")

    def __init__(self, at, nz, arrays, ssem, rsem):
        self.at, self.nz, self.arrays = at, nz, arrays
        self.ssem, self.rsem = ssem, rsem
        self.sent, self.groups = {}, []

    @staticmethod
    def buffers(nz, t, r):
        return [
            pltpu.VMEM((2, 4, t, nz, r, 128), BF16),
            pltpu.VMEM((4, t, nz, r, 128), BF16),
            pltpu.VMEM((t, nz, r // 2, 128), BF16),
            pltpu.VMEM((t, nz, r // 2, 128), BF16),
            pltpu.VMEM((t, nz, r, 128), BF16),
            pltpu.VMEM((t, nz, r, 128), BF16),
            pltpu.VMEM((t, nz, r, 128), BF16),
            pltpu.VMEM((nz - 1, t, r, 128), BF16),
        ]

    def send(self, g, j, src, dst, dev):
        self.sent[g, j] = remote(src, dst, self.ssem.at[g, j], self.rsem.at[g, j], dev)

    def add(self, a, t0, t1):
        g = len(self.groups)
        self.groups.append((a, t0, t1))
        b = self.arrays[a][1]
        self.send(g, 0, b["d"].at[1 - self.at.c, :, t0:t1], b["sb"].at[:, t0:t1], self.at.sib)

    def run(self, stage, *groups):
        one = (self.stage1, self.stage2, self.stage3, self.stage4)[stage - 1]
        for g in groups:
            one(g, *self.groups[g])

    def stage1(self, g, a, t0, t1):
        b, at = self.arrays[a][1], self.at
        d, sb = b["d"], b["sb"]
        self.sent[g, 0].wait_recv()
        n = t1 - t0

        def add(j, _):
            ii, tt = lax.div(j, n), t0 + lax.rem(j, n)
            d[at.c, ii, tt] = (d[at.c, ii, tt].astype(F32) + sb[ii, tt].astype(F32)).astype(BF16)
            return 0

        lax.fori_loop(0, 4 * n, add, 0)
        h = d.shape[4] // 2
        self.send(g, 1, d.at[at.c, at.id, t0:t1, :, :h], b["da"].at[t0:t1], at.yn)
        self.send(g, 2, d.at[at.c, at.id, t0:t1, :, h:], b["db"].at[t0:t1], at.xn)

    def stage2(self, g, a, t0, t1):
        b, at = self.arrays[a][1], self.at
        d = b["d"]
        h = d.shape[4] // 2
        self.sent[g, 1].wait_recv()
        self.sent[g, 2].wait_recv()

        def add(tt, _):
            d[at.c, at.ix, tt, :, :h] = (
                d[at.c, at.ix, tt, :, :h].astype(F32) + b["da"][tt].astype(F32)
            ).astype(BF16)
            d[at.c, at.iy, tt, :, h:] = (
                d[at.c, at.iy, tt, :, h:].astype(F32) + b["db"][tt].astype(F32)
            ).astype(BF16)
            return 0

        lax.fori_loop(t0, t1, add, 0)
        self.send(g, 3, d.at[at.c, at.ix, t0:t1], b["rx"].at[t0:t1], at.xn)
        self.send(g, 4, d.at[at.c, at.iy, t0:t1], b["ry"].at[t0:t1], at.yn)

    def stage3(self, g, a, t0, t1):
        b, at = self.arrays[a][1], self.at
        self.sent[g, 3].wait_recv()
        self.sent[g, 4].wait_recv()

        def add(tt, _):
            total = b["d"][at.c, at.i, tt].astype(F32) + b["rx"][tt].astype(F32) + b["ry"][tt].astype(F32)
            b["r"][tt] = total.astype(BF16)
            return 0

        lax.fori_loop(t0, t1, add, 0)
        for k in range(1, self.nz):
            there = lax.rem(at.z + k, self.nz)
            self.send(g, 4 + k, b["r"].at[t0:t1, there], b["zr"].at[k - 1, t0:t1], at.zp(k, self.nz))

    def stage4(self, g, a, t0, t1):
        (out, b), at = self.arrays[a], self.at
        for k in range(1, self.nz):
            self.sent[g, 4 + k].wait_recv()

        def add(tt, _):
            total = (
                b["d"][at.c, at.i, tt, at.z].astype(F32)
                + b["rx"][tt, at.z].astype(F32)
                + b["ry"][tt, at.z].astype(F32)
            )
            for k in range(1, self.nz):
                total = total + b["zr"][k - 1, tt].astype(F32)
            out[tt] = total
            return 0

        lax.fori_loop(t0, t1, add, 0)

    def finish(self):
        for cp in self.sent.values():
            cp.wait_send()


BACK_MAIL = 6 + 14 + 6 + 3 + 7 + 9 + 9
BACK_GROUPS = 7
BIG = 12


def conv_taps(t0, t1, w, ring, rsem, one):
    slots = ring.shape[0]

    def step(tap, _):
        slot = lax.rem(tap, slots)
        pltpu.make_async_copy(w.at[:, tap], ring.at[slot], rsem.at[slot]).wait()
        one(tap, jnp.concatenate([ring[slot, j] for j in range(4)], axis=-1))

        @pl.when(tap + slots < 9)
        def _():
            pltpu.make_async_copy(w.at[:, tap + slots], ring.at[slot], rsem.at[slot]).start()

        return 0

    lax.fori_loop(t0, t1, step, 0)


def ring_start(w, ring, rsem):
    for j in range(ring.shape[0]):
        pltpu.make_async_copy(w.at[:, j], ring.at[j], rsem.at[j]).start()


def backward_kernel(nz, width, *refs):
    hbm, refs = refs[:BIG], refs[BIG:]
    w_in, w_out = refs[:2]
    (st0, st1, st2, rows, ca, cb, ra, rb, ha, hb, dt_all, cap_all, emb_all, w_emb, w_cap, temb) = refs[2:18]
    output_o, image_o, s_in, s_out, s_small, g_temb, g_cap, g_wemb, g_wcap, g_aff = refs[18:28]
    refs = refs[28:]
    big, refs = refs[:BIG], refs[BIG:]
    bufs = [dict(zip(Reducer.NAMES, refs[8 * a : 8 * a + 8])) for a in range(3)]
    (bsem, gsend, grecv, msend, mrecv, ring, rsem, g3, gt, acc, ng, pre_grad, res_grad,
     mine, every, edge_s, na, nb, pa, pb, tg_s, tg_r, mod_s, mod_r,
     gc_s, gc_r, pe_s, pe_r, gs_s, gs_r, ps_s, ps_r, aff_s, aff_r, output, image_grad, osem) = refs[24:]
    n_sp = 2 * nz
    at = Place()
    line = [at.rp(k, n_sp) for k in range(1, n_sp)]
    grid = img_peers(at)
    greet(line + grid)
    loads = []
    for j in range(BIG):
        loads.append(pltpu.make_async_copy(hbm[j], big[j], bsem.at[j]))
    for cp in loads[:8]:
        cp.start()
    of, qf, dkv, w_qkv, w_proj, res, cot, normed, a3_out, hidden, a3_in, x = big
    mail = Mail(msend, mrecv)
    red = Reducer(at, nz, [(s_out, bufs[0]), (s_small, bufs[1]), (s_in, bufs[2])], gsend, grecv)
    px, c = res.shape
    height = px // width
    members = px * n_sp * (c // GROUPS)
    d = c // HEADS
    cols = 3 * c // n_sp

    def publish(j, rows01, edges):
        out = []
        put_rows(mine.at[j], rows01)
        for ref, above, below in edges:
            mean = rows01[0] / px
            edge_s[j - 1, 0] = (ref[px - width :, :] - mean).astype(BF16)
            edge_s[j - 1, 1] = (ref[:width, :] - mean).astype(BF16)
            out.append(mail.send(edge_s.at[j - 1, 0], above, line[0]))
            out.append(mail.send(edge_s.at[j - 1, 1], below, line[-1]))
        for dev in line:
            out.append(mail.send(mine.at[j], every.at[j, at.s], dev))
        every[j, at.s] = mine[j]
        return out

    for j in range(8):
        loads[j].wait()
    for cp in loads[8:]:
        cp.start()
    ring_start(w_out, ring, rsem)
    unfold = lambda v: jnp.concatenate([v[:, :d], v[:, d:]], axis=0)
    att = jnp.concatenate([unfold(of[h]) for h in range(HEADS)], axis=1)
    pg = jnp.concatenate(
        [unfold(qf[h]) for h in range(HEADS)]
        + [dkv[h][:, :d] for h in range(HEADS)]
        + [dkv[h][:, d:] for h in range(HEADS)],
        axis=1,
    )
    wq, wp = joined(w_qkv), joined(w_proj)
    ng[...] = dot(pg, wq, 1, 0)
    center2, inverse2 = combine_stats(st2, px)
    hat = (res[...] - center2) * inverse2
    u = ng[...]
    sums = (jnp.sum(u, axis=0, keepdims=True), jnp.sum(u * hat, axis=0, keepdims=True))
    greeted(n_sp + 2)
    round_2 = publish(2, sums, [(ng, na, nb)])
    gq = dot(pg, normed[...], 0, 0).astype(BF16)
    go = dot(cot[...], att, 0, 0).astype(BF16)
    small = bufs[1]["d"]
    for j in range(n_sp):
        for b in range(4):
            lanes = slice(b * 128, (b + 1) * 128)
            small[j % 2, b, 0, j // 2, :cols] = gq[j * cols : (j + 1) * cols, lanes]
            small[j % 2, b, 0, j // 2, cols:] = go[j * (c // n_sp) : (j + 1) * (c // n_sp), lanes]
    red.add(1, 0, 1)
    output[...] = (res[...] + dot(att, wp, 1, 1)).astype(BF16)
    handed = [pltpu.make_async_copy(output, output_o, osem.at[0]), pltpu.make_async_copy(image_grad, image_o, osem.at[1])]
    handed[0].start()

    first = 2 * lax.rem(at.s, nz)
    value = lax.div(at.s, nz)
    halves = []
    for j in range(2):
        blk = dt_all[first + j].astype(F32)
        halves.append(jnp.where(value > 0, blk[:, d:], blk[:, :d]))
    tg_s[...] = jnp.concatenate(halves, axis=1).astype(BF16)
    round_a = [mail.send(tg_s, tg_r.at[at.i], dev) for dev in grid]
    tg_r[at.i] = tg_s[...]

    has_up, has_dn = edge_flags(n_sp, at.s)

    def upstream(j, uu, ua, ub, center, inverse, yy, ya, yb, base, keep):
        total = combine_sums(every[j])
        mul = rows[j, 0:1] * rows[j, 2:3]
        back = group_total(total * mul) / members
        s1, s2 = back[0:1, :], back[1:2, :]
        for r in range(height + 2):
            cut = slice((r - 1) * width, r * width)
            top, end = r == 0, r == height + 1
            if top or end:
                near = line[-1] if top else line[0]
                un = (ua if top else ub)[...].astype(F32) + get_rows(every[j, near[1]])[0] / px
            else:
                un = uu[cut, :]
            yn = ya[...] if top else yb[...] if end else yy[cut, :]
            g = inverse * (un * mul - s1 - (yn - center) * inverse * s2)
            if base:
                g = g + (base[1][...] if top else base[2][...] if end else base[0][cut, :]).astype(F32)
            if top:
                g = g * has_up
            elif end:
                g = g * has_dn
            elif keep is not None:
                keep[cut, :] = g
            shifted(g3, r, width, g.astype(BF16).astype(F32))
        gt[...] = g3[1, width : width + px, :].T
        return total

    def weight_taps(a, t0, t1):
        dst = bufs[a]["d"]
        a3 = a3_in if a == 2 else a3_out

        def one(tap, _):
            i, j = lax.div(tap, 3), lax.rem(tap, 3)
            part = dot(gt[...], a3[j, pl.ds(pl.multiple_of(i * width, width), px), :], 1, 0).astype(BF16)
            r = c // n_sp
            for k in range(n_sp):
                for b in range(4):
                    dst[k % 2, b, tap, k // 2] = part[k * r : (k + 1) * r, b * 128 : (b + 1) * 128]
            return 0

        lax.fori_loop(t0, t1, one, 0)
        red.add(a, t0, t1)

    def input_taps(w):
        def one(tap, wt):
            i, j = lax.div(tap, 3), lax.rem(tap, 3)
            lhs = g3[2 - j, pl.ds(pl.multiple_of((2 - i) * width, width), px), :]
            acc[...] = dot(lhs, wt, 1, 0) + jnp.where(tap > 0, acc[...], 0.0)

        conv_taps(0, 9, w, ring, rsem, one)

    for cp in round_2:
        cp.wait_recv()
    t2 = upstream(2, ng, na, nb, center2, inverse2, res, ra, rb, (cot, ca, cb), res_grad)
    red.run(1, 0)
    loads[8].wait()
    for tap in (0, 3, 6):
        weight_taps(0, tap, tap + 3)
    red.run(2, 0)
    input_taps(w_out)
    ring_start(w_in, ring, rsem)
    for j in range(9, BIG):
        loads[j].wait()
    center1, inverse1 = combine_stats(st1, px)
    hat = (hidden[...] - center1) * inverse1
    gain1, bias1, fac1 = rows[1, 0:1], rows[1, 1:2], rows[1, 2:3]
    v = acc[...] * silu_slope(hat * (gain1 * fac1) + (bias1 * fac1 + rows[1, 3:4]))
    pre_grad[...] = v
    sums = (jnp.sum(v, axis=0, keepdims=True), jnp.sum(v * hat, axis=0, keepdims=True))
    round_1 = publish(1, sums, [(pre_grad, pa, pb)])
    red.run(1, 1, 2, 3)
    red.run(3, 0)

    exact = lambda a, b, ca_, cb_: lax.dot_general(
        a, b, (((ca_,), (cb_,)), ((), ())), preferred_element_type=F32, precision=PRECISE
    )
    tokens = tg_s.shape[0]
    share = tokens // n_sp
    for cp in round_a:
        cp.wait_recv()
    flat_tg = tg_r[...].reshape(4 * tokens, 128)
    g_wcap[...] = dot(cap_all[...].reshape(4 * tokens, cap_all.shape[2]), flat_tg, 0, 0)
    gc_s[...] = dot(flat_tg, w_cap[...], 1, 1).astype(BF16).reshape(gc_s.shape)
    round_b = []
    for dev in line:
        cut = pl.ds(pl.multiple_of(dev[1] * share, share), share)
        round_b.append(mail.send(gc_s.at[:, cut, :], gc_r.at[at.s], dev))
    gc_r[at.s] = gc_s[:, pl.ds(pl.multiple_of(at.s * share, share), share), :]

    for cp in round_1:
        cp.wait_recv()
    t1 = upstream(1, pre_grad, pa, pb, center1, inverse1, hidden, ha, hb, None, None)
    mod = jnp.concatenate([t1[1:2] * gain1 + t1[0:1] * bias1, t1[0:1]], axis=1)
    for j in range(n_sp):
        mod_s[j] = jnp.broadcast_to(mod[:, j * 128 : (j + 1) * 128], (8, 128))
    round_m = [mail.send(mod_s.at[at.s], mod_r.at[at.i], dev) for dev in grid]
    mod_r[at.i] = mod_s[at.s]
    red.run(2, 1)
    weight_taps(2, 0, 3)
    red.run(2, 2)
    weight_taps(2, 3, 6)
    red.run(2, 3)
    weight_taps(2, 6, 9)
    red.run(1, 4, 5, 6)
    input_taps(w_in)

    center0, inverse0 = combine_stats(st0, px)
    hat = (x[...].astype(F32) - center0) * inverse0
    gain0 = rows[0, 0:1]
    v = acc[...] * silu_slope(hat * gain0 + rows[0, 1:2])
    acc[...] = v
    sums = (jnp.sum(v, axis=0, keepdims=True), jnp.sum(v * hat, axis=0, keepdims=True))
    round_0 = publish(0, sums, [])
    red.run(4, 0)
    red.run(3, 1)
    red.run(2, 4)
    for cp in round_m:
        cp.wait_recv()
    mods = jnp.concatenate([mod_r[j][0:1] for j in range(4)] + [jnp.zeros((4, 128), F32)])
    emb_t = emb_all[...].T
    g_wemb[...] = sum(emb_t[:, j : j + 1] * mods[j : j + 1] for j in range(4))
    pe_s[...] = exact(mods, w_emb[...].astype(F32), 1, 1)
    round_p = [mail.send(pe_s, pe_r.at[at.s], dev) for dev in line]
    pe_r[at.s] = pe_s[...]
    for cp in round_0:
        cp.wait_recv()
    t0 = combine_sums(every[0])
    zero = jnp.zeros((2, c), F32)
    aff = jnp.concatenate([t0[1:2], t1[1:2] * fac1, t2[1:2], t0[0:1], t1[0:1] * fac1, t2[0:1], zero])
    for j in range(4):
        aff_s[j] = aff[:, j * 128 : (j + 1) * 128]
    round_e = [mail.send(aff_s.at[dev[0]], aff_r.at[at.i], dev) for dev in grid]
    aff_r[at.i] = aff_s[at.i]
    total = group_total(t0 * gain0) / members
    image_grad[...] = res_grad[...] + inverse0 * (acc[...] * gain0 - total[0:1] - hat * total[1:2])
    handed[1].start()
    for g in (2, 3):
        red.run(3, g)
        red.run(2, g + 3)
    for cp in round_b + round_p:
        cp.wait_recv()
    gc = gc_r[0].astype(F32)
    pe = pe_r[0]
    for j in range(1, n_sp):
        gc = gc + gc_r[j].astype(F32)
        pe = pe + pe_r[j]
    gs_s[...] = gc
    for j in range(4):
        ps_s[j] = jnp.broadcast_to(pe[j : j + 1], pe.shape)
    round_c = []
    for dev in grid:
        round_c.append(mail.send(gs_s.at[dev[0]], gs_r.at[at.i], dev))
        round_c.append(mail.send(ps_s.at[dev[0]], ps_r.at[at.i], dev))
    gs_r[at.i] = gs_s[at.i]
    ps_r[at.i] = ps_s[at.i]
    red.run(4, 1, 2, 3)
    red.run(3, 4, 5, 6)
    red.run(4, 4, 5, 6)
    red.finish()
    for cp in round_c + round_e:
        cp.wait_recv()
    g_cap[...] = jnp.concatenate([gs_r[j] for j in range(4)], axis=1)
    g_temb[...] = jnp.concatenate([ps_r[j] for j in range(4)], axis=1) * silu_slope(temb[...].astype(F32))
    g_aff[...] = aff_r[0] + aff_r[1] + aff_r[2] + aff_r[3]
    for cp in handed:
        cp.wait()
    for cp in mail.sent:
        cp.wait_send()


def backward_call(big, w_in, w_out, small, nz, width, cid):
    px, c = big[5].shape
    n_sp = 2 * nz
    padded = px + 2 * width
    r = c // n_sp
    rs = (big[3].shape[1] + big[4].shape[1]) // n_sp
    dt_all, cap_all = small[10], small[11]
    tokens = dt_all.shape[1]
    e = cap_all.shape[2]
    share = tokens // n_sp
    outs = [
        ((px, c), BF16), ((px, c), F32), ((9, r, 128), F32), ((9, r, 128), F32), ((1, rs, 128), F32),
        ((8, 4 * e), F32), ((share, 4 * e), F32), ((e, 128), F32), ((e, 128), F32), ((8, 128), F32),
    ]
    vm = pltpu.VMEM
    return pl.pallas_call(
        functools.partial(backward_kernel, nz, width),
        out_shape=[jax.ShapeDtypeStruct(s, ty) for s, ty in outs],
        in_specs=[ANY] * (len(big) + 2) + [VM] * len(small),
        out_specs=[ANY] * 2 + [VM] * (len(outs) - 2),
        scratch_shapes=[vm(v.shape, v.dtype) for v in big]
        + Reducer.buffers(nz, 9, r) + Reducer.buffers(nz, 1, rs) + Reducer.buffers(nz, 9, r)
        + [
            pltpu.SemaphoreType.DMA((len(big),)),
            pltpu.SemaphoreType.DMA((BACK_GROUPS, 4 + nz)),
            pltpu.SemaphoreType.DMA((BACK_GROUPS, 4 + nz)),
            pltpu.SemaphoreType.DMA((BACK_MAIL,)),
            pltpu.SemaphoreType.DMA((BACK_MAIL,)),
            vm((3, 4, c, 128), BF16),
            pltpu.SemaphoreType.DMA((3,)),
            vm((3, padded, c), BF16), vm((c, px), BF16),
            vm((px, c), F32), vm((px, c), F32), vm((px, c), F32), vm((px, c), F32),
            vm((3, 8, c // 4), F32), vm((3, n_sp, 8, c // 4), F32), vm((2, 2, width, c), BF16),
            vm((width, c), BF16), vm((width, c), BF16), vm((width, c), BF16), vm((width, c), BF16),
            vm((tokens, 128), BF16), vm((4, tokens, 128), BF16),
            vm((n_sp, 8, 128), F32), vm((4, 8, 128), F32),
            vm((4, tokens, e), BF16), vm((n_sp, 4, share, e), BF16),
            vm((8, e), F32), vm((n_sp, 8, e), F32),
            vm((4, share, e), F32), vm((4, share, e), F32),
            vm((4, 8, e), F32), vm((4, 8, e), F32),
            vm((4, 8, 128), F32), vm((4, 8, 128), F32),
            vm((px, c), BF16), vm((px, c), F32), pltpu.SemaphoreType.DMA((2,)),
        ],
        compiler_params=params(cid),
        name="backward",
    )(*big, w_in, w_out, *small)


def emit_kernel(cut, *refs):
    ins, outs, mids, loads, stores = refs[:10], refs[10:22], refs[22:31], refs[31], refs[32]
    output, image, s_in, s_out, s_small, g_temb, g_cap, g_wemb, g_wcap, g_aff = ins
    pairs = [
        (output, outs[0]), (image, outs[1]), (g_cap, outs[3]), (s_in, outs[4]), (s_out, outs[5]), (g_wemb, outs[6]),
        (s_small.at[0, :cut], outs[7]), (g_wcap, outs[8]), (s_small.at[0, cut:], outs[9]),
    ]
    copies = [pltpu.make_async_copy(src, mid, loads.at[j]) for j, ((src, _), mid) in enumerate(zip(pairs, mids))]
    for cp in copies:
        cp.start()
    backs = []
    for j, cp in enumerate(copies):
        cp.wait()
        backs.append(pltpu.make_async_copy(mids[j], pairs[j][1], stores.at[j]))
        backs[-1].start()
    outs[2][...] = g_temb[0:1, :]
    outs[10][...] = g_aff[0:3, :]
    outs[11][...] = g_aff[3:6, :]
    for cp in backs:
        cp.wait()


def emit_call(parts, cut):
    output, image, s_in, s_out, s_small, g_temb, g_cap, g_wemb, g_wcap, g_aff = parts
    rest = s_small.shape[1] - cut
    like = lambda v: jax.ShapeDtypeStruct(v.shape, v.dtype)
    f32 = lambda *s: jax.ShapeDtypeStruct(s, F32)
    shapes = [
        like(output), like(image), f32(1, g_temb.shape[1]), like(g_cap), like(s_in), like(s_out), like(g_wemb),
        f32(cut, 128), like(g_wcap), f32(rest, 128), f32(3, 128), f32(3, 128),
    ]
    in_specs = [ANY] * 10
    in_specs[5] = in_specs[9] = VM
    out_specs = [ANY] * 12
    out_specs[2] = out_specs[10] = out_specs[11] = VM
    return pl.pallas_call(
        functools.partial(emit_kernel, cut),
        out_shape=shapes,
        in_specs=in_specs,
        out_specs=out_specs,
        scratch_shapes=[pltpu.VMEM(shapes[j].shape, shapes[j].dtype) for j in (0, 1, 3, 4, 5, 6, 7, 8, 9)]
        + [pltpu.SemaphoreType.DMA((9,)), pltpu.SemaphoreType.DMA((9,))],
        compiler_params=params(),
        name="emit",
    )(*parts)


def fast_body(
    image_in, time_embed, caption, caption_mask, conv_in, conv_out, embed_proj, qkv_proj,
    caption_proj, out_proj, norm_gains, norm_biases, cotangent,
):
    n, height, width, c = image_in.shape
    n_sp = lax.axis_size("sp")
    nz = n_sp // 2
    px = height * width
    x = image_in.reshape(px, c)
    cot = cotangent.reshape(px, c)

    flat = lambda w: w.transpose(1, 2, 3, 0).reshape(9, w.shape[3], w.shape[0])
    (w_proj, w_in, w_out, w_qkv, hidden, a3_in, res, a3_out, g, normed, kv, q,
     st0, st1, st2, rows, ca, cb, ra, rb, ha, hb, kv_all, cap_all, emb_all) = forward_call(
        [out_proj.T[None], flat(conv_in), flat(conv_out), qkv_proj.T[None]], x, cot, time_embed, caption[0], embed_proj, caption_proj,
        norm_gains, norm_biases, nz, width, 0,
    )
    w_proj, w_qkv = w_proj[:, 0], w_qkv[:, 0]
    of, qf, dkv, dt_all = attention_call(kv, q, g, kv_all, caption_mask, 1)

    parts = backward_call(
        [of, qf, dkv, w_qkv, w_proj, res, cot, normed, a3_out, hidden, a3_in, x], w_in, w_out,
        [st0, st1, st2, rows, ca, cb, ra, rb, ha, hb, dt_all, cap_all, emb_all, embed_proj, caption_proj, time_embed],
        nz, width, 2,
    )
    output, image, g_temb, g_cap, s_in, s_out, g_wemb, g_qkv, g_wcap, g_out, g_gains, g_biases = emit_call(
        parts, qkv_proj.shape[1]
    )
    unflat = lambda g: g.reshape(3, 3, g.shape[1], 128).transpose(3, 0, 1, 2)
    return (
        output.reshape(image_in.shape), image.reshape(image_in.shape), g_temb, g_cap[None], unflat(s_in), unflat(s_out),
        g_wemb, g_qkv.T, g_wcap, g_out.T, g_gains, g_biases,
    )


def body(*args):
    image_in, qkv_proj = args[0], args[7]
    n, height, width, c = image_in.shape
    n_img, n_sp = lax.axis_size("img"), lax.axis_size("sp")
    fits = n == 1 and n_img == 4 and n_sp == HEADS and c == 512 and width == 64
    return fast_body(*args) if fits else plain_body(*args)


def solution(mesh):
    rows = P("img", "sp", None, None)
    kernel = P("img", None, None, "sp")
    flat = P("img", "sp")
    return jax.shard_map(
        body,
        mesh=mesh,
        in_specs=(
            rows, P("img", None), P("img", None, None), P("img", None), kernel, kernel,
            flat, flat, flat, flat, P(None, "img"), P(None, "img"), rows,
        ),
        out_specs=(
            rows, rows, P("img", None), P("img", "sp", None), kernel, kernel,
            flat, flat, flat, flat, P(None, "img"), P(None, "img"),
        ),
        check_vma=False,
    )
```
